32 devices in a mesh: seq: 8 (over y, x, core), dp: 4 (over z).
Axes of the slice: x: 2, y: 2, z: 4, core: 2. Of those that a mesh axis runs over, the one named last changes fastest.
Arguments:
- points: bfloat16 [4, 4096, 512], P('dp', 'seq'), may hold values from -6 to 6
- cotangent: bfloat16 [4, 4096, 512], P('dp', 'seq'), may hold values from -6 to 6
- dest: int32 [4, 4096], P('dp', 'seq'), may hold values from 0 to 4095, as said below
- w_qkv: bfloat16 [512, 1536], replicated
- w_proj: bfloat16 [512, 512], replicated, may hold values from -0.25 to 0.25
- gain: float32 [512], replicated, may hold values from 0.5 to 1.5
Outputs:
- grad_points: bfloat16 [4, 4096, 512], P('dp', 'seq')
- grad_qkv: float32 [512, 1536], replicated
- grad_proj: float32 [512, 512], replicated
- gain_gradient: float32 [512], replicated
The draws below stay inside these ranges and needn't reach their ends.
Inputs may be any that keep to these rules, and one draw needn't show every extreme that they name: For each scan, dest is a permutation of the 4096 positions, one serialization order of the points. Of the 512 points of one device, at most 128 have positions on any one device's range of 512 positions, and exactly 128 for some device.
All inputs are finite; a program needn't handle non-finite values.
Results may differ from the reference program's by a relative error of at most 0.013.
The reference program's roundings to bfloat16 on the way count: a program that leaves them out, or rounds other values in their place, can miss the bound.
Values may be sent and summed in bfloat16 or wider, within the bound.
No kernel may reach another device: no remote copies, remote signals or barrier semaphores. Data moves between devices by JAX's collectives and lax.ppermute only.
A program may use at most 64 MiB of HBM per device.

```python
import jax
import jax.numpy as jnp
from jax import lax

C = 512
HEADS = 8
HD = 64
PATCH = 512
P_DEV = 512
N_PTS = 4096
SCANS = 4
N_SEQ = 8


def draw_dest(key, part):

    def one_scan(scan_key):
        unit = P_DEV // N_SEQ
        key_gain, key_loss, key_source, key_target = jax.random.split(scan_key, 4)
        shift_gain = jax.random.randint(key_gain, (), 0, N_SEQ)
        shift_loss = (shift_gain + jax.random.randint(key_loss, (), 1, N_SEQ)) % N_SEQ
        device = jnp.arange(N_SEQ, dtype=jnp.int32)[:, None]
        local = jnp.arange(P_DEV, dtype=jnp.int32)[None, :]
        block = local // unit
        offset = local % unit
        moved = block == (device + shift_loss) % N_SEQ
        target = jnp.where(moved, (device + shift_gain) % N_SEQ, block)
        slot = jnp.where(moved, (device + shift_gain - shift_loss) % N_SEQ * unit + offset, device * unit + offset)
        orders = jax.vmap(lambda sub: jax.random.permutation(sub, P_DEV))(jax.random.split(key_target, N_SEQ))
        within = orders[target, slot]
        position = target * P_DEV + within
        mixing = jax.vmap(lambda sub: jax.random.permutation(sub, P_DEV))(jax.random.split(key_source, N_SEQ))
        device_full = jnp.broadcast_to(device, (N_SEQ, P_DEV))
        placed = jnp.zeros((N_SEQ, P_DEV), jnp.int32).at[device_full, mixing].set(position.astype(jnp.int32))
        return placed.reshape(-1)
    return jax.vmap(one_scan)(jax.random.split(key, SCANS))


def draw_w_qkv(key, part):
    base = jax.random.normal(key, (C, 3 * C), jnp.float32) * C ** (-0.5)
    return base.astype(jnp.bfloat16)


def block_levels(rng, dims, cuts, smallest, high):
    def one(dim, blocks):
        heights = jax.random.uniform(jax.random.fold_in(jax.random.fold_in(rng, 6), dim), (blocks,), jnp.float32, smallest / len(cuts), high / len(cuts))
        return jnp.repeat(jnp.exp(heights), dims[dim] // blocks).reshape((-1,) + (1,) * (len(dims) - dim - 1))

    level = one(*cuts[0])
    for cut in cuts[1:]:
        level = level * one(*cut)
    return level


def noise(rng, extent, deviation, limit, cuts=(), kind=jnp.bfloat16):
    array = jax.random.normal(rng, extent, jnp.float32) * deviation
    if len(cuts) > 0:
        array = block_levels(rng, extent, cuts, -0.22, 0.18) * array
    return jnp.clip(array, min=-limit, max=limit).astype(kind)


def setup_inputs(seed: int = 0) -> dict:
    key_list = jax.random.split(jax.random.key(seed), 7)
    points = noise(key_list[0], (SCANS, N_PTS, C), 1.0, 6.0, ((0, 4), (1, 8)))
    cotangent = noise(key_list[1], (SCANS, N_PTS, C), 1.0, 6.0, ((0, 4), (1, 8)))
    dest = draw_dest(jax.random.fold_in(key_list[6], 71), 0)
    w_qkv = draw_w_qkv(jax.random.fold_in(key_list[6], 71), 0)
    w_proj = noise(key_list[4], (C, C), C ** -0.5, 0.25)
    gain = jnp.clip(1.0 + 0.1 * jax.random.normal(key_list[5], (C,), jnp.float32), 0.5, 1.5)
    return dict(points=points, cotangent=cotangent, dest=dest, w_qkv=w_qkv, w_proj=w_proj, gain=gain)


def block_backward(serial, serial_grad, w_qkv, w_proj, gain):
    rows_all = serial.shape[0]
    feats = serial.astype(jnp.float32)
    centered_input = feats - lax.optimization_barrier(jnp.mean(feats, axis=1, keepdims=True))
    inverse_deviation = lax.rsqrt(lax.optimization_barrier(jnp.mean(centered_input * centered_input, axis=1, keepdims=True)) + 1e-05)
    standardized_input = centered_input * inverse_deviation
    normalized_input = (standardized_input * gain[None, :]).astype(jnp.bfloat16)
    qkv = jnp.dot(normalized_input, w_qkv, preferred_element_type=jnp.float32).astype(jnp.bfloat16)
    d_attn = jnp.dot(serial_grad, w_proj.T, preferred_element_type=jnp.float32).astype(jnp.bfloat16)
    patches = rows_all // PATCH
    scale = 1.0 / HD ** 0.5
    attn_list, dq_list, dk_list, dv_list = ([], [], [], [])
    for head_idx in range(HEADS):
        lo_col = head_idx * HD
        query = qkv[:, lo_col:lo_col + HD].reshape(patches, PATCH, HD).astype(jnp.float32)
        keys = qkv[:, C + lo_col:C + lo_col + HD].reshape(patches, PATCH, HD).astype(jnp.float32)
        values = qkv[:, 2 * C + lo_col:2 * C + lo_col + HD].reshape(patches, PATCH, HD).astype(jnp.float32)
        grad_head = d_attn[:, lo_col:lo_col + HD].reshape(patches, PATCH, HD).astype(jnp.float32)
        scores = jnp.einsum('pqd,pkd->pqk', query, keys) * scale
        top = lax.optimization_barrier(jnp.max(scores, axis=2, keepdims=True))
        expo = jnp.exp(scores - top)
        probs = expo / lax.optimization_barrier(jnp.sum(expo, axis=2, keepdims=True))
        probs_b = probs.astype(jnp.bfloat16).astype(jnp.float32)
        attn_list.append(jnp.einsum('pqk,pkd->pqd', probs_b, values).astype(jnp.bfloat16).reshape(rows_all, HD))
        d_probs = jnp.einsum('pqd,pkd->pqk', grad_head, values)
        d_scores = probs * (d_probs - lax.optimization_barrier(jnp.sum(d_probs * probs, axis=2, keepdims=True))) * scale
        d_scores = d_scores.astype(jnp.bfloat16).astype(jnp.float32)
        dq_list.append(jnp.einsum('pqk,pkd->pqd', d_scores, keys).astype(jnp.bfloat16).reshape(rows_all, HD))
        dk_list.append(jnp.einsum('pqk,pqd->pkd', d_scores, query).astype(jnp.bfloat16).reshape(rows_all, HD))
        dv_list.append(jnp.einsum('pqk,pqd->pkd', probs_b, grad_head).astype(jnp.bfloat16).reshape(rows_all, HD))
    attn = jnp.concatenate(attn_list, axis=1)
    d_qkv = jnp.concatenate(dq_list + dk_list + dv_list, axis=1)
    grad_proj = jnp.dot(attn.T, serial_grad, preferred_element_type=jnp.float32)
    grad_qkv = jnp.dot(normalized_input.T, d_qkv, preferred_element_type=jnp.float32)
    normalized_gradient = jnp.dot(d_qkv, w_qkv.T, preferred_element_type=jnp.float32)
    gain_gradient = lax.optimization_barrier(jnp.sum(normalized_gradient * standardized_input, axis=0))
    gain_scaled = normalized_gradient * gain[None, :]
    residual_branch = inverse_deviation * (gain_scaled - lax.optimization_barrier(jnp.mean(gain_scaled, axis=1, keepdims=True)) - standardized_input * lax.optimization_barrier(jnp.mean(gain_scaled * standardized_input, axis=1, keepdims=True)))
    serial_dx = (serial_grad.astype(jnp.float32) + residual_branch).astype(jnp.bfloat16)
    return (serial_dx, grad_qkv, grad_proj, gain_gradient)

def reference(points, cotangent, dest, w_qkv, w_proj, gain):

    def one_scan(operands):
        feats, grads, places = operands
        serial = jnp.zeros_like(feats).at[places].set(feats)
        serial_grad = jnp.zeros_like(grads).at[places].set(grads)
        serial_dx, grad_qkv, grad_proj, gain_gradient = block_backward(serial, serial_grad, w_qkv, w_proj, gain)
        return (serial_dx[places], grad_qkv, grad_proj, gain_gradient)
    grad_points, grad_qkv, grad_proj, gain_gradient = lax.map(one_scan, (points, cotangent, dest))
    return (grad_points, lax.optimization_barrier(jnp.sum(grad_qkv, axis=0)), lax.optimization_barrier(jnp.sum(grad_proj, axis=0)), lax.optimization_barrier(jnp.sum(gain_gradient, axis=0)))
```

```python
import functools

import jax
import jax.numpy as jnp
from jax import lax
from jax.experimental import pallas as pl
from jax.experimental.pallas import tpu as pltpu
from jax.sharding import PartitionSpec as P

HEADS = 8
PATCH = 512
EXTRA = 16
LANES = 128
VMEM_LIMIT = 48 * 1024 * 1024
F32 = jnp.float32
BF16 = jnp.bfloat16
NN = (((1,), (0,)), ((), ()))
NT = (((1,), (1,)), ((), ()))


def mm(lhs, rhs, dims=NN):
    return lax.dot_general(lhs, rhs, dims, preferred_element_type=F32)


def iota(shape, dim):
    return lax.broadcasted_iota(jnp.int32, shape, dim)


def hot(mask):
    return jnp.where(mask, jnp.float32(1), jnp.float32(0)).astype(BF16)


def column_hot(row, count):
    size = row.shape[1]
    column = jnp.transpose(jnp.broadcast_to(row, (LANES, size)))
    lane = iota((size, LANES), 1)
    return jnp.concatenate([hot(column == lane + j * LANES) for j in range(count // LANES)], axis=1)


def pack_kernel(n_seq, capacity, me_ref, dest_ref, feats_ref, grads_ref, feats_out, grads_out, slot_out):
    rows, width = feats_ref.shape
    slots = n_seq * capacity
    shift = rows.bit_length() - 1
    places = dest_ref[...]
    owner = lax.shift_right_logical(places, shift)
    within = lax.bitwise_and(places, rows - 1) + 1
    member = iota((n_seq, rows), 0) == owner
    upper = hot(iota((rows, rows), 0) <= iota((rows, rows), 1))
    counts = mm(hot(member), upper)
    rank = jnp.sum(jnp.where(member, counts, 0.0), axis=0, keepdims=True).astype(jnp.int32) - 1
    slot = owner * capacity + rank
    slot_out[...] = slot
    select = hot(iota((slots, rows), 0) == slot)
    feats = mm(select, feats_ref[...]).astype(BF16)
    target = rank + me_ref[0] * capacity
    upper_half = target >= width
    high = lax.shift_right_logical(within, 8).astype(F32)
    low = lax.bitwise_and(within, 255).astype(F32)
    line = iota((n_seq * EXTRA, rows), 0)
    kind = lax.bitwise_and(line, EXTRA - 1)
    digit = jnp.where(kind < 2, high, low)
    wanted = (
        (lax.shift_right_logical(line, EXTRA.bit_length() - 1) == owner)
        & (kind < 4)
        & ((lax.bitwise_and(kind, 1) == 1) == upper_half)
    )
    digits = jnp.where(wanted, digit, 0.0).astype(BF16)
    spread = hot(iota((width, rows), 0) == lax.bitwise_and(target, width - 1))
    position = mm(digits, spread, NT).astype(BF16)
    block = capacity + EXTRA
    for d in range(n_seq):
        feats_out[d * block : d * block + capacity, :] = feats[d * capacity : (d + 1) * capacity]
        feats_out[d * block + capacity : (d + 1) * block, :] = position[d * EXTRA : (d + 1) * EXTRA]
    grads_out[...] = mm(select, grads_ref[...]).astype(BF16)


def forward_kernel(
    n_seq,
    capacity,
    recv_ref,
    w_ref,
    gain_ref,
    pos_out,
    xhat_out,
    inv_out,
    normed_out,
    qkv_out,
    attn_out,
    probs_out,
    trans,
):
    width = w_ref.shape[0]
    rows = xhat_out.shape[0]
    head = width // HEADS
    pair = 2 * head
    step = pl.program_id(0)

    @pl.when(step == 0)
    def _():
        block = capacity + EXTRA
        tile = recv_ref[capacity:block, :].astype(F32)
        for s in range(1, n_seq):
            tile = tile + recv_ref[s * block + capacity : (s + 1) * block, :].astype(F32)
        high = jnp.concatenate([tile[0:1], tile[1:2]], axis=1)
        low = jnp.concatenate([tile[2:3], tile[3:4]], axis=1)
        pos = (high * 256.0 + low).astype(jnp.int32) - 1
        pos_out[...] = pos
        place = hot(iota((rows, n_seq * capacity), 0) == pos)
        values = jnp.concatenate(
            [recv_ref[s * block : s * block + capacity, :] for s in range(n_seq)], axis=0
        )
        feats = mm(place, values)
        centered = feats - jnp.mean(feats, axis=1, keepdims=True)
        inv = lax.rsqrt(jnp.mean(centered * centered, axis=1, keepdims=True) + 1e-05)
        xhat = centered * inv
        xhat_out[...] = xhat
        inv_out[...] = jnp.broadcast_to(inv, inv_out.shape)
        normed = (xhat * gain_ref[...]).astype(BF16)
        normed_out[...] = normed
        qkv = mm(normed, w_ref[...])
        qkv_out[...] = qkv.astype(BF16)
        trans[...] = jnp.transpose(qkv).astype(BF16)

    lo = pl.multiple_of(step * pair, pair)
    keys = qkv_out[:, pl.ds(pl.multiple_of(width + step * pair, pair), pair)]
    query_t = trans[pl.ds(lo, pair), :] * BF16(0.125)
    zero = jnp.zeros((head, rows), BF16)
    for j in range(2):
        part = query_t[j * head : (j + 1) * head]
        part = jnp.concatenate([part, zero] if j == 0 else [zero, part], axis=0)
        scores = mm(keys, part)
        expo = jnp.exp(scores - jnp.max(scores, axis=0, keepdims=True))
        probs = expo * (1.0 / jnp.sum(expo, axis=0, keepdims=True))
        probs_out[j] = probs
        values_t = trans[pl.ds(pl.multiple_of(2 * width + step * pair + j * head, head), head), :]
        attn_out[j * head : (j + 1) * head, :] = mm(values_t, probs.astype(BF16)).astype(BF16)


def backward_kernel(
    recv_ref,
    pos_ref,
    w_qkv_ref,
    w_proj_ref,
    gain_ref,
    xhat_ref,
    inv_ref,
    normed_ref,
    qkv_ref,
    attn_ref,
    probs_ref,
    grad_qkv_out,
    grad_proj_out,
    gain_out,
    back_out,
    serial_grad,
    d_attn,
    d_attn_t,
    keys_t,
    d_qkv,
):
    width = w_proj_ref.shape[0]
    rows = xhat_ref.shape[0]
    head = width // HEADS
    pair = 2 * head
    step = pl.program_id(0)

    @pl.when(step == 0)
    def _():
        place = hot(iota((rows, recv_ref.shape[0]), 0) == pos_ref[...])
        grads = mm(place, recv_ref[...]).astype(BF16)
        serial_grad[...] = grads
        d_att = mm(grads, w_proj_ref[...], NT).astype(BF16)
        d_attn[...] = d_att
        d_attn_t[...] = jnp.transpose(d_att.astype(F32)).astype(BF16)
        keys_t[...] = jnp.transpose(qkv_ref[:, width : 2 * width].astype(F32)).astype(BF16)

    lo = pl.multiple_of(step * pair, pair)
    queries = qkv_ref[:, pl.ds(lo, pair)]
    values = qkv_ref[:, pl.ds(pl.multiple_of(2 * width + step * pair, pair), pair)]
    d_att_t = d_attn_t[pl.ds(lo, pair), :] * BF16(0.125)
    d_att = d_attn[:, pl.ds(lo, pair)]
    zero = jnp.zeros((head, rows), BF16)
    d_q, d_k, d_v = [], [], []
    for j in range(2):
        part = d_att_t[j * head : (j + 1) * head]
        part = jnp.concatenate([part, zero] if j == 0 else [zero, part], axis=0)
        probs = probs_ref[j]
        d_probs = mm(values, part)
        total = jnp.sum(d_probs * probs, axis=0, keepdims=True)
        d_scores = (probs * (d_probs - total)).astype(BF16)
        k_t = keys_t[pl.ds(pl.multiple_of(step * pair + j * head, head), head), :]
        d_q.append(mm(k_t, d_scores))
        d_k.append(mm(d_scores, queries))
        d_v.append(mm(probs.astype(BF16), d_att))
    first = iota((rows, pair), 1) < head
    d_qkv[:, pl.ds(lo, pair)] = jnp.transpose(jnp.concatenate(d_q, axis=0)).astype(BF16)
    d_qkv[:, pl.ds(pl.multiple_of(width + step * pair, pair), pair)] = jnp.where(
        first, d_k[0], d_k[1]
    ).astype(BF16)
    d_qkv[:, pl.ds(pl.multiple_of(2 * width + step * pair, pair), pair)] = jnp.where(
        first, d_v[0], d_v[1]
    ).astype(BF16)

    @pl.when(step == pl.num_programs(0) - 1)
    def _():
        normed_t = jnp.transpose(normed_ref[...].astype(F32)).astype(BF16)
        grad_qkv_out[...] = mm(normed_t, d_qkv[...])
        grad_proj_out[...] = mm(attn_ref[...], serial_grad[...])
        d_normed = mm(d_qkv[...], w_qkv_ref[...], NT)
        xhat = xhat_ref[...]
        gain_out[...] = jnp.sum(d_normed * xhat, axis=0, keepdims=True)
        scaled = d_normed * gain_ref[...]
        residual = inv_ref[:, 0:1] * (
            scaled
            - jnp.mean(scaled, axis=1, keepdims=True)
            - xhat * jnp.mean(scaled * xhat, axis=1, keepdims=True)
        )
        serial_dx = (serial_grad[...].astype(F32) + residual).astype(BF16)
        back_out[...] = mm(column_hot(pos_ref[...], rows), serial_dx).astype(BF16)


def unpack_kernel(slot_ref, recv_ref, out_ref):
    out_ref[...] = mm(column_hot(slot_ref[...], recv_ref.shape[0]), recv_ref[...]).astype(BF16)


def whole(shape):
    return pl.BlockSpec(shape, lambda *_: (0,) * len(shape))


def shape_of(shape, dtype):
    return jax.ShapeDtypeStruct(shape, dtype)


def per_device(points, cotangent, dest, w_qkv, w_proj, gain):
    feats = points[0]
    grads = cotangent[0]
    rows, width = feats.shape
    n_seq = lax.axis_size("seq")
    capacity = 2 * (rows // n_seq)
    slots = n_seq * capacity
    block = capacity + EXTRA
    pairs = HEADS // 2
    pair = width // pairs
    me = jnp.reshape(lax.axis_index("seq").astype(jnp.int32), (1,))
    gain_row = gain.reshape(1, width)
    params = pltpu.CompilerParams(vmem_limit_bytes=VMEM_LIMIT)
    in_vmem = pl.BlockSpec(memory_space=pltpu.VMEM)

    feats_sent, grads_sent, slot = pl.pallas_call(
        functools.partial(pack_kernel, n_seq, capacity),
        out_shape=(
            shape_of((n_seq * block, width), BF16),
            shape_of((slots, width), BF16),
            shape_of((1, rows), jnp.int32),
        ),
        in_specs=[pl.BlockSpec(memory_space=pltpu.SMEM), in_vmem, in_vmem, in_vmem],
        out_specs=[in_vmem] * 3,
        compiler_params=params,
        cost_estimate=pl.CostEstimate(flops=2 * slots * rows * width * 2, bytes_accessed=4 << 20, transcendentals=0),
        name="pack",
    )(me, dest, feats, grads)

    def exchange(sent, size):
        sent = sent.reshape(n_seq, size, width)
        got = lax.all_to_all(sent, "seq", split_axis=0, concat_axis=0, tiled=True)
        return got.reshape(n_seq * size, width)

    feats_got = exchange(feats_sent, block)
    grads_got = exchange(grads_sent, capacity)

    pos, xhat, inv, normed, qkv, attn_t, probs = pl.pallas_call(
        functools.partial(forward_kernel, n_seq, capacity),
        grid=(pairs,),
        out_shape=(
            shape_of((1, slots), jnp.int32),
            shape_of((rows, width), F32),
            shape_of((rows, LANES), F32),
            shape_of((rows, width), BF16),
            shape_of((rows, 3 * width), BF16),
            shape_of((width, rows), BF16),
            shape_of((HEADS, rows, rows), F32),
        ),
        in_specs=[whole((n_seq * block, width)), whole((width, 3 * width)), whole((1, width))],
        out_specs=[
            whole((1, slots)),
            whole((rows, width)),
            whole((rows, LANES)),
            whole((rows, width)),
            whole((rows, 3 * width)),
            pl.BlockSpec((pair, rows), lambda i: (i, 0)),
            pl.BlockSpec((2, rows, rows), lambda i: (i, 0, 0)),
        ],
        scratch_shapes=[pltpu.VMEM((3 * width, rows), BF16)],
        compiler_params=params,
        cost_estimate=pl.CostEstimate(
            flops=6 * rows * width * width + 8 * HEADS * rows * rows * pair,
            bytes_accessed=16 << 20,
            transcendentals=HEADS * rows * rows,
        ),
        name="forward",
    )(feats_got, w_qkv, gain_row)

    grad_qkv, grad_proj, gain_grad, back = pl.pallas_call(
        backward_kernel,
        grid=(pairs,),
        out_shape=(
            shape_of((width, 3 * width), F32),
            shape_of((width, width), F32),
            shape_of((1, width), F32),
            shape_of((slots, width), BF16),
        ),
        in_specs=[
            whole((slots, width)),
            whole((1, slots)),
            whole((width, 3 * width)),
            whole((width, width)),
            whole((1, width)),
            whole((rows, width)),
            whole((rows, LANES)),
            whole((rows, width)),
            whole((rows, 3 * width)),
            whole((width, rows)),
            pl.BlockSpec((2, rows, rows), lambda i: (i, 0, 0)),
        ],
        out_specs=[
            whole((width, 3 * width)),
            whole((width, width)),
            whole((1, width)),
            whole((slots, width)),
        ],
        scratch_shapes=[
            pltpu.VMEM((rows, width), BF16),
            pltpu.VMEM((rows, width), BF16),
            pltpu.VMEM((width, rows), BF16),
            pltpu.VMEM((width, rows), BF16),
            pltpu.VMEM((rows, 3 * width), BF16),
        ],
        compiler_params=params,
        cost_estimate=pl.CostEstimate(
            flops=14 * rows * width * width + 8 * HEADS * rows * rows * pair,
            bytes_accessed=24 << 20,
            transcendentals=0,
        ),
        name="backward",
    )(grads_got, pos, w_qkv, w_proj, gain_row, xhat, inv, normed, qkv, attn_t, probs)

    returned = exchange(back, capacity)
    grad_local = pl.pallas_call(
        unpack_kernel,
        out_shape=shape_of((rows, width), BF16),
        in_specs=[in_vmem] * 2,
        out_specs=in_vmem,
        compiler_params=params,
        cost_estimate=pl.CostEstimate(flops=2 * slots * rows * width, bytes_accessed=2 << 20, transcendentals=0),
        name="unpack",
    )(slot, returned)
    grad_qkv, grad_proj, gain_grad = lax.psum((grad_qkv, grad_proj, gain_grad[0]), ("seq", "dp"))
    return (grad_local[None], grad_qkv, grad_proj, gain_grad)


def solution(mesh):
    return jax.shard_map(
        per_device,
        mesh=mesh,
        in_specs=(P("dp", "seq", None), P("dp", "seq", None), P("dp", "seq"), P(), P(), P()),
        out_specs=(P("dp", "seq", None), P(), P(), P()),
        check_vma=False,
    )
```

```python
import functools

import jax
import jax.numpy as jnp
from jax import lax
from jax.experimental import pallas as pl
from jax.experimental.pallas import tpu as pltpu
from jax.sharding import PartitionSpec as P

HEADS = 8
PATCH = 512
EXTRA = 16
LANES = 128
MIB = 1024 * 1024
F32 = jnp.float32
BF16 = jnp.bfloat16
NN = (((1,), (0,)), ((), ()))
NT = (((1,), (1,)), ((), ()))


def mm(lhs, rhs, dims=NN):
    return lax.dot_general(lhs, rhs, dims, preferred_element_type=F32)


def iota(shape, dim):
    return lax.broadcasted_iota(jnp.int32, shape, dim)


def hot(mask):
    return jnp.where(mask, jnp.float32(1), jnp.float32(0)).astype(BF16)


def column_hot(row, count):
    size = row.shape[1]
    column = jnp.transpose(jnp.broadcast_to(row, (LANES, size)))
    lane = iota((size, LANES), 1)
    return jnp.concatenate([hot(column == lane + j * LANES) for j in range(count // LANES)], axis=1)


def pack_kernel(n_seq, capacity, me_ref, dest_ref, feats_ref, grads_ref, feats_out, grads_out, slot_out):
    rows, width = feats_ref.shape
    slots = n_seq * capacity
    shift = rows.bit_length() - 1
    places = dest_ref[...]
    owner = lax.shift_right_logical(places, shift)
    within = lax.bitwise_and(places, rows - 1) + 1
    member = iota((n_seq, rows), 0) == owner
    upper = hot(iota((rows, rows), 0) <= iota((rows, rows), 1))
    counts = mm(hot(member), upper)
    rank = jnp.sum(jnp.where(member, counts, 0.0), axis=0, keepdims=True).astype(jnp.int32) - 1
    slot = owner * capacity + rank
    slot_out[...] = slot
    select = hot(iota((slots, rows), 0) == slot)
    feats = mm(select, feats_ref[...]).astype(BF16)
    target = rank + me_ref[0] * capacity
    upper_half = target >= width
    high = lax.shift_right_logical(within, 8).astype(F32)
    low = lax.bitwise_and(within, 255).astype(F32)
    line = iota((n_seq * EXTRA, rows), 0)
    kind = lax.bitwise_and(line, EXTRA - 1)
    digit = jnp.where(kind < 2, high, low)
    wanted = (
        (lax.shift_right_logical(line, EXTRA.bit_length() - 1) == owner)
        & (kind < 4)
        & ((lax.bitwise_and(kind, 1) == 1) == upper_half)
    )
    digits = jnp.where(wanted, digit, 0.0).astype(BF16)
    spread = hot(iota((width, rows), 0) == lax.bitwise_and(target, width - 1))
    position = mm(digits, spread, NT).astype(BF16)
    block = capacity + EXTRA
    for d in range(n_seq):
        feats_out[d * block : d * block + capacity, :] = feats[d * capacity : (d + 1) * capacity]
        feats_out[d * block + capacity : (d + 1) * block, :] = position[d * EXTRA : (d + 1) * EXTRA]
    grads_out[...] = mm(select, grads_ref[...]).astype(BF16)


def forward_kernel(
    n_seq,
    capacity,
    recv_ref,
    w_ref,
    gain_ref,
    pos_out,
    xhat_out,
    inv_out,
    normed_out,
    qkv_out,
    attn_out,
    probs_out,
    trans,
):
    width = w_ref.shape[0]
    rows = xhat_out.shape[0]
    head = width // HEADS
    pair = 2 * head
    step = pl.program_id(0)

    @pl.when(step == 0)
    def _():
        block = capacity + EXTRA
        tile = recv_ref[capacity:block, :].astype(F32)
        for s in range(1, n_seq):
            tile = tile + recv_ref[s * block + capacity : (s + 1) * block, :].astype(F32)
        high = jnp.concatenate([tile[0:1], tile[1:2]], axis=1)
        low = jnp.concatenate([tile[2:3], tile[3:4]], axis=1)
        pos = (high * 256.0 + low).astype(jnp.int32) - 1
        pos_out[...] = pos
        place = hot(iota((rows, n_seq * capacity), 0) == pos)
        values = jnp.concatenate(
            [recv_ref[s * block : s * block + capacity, :] for s in range(n_seq)], axis=0
        )
        feats = mm(place, values)
        centered = feats - jnp.mean(feats, axis=1, keepdims=True)
        inv = lax.rsqrt(jnp.mean(centered * centered, axis=1, keepdims=True) + 1e-05)
        xhat = centered * inv
        xhat_out[...] = xhat
        inv_out[...] = jnp.broadcast_to(inv, inv_out.shape)
        normed = (xhat * gain_ref[...]).astype(BF16)
        normed_out[...] = normed
        qkv = mm(normed, w_ref[...])
        qkv_out[...] = qkv.astype(BF16)
        trans[...] = jnp.transpose(qkv).astype(BF16)

    lo = pl.multiple_of(step * pair, pair)
    keys = qkv_out[:, pl.ds(pl.multiple_of(width + step * pair, pair), pair)]
    query_t = trans[pl.ds(lo, pair), :] * BF16(0.125)
    zero = jnp.zeros((head, rows), BF16)
    for j in range(2):
        part = query_t[j * head : (j + 1) * head]
        part = jnp.concatenate([part, zero] if j == 0 else [zero, part], axis=0)
        scores = mm(keys, part)
        expo = jnp.exp(scores - jnp.max(scores, axis=0, keepdims=True))
        probs = expo * (1.0 / jnp.sum(expo, axis=0, keepdims=True))
        probs_out[j] = probs
        values_t = trans[pl.ds(pl.multiple_of(2 * width + step * pair + j * head, head), head), :]
        attn_out[j * head : (j + 1) * head, :] = mm(values_t, probs.astype(BF16)).astype(BF16)


def backward_kernel(
    me_ref,
    recv_ref,
    pos_ref,
    w_qkv_ref,
    w_proj_ref,
    gain_ref,
    xhat_ref,
    inv_ref,
    normed_ref,
    qkv_ref,
    attn_ref,
    probs_ref,
    send_out,
    keep_out,
    back_out,
    serial_grad,
    d_attn,
    d_attn_t,
    keys_t,
    d_qkv,
    normed_t,
    gain_column,
):
    width = w_proj_ref.shape[0]
    rows = xhat_ref.shape[0]
    head = width // HEADS
    pair = 2 * head
    step = pl.program_id(0)

    @pl.when(step == 0)
    def _():
        place = hot(iota((rows, recv_ref.shape[0]), 0) == pos_ref[...])
        grads = mm(place, recv_ref[...]).astype(BF16)
        serial_grad[...] = grads
        d_att = mm(grads, w_proj_ref[...], NT).astype(BF16)
        d_attn[...] = d_att
        d_attn_t[...] = jnp.transpose(d_att.astype(F32)).astype(BF16)
        keys_t[...] = jnp.transpose(qkv_ref[:, width : 2 * width].astype(F32)).astype(BF16)

    lo = pl.multiple_of(step * pair, pair)
    queries = qkv_ref[:, pl.ds(lo, pair)]
    values = qkv_ref[:, pl.ds(pl.multiple_of(2 * width + step * pair, pair), pair)]
    d_att_t = d_attn_t[pl.ds(lo, pair), :] * BF16(0.125)
    d_att = d_attn[:, pl.ds(lo, pair)]
    zero = jnp.zeros((head, rows), BF16)
    d_q, d_k, d_v = [], [], []
    for j in range(2):
        part = d_att_t[j * head : (j + 1) * head]
        part = jnp.concatenate([part, zero] if j == 0 else [zero, part], axis=0)
        probs = probs_ref[j]
        d_probs = mm(values, part)
        total = jnp.sum(d_probs * probs, axis=0, keepdims=True)
        d_scores = (probs * (d_probs - total)).astype(BF16)
        k_t = keys_t[pl.ds(pl.multiple_of(step * pair + j * head, head), head), :]
        d_q.append(mm(k_t, d_scores))
        d_k.append(mm(d_scores, queries))
        d_v.append(mm(probs.astype(BF16), d_att))
    first = iota((rows, pair), 1) < head
    d_qkv[:, pl.ds(lo, pair)] = jnp.transpose(jnp.concatenate(d_q, axis=0)).astype(BF16)
    d_qkv[:, pl.ds(pl.multiple_of(width + step * pair, pair), pair)] = jnp.where(
        first, d_k[0], d_k[1]
    ).astype(BF16)
    d_qkv[:, pl.ds(pl.multiple_of(2 * width + step * pair, pair), pair)] = jnp.where(
        first, d_v[0], d_v[1]
    ).astype(BF16)

    @pl.when(step == pl.num_programs(0) - 1)
    def _():
        normed_t[...] = jnp.transpose(normed_ref[...].astype(F32)).astype(BF16)
        d_normed = mm(d_qkv[...], w_qkv_ref[...], NT)
        xhat = xhat_ref[...]
        gain_row = jnp.sum(d_normed * xhat, axis=0, keepdims=True)
        gain_column[...] = jnp.transpose(jnp.broadcast_to(gain_row, (LANES, width)))
        half = width // 2
        bit = lax.bitwise_and(me_ref[0], 1)
        for out, start in ((send_out, (1 - bit) * half), (keep_out, bit * half)):
            part = pl.ds(pl.multiple_of(start, half), half)
            out[:, : 3 * width] = mm(normed_t[part, :], d_qkv[...])
            out[:, 3 * width : 4 * width] = mm(attn_ref[part, :], serial_grad[...])
            out[:, 4 * width :] = gain_column[part, :]
        scaled = d_normed * gain_ref[...]
        residual = inv_ref[:, 0:1] * (
            scaled
            - jnp.mean(scaled, axis=1, keepdims=True)
            - xhat * jnp.mean(scaled * xhat, axis=1, keepdims=True)
        )
        serial_dx = (serial_grad[...].astype(F32) + residual).astype(BF16)
        back_out[...] = mm(column_hot(pos_ref[...], rows), serial_dx).astype(BF16)


def unpack_kernel(slot_ref, recv_ref, out_ref):
    out_ref[...] = mm(column_hot(slot_ref[...], recv_ref.shape[0]), recv_ref[...]).astype(BF16)


def whole(shape):
    return pl.BlockSpec(shape, lambda *_: (0,) * len(shape), pipeline_mode=pl.Buffered(1))


def params(mib):
    return pltpu.CompilerParams(vmem_limit_bytes=mib * MIB)


def shape_of(shape, dtype):
    return jax.ShapeDtypeStruct(shape, dtype)


def reduce_and_share(send, keep):
    n_seq, n_dp = lax.axis_size("seq"), lax.axis_size("dp")
    me, plane = lax.axis_index("seq"), lax.axis_index("dp")
    seq_bits = list(range(1, n_seq.bit_length() - 1))
    middle = len(seq_bits) // 2
    orders = (seq_bits, seq_bits[middle:] + seq_bits[:middle])
    odd = lax.bitwise_and(me, 1)

    def bit_of(index, bit):
        return lax.bitwise_and(lax.shift_right_logical(index, jnp.asarray(bit, index.dtype)), 1)

    steps = [("seq", [(i, i ^ 1) for i in range(n_seq)], odd)]
    for even_bit, odd_bit in zip(*orders):
        pairs = [(i, i ^ (1 << (odd_bit if i & 1 else even_bit))) for i in range(n_seq)]
        steps.append(("seq", pairs, jnp.where(odd == 1, bit_of(me, odd_bit), bit_of(me, even_bit))))
    for bit in range(n_dp.bit_length() - 1):
        steps.append(("dp", [(i, i ^ (1 << bit)) for i in range(n_dp)], bit_of(plane, bit)))

    for i, (axis, pairs, bit) in enumerate(steps):
        if i > 0:
            half = part.shape[0] // 2
            send = lax.dynamic_slice_in_dim(part, (1 - bit) * half, half)
            keep = lax.dynamic_slice_in_dim(part, bit * half, half)
        part = keep + lax.ppermute(send, axis, pairs)
    part = part.astype(BF16)
    for axis, pairs, bit in reversed(steps):
        other = lax.ppermute(part, axis, pairs)
        part = jnp.where(
            bit == 0, jnp.concatenate([part, other], axis=0), jnp.concatenate([other, part], axis=0)
        )
    return part


def per_device(points, cotangent, dest, w_qkv, w_proj, gain):
    feats = points[0]
    grads = cotangent[0]
    rows, width = feats.shape
    n_seq = lax.axis_size("seq")
    capacity = 2 * (rows // n_seq)
    slots = n_seq * capacity
    block = capacity + EXTRA
    pairs = HEADS // 2
    pair = width // pairs
    me = jnp.reshape(lax.axis_index("seq").astype(jnp.int32), (1,))
    gain_row = gain.reshape(1, width)
    smem = pl.BlockSpec(memory_space=pltpu.SMEM)
    in_vmem = pl.BlockSpec(memory_space=pltpu.VMEM)

    feats_sent, grads_sent, slot = pl.pallas_call(
        functools.partial(pack_kernel, n_seq, capacity),
        out_shape=(
            shape_of((n_seq * block, width), BF16),
            shape_of((slots, width), BF16),
            shape_of((1, rows), jnp.int32),
        ),
        in_specs=[smem, in_vmem, in_vmem, in_vmem],
        out_specs=[in_vmem] * 3,
        compiler_params=params(20),
        cost_estimate=pl.CostEstimate(flops=2 * slots * rows * width * 2, bytes_accessed=4 << 20, transcendentals=0),
        name="pack",
    )(me, dest, feats, grads)

    def exchange(sent, size):
        sent = sent.reshape(n_seq, size, width)
        got = lax.all_to_all(sent, "seq", split_axis=0, concat_axis=0, tiled=True)
        return got.reshape(n_seq * size, width)

    feats_got = exchange(feats_sent, block)
    grads_got = exchange(grads_sent, capacity)

    pos, xhat, inv, normed, qkv, attn_t, probs = pl.pallas_call(
        functools.partial(forward_kernel, n_seq, capacity),
        grid=(pairs,),
        out_shape=(
            shape_of((1, slots), jnp.int32),
            shape_of((rows, width), F32),
            shape_of((rows, LANES), F32),
            shape_of((rows, width), BF16),
            shape_of((rows, 3 * width), BF16),
            shape_of((width, rows), BF16),
            shape_of((HEADS, rows, rows), F32),
        ),
        in_specs=[whole((n_seq * block, width)), whole((width, 3 * width)), whole((1, width))],
        out_specs=[
            whole((1, slots)),
            whole((rows, width)),
            whole((rows, LANES)),
            whole((rows, width)),
            whole((rows, 3 * width)),
            pl.BlockSpec((pair, rows), lambda i: (i, 0)),
            pl.BlockSpec((2, rows, rows), lambda i: (i, 0, 0)),
        ],
        scratch_shapes=[pltpu.VMEM((3 * width, rows), BF16)],
        compiler_params=params(32),
        cost_estimate=pl.CostEstimate(
            flops=6 * rows * width * width + 8 * HEADS * rows * rows * pair,
            bytes_accessed=16 << 20,
            transcendentals=HEADS * rows * rows,
        ),
        name="forward",
    )(feats_got, w_qkv, gain_row)

    send, keep, back = pl.pallas_call(
        backward_kernel,
        grid=(pairs,),
        out_shape=(
            shape_of((width // 2, 4 * width + LANES), F32),
            shape_of((width // 2, 4 * width + LANES), F32),
            shape_of((slots, width), BF16),
        ),
        in_specs=[
            smem,
            whole((slots, width)),
            whole((1, slots)),
            whole((width, 3 * width)),
            whole((width, width)),
            whole((1, width)),
            whole((rows, width)),
            whole((rows, LANES)),
            whole((rows, width)),
            whole((rows, 3 * width)),
            whole((width, rows)),
            pl.BlockSpec((2, rows, rows), lambda i: (i, 0, 0)),
        ],
        out_specs=[
            whole((width // 2, 4 * width + LANES)),
            whole((width // 2, 4 * width + LANES)),
            whole((slots, width)),
        ],
        scratch_shapes=[
            pltpu.VMEM((rows, width), BF16),
            pltpu.VMEM((rows, width), BF16),
            pltpu.VMEM((width, rows), BF16),
            pltpu.VMEM((width, rows), BF16),
            pltpu.VMEM((rows, 3 * width), BF16),
            pltpu.VMEM((width, rows), BF16),
            pltpu.VMEM((width, LANES), F32),
        ],
        compiler_params=params(40),
        cost_estimate=pl.CostEstimate(
            flops=14 * rows * width * width + 8 * HEADS * rows * rows * pair,
            bytes_accessed=24 << 20,
            transcendentals=0,
        ),
        name="backward",
    )(me, grads_got, pos, w_qkv, w_proj, gain_row, xhat, inv, normed, qkv, attn_t, probs)

    returned = exchange(back, capacity)
    grad_local = pl.pallas_call(
        unpack_kernel,
        out_shape=shape_of((rows, width), BF16),
        in_specs=[in_vmem] * 2,
        out_specs=in_vmem,
        compiler_params=params(20),
        cost_estimate=pl.CostEstimate(flops=2 * slots * rows * width, bytes_accessed=2 << 20, transcendentals=0),
        name="unpack",
    )(slot, returned)
    total = reduce_and_share(send, keep).astype(F32)
    return (grad_local[None], total[:, : 3 * width], total[:, 3 * width : 4 * width], total[:, 4 * width])


def solution(mesh):
    return jax.shard_map(
        per_device,
        mesh=mesh,
        in_specs=(P("dp", "seq", None), P("dp", "seq", None), P("dp", "seq"), P(), P(), P()),
        out_specs=(P("dp", "seq", None), P(), P(), P()),
        check_vma=False,
    )
```

```python
import functools

import jax
import jax.numpy as jnp
from jax import lax
from jax.experimental import pallas as pl
from jax.experimental.pallas import tpu as pltpu
from jax.sharding import PartitionSpec as P

HEADS = 8
PATCH = 512
EXTRA = 16
LANES = 128
MIB = 1024 * 1024
F32 = jnp.float32
BF16 = jnp.bfloat16
NN = (((1,), (0,)), ((), ()))
NT = (((1,), (1,)), ((), ()))


def mm(lhs, rhs, dims=NN):
    return lax.dot_general(lhs, rhs, dims, preferred_element_type=F32)


def iota(shape, dim):
    return lax.broadcasted_iota(jnp.int32, shape, dim)


def hot(mask):
    return jnp.where(mask, jnp.float32(1), jnp.float32(0)).astype(BF16)


def column_hot(row, count):
    size = row.shape[1]
    column = jnp.transpose(jnp.broadcast_to(row, (LANES, size)))
    lane = iota((size, LANES), 1)
    return jnp.concatenate([hot(column == lane + j * LANES) for j in range(count // LANES)], axis=1)


def pack_kernel(n_seq, capacity, me_ref, dest_ref, feats_ref, grads_ref, slot_out, *outs):
    rows, width = feats_ref.shape
    slots = n_seq * capacity
    shift = rows.bit_length() - 1
    places = dest_ref[...]
    distance = lax.bitwise_xor(lax.shift_right_logical(places, shift), me_ref[0])
    within = lax.bitwise_and(places, rows - 1) + 1
    member = iota((n_seq, rows), 0) == distance
    upper = hot(iota((rows, rows), 0) <= iota((rows, rows), 1))
    counts = mm(hot(member), upper)
    rank = jnp.sum(jnp.where(member, counts, 0.0), axis=0, keepdims=True).astype(jnp.int32) - 1
    slot = distance * capacity + rank
    slot_out[...] = slot
    select = hot(iota((slots, rows), 0) == slot)
    feats = mm(select, feats_ref[...]).astype(BF16)
    upper_half = slot >= width
    high = lax.shift_right_logical(within, 8).astype(F32)
    low = lax.bitwise_and(within, 255).astype(F32)
    line = iota((n_seq * EXTRA, rows), 0)
    kind = lax.bitwise_and(line, EXTRA - 1)
    digit = jnp.where(kind < 2, high, low)
    wanted = (
        (lax.shift_right_logical(line, EXTRA.bit_length() - 1) == distance)
        & (kind < 4)
        & ((lax.bitwise_and(kind, 1) == 1) == upper_half)
    )
    digits = jnp.where(wanted, digit, 0.0).astype(BF16)
    spread = hot(iota((width, rows), 0) == lax.bitwise_and(slot, width - 1))
    position = mm(digits, spread, NT).astype(BF16)
    for d in range(n_seq):
        outs[d][:capacity, :] = feats[d * capacity : (d + 1) * capacity]
        outs[d][capacity:, :] = position[d * EXTRA : (d + 1) * EXTRA]
    grads = mm(select, grads_ref[...]).astype(BF16)
    for d in range(n_seq):
        outs[n_seq + d][...] = grads[d * capacity : (d + 1) * capacity]


def forward_kernel(n_seq, capacity, w_hbm, gain_ref, *refs):
    recv, refs = refs[:n_seq], refs[n_seq:]
    pos_out, xhat_hbm, inv_hbm, normed_hbm, qkv_hbm, attn_out, probs_out = refs[:7]
    w_ref, xhat_ref, inv_ref, normed_ref, qkv_ref, trans, sems = refs[7:]
    width = w_ref.shape[0]
    rows = xhat_ref.shape[0]
    head = width // HEADS
    pair = 2 * head
    step = pl.program_id(0)
    w_copy = pltpu.make_async_copy(w_hbm, w_ref, sems.at[0])
    saves = [
        pltpu.make_async_copy(source, target, sems.at[1 + i])
        for i, (source, target) in enumerate(
            ((xhat_ref, xhat_hbm), (inv_ref, inv_hbm), (normed_ref, normed_hbm), (qkv_ref, qkv_hbm))
        )
    ]

    @pl.when(step == 0)
    def _():
        w_copy.start()
        tile = recv[0][capacity:, :].astype(F32)
        for s in range(1, n_seq):
            tile = tile + recv[s][capacity:, :].astype(F32)
        high = jnp.concatenate([tile[0:1], tile[1:2]], axis=1)
        low = jnp.concatenate([tile[2:3], tile[3:4]], axis=1)
        pos = (high * 256.0 + low).astype(jnp.int32) - 1
        pos_out[...] = pos
        place = hot(iota((rows, n_seq * capacity), 0) == pos)
        values = jnp.concatenate([recv[s][:capacity, :] for s in range(n_seq)], axis=0)
        feats = mm(place, values)
        centered = feats - jnp.mean(feats, axis=1, keepdims=True)
        inv = lax.rsqrt(jnp.mean(centered * centered, axis=1, keepdims=True) + 1e-05)
        xhat = centered * inv
        xhat_ref[...] = xhat
        inv_ref[...] = jnp.broadcast_to(inv, inv_ref.shape)
        normed = (xhat * gain_ref[...]).astype(BF16)
        normed_ref[...] = normed
        w_copy.wait()
        qkv = mm(normed, w_ref[...])
        qkv_ref[...] = qkv.astype(BF16)
        for save in saves:
            save.start()
        trans[...] = jnp.transpose(qkv).astype(BF16)

    lo = pl.multiple_of(step * pair, pair)
    keys = qkv_ref[:, pl.ds(pl.multiple_of(width + step * pair, pair), pair)]
    query_t = trans[pl.ds(lo, pair), :] * BF16(0.125)
    zero = jnp.zeros((head, rows), BF16)
    for j in range(2):
        part = query_t[j * head : (j + 1) * head]
        part = jnp.concatenate([part, zero] if j == 0 else [zero, part], axis=0)
        scores = mm(keys, part)
        expo = jnp.exp(scores - jnp.max(scores, axis=0, keepdims=True))
        probs = expo * (1.0 / jnp.sum(expo, axis=0, keepdims=True))
        probs_out[j] = probs
        values_t = trans[pl.ds(pl.multiple_of(2 * width + step * pair + j * head, head), head), :]
        attn_out[j * head : (j + 1) * head, :] = mm(values_t, probs.astype(BF16)).astype(BF16)

    @pl.when(step == pl.num_programs(0) - 1)
    def _():
        for save in saves:
            save.wait()


def backward_kernel(n_seq, me_ref, pos_ref, w_proj_ref, gain_ref, qkv_ref, probs_ref, *refs):
    (w_hbm, xhat_hbm, inv_hbm, normed_hbm, attn_hbm), refs = refs[:5], refs[5:]
    recv, refs = refs[:n_seq], refs[n_seq:]
    send_hbm, keep_hbm, refs = refs[0], refs[1], refs[2:]
    back, refs = refs[:n_seq], refs[n_seq:]
    w_ref, xhat_ref, inv_ref, normed_ref, attn_ref, send_ref, keep_ref, refs = *refs[:7], refs[7:]
    serial_grad, d_attn, d_attn_t, keys_t, d_qkv, normed_t, gain_column, sems = refs
    width = w_proj_ref.shape[0]
    rows = xhat_ref.shape[0]
    capacity = recv[0].shape[0]
    head = width // HEADS
    pair = 2 * head
    step = pl.program_id(0)
    loads = [
        pltpu.make_async_copy(source, target, sems.at[i])
        for i, (source, target) in enumerate(
            (
                (normed_hbm, normed_ref),
                (w_hbm, w_ref),
                (xhat_hbm, xhat_ref),
                (inv_hbm, inv_ref),
                (attn_hbm, attn_ref),
            )
        )
    ]
    saves = [
        pltpu.make_async_copy(send_ref, send_hbm, sems.at[5]),
        pltpu.make_async_copy(keep_ref, keep_hbm, sems.at[6]),
    ]

    @pl.when(step == 0)
    def _():
        for load in loads:
            load.start()
        place = hot(iota((rows, n_seq * capacity), 0) == pos_ref[...])
        grads = mm(place, jnp.concatenate([ref[...] for ref in recv], axis=0)).astype(BF16)
        serial_grad[...] = grads
        d_att = mm(grads, w_proj_ref[...], NT).astype(BF16)
        d_attn[...] = d_att
        d_attn_t[...] = jnp.transpose(d_att.astype(F32)).astype(BF16)
        keys_t[...] = jnp.transpose(qkv_ref[:, width : 2 * width].astype(F32)).astype(BF16)

    lo = pl.multiple_of(step * pair, pair)
    queries = qkv_ref[:, pl.ds(lo, pair)]
    values = qkv_ref[:, pl.ds(pl.multiple_of(2 * width + step * pair, pair), pair)]
    d_att_t = d_attn_t[pl.ds(lo, pair), :] * BF16(0.125)
    d_att = d_attn[:, pl.ds(lo, pair)]
    zero = jnp.zeros((head, rows), BF16)
    d_q, d_k, d_v = [], [], []
    for j in range(2):
        part = d_att_t[j * head : (j + 1) * head]
        part = jnp.concatenate([part, zero] if j == 0 else [zero, part], axis=0)
        probs = probs_ref[j]
        d_probs = mm(values, part)
        total = jnp.sum(d_probs * probs, axis=0, keepdims=True)
        d_scores = (probs * (d_probs - total)).astype(BF16)
        k_t = keys_t[pl.ds(pl.multiple_of(step * pair + j * head, head), head), :]
        d_q.append(mm(k_t, d_scores))
        d_k.append(mm(d_scores, queries))
        d_v.append(mm(probs.astype(BF16), d_att))
    first = iota((rows, pair), 1) < head
    d_qkv[:, pl.ds(lo, pair)] = jnp.transpose(jnp.concatenate(d_q, axis=0)).astype(BF16)
    d_qkv[:, pl.ds(pl.multiple_of(width + step * pair, pair), pair)] = jnp.where(
        first, d_k[0], d_k[1]
    ).astype(BF16)
    d_qkv[:, pl.ds(pl.multiple_of(2 * width + step * pair, pair), pair)] = jnp.where(
        first, d_v[0], d_v[1]
    ).astype(BF16)

    @pl.when(step == pl.num_programs(0) - 1)
    def _():
        for load in loads:
            load.wait()
        normed_t[...] = jnp.transpose(normed_ref[...].astype(F32)).astype(BF16)
        d_normed = mm(d_qkv[...], w_ref[...], NT)
        xhat = xhat_ref[...]
        gain_row = jnp.sum(d_normed * xhat, axis=0, keepdims=True)
        gain_column[...] = jnp.transpose(jnp.broadcast_to(gain_row, (LANES, width)))
        half = width // 2
        bit = lax.bitwise_and(me_ref[0], 1)
        for out, start, save in ((send_ref, (1 - bit) * half, saves[0]), (keep_ref, bit * half, saves[1])):
            part = pl.ds(pl.multiple_of(start, half), half)
            out[:, : 3 * width] = mm(normed_t[part, :], d_qkv[...])
            out[:, 3 * width : 4 * width] = mm(attn_ref[part, :], serial_grad[...])
            out[:, 4 * width :] = gain_column[part, :]
            save.start()
        scaled = d_normed * gain_ref[...]
        residual = inv_ref[:, 0:1] * (
            scaled
            - jnp.mean(scaled, axis=1, keepdims=True)
            - xhat * jnp.mean(scaled * xhat, axis=1, keepdims=True)
        )
        serial_dx = (serial_grad[...].astype(F32) + residual).astype(BF16)
        returned = mm(column_hot(pos_ref[...], rows), serial_dx).astype(BF16)
        for d in range(n_seq):
            back[d][...] = returned[d * capacity : (d + 1) * capacity]
        for save in saves:
            save.wait()


def unpack_kernel(slot_ref, *refs):
    values = jnp.concatenate([ref[...] for ref in refs[:-1]], axis=0)
    refs[-1][...] = mm(column_hot(slot_ref[...], values.shape[0]), values).astype(BF16)


def whole(shape):
    return pl.BlockSpec(shape, lambda *_: (0,) * len(shape), pipeline_mode=pl.Buffered(1))


def params(mib):
    return pltpu.CompilerParams(vmem_limit_bytes=mib * MIB)


def shape_of(shape, dtype):
    return jax.ShapeDtypeStruct(shape, dtype)


def by_distance(blocks, axis):
    count = len(blocks)
    return [blocks[0]] + [
        lax.ppermute(blocks[k], axis, [(i, i ^ k) for i in range(count)]) for k in range(1, count)
    ]


def chip_steps():
    n_seq, me = lax.axis_size("seq"), lax.axis_index("seq")
    bits = list(range(1, n_seq.bit_length() - 1))
    middle = len(bits) // 2
    orders = (bits, bits[middle:] + bits[:middle])
    odd = lax.bitwise_and(me, 1) == 1

    def side(bit):
        return lax.bitwise_and(lax.shift_right_logical(me, jnp.asarray(bit, me.dtype)), 1)

    steps = [([(i, i ^ 1) for i in range(n_seq)], side(0))]
    for even_bit, odd_bit in zip(*orders):
        pairs = [(i, i ^ (1 << (odd_bit if i & 1 else even_bit))) for i in range(n_seq)]
        steps.append((pairs, jnp.where(odd, side(odd_bit), side(even_bit))))
    return steps


def reduce_in_plane(send, keep, steps):
    part = keep + lax.ppermute(send, "seq", steps[0][0])
    for pairs, side in steps[1:]:
        half = part.shape[0] // 2
        send = lax.dynamic_slice_in_dim(part, (1 - side) * half, half)
        keep = lax.dynamic_slice_in_dim(part, side * half, half)
        part = keep + lax.ppermute(send, "seq", pairs)
    return part


def sum_over_planes(part):
    n_dp, plane = lax.axis_size("dp"), lax.axis_index("dp")
    size = part.shape[0] // n_dp
    pieces = [
        lax.dynamic_slice_in_dim(part, lax.bitwise_xor(plane, k) * size, size) for k in range(n_dp)
    ]
    total = functools.reduce(jnp.add, by_distance(pieces, "dp")).astype(BF16)
    shares = jnp.stack(by_distance([total] * n_dp, "dp"))
    return jnp.concatenate(
        [lax.dynamic_index_in_dim(shares, lax.bitwise_xor(plane, p), keepdims=False) for p in range(n_dp)],
        axis=0,
    )


def share_in_plane(part, steps):
    for pairs, side in reversed(steps):
        other = lax.ppermute(part, "seq", pairs)
        part = jnp.where(
            side == 0, jnp.concatenate([part, other], axis=0), jnp.concatenate([other, part], axis=0)
        )
    return part


def per_device(points, cotangent, dest, w_qkv, w_proj, gain):
    feats = points[0]
    grads = cotangent[0]
    rows, width = feats.shape
    n_seq = lax.axis_size("seq")
    capacity = 2 * (rows // n_seq)
    slots = n_seq * capacity
    block = capacity + EXTRA
    pairs = HEADS // 2
    pair = width // pairs
    sum_shape = (width // 2, 4 * width + LANES)
    me = jnp.reshape(lax.axis_index("seq").astype(jnp.int32), (1,))
    gain_row = gain.reshape(1, width)
    in_smem = pl.BlockSpec(memory_space=pltpu.SMEM)
    in_vmem = pl.BlockSpec(memory_space=pltpu.VMEM)
    in_hbm = pl.BlockSpec(memory_space=pl.ANY)

    slot, *packed = pl.pallas_call(
        functools.partial(pack_kernel, n_seq, capacity),
        out_shape=[shape_of((1, rows), jnp.int32)]
        + [shape_of((block, width), BF16)] * n_seq
        + [shape_of((capacity, width), BF16)] * n_seq,
        in_specs=[in_smem, in_vmem, in_vmem, in_vmem],
        out_specs=[in_vmem] * (1 + 2 * n_seq),
        compiler_params=params(20),
        cost_estimate=pl.CostEstimate(
            flops=4 * slots * rows * width, bytes_accessed=4 * MIB, transcendentals=0
        ),
        name="pack",
    )(me, dest, feats, grads)
    feats_got = by_distance(packed[:n_seq], "seq")
    feats_got, grads_sent = lax.optimization_barrier((feats_got, packed[n_seq:]))
    grads_got = by_distance(grads_sent, "seq")

    pos, xhat, inv, normed, qkv, attn_t, probs = pl.pallas_call(
        functools.partial(forward_kernel, n_seq, capacity),
        grid=(pairs,),
        out_shape=(
            shape_of((1, slots), jnp.int32),
            shape_of((rows, width), F32),
            shape_of((rows, LANES), F32),
            shape_of((rows, width), BF16),
            shape_of((rows, 3 * width), BF16),
            shape_of((width, rows), BF16),
            shape_of((HEADS, rows, rows), F32),
        ),
        in_specs=[in_hbm, whole((1, width))] + [whole((block, width))] * n_seq,
        out_specs=[whole((1, slots))]
        + [in_hbm] * 4
        + [
            pl.BlockSpec((pair, rows), lambda i: (i, 0)),
            pl.BlockSpec((2, rows, rows), lambda i: (i, 0, 0)),
        ],
        scratch_shapes=[
            pltpu.VMEM((width, 3 * width), BF16),
            pltpu.VMEM((rows, width), F32),
            pltpu.VMEM((rows, LANES), F32),
            pltpu.VMEM((rows, width), BF16),
            pltpu.VMEM((rows, 3 * width), BF16),
            pltpu.VMEM((3 * width, rows), BF16),
            pltpu.SemaphoreType.DMA((5,)),
        ],
        compiler_params=params(26),
        cost_estimate=pl.CostEstimate(
            flops=6 * rows * width * width + 8 * HEADS * rows * rows * pair,
            bytes_accessed=16 * MIB,
            transcendentals=HEADS * rows * rows,
        ),
        name="forward",
    )(w_qkv, gain_row, *feats_got)

    send, keep, *back = pl.pallas_call(
        functools.partial(backward_kernel, n_seq),
        grid=(pairs,),
        out_shape=[shape_of(sum_shape, F32)] * 2 + [shape_of((capacity, width), BF16)] * n_seq,
        in_specs=[
            in_smem,
            whole((1, slots)),
            whole((width, width)),
            whole((1, width)),
            whole((rows, 3 * width)),
            pl.BlockSpec((2, rows, rows), lambda i: (i, 0, 0)),
        ]
        + [in_hbm] * 5
        + [whole((capacity, width))] * n_seq,
        out_specs=[in_hbm] * 2 + [whole((capacity, width))] * n_seq,
        scratch_shapes=[
            pltpu.VMEM((width, 3 * width), BF16),
            pltpu.VMEM((rows, width), F32),
            pltpu.VMEM((rows, LANES), F32),
            pltpu.VMEM((rows, width), BF16),
            pltpu.VMEM((width, rows), BF16),
            pltpu.VMEM(sum_shape, F32),
            pltpu.VMEM(sum_shape, F32),
            pltpu.VMEM((rows, width), BF16),
            pltpu.VMEM((rows, width), BF16),
            pltpu.VMEM((width, rows), BF16),
            pltpu.VMEM((width, rows), BF16),
            pltpu.VMEM((rows, 3 * width), BF16),
            pltpu.VMEM((width, rows), BF16),
            pltpu.VMEM((width, LANES), F32),
            pltpu.SemaphoreType.DMA((7,)),
        ],
        compiler_params=params(34),
        cost_estimate=pl.CostEstimate(
            flops=14 * rows * width * width + 8 * HEADS * rows * rows * pair,
            bytes_accessed=24 * MIB,
            transcendentals=0,
        ),
        name="backward",
    )(me, pos, w_proj, gain_row, qkv, probs, w_qkv, xhat, inv, normed, attn_t, *grads_got)

    steps = chip_steps()
    part = reduce_in_plane(send, keep, steps)
    back, part = lax.optimization_barrier((back, part))
    returned = by_distance(back, "seq")
    part, returned = lax.optimization_barrier((sum_over_planes(part), returned))
    total = share_in_plane(part, steps).astype(F32)
    grad_local = pl.pallas_call(
        unpack_kernel,
        out_shape=shape_of((rows, width), BF16),
        in_specs=[in_vmem] * (1 + n_seq),
        out_specs=in_vmem,
        compiler_params=params(20),
        cost_estimate=pl.CostEstimate(
            flops=2 * slots * rows * width, bytes_accessed=2 * MIB, transcendentals=0
        ),
        name="unpack",
    )(slot, *returned)
    return (grad_local[None], total[:, : 3 * width], total[:, 3 * width : 4 * width], total[:, 4 * width])


def solution(mesh):
    return jax.shard_map(
        per_device,
        mesh=mesh,
        in_specs=(P("dp", "seq", None), P("dp", "seq", None), P("dp", "seq"), P(), P(), P()),
        out_specs=(P("dp", "seq", None), P(), P(), P()),
        check_vma=False,
    )
```

```python
import functools

import jax
import jax.numpy as jnp
from jax import lax
from jax.experimental import pallas as pl
from jax.experimental.pallas import tpu as pltpu
from jax.sharding import PartitionSpec as P

HEADS = 8
PATCH = 512
EXTRA = 16
LANES = 128
MIB = 1024 * 1024
F32 = jnp.float32
BF16 = jnp.bfloat16
NN = (((1,), (0,)), ((), ()))
NT = (((1,), (1,)), ((), ()))


def mm(lhs, rhs, dims=NN):
    return lax.dot_general(lhs, rhs, dims, preferred_element_type=F32)


def iota(shape, dim):
    return lax.broadcasted_iota(jnp.int32, shape, dim)


def hot(mask):
    return jnp.where(mask, jnp.float32(1), jnp.float32(0)).astype(BF16)


def column_hot(row, count):
    size = row.shape[1]
    column = jnp.transpose(jnp.broadcast_to(row, (LANES, size)))
    lane = iota((size, LANES), 1)
    return jnp.concatenate([hot(column == lane + j * LANES) for j in range(count // LANES)], axis=1)


def by_receiver(me, distance, capacity):
    return pl.ds(pl.multiple_of(lax.bitwise_xor(me, distance) * capacity, capacity), capacity)


def pack_kernel(n_seq, capacity, me_ref, dest_hbm, feats_hbm, grads_hbm, slot_out, grads_out, *refs):
    outs, (dest_ref, feats_ref, grads_ref, sems) = refs[:n_seq], refs[n_seq:]
    rows, width = feats_ref.shape
    slots = n_seq * capacity
    loads = [
        pltpu.make_async_copy(source, target, sems.at[i])
        for i, (source, target) in enumerate(
            ((dest_hbm, dest_ref), (feats_hbm, feats_ref), (grads_hbm, grads_ref))
        )
    ]
    for load in loads:
        load.start()
    loads[0].wait()
    shift = rows.bit_length() - 1
    places = dest_ref[...]
    distance = lax.bitwise_xor(lax.shift_right_logical(places, shift), me_ref[0])
    within = lax.bitwise_and(places, rows - 1) + 1
    member = iota((n_seq, rows), 0) == distance
    upper = hot(iota((rows, rows), 0) <= iota((rows, rows), 1))
    counts = mm(hot(member), upper)
    rank = jnp.sum(jnp.where(member, counts, 0.0), axis=0, keepdims=True).astype(jnp.int32) - 1
    slot = distance * capacity + rank
    slot_out[...] = slot
    select = hot(iota((slots, rows), 0) == slot)
    loads[1].wait()
    feats = mm(select, feats_ref[...]).astype(BF16)
    upper_half = slot >= width
    high = lax.shift_right_logical(within, 8).astype(F32)
    low = lax.bitwise_and(within, 255).astype(F32)
    line = iota((n_seq * EXTRA, rows), 0)
    kind = lax.bitwise_and(line, EXTRA - 1)
    digit = jnp.where(kind < 2, high, low)
    wanted = (
        (lax.shift_right_logical(line, EXTRA.bit_length() - 1) == distance)
        & (kind < 4)
        & ((lax.bitwise_and(kind, 1) == 1) == upper_half)
    )
    digits = jnp.where(wanted, digit, 0.0).astype(BF16)
    spread = hot(iota((width, rows), 0) == lax.bitwise_and(slot, width - 1))
    position = mm(digits, spread, NT).astype(BF16)
    for d in range(n_seq):
        outs[d][:capacity, :] = feats[d * capacity : (d + 1) * capacity]
        outs[d][capacity:, :] = position[d * EXTRA : (d + 1) * EXTRA]
    loads[2].wait()
    grads = mm(select, grads_ref[...]).astype(BF16)
    for d in range(n_seq):
        grads_out[by_receiver(me_ref[0], d, capacity), :] = grads[d * capacity : (d + 1) * capacity]


def forward_kernel(n_seq, capacity, w_hbm, gain_ref, *refs):
    recv, refs = refs[:n_seq], refs[n_seq:]
    pos_out, xhat_hbm, inv_hbm, normed_hbm, qkv_hbm, attn_out, probs_out = refs[:7]
    w_ref, xhat_ref, inv_ref, normed_ref, qkv_ref, trans, sems = refs[7:]
    width = w_ref.shape[0]
    rows = xhat_ref.shape[0]
    head = width // HEADS
    pair = 2 * head
    step = pl.program_id(0)
    w_copy = pltpu.make_async_copy(w_hbm, w_ref, sems.at[0])
    saves = [
        pltpu.make_async_copy(source, target, sems.at[1 + i])
        for i, (source, target) in enumerate(
            ((xhat_ref, xhat_hbm), (inv_ref, inv_hbm), (normed_ref, normed_hbm), (qkv_ref, qkv_hbm))
        )
    ]

    @pl.when(step == 0)
    def _():
        w_copy.start()
        tile = recv[0][capacity:, :].astype(F32)
        for s in range(1, n_seq):
            tile = tile + recv[s][capacity:, :].astype(F32)
        high = jnp.concatenate([tile[0:1], tile[1:2]], axis=1)
        low = jnp.concatenate([tile[2:3], tile[3:4]], axis=1)
        pos = (high * 256.0 + low).astype(jnp.int32) - 1
        pos_out[...] = pos
        place = hot(iota((rows, n_seq * capacity), 0) == pos)
        values = jnp.concatenate([recv[s][:capacity, :] for s in range(n_seq)], axis=0)
        feats = mm(place, values)
        centered = feats - jnp.mean(feats, axis=1, keepdims=True)
        inv = lax.rsqrt(jnp.mean(centered * centered, axis=1, keepdims=True) + 1e-05)
        xhat = centered * inv
        xhat_ref[...] = xhat
        inv_ref[...] = jnp.broadcast_to(inv, inv_ref.shape)
        normed = (xhat * gain_ref[...]).astype(BF16)
        normed_ref[...] = normed
        w_copy.wait()
        qkv = mm(normed, w_ref[...])
        qkv_ref[...] = qkv.astype(BF16)
        for save in saves:
            save.start()
        trans[...] = jnp.transpose(qkv).astype(BF16)

    lo = pl.multiple_of(step * pair, pair)
    keys = qkv_ref[:, pl.ds(pl.multiple_of(width + step * pair, pair), pair)]
    query_t = trans[pl.ds(lo, pair), :] * BF16(0.125)
    zero = jnp.zeros((head, rows), BF16)
    for j in range(2):
        part = query_t[j * head : (j + 1) * head]
        part = jnp.concatenate([part, zero] if j == 0 else [zero, part], axis=0)
        scores = mm(keys, part)
        expo = jnp.exp(scores - jnp.max(scores, axis=0, keepdims=True))
        probs = expo * (1.0 / jnp.sum(expo, axis=0, keepdims=True))
        probs_out[j] = probs
        values_t = trans[pl.ds(pl.multiple_of(2 * width + step * pair + j * head, head), head), :]
        attn_out[j * head : (j + 1) * head, :] = mm(values_t, probs.astype(BF16)).astype(BF16)

    @pl.when(step == pl.num_programs(0) - 1)
    def _():
        for save in saves:
            save.wait()


def backward_kernel(n_seq, first_bits, me_ref, pos_ref, w_proj_ref, probs_ref, *refs):
    (recv_hbm, qkv_hbm, w_hbm, xhat_hbm, normed_hbm, attn_hbm), refs = refs[:6], refs[6:]
    outs, serial_grad_hbm, d_normed_hbm, refs = refs[:4], refs[4], refs[5], refs[6:]
    recv_ref, qkv_ref, w_ref, xhat_ref, normed_ref, attn_ref, refs = *refs[:6], refs[6:]
    sums, refs = refs[:4], refs[4:]
    serial_grad, d_normed_ref, d_attn, d_attn_t, keys_t, d_qkv, normed_t, gain_column, sems = refs
    width = w_proj_ref.shape[0]
    rows = xhat_ref.shape[0]
    capacity = recv_ref.shape[0] // n_seq
    head = width // HEADS
    pair = 2 * head
    step = pl.program_id(0)
    me = me_ref[0]
    loads = [
        pltpu.make_async_copy(source, target, sems.at[i])
        for i, (source, target) in enumerate(
            (
                (recv_hbm, recv_ref),
                (qkv_hbm, qkv_ref),
                (normed_hbm, normed_ref),
                (w_hbm, w_ref),
                (xhat_hbm, xhat_ref),
                (attn_hbm, attn_ref),
            )
        )
    ]
    saves = [
        pltpu.make_async_copy(source, target, sems.at[6 + i])
        for i, (source, target) in enumerate(
            [*zip(sums, outs), (serial_grad, serial_grad_hbm), (d_normed_ref, d_normed_hbm)]
        )
    ]

    @pl.when(step == 0)
    def _():
        for load in loads:
            load.start()
        place = hot(iota((rows, n_seq * capacity), 0) == pos_ref[...])
        loads[0].wait()
        values = jnp.concatenate(
            [recv_ref[by_receiver(me, d, capacity), :] for d in range(n_seq)], axis=0
        )
        grads = mm(place, values).astype(BF16)
        serial_grad[...] = grads
        saves[4].start()
        d_att = mm(grads, w_proj_ref[...], NT).astype(BF16)
        d_attn[...] = d_att
        d_attn_t[...] = jnp.transpose(d_att.astype(F32)).astype(BF16)
        loads[1].wait()
        keys_t[...] = jnp.transpose(qkv_ref[:, width : 2 * width].astype(F32)).astype(BF16)

    lo = pl.multiple_of(step * pair, pair)
    queries = qkv_ref[:, pl.ds(lo, pair)]
    values = qkv_ref[:, pl.ds(pl.multiple_of(2 * width + step * pair, pair), pair)]
    d_att_t = d_attn_t[pl.ds(lo, pair), :] * BF16(0.125)
    d_att = d_attn[:, pl.ds(lo, pair)]
    zero = jnp.zeros((head, rows), BF16)
    d_q, d_k, d_v = [], [], []
    for j in range(2):
        part = d_att_t[j * head : (j + 1) * head]
        part = jnp.concatenate([part, zero] if j == 0 else [zero, part], axis=0)
        probs = probs_ref[j]
        d_probs = mm(values, part)
        total = jnp.sum(d_probs * probs, axis=0, keepdims=True)
        d_scores = (probs * (d_probs - total)).astype(BF16)
        k_t = keys_t[pl.ds(pl.multiple_of(step * pair + j * head, head), head), :]
        d_q.append(mm(k_t, d_scores))
        d_k.append(mm(d_scores, queries))
        d_v.append(mm(probs.astype(BF16), d_att))
    first = iota((rows, pair), 1) < head
    d_qkv[:, pl.ds(lo, pair)] = jnp.transpose(jnp.concatenate(d_q, axis=0)).astype(BF16)
    d_qkv[:, pl.ds(pl.multiple_of(width + step * pair, pair), pair)] = jnp.where(
        first, d_k[0], d_k[1]
    ).astype(BF16)
    d_qkv[:, pl.ds(pl.multiple_of(2 * width + step * pair, pair), pair)] = jnp.where(
        first, d_v[0], d_v[1]
    ).astype(BF16)

    @pl.when(step == pl.num_programs(0) - 1)
    def _():
        for load in loads[2:]:
            load.wait()
        normed_t[...] = jnp.transpose(normed_ref[...].astype(F32)).astype(BF16)
        d_normed = mm(d_qkv[...], w_ref[...], NT)
        d_normed_ref[...] = d_normed
        saves[5].start()
        gain_row = jnp.sum(d_normed * xhat_ref[...], axis=0, keepdims=True)
        gain_column[...] = jnp.transpose(jnp.broadcast_to(gain_row, (LANES, width)))
        quarter = width // 4
        odd = lax.bitwise_and(me, 1)
        even_bit, odd_bit = first_bits
        even_side = lax.bitwise_and(lax.shift_right_logical(me, even_bit), 1)
        odd_side = lax.bitwise_and(lax.shift_right_logical(me, odd_bit), 1)
        mine = jnp.where(odd == 1, odd_side, even_side)
        other = jnp.where(odd == 1, even_side, odd_side)
        starts = (
            (1 - odd) * 2 + 1 - other,
            (1 - odd) * 2 + other,
            odd * 2 + 1 - mine,
            odd * 2 + mine,
        )
        for out, start, save in zip(sums, starts, saves):
            part = pl.ds(pl.multiple_of(start * quarter, quarter), quarter)
            out[:, : 3 * width] = mm(normed_t[part, :], d_qkv[...])
            out[:, 3 * width : 4 * width] = mm(attn_ref[part, :], serial_grad[...])
            out[:, 4 * width :] = gain_column[part, :]
            save.start()
        for save in saves:
            save.wait()


def residual_kernel(
    n_seq, me_ref, pos_ref, gain_ref, inv_ref, xhat_ref, serial_grad_ref, d_normed_ref, back_out
):
    xhat = xhat_ref[...]
    rows = xhat.shape[0]
    capacity = pos_ref.shape[1] // n_seq
    scaled = d_normed_ref[...] * gain_ref[...]
    residual = inv_ref[:, 0:1] * (
        scaled
        - jnp.mean(scaled, axis=1, keepdims=True)
        - xhat * jnp.mean(scaled * xhat, axis=1, keepdims=True)
    )
    serial_dx = (serial_grad_ref[...].astype(F32) + residual).astype(BF16)
    returned = mm(column_hot(pos_ref[...], rows), serial_dx).astype(BF16)
    for d in range(n_seq):
        back_out[by_receiver(me_ref[0], d, capacity), :] = returned[d * capacity : (d + 1) * capacity]


def unpack_kernel(n_seq, me_ref, slot_ref, recv_ref, out_ref):
    capacity = recv_ref.shape[0] // n_seq
    values = jnp.concatenate(
        [recv_ref[by_receiver(me_ref[0], d, capacity), :] for d in range(n_seq)], axis=0
    )
    out_ref[...] = mm(column_hot(slot_ref[...], values.shape[0]), values).astype(BF16)


def split_kernel(side_ref, own_ref, other_ref, qkv_out, proj_out, gain_out):
    width = proj_out.shape[1]

    def write(ref):
        qkv_out[...] = ref[:, : 3 * width].astype(F32)
        proj_out[...] = ref[:, 3 * width : 4 * width].astype(F32)
        gain_out[...] = jnp.transpose(ref[:, 4 * width :].astype(F32))[0:1]

    own = pl.program_id(0) == side_ref[0]
    pl.when(own)(lambda: write(own_ref))
    pl.when(jnp.logical_not(own))(lambda: write(other_ref))


def whole(shape):
    return pl.BlockSpec(shape, lambda *_: (0,) * len(shape), pipeline_mode=pl.Buffered(1))


def params(mib):
    return pltpu.CompilerParams(vmem_limit_bytes=mib * MIB)


def shape_of(shape, dtype):
    return jax.ShapeDtypeStruct(shape, dtype)


def by_distance(blocks, axis):
    count = len(blocks)
    return [blocks[0]] + [
        lax.ppermute(blocks[k], axis, [(i, i ^ k) for i in range(count)]) for k in range(1, count)
    ]


def chip_orders(n_seq):
    bits = list(range(1, n_seq.bit_length() - 1))
    middle = len(bits) // 2
    return bits, bits[middle:] + bits[:middle]


def chip_steps():
    n_seq, me = lax.axis_size("seq"), lax.axis_index("seq")
    odd = lax.bitwise_and(me, 1) == 1

    def side(bit):
        return lax.bitwise_and(lax.shift_right_logical(me, jnp.asarray(bit, me.dtype)), 1)

    steps = []
    for even_bit, odd_bit in zip(*chip_orders(n_seq)):
        pairs = [(i, i ^ (1 << (odd_bit if i & 1 else even_bit))) for i in range(n_seq)]
        steps.append((pairs, jnp.where(odd, side(odd_bit), side(even_bit))))
    return steps


def piece(terms, index, count):
    size = terms[0].shape[0] // count
    return functools.reduce(jnp.add, [lax.dynamic_slice_in_dim(t, index * size, size) for t in terms])


def core_pairs():
    return [(i, i ^ 1) for i in range(lax.axis_size("seq"))]


def reduce_in_plane(quarters, steps):
    pass_on, pass_keep, own_on, own_keep = quarters
    send = own_on + lax.ppermute(pass_on, "seq", core_pairs())
    keep = own_keep + lax.ppermute(pass_keep, "seq", core_pairs())
    terms = [keep, lax.ppermute(send, "seq", steps[0][0])]
    for pairs, side in steps[1:]:
        got = lax.ppermute(piece(terms, 1 - side, 2), "seq", pairs)
        terms = [piece(terms, side, 2), got]
    return terms


def reduce_over_planes(terms):
    n_dp, plane = lax.axis_size("dp"), lax.axis_index("dp")
    pieces = [piece(terms, lax.bitwise_xor(plane, k), n_dp) for k in range(n_dp)]
    return functools.reduce(jnp.add, by_distance(pieces, "dp")).astype(BF16)


def share_over_planes(part):
    n_dp, plane = lax.axis_size("dp"), lax.axis_index("dp")
    shares = jnp.stack(by_distance([part] * n_dp, "dp"))
    return jnp.concatenate(
        [lax.dynamic_index_in_dim(shares, lax.bitwise_xor(plane, p), keepdims=False) for p in range(n_dp)],
        axis=0,
    )


def share_in_plane(part, steps):
    for pairs, side in reversed(steps):
        other = lax.ppermute(part, "seq", pairs)
        part = jnp.where(
            side == 0, jnp.concatenate([part, other], axis=0), jnp.concatenate([other, part], axis=0)
        )
    return part


def per_device(points, cotangent, dest, w_qkv, w_proj, gain):
    feats = points[0]
    grads = cotangent[0]
    rows, width = feats.shape
    n_seq = lax.axis_size("seq")
    capacity = 2 * (rows // n_seq)
    slots = n_seq * capacity
    block = capacity + EXTRA
    pairs = HEADS // 2
    pair = width // pairs
    sum_shape = (width // 4, 4 * width + LANES)
    me = jnp.reshape(lax.axis_index("seq").astype(jnp.int32), (1,))
    gain_row = gain.reshape(1, width)
    in_smem = pl.BlockSpec(memory_space=pltpu.SMEM)
    in_vmem = pl.BlockSpec(memory_space=pltpu.VMEM)
    in_hbm = pl.BlockSpec(memory_space=pl.ANY)
    stay_hbm = pl.BlockSpec(memory_space=pltpu.HBM)

    slot, grads_sent, *feats_sent = pl.pallas_call(
        functools.partial(pack_kernel, n_seq, capacity),
        out_shape=[shape_of((1, rows), jnp.int32), shape_of((slots, width), BF16)]
        + [shape_of((block, width), BF16)] * n_seq,
        in_specs=[in_smem] + [stay_hbm] * 3,
        out_specs=[in_vmem] * (2 + n_seq),
        scratch_shapes=[
            pltpu.VMEM((1, rows), jnp.int32),
            pltpu.VMEM((rows, width), BF16),
            pltpu.VMEM((rows, width), BF16),
            pltpu.SemaphoreType.DMA((3,)),
        ],
        compiler_params=params(60),
        cost_estimate=pl.CostEstimate(
            flops=4 * slots * rows * width, bytes_accessed=4 * MIB, transcendentals=0
        ),
        name="pack",
    )(me, dest, feats, grads)

    def exchange(sent):
        sent = sent.reshape(n_seq, capacity, width)
        got = lax.all_to_all(sent, "seq", split_axis=0, concat_axis=0, tiled=True)
        return got.reshape(slots, width)

    feats_got = by_distance(feats_sent, "seq")
    feats_got, grads_sent = lax.optimization_barrier((feats_got, grads_sent))
    grads_got = exchange(grads_sent)

    pos, xhat, inv, normed, qkv, attn_t, probs = pl.pallas_call(
        functools.partial(forward_kernel, n_seq, capacity),
        grid=(pairs,),
        out_shape=(
            shape_of((1, slots), jnp.int32),
            shape_of((rows, width), F32),
            shape_of((rows, LANES), F32),
            shape_of((rows, width), BF16),
            shape_of((rows, 3 * width), BF16),
            shape_of((width, rows), BF16),
            shape_of((HEADS, rows, rows), F32),
        ),
        in_specs=[in_hbm, whole((1, width))] + [whole((block, width))] * n_seq,
        out_specs=[whole((1, slots))]
        + [in_hbm] * 4
        + [
            pl.BlockSpec((pair, rows), lambda i: (i, 0)),
            pl.BlockSpec((2, rows, rows), lambda i: (i, 0, 0)),
        ],
        scratch_shapes=[
            pltpu.VMEM((width, 3 * width), BF16),
            pltpu.VMEM((rows, width), F32),
            pltpu.VMEM((rows, LANES), F32),
            pltpu.VMEM((rows, width), BF16),
            pltpu.VMEM((rows, 3 * width), BF16),
            pltpu.VMEM((3 * width, rows), BF16),
            pltpu.SemaphoreType.DMA((5,)),
        ],
        compiler_params=params(24),
        cost_estimate=pl.CostEstimate(
            flops=6 * rows * width * width + 8 * HEADS * rows * rows * pair,
            bytes_accessed=16 * MIB,
            transcendentals=HEADS * rows * rows,
        ),
        name="forward",
    )(w_qkv, gain_row, *feats_got)

    first_bits = tuple(order[0] for order in chip_orders(n_seq))
    *quarters, serial_grad, d_normed = pl.pallas_call(
        functools.partial(backward_kernel, n_seq, first_bits),
        grid=(pairs,),
        out_shape=[shape_of(sum_shape, F32)] * 4
        + [shape_of((rows, width), BF16), shape_of((rows, width), F32)],
        in_specs=[
            in_smem,
            whole((1, slots)),
            whole((width, width)),
            pl.BlockSpec((2, rows, rows), lambda i: (i, 0, 0)),
        ]
        + [in_hbm] * 6,
        out_specs=[in_hbm] * 6,
        scratch_shapes=[
            pltpu.VMEM((slots, width), BF16),
            pltpu.VMEM((rows, 3 * width), BF16),
            pltpu.VMEM((width, 3 * width), BF16),
            pltpu.VMEM((rows, width), F32),
            pltpu.VMEM((rows, width), BF16),
            pltpu.VMEM((width, rows), BF16),
        ]
        + [pltpu.VMEM(sum_shape, F32)] * 4
        + [
            pltpu.VMEM((rows, width), BF16),
            pltpu.VMEM((rows, width), F32),
            pltpu.VMEM((rows, width), BF16),
            pltpu.VMEM((width, rows), BF16),
            pltpu.VMEM((width, rows), BF16),
            pltpu.VMEM((rows, 3 * width), BF16),
            pltpu.VMEM((width, rows), BF16),
            pltpu.VMEM((width, LANES), F32),
            pltpu.SemaphoreType.DMA((12,)),
        ],
        compiler_params=params(32),
        cost_estimate=pl.CostEstimate(
            flops=12 * rows * width * width + 8 * HEADS * rows * rows * pair,
            bytes_accessed=24 * MIB,
            transcendentals=0,
        ),
        name="backward",
    )(me, pos, w_proj, probs, grads_got, qkv, w_qkv, xhat, normed, attn_t)

    back = pl.pallas_call(
        functools.partial(residual_kernel, n_seq),
        out_shape=shape_of((slots, width), BF16),
        in_specs=[in_smem] + [in_vmem] * 6,
        out_specs=in_vmem,
        compiler_params=params(20),
        cost_estimate=pl.CostEstimate(
            flops=2 * slots * rows * width, bytes_accessed=4 * MIB, transcendentals=0
        ),
        name="residual",
    )(me, pos, gain_row, inv, xhat, serial_grad, d_normed)

    steps = chip_steps()
    terms = reduce_in_plane(quarters, steps)
    back, terms = lax.optimization_barrier((back, terms))
    returned = exchange(back)
    part, returned = lax.optimization_barrier((reduce_over_planes(terms), returned))
    own = share_in_plane(share_over_planes(part), steps)
    other = lax.ppermute(own, "seq", core_pairs())
    grad_local = pl.pallas_call(
        functools.partial(unpack_kernel, n_seq),
        out_shape=shape_of((rows, width), BF16),
        in_specs=[in_smem] + [in_vmem] * 2,
        out_specs=in_vmem,
        compiler_params=params(20),
        cost_estimate=pl.CostEstimate(
            flops=2 * slots * rows * width, bytes_accessed=2 * MIB, transcendentals=0
        ),
        name="unpack",
    )(me, slot, returned)
    half = width // 2
    grad_qkv, grad_proj, gain_grad = pl.pallas_call(
        split_kernel,
        grid=(2,),
        out_shape=(
            shape_of((width, 3 * width), F32),
            shape_of((width, width), F32),
            shape_of((1, width), F32),
        ),
        in_specs=[in_smem] + [whole(own.shape)] * 2,
        out_specs=[
            pl.BlockSpec((half, 3 * width), lambda i: (i, 0)),
            pl.BlockSpec((half, width), lambda i: (i, 0)),
            pl.BlockSpec((1, half), lambda i: (0, i)),
        ],
        compiler_params=params(20),
        cost_estimate=pl.CostEstimate(flops=0, bytes_accessed=8 * MIB, transcendentals=0),
        name="split",
    )(lax.bitwise_and(me, 1), own, other)
    return (grad_local[None], grad_qkv, grad_proj, gain_grad[0])


def solution(mesh):
    return jax.shard_map(
        per_device,
        mesh=mesh,
        in_specs=(P("dp", "seq", None), P("dp", "seq", None), P("dp", "seq"), P(), P(), P()),
        out_specs=(P("dp", "seq", None), P(), P(), P()),
        check_vma=False,
    )
```

```python
import functools

import jax
import jax.numpy as jnp
from jax import lax
from jax.experimental import pallas as pl
from jax.experimental.pallas import tpu as pltpu
from jax.sharding import PartitionSpec as P

HEADS = 8
PATCH = 512
EXTRA = 16
LANES = 128
MIB = 1024 * 1024
F32 = jnp.float32
BF16 = jnp.bfloat16
NN = (((1,), (0,)), ((), ()))
NT = (((1,), (1,)), ((), ()))


def mm(lhs, rhs, dims=NN):
    return lax.dot_general(lhs, rhs, dims, preferred_element_type=F32)


def iota(shape, dim):
    return lax.broadcasted_iota(jnp.int32, shape, dim)


def hot(mask):
    return jnp.where(mask, jnp.float32(1), jnp.float32(0)).astype(BF16)


def column_hot(row, count):
    size = row.shape[1]
    column = jnp.transpose(jnp.broadcast_to(row, (LANES, size)))
    lane = iota((size, LANES), 1)
    return jnp.concatenate([hot(column == lane + j * LANES) for j in range(count // LANES)], axis=1)


def by_receiver(me, distance, capacity):
    return pl.ds(pl.multiple_of(lax.bitwise_xor(me, distance) * capacity, capacity), capacity)


def pack_kernel(n_seq, capacity, me_ref, dest_hbm, feats_hbm, slot_out, *refs):
    outs, (dest_ref, feats_ref, sems) = refs[:n_seq], refs[n_seq:]
    rows, width = feats_ref.shape
    slots = n_seq * capacity
    loads = [
        pltpu.make_async_copy(source, target, sems.at[i])
        for i, (source, target) in enumerate(((dest_hbm, dest_ref), (feats_hbm, feats_ref)))
    ]
    for load in loads:
        load.start()
    loads[0].wait()
    shift = rows.bit_length() - 1
    places = dest_ref[...]
    distance = lax.bitwise_xor(lax.shift_right_logical(places, shift), me_ref[0])
    within = lax.bitwise_and(places, rows - 1) + 1
    member = iota((n_seq, rows), 0) == distance
    upper = hot(iota((rows, rows), 0) <= iota((rows, rows), 1))
    counts = mm(hot(member), upper)
    rank = jnp.sum(jnp.where(member, counts, 0.0), axis=0, keepdims=True).astype(jnp.int32) - 1
    slot = distance * capacity + rank
    slot_out[...] = slot
    select = hot(iota((slots, rows), 0) == slot)
    loads[1].wait()
    feats = mm(select, feats_ref[...]).astype(BF16)
    upper_half = slot >= width
    high = lax.shift_right_logical(within, 8).astype(F32)
    low = lax.bitwise_and(within, 255).astype(F32)
    line = iota((n_seq * EXTRA, rows), 0)
    kind = lax.bitwise_and(line, EXTRA - 1)
    digit = jnp.where(kind < 2, high, low)
    wanted = (
        (lax.shift_right_logical(line, EXTRA.bit_length() - 1) == distance)
        & (kind < 4)
        & ((lax.bitwise_and(kind, 1) == 1) == upper_half)
    )
    digits = jnp.where(wanted, digit, 0.0).astype(BF16)
    spread = hot(iota((width, rows), 0) == lax.bitwise_and(slot, width - 1))
    position = mm(digits, spread, NT).astype(BF16)
    for d in range(n_seq):
        outs[d][:capacity, :] = feats[d * capacity : (d + 1) * capacity]
        outs[d][capacity:, :] = position[d * EXTRA : (d + 1) * EXTRA]


def pack_grads_kernel(n_seq, capacity, me_ref, slot_ref, grads_ref, grads_out):
    select = hot(iota((n_seq * capacity, grads_ref.shape[0]), 0) == slot_ref[...])
    grads = mm(select, grads_ref[...]).astype(BF16)
    for d in range(n_seq):
        grads_out[by_receiver(me_ref[0], d, capacity), :] = grads[d * capacity : (d + 1) * capacity]


def forward_kernel(n_seq, capacity, w_hbm, gain_ref, *refs):
    recv, refs = refs[:n_seq], refs[n_seq:]
    pos_out, xhat_hbm, inv_hbm, normed_hbm, qkv_hbm, attn_out, probs_out = refs[:7]
    w_ref, xhat_ref, inv_ref, normed_ref, qkv_ref, trans, sems = refs[7:]
    width = w_ref.shape[0]
    rows = xhat_ref.shape[0]
    head = width // HEADS
    pair = 2 * head
    step = pl.program_id(0)
    w_copy = pltpu.make_async_copy(w_hbm, w_ref, sems.at[0])
    saves = [
        pltpu.make_async_copy(source, target, sems.at[1 + i])
        for i, (source, target) in enumerate(
            ((xhat_ref, xhat_hbm), (inv_ref, inv_hbm), (normed_ref, normed_hbm), (qkv_ref, qkv_hbm))
        )
    ]

    @pl.when(step == 0)
    def _():
        w_copy.start()
        tile = recv[0][capacity:, :].astype(F32)
        for s in range(1, n_seq):
            tile = tile + recv[s][capacity:, :].astype(F32)
        high = jnp.concatenate([tile[0:1], tile[1:2]], axis=1)
        low = jnp.concatenate([tile[2:3], tile[3:4]], axis=1)
        pos = (high * 256.0 + low).astype(jnp.int32) - 1
        pos_out[...] = pos
        place = hot(iota((rows, n_seq * capacity), 0) == pos)
        values = jnp.concatenate([recv[s][:capacity, :] for s in range(n_seq)], axis=0)
        feats = mm(place, values)
        centered = feats - jnp.mean(feats, axis=1, keepdims=True)
        inv = lax.rsqrt(jnp.mean(centered * centered, axis=1, keepdims=True) + 1e-05)
        xhat = centered * inv
        xhat_ref[...] = xhat
        inv_ref[...] = jnp.broadcast_to(inv, inv_ref.shape)
        normed = (xhat * gain_ref[...]).astype(BF16)
        normed_ref[...] = normed
        w_copy.wait()
        qkv = mm(normed, w_ref[...])
        qkv_ref[...] = qkv.astype(BF16)
        for save in saves:
            save.start()
        trans[...] = jnp.transpose(qkv).astype(BF16)

    lo = pl.multiple_of(step * pair, pair)
    keys = qkv_ref[:, pl.ds(pl.multiple_of(width + step * pair, pair), pair)]
    query_t = trans[pl.ds(lo, pair), :] * BF16(0.125)
    zero = jnp.zeros((head, rows), BF16)
    for j in range(2):
        part = query_t[j * head : (j + 1) * head]
        part = jnp.concatenate([part, zero] if j == 0 else [zero, part], axis=0)
        scores = mm(keys, part)
        expo = jnp.exp(scores - jnp.max(scores, axis=0, keepdims=True))
        probs = expo * (1.0 / jnp.sum(expo, axis=0, keepdims=True))
        probs_out[j] = probs
        values_t = trans[pl.ds(pl.multiple_of(2 * width + step * pair + j * head, head), head), :]
        attn_out[j * head : (j + 1) * head, :] = mm(values_t, probs.astype(BF16)).astype(BF16)

    @pl.when(step == pl.num_programs(0) - 1)
    def _():
        for save in saves:
            save.wait()


def backward_kernel(n_seq, chip_bits, me_ref, pos_ref, w_proj_ref, probs_ref, *refs):
    (recv_hbm, qkv_hbm, w_hbm, xhat_hbm, normed_hbm, attn_hbm), refs = refs[:6], refs[6:]
    outs, serial_grad_hbm, d_normed_hbm, refs = refs[:4], refs[4], refs[5], refs[6:]
    recv_ref, qkv_ref, w_ref, xhat_ref, normed_ref, attn_ref, refs = *refs[:6], refs[6:]
    sums, refs = refs[:4], refs[4:]
    serial_grad, d_normed_ref, d_attn, d_attn_t, keys_t, d_qkv, normed_t, gain_column, sems = refs
    width = w_proj_ref.shape[0]
    rows = xhat_ref.shape[0]
    capacity = recv_ref.shape[0] // n_seq
    head = width // HEADS
    pair = 2 * head
    step = pl.program_id(0)
    me = me_ref[0]
    loads = [
        pltpu.make_async_copy(source, target, sems.at[i])
        for i, (source, target) in enumerate(
            (
                (recv_hbm, recv_ref),
                (qkv_hbm, qkv_ref),
                (normed_hbm, normed_ref),
                (w_hbm, w_ref),
                (xhat_hbm, xhat_ref),
                (attn_hbm, attn_ref),
            )
        )
    ]
    saves = [
        pltpu.make_async_copy(source, target, sems.at[6 + i])
        for i, (source, target) in enumerate(
            [*zip(sums, outs), (serial_grad, serial_grad_hbm), (d_normed_ref, d_normed_hbm)]
        )
    ]

    @pl.when(step == 0)
    def _():
        for load in loads:
            load.start()
        place = hot(iota((rows, n_seq * capacity), 0) == pos_ref[...])
        loads[0].wait()
        values = jnp.concatenate(
            [recv_ref[by_receiver(me, d, capacity), :] for d in range(n_seq)], axis=0
        )
        grads = mm(place, values).astype(BF16)
        serial_grad[...] = grads
        saves[4].start()
        d_att = mm(grads, w_proj_ref[...], NT).astype(BF16)
        d_attn[...] = d_att
        d_attn_t[...] = jnp.transpose(d_att.astype(F32)).astype(BF16)
        loads[1].wait()
        keys_t[...] = jnp.transpose(qkv_ref[:, width : 2 * width].astype(F32)).astype(BF16)

    lo = pl.multiple_of(step * pair, pair)
    queries = qkv_ref[:, pl.ds(lo, pair)]
    values = qkv_ref[:, pl.ds(pl.multiple_of(2 * width + step * pair, pair), pair)]
    d_att_t = d_attn_t[pl.ds(lo, pair), :] * BF16(0.125)
    d_att = d_attn[:, pl.ds(lo, pair)]
    zero = jnp.zeros((head, rows), BF16)
    d_q, d_k, d_v = [], [], []
    for j in range(2):
        part = d_att_t[j * head : (j + 1) * head]
        part = jnp.concatenate([part, zero] if j == 0 else [zero, part], axis=0)
        probs = probs_ref[j]
        d_probs = mm(values, part)
        total = jnp.sum(d_probs * probs, axis=0, keepdims=True)
        d_scores = (probs * (d_probs - total)).astype(BF16)
        k_t = keys_t[pl.ds(pl.multiple_of(step * pair + j * head, head), head), :]
        d_q.append(mm(k_t, d_scores))
        d_k.append(mm(d_scores, queries))
        d_v.append(mm(probs.astype(BF16), d_att))
    first = iota((rows, pair), 1) < head
    d_qkv[:, pl.ds(lo, pair)] = jnp.transpose(jnp.concatenate(d_q, axis=0)).astype(BF16)
    d_qkv[:, pl.ds(pl.multiple_of(width + step * pair, pair), pair)] = jnp.where(
        first, d_k[0], d_k[1]
    ).astype(BF16)
    d_qkv[:, pl.ds(pl.multiple_of(2 * width + step * pair, pair), pair)] = jnp.where(
        first, d_v[0], d_v[1]
    ).astype(BF16)

    @pl.when(step == pl.num_programs(0) - 1)
    def _():
        for load in loads[2:]:
            load.wait()
        normed_t[...] = jnp.transpose(normed_ref[...].astype(F32)).astype(BF16)
        d_normed = mm(d_qkv[...], w_ref[...], NT)
        d_normed_ref[...] = d_normed
        saves[5].start()
        gain_row = jnp.sum(d_normed * xhat_ref[...], axis=0, keepdims=True)
        gain_column[...] = jnp.transpose(jnp.broadcast_to(gain_row, (LANES, width)))
        eighth = width // 8
        odd = lax.bitwise_and(me, 1)

        def sides(even_bit, odd_bit):
            even_side = lax.bitwise_and(lax.shift_right_logical(me, even_bit), 1)
            odd_side = lax.bitwise_and(lax.shift_right_logical(me, odd_bit), 1)
            mine = jnp.where(odd == 1, odd_side, even_side)
            return mine, even_side + odd_side - mine

        (mine, other), (mine_next, other_next) = (sides(*bits) for bits in chip_bits)
        starts = (
            ((1 - odd) * 2 + 1 - other, other_next),
            ((1 - odd) * 2 + other, other_next),
            (odd * 2 + 1 - mine, mine_next),
            (odd * 2 + mine, mine_next),
        )
        for out, (start, side), save in zip(sums, starts, saves):
            for j, half in enumerate((1 - side, side)):
                part = pl.ds(pl.multiple_of((start * 2 + half) * eighth, eighth), eighth)
                lines = slice(j * eighth, (j + 1) * eighth)
                out[lines, : 3 * width] = mm(normed_t[part, :], d_qkv[...])
                out[lines, 3 * width : 4 * width] = mm(attn_ref[part, :], serial_grad[...])
                out[lines, 4 * width :] = gain_column[part, :]
            save.start()
        for save in saves:
            save.wait()


def residual_kernel(
    n_seq, me_ref, pos_ref, gain_ref, inv_ref, xhat_ref, serial_grad_ref, d_normed_ref, back_out
):
    xhat = xhat_ref[...]
    rows = xhat.shape[0]
    capacity = pos_ref.shape[1] // n_seq
    scaled = d_normed_ref[...] * gain_ref[...]
    residual = inv_ref[:, 0:1] * (
        scaled
        - jnp.mean(scaled, axis=1, keepdims=True)
        - xhat * jnp.mean(scaled * xhat, axis=1, keepdims=True)
    )
    serial_dx = (serial_grad_ref[...].astype(F32) + residual).astype(BF16)
    returned = mm(column_hot(pos_ref[...], rows), serial_dx).astype(BF16)
    for d in range(n_seq):
        back_out[by_receiver(me_ref[0], d, capacity), :] = returned[d * capacity : (d + 1) * capacity]


def unpack_kernel(n_seq, me_ref, slot_ref, recv_ref, out_ref):
    capacity = recv_ref.shape[0] // n_seq
    values = jnp.concatenate(
        [recv_ref[by_receiver(me_ref[0], d, capacity), :] for d in range(n_seq)], axis=0
    )
    out_ref[...] = mm(column_hot(slot_ref[...], values.shape[0]), values).astype(BF16)


def split_kernel(side_ref, own_ref, other_ref, qkv_out, proj_out, gain_out):
    width = proj_out.shape[1]

    def write(ref):
        qkv_out[...] = ref[:, : 3 * width].astype(F32)
        proj_out[...] = ref[:, 3 * width : 4 * width].astype(F32)
        gain_out[...] = jnp.transpose(ref[:, 4 * width :].astype(F32))[0:1]

    own = pl.program_id(0) == side_ref[0]
    pl.when(own)(lambda: write(own_ref))
    pl.when(jnp.logical_not(own))(lambda: write(other_ref))


def whole(shape):
    return pl.BlockSpec(shape, lambda *_: (0,) * len(shape), pipeline_mode=pl.Buffered(1))


def params(mib):
    return pltpu.CompilerParams(vmem_limit_bytes=mib * MIB)


def shape_of(shape, dtype):
    return jax.ShapeDtypeStruct(shape, dtype)


def by_distance(blocks, axis):
    count = len(blocks)
    return [blocks[0]] + [
        lax.ppermute(blocks[k], axis, [(i, i ^ k) for i in range(count)]) for k in range(1, count)
    ]


def chip_orders(n_seq):
    bits = list(range(1, n_seq.bit_length() - 1))
    middle = len(bits) // 2
    return bits, bits[middle:] + bits[:middle]


def chip_steps():
    n_seq, me = lax.axis_size("seq"), lax.axis_index("seq")
    odd = lax.bitwise_and(me, 1) == 1

    def side(bit):
        return lax.bitwise_and(lax.shift_right_logical(me, jnp.asarray(bit, me.dtype)), 1)

    steps = []
    for even_bit, odd_bit in zip(*chip_orders(n_seq)):
        pairs = [(i, i ^ (1 << (odd_bit if i & 1 else even_bit))) for i in range(n_seq)]
        steps.append((pairs, jnp.where(odd, side(odd_bit), side(even_bit))))
    return steps


def piece(terms, index, count):
    size = terms[0].shape[0] // count
    return functools.reduce(jnp.add, [lax.dynamic_slice_in_dim(t, index * size, size) for t in terms])


def core_pairs():
    return [(i, i ^ 1) for i in range(lax.axis_size("seq"))]


def first_step(quarters, steps):
    pass_on, pass_keep, own_on, own_keep = quarters
    send = own_on + lax.ppermute(pass_on, "seq", core_pairs())
    keep = own_keep + lax.ppermute(pass_keep, "seq", core_pairs())
    return [keep, lax.ppermute(send, "seq", steps[0][0])]


def next_steps(terms, steps):
    half = terms[0].shape[0] // 2
    got = lax.ppermute(terms[0][:half] + terms[1][:half], "seq", steps[1][0])
    terms = [terms[0][half:] + terms[1][half:], got]
    for pairs, side in steps[2:]:
        got = lax.ppermute(piece(terms, 1 - side, 2), "seq", pairs)
        terms = [piece(terms, side, 2), got]
    return terms


def reduce_over_planes(terms):
    n_dp, plane = lax.axis_size("dp"), lax.axis_index("dp")
    pieces = [piece(terms, lax.bitwise_xor(plane, k), n_dp) for k in range(n_dp)]
    return functools.reduce(jnp.add, by_distance(pieces, "dp")).astype(BF16)


def share_over_planes(part):
    n_dp, plane = lax.axis_size("dp"), lax.axis_index("dp")
    shares = jnp.stack(by_distance([part] * n_dp, "dp"))
    return jnp.concatenate(
        [lax.dynamic_index_in_dim(shares, lax.bitwise_xor(plane, p), keepdims=False) for p in range(n_dp)],
        axis=0,
    )


def share_in_plane(part, steps):
    for pairs, side in reversed(steps):
        other = lax.ppermute(part, "seq", pairs)
        part = jnp.where(
            side == 0, jnp.concatenate([part, other], axis=0), jnp.concatenate([other, part], axis=0)
        )
    return part


def per_device(points, cotangent, dest, w_qkv, w_proj, gain):
    feats = points[0]
    grads = cotangent[0]
    rows, width = feats.shape
    n_seq = lax.axis_size("seq")
    capacity = 2 * (rows // n_seq)
    slots = n_seq * capacity
    block = capacity + EXTRA
    pairs = HEADS // 2
    pair = width // pairs
    sum_shape = (width // 4, 4 * width + LANES)
    me = jnp.reshape(lax.axis_index("seq").astype(jnp.int32), (1,))
    gain_row = gain.reshape(1, width)
    in_smem = pl.BlockSpec(memory_space=pltpu.SMEM)
    in_vmem = pl.BlockSpec(memory_space=pltpu.VMEM)
    in_hbm = pl.BlockSpec(memory_space=pl.ANY)
    stay_hbm = pl.BlockSpec(memory_space=pltpu.HBM)

    slot, *feats_sent = pl.pallas_call(
        functools.partial(pack_kernel, n_seq, capacity),
        out_shape=[shape_of((1, rows), jnp.int32)] + [shape_of((block, width), BF16)] * n_seq,
        in_specs=[in_smem] + [stay_hbm] * 2,
        out_specs=[in_vmem] * (1 + n_seq),
        scratch_shapes=[
            pltpu.VMEM((1, rows), jnp.int32),
            pltpu.VMEM((rows, width), BF16),
            pltpu.SemaphoreType.DMA((2,)),
        ],
        compiler_params=params(60),
        cost_estimate=pl.CostEstimate(
            flops=2 * slots * rows * width, bytes_accessed=2 * MIB, transcendentals=0
        ),
        name="pack",
    )(me, dest, feats)
    feats_got = by_distance(feats_sent, "seq")
    feats_got[1], slot = lax.optimization_barrier((feats_got[1], slot))
    grads_sent = pl.pallas_call(
        functools.partial(pack_grads_kernel, n_seq, capacity),
        out_shape=shape_of((slots, width), BF16),
        in_specs=[in_smem] + [in_vmem] * 2,
        out_specs=in_vmem,
        compiler_params=params(20),
        cost_estimate=pl.CostEstimate(
            flops=2 * slots * rows * width, bytes_accessed=2 * MIB, transcendentals=0
        ),
        name="pack_grads",
    )(me, slot, grads)

    def exchange(sent):
        sent = sent.reshape(n_seq, capacity, width)
        got = lax.all_to_all(sent, "seq", split_axis=0, concat_axis=0, tiled=True)
        return got.reshape(slots, width)

    feats_got, grads_sent = lax.optimization_barrier((feats_got, grads_sent))
    grads_got = exchange(grads_sent)

    pos, xhat, inv, normed, qkv, attn_t, probs = pl.pallas_call(
        functools.partial(forward_kernel, n_seq, capacity),
        grid=(pairs,),
        out_shape=(
            shape_of((1, slots), jnp.int32),
            shape_of((rows, width), F32),
            shape_of((rows, LANES), F32),
            shape_of((rows, width), BF16),
            shape_of((rows, 3 * width), BF16),
            shape_of((width, rows), BF16),
            shape_of((HEADS, rows, rows), F32),
        ),
        in_specs=[in_hbm, whole((1, width))] + [whole((block, width))] * n_seq,
        out_specs=[whole((1, slots))]
        + [in_hbm] * 4
        + [
            pl.BlockSpec((pair, rows), lambda i: (i, 0)),
            pl.BlockSpec((2, rows, rows), lambda i: (i, 0, 0)),
        ],
        scratch_shapes=[
            pltpu.VMEM((width, 3 * width), BF16),
            pltpu.VMEM((rows, width), F32),
            pltpu.VMEM((rows, LANES), F32),
            pltpu.VMEM((rows, width), BF16),
            pltpu.VMEM((rows, 3 * width), BF16),
            pltpu.VMEM((3 * width, rows), BF16),
            pltpu.SemaphoreType.DMA((5,)),
        ],
        compiler_params=params(60),
        cost_estimate=pl.CostEstimate(
            flops=6 * rows * width * width + 8 * HEADS * rows * rows * pair,
            bytes_accessed=16 * MIB,
            transcendentals=HEADS * rows * rows,
        ),
        name="forward",
    )(w_qkv, gain_row, *feats_got)

    chip_bits = tuple(zip(*chip_orders(n_seq)))[:2]
    *quarters, serial_grad, d_normed = pl.pallas_call(
        functools.partial(backward_kernel, n_seq, chip_bits),
        grid=(pairs,),
        out_shape=[shape_of(sum_shape, F32)] * 4
        + [shape_of((rows, width), BF16), shape_of((rows, width), F32)],
        in_specs=[
            in_smem,
            whole((1, slots)),
            whole((width, width)),
            pl.BlockSpec((2, rows, rows), lambda i: (i, 0, 0)),
        ]
        + [in_hbm] * 6,
        out_specs=[in_hbm] * 6,
        scratch_shapes=[
            pltpu.VMEM((slots, width), BF16),
            pltpu.VMEM((rows, 3 * width), BF16),
            pltpu.VMEM((width, 3 * width), BF16),
            pltpu.VMEM((rows, width), F32),
            pltpu.VMEM((rows, width), BF16),
            pltpu.VMEM((width, rows), BF16),
        ]
        + [pltpu.VMEM(sum_shape, F32)] * 4
        + [
            pltpu.VMEM((rows, width), BF16),
            pltpu.VMEM((rows, width), F32),
            pltpu.VMEM((rows, width), BF16),
            pltpu.VMEM((width, rows), BF16),
            pltpu.VMEM((width, rows), BF16),
            pltpu.VMEM((rows, 3 * width), BF16),
            pltpu.VMEM((width, rows), BF16),
            pltpu.VMEM((width, LANES), F32),
            pltpu.SemaphoreType.DMA((12,)),
        ],
        compiler_params=params(60),
        cost_estimate=pl.CostEstimate(
            flops=12 * rows * width * width + 8 * HEADS * rows * rows * pair,
            bytes_accessed=24 * MIB,
            transcendentals=0,
        ),
        name="backward",
    )(me, pos, w_proj, probs, grads_got, qkv, w_qkv, xhat, normed, attn_t)

    steps = chip_steps()
    terms = first_step(quarters, steps)
    d_normed, terms = lax.optimization_barrier((d_normed, terms))
    back = pl.pallas_call(
        functools.partial(residual_kernel, n_seq),
        out_shape=shape_of((slots, width), BF16),
        in_specs=[in_smem] + [in_vmem] * 6,
        out_specs=in_vmem,
        compiler_params=params(20),
        cost_estimate=pl.CostEstimate(
            flops=2 * slots * rows * width, bytes_accessed=4 * MIB, transcendentals=0
        ),
        name="residual",
    )(me, pos, gain_row, inv, xhat, serial_grad, d_normed)
    returned = exchange(back)
    terms = next_steps(terms, steps)
    part, returned = lax.optimization_barrier((reduce_over_planes(terms), returned))
    own = share_in_plane(share_over_planes(part), steps)
    other = lax.ppermute(own, "seq", core_pairs())
    grad_local = pl.pallas_call(
        functools.partial(unpack_kernel, n_seq),
        out_shape=shape_of((rows, width), BF16),
        in_specs=[in_smem] + [in_vmem] * 2,
        out_specs=in_vmem,
        compiler_params=params(20),
        cost_estimate=pl.CostEstimate(
            flops=2 * slots * rows * width, bytes_accessed=2 * MIB, transcendentals=0
        ),
        name="unpack",
    )(me, slot, returned)
    half = width // 2
    grad_qkv, grad_proj, gain_grad = pl.pallas_call(
        split_kernel,
        grid=(2,),
        out_shape=(
            shape_of((width, 3 * width), F32),
            shape_of((width, width), F32),
            shape_of((1, width), F32),
        ),
        in_specs=[in_smem] + [whole(own.shape)] * 2,
        out_specs=[
            pl.BlockSpec((half, 3 * width), lambda i: (i, 0)),
            pl.BlockSpec((half, width), lambda i: (i, 0)),
            pl.BlockSpec((1, half), lambda i: (0, i)),
        ],
        compiler_params=params(20),
        cost_estimate=pl.CostEstimate(flops=0, bytes_accessed=8 * MIB, transcendentals=0),
        name="split",
    )(lax.bitwise_and(me, 1), own, other)
    return (grad_local[None], grad_qkv, grad_proj, gain_grad[0])


def solution(mesh):
    return jax.shard_map(
        per_device,
        mesh=mesh,
        in_specs=(P("dp", "seq", None), P("dp", "seq", None), P("dp", "seq"), P(), P(), P()),
        out_specs=(P("dp", "seq", None), P(), P(), P()),
        check_vma=False,
    )
```

```python
import functools

import jax
import jax.numpy as jnp
from jax import lax
from jax.experimental import pallas as pl
from jax.experimental.pallas import tpu as pltpu
from jax.sharding import PartitionSpec as P

HEADS = 8
PATCH = 512
EXTRA = 16
LANES = 128
MIB = 1024 * 1024
F32 = jnp.float32
BF16 = jnp.bfloat16
NN = (((1,), (0,)), ((), ()))
NT = (((1,), (1,)), ((), ()))


def mm(lhs, rhs, dims=NN):
    return lax.dot_general(lhs, rhs, dims, preferred_element_type=F32)


def iota(shape, dim):
    return lax.broadcasted_iota(jnp.int32, shape, dim)


def hot(mask):
    return jnp.where(mask, jnp.float32(1), jnp.float32(0)).astype(BF16)


def column_hot(row, count):
    size = row.shape[1]
    column = jnp.transpose(jnp.broadcast_to(row, (LANES, size)))
    lane = iota((size, LANES), 1)
    return jnp.concatenate([hot(column == lane + j * LANES) for j in range(count // LANES)], axis=1)


def by_receiver(me, distance, capacity):
    return pl.ds(pl.multiple_of(lax.bitwise_xor(me, distance) * capacity, capacity), capacity)


def pack_kernel(n_seq, capacity, me_ref, dest_hbm, feats_hbm, slot_out, *refs):
    outs, (dest_ref, feats_ref, sems) = refs[:n_seq], refs[n_seq:]
    rows, width = feats_ref.shape
    slots = n_seq * capacity
    loads = [
        pltpu.make_async_copy(source, target, sems.at[i])
        for i, (source, target) in enumerate(((dest_hbm, dest_ref), (feats_hbm, feats_ref)))
    ]
    for load in loads:
        load.start()
    loads[0].wait()
    shift = rows.bit_length() - 1
    places = dest_ref[...]
    distance = lax.bitwise_xor(lax.shift_right_logical(places, shift), me_ref[0])
    within = lax.bitwise_and(places, rows - 1) + 1
    member = iota((n_seq, rows), 0) == distance
    upper = hot(iota((rows, rows), 0) <= iota((rows, rows), 1))
    counts = mm(hot(member), upper)
    rank = jnp.sum(jnp.where(member, counts, 0.0), axis=0, keepdims=True).astype(jnp.int32) - 1
    slot = distance * capacity + rank
    slot_out[...] = slot
    select = hot(iota((slots, rows), 0) == slot)
    loads[1].wait()
    feats = mm(select, feats_ref[...]).astype(BF16)
    upper_half = slot >= width
    high = lax.shift_right_logical(within, 8).astype(F32)
    low = lax.bitwise_and(within, 255).astype(F32)
    line = iota((n_seq * EXTRA, rows), 0)
    kind = lax.bitwise_and(line, EXTRA - 1)
    digit = jnp.where(kind < 2, high, low)
    wanted = (
        (lax.shift_right_logical(line, EXTRA.bit_length() - 1) == distance)
        & (kind < 4)
        & ((lax.bitwise_and(kind, 1) == 1) == upper_half)
    )
    digits = jnp.where(wanted, digit, 0.0).astype(BF16)
    spread = hot(iota((width, rows), 0) == lax.bitwise_and(slot, width - 1))
    position = mm(digits, spread, NT).astype(BF16)
    for d in range(n_seq):
        outs[d][:capacity, :] = feats[d * capacity : (d + 1) * capacity]
        outs[d][capacity:, :] = position[d * EXTRA : (d + 1) * EXTRA]


def pack_grads_kernel(n_seq, capacity, me_ref, slot_ref, grads_ref, grads_out):
    select = hot(iota((n_seq * capacity, grads_ref.shape[0]), 0) == slot_ref[...])
    grads = mm(select, grads_ref[...]).astype(BF16)
    for d in range(n_seq):
        grads_out[by_receiver(me_ref[0], d, capacity), :] = grads[d * capacity : (d + 1) * capacity]


def forward_kernel(n_seq, capacity, w_hbm, gain_ref, *refs):
    recv, refs = refs[:n_seq], refs[n_seq:]
    pos_out, xhat_hbm, inv_hbm, normed_hbm, qkv_hbm, trans_hbm, attn_out, stats_out = refs[:8]
    w_ref, xhat_ref, inv_ref, normed_ref, qkv_ref, trans, sems = refs[8:]
    width = w_ref.shape[0]
    rows = xhat_ref.shape[0]
    head = width // HEADS
    pair = 2 * head
    step = pl.program_id(0)
    w_copy = pltpu.make_async_copy(w_hbm, w_ref, sems.at[0])
    saves = [
        pltpu.make_async_copy(source, target, sems.at[1 + i])
        for i, (source, target) in enumerate(
            (
                (xhat_ref, xhat_hbm),
                (inv_ref, inv_hbm),
                (normed_ref, normed_hbm),
                (qkv_ref, qkv_hbm),
                (trans.at[pl.ds(0, 2 * width)], trans_hbm),
            )
        )
    ]

    @pl.when(step == 0)
    def _():
        w_copy.start()
        tile = recv[0][capacity:, :].astype(F32)
        for s in range(1, n_seq):
            tile = tile + recv[s][capacity:, :].astype(F32)
        high = jnp.concatenate([tile[0:1], tile[1:2]], axis=1)
        low = jnp.concatenate([tile[2:3], tile[3:4]], axis=1)
        pos = (high * 256.0 + low).astype(jnp.int32) - 1
        pos_out[...] = pos
        place = hot(iota((rows, n_seq * capacity), 0) == pos)
        values = jnp.concatenate([recv[s][:capacity, :] for s in range(n_seq)], axis=0)
        feats = mm(place, values)
        centered = feats - jnp.mean(feats, axis=1, keepdims=True)
        inv = lax.rsqrt(jnp.mean(centered * centered, axis=1, keepdims=True) + 1e-05)
        xhat = centered * inv
        xhat_ref[...] = xhat
        inv_ref[...] = jnp.broadcast_to(inv, inv_ref.shape)
        normed = (xhat * gain_ref[...]).astype(BF16)
        normed_ref[...] = normed
        w_copy.wait()
        qkv = mm(normed, w_ref[...])
        qkv_ref[...] = qkv.astype(BF16)
        trans[...] = jnp.transpose(qkv).astype(BF16)
        for save in saves:
            save.start()

    lo = pl.multiple_of(step * pair, pair)
    keys = qkv_ref[:, pl.ds(pl.multiple_of(width + step * pair, pair), pair)]
    query_t = trans[pl.ds(lo, pair), :] * BF16(0.125)
    zero = jnp.zeros((head, rows), BF16)
    for j in range(2):
        part = query_t[j * head : (j + 1) * head]
        part = jnp.concatenate([part, zero] if j == 0 else [zero, part], axis=0)
        scores = mm(keys, part)
        top = jnp.max(scores, axis=0, keepdims=True)
        expo = jnp.exp(scores - top)
        share = 1.0 / jnp.sum(expo, axis=0, keepdims=True)
        probs = expo * share
        stats_out[pl.ds(2 * step + j, 1), :] = top
        stats_out[pl.ds(HEADS + 2 * step + j, 1), :] = share
        values_t = trans[pl.ds(pl.multiple_of(2 * width + step * pair + j * head, head), head), :]
        attn_out[j * head : (j + 1) * head, :] = mm(values_t, probs.astype(BF16)).astype(BF16)

    @pl.when(step == pl.num_programs(0) - 1)
    def _():
        for save in saves:
            save.wait()


def backward_kernel(n_seq, chip_bits, me_ref, pos_ref, w_proj_ref, stats_ref, *refs):
    (recv_hbm, qkv_hbm, trans_hbm, w_hbm, xhat_hbm, normed_hbm, attn_hbm), refs = refs[:7], refs[7:]
    outs, serial_grad_hbm, d_normed_hbm, refs = refs[:4], refs[4], refs[5], refs[6:]
    recv_ref, qkv_ref, trans_ref, w_ref, xhat_ref, normed_ref, attn_ref, refs = *refs[:7], refs[7:]
    sums, refs = refs[:4], refs[4:]
    serial_grad, d_normed_ref, d_attn, d_attn_t, d_qkv, normed_t, gain_column, sems = refs
    width = w_proj_ref.shape[0]
    rows = xhat_ref.shape[0]
    capacity = recv_ref.shape[0] // n_seq
    head = width // HEADS
    pair = 2 * head
    step = pl.program_id(0)
    me = me_ref[0]
    loads = [
        pltpu.make_async_copy(source, target, sems.at[i])
        for i, (source, target) in enumerate(
            (
                (recv_hbm, recv_ref),
                (qkv_hbm, qkv_ref),
                (trans_hbm, trans_ref),
                (normed_hbm, normed_ref),
                (w_hbm, w_ref),
                (xhat_hbm, xhat_ref),
                (attn_hbm, attn_ref),
            )
        )
    ]
    saves = [
        pltpu.make_async_copy(source, target, sems.at[7 + i])
        for i, (source, target) in enumerate(
            [*zip(sums, outs), (serial_grad, serial_grad_hbm), (d_normed_ref, d_normed_hbm)]
        )
    ]

    @pl.when(step == 0)
    def _():
        for load in loads:
            load.start()
        place = hot(iota((rows, n_seq * capacity), 0) == pos_ref[...])
        loads[0].wait()
        values = jnp.concatenate(
            [recv_ref[by_receiver(me, d, capacity), :] for d in range(n_seq)], axis=0
        )
        grads = mm(place, values).astype(BF16)
        serial_grad[...] = grads
        saves[4].start()
        d_att = mm(grads, w_proj_ref[...], NT).astype(BF16)
        d_attn[...] = d_att
        d_attn_t[...] = jnp.transpose(d_att.astype(F32)).astype(BF16)
        loads[1].wait()
        loads[2].wait()

    lo = pl.multiple_of(step * pair, pair)
    queries = qkv_ref[:, pl.ds(lo, pair)]
    values = qkv_ref[:, pl.ds(pl.multiple_of(2 * width + step * pair, pair), pair)]
    d_att_t = d_attn_t[pl.ds(lo, pair), :] * BF16(0.125)
    d_att = d_attn[:, pl.ds(lo, pair)]
    keys = qkv_ref[:, pl.ds(pl.multiple_of(width + step * pair, pair), pair)]
    query_t = trans_ref[pl.ds(lo, pair), :] * BF16(0.125)
    zero = jnp.zeros((head, rows), BF16)
    d_q, d_k, d_v = [], [], []
    for j in range(2):
        def alone(both):
            part = both[j * head : (j + 1) * head]
            return jnp.concatenate([part, zero] if j == 0 else [zero, part], axis=0)

        top = stats_ref[pl.ds(2 * step + j, 1), :]
        share = stats_ref[pl.ds(HEADS + 2 * step + j, 1), :]
        probs = jnp.exp(mm(keys, alone(query_t)) - top) * share
        d_probs = mm(values, alone(d_att_t))
        total = jnp.sum(d_probs * probs, axis=0, keepdims=True)
        d_scores = (probs * (d_probs - total)).astype(BF16)
        k_t = trans_ref[pl.ds(pl.multiple_of(width + step * pair + j * head, head), head), :]
        d_q.append(mm(k_t, d_scores))
        d_k.append(mm(d_scores, queries))
        d_v.append(mm(probs.astype(BF16), d_att))
    first = iota((rows, pair), 1) < head
    d_qkv[:, pl.ds(lo, pair)] = jnp.transpose(jnp.concatenate(d_q, axis=0)).astype(BF16)
    d_qkv[:, pl.ds(pl.multiple_of(width + step * pair, pair), pair)] = jnp.where(
        first, d_k[0], d_k[1]
    ).astype(BF16)
    d_qkv[:, pl.ds(pl.multiple_of(2 * width + step * pair, pair), pair)] = jnp.where(
        first, d_v[0], d_v[1]
    ).astype(BF16)

    @pl.when(step == pl.num_programs(0) - 1)
    def _():
        for load in loads[3:]:
            load.wait()
        normed_t[...] = jnp.transpose(normed_ref[...].astype(F32)).astype(BF16)
        d_normed = mm(d_qkv[...], w_ref[...], NT)
        d_normed_ref[...] = d_normed
        saves[5].start()
        gain_row = jnp.sum(d_normed * xhat_ref[...], axis=0, keepdims=True)
        gain_column[...] = jnp.transpose(jnp.broadcast_to(gain_row, (LANES, width)))
        eighth = width // 8
        odd = lax.bitwise_and(me, 1)

        def sides(even_bit, odd_bit):
            even_side = lax.bitwise_and(lax.shift_right_logical(me, even_bit), 1)
            odd_side = lax.bitwise_and(lax.shift_right_logical(me, odd_bit), 1)
            mine = jnp.where(odd == 1, odd_side, even_side)
            return mine, even_side + odd_side - mine

        (mine, other), (mine_next, other_next) = (sides(*bits) for bits in chip_bits)
        starts = (
            ((1 - odd) * 2 + 1 - other, other_next),
            ((1 - odd) * 2 + other, other_next),
            (odd * 2 + 1 - mine, mine_next),
            (odd * 2 + mine, mine_next),
        )
        for out, (start, side), save in zip(sums, starts, saves):
            for j, half in enumerate((1 - side, side)):
                part = pl.ds(pl.multiple_of((start * 2 + half) * eighth, eighth), eighth)
                lines = slice(j * eighth, (j + 1) * eighth)
                out[lines, : 3 * width] = mm(normed_t[part, :], d_qkv[...])
                out[lines, 3 * width : 4 * width] = mm(attn_ref[part, :], serial_grad[...])
                out[lines, 4 * width :] = gain_column[part, :]
            save.start()
        for save in saves:
            save.wait()


def residual_kernel(
    n_seq, me_ref, pos_ref, gain_ref, inv_ref, xhat_ref, serial_grad_ref, d_normed_ref, back_out
):
    xhat = xhat_ref[...]
    rows = xhat.shape[0]
    capacity = pos_ref.shape[1] // n_seq
    scaled = d_normed_ref[...] * gain_ref[...]
    residual = inv_ref[:, 0:1] * (
        scaled
        - jnp.mean(scaled, axis=1, keepdims=True)
        - xhat * jnp.mean(scaled * xhat, axis=1, keepdims=True)
    )
    serial_dx = (serial_grad_ref[...].astype(F32) + residual).astype(BF16)
    returned = mm(column_hot(pos_ref[...], rows), serial_dx).astype(BF16)
    for d in range(n_seq):
        back_out[by_receiver(me_ref[0], d, capacity), :] = returned[d * capacity : (d + 1) * capacity]


def unpack_kernel(n_seq, me_ref, slot_ref, recv_ref, out_ref):
    capacity = recv_ref.shape[0] // n_seq
    values = jnp.concatenate(
        [recv_ref[by_receiver(me_ref[0], d, capacity), :] for d in range(n_seq)], axis=0
    )
    out_ref[...] = mm(column_hot(slot_ref[...], values.shape[0]), values).astype(BF16)


def split_kernel(side_ref, own_ref, other_ref, qkv_out, proj_out, gain_out):
    width = proj_out.shape[1]

    def write(ref):
        qkv_out[...] = ref[:, : 3 * width].astype(F32)
        proj_out[...] = ref[:, 3 * width : 4 * width].astype(F32)
        gain_out[...] = jnp.transpose(ref[:, 4 * width :].astype(F32))[0:1]

    own = pl.program_id(0) == side_ref[0]
    pl.when(own)(lambda: write(own_ref))
    pl.when(jnp.logical_not(own))(lambda: write(other_ref))


def whole(shape):
    return pl.BlockSpec(shape, lambda *_: (0,) * len(shape), pipeline_mode=pl.Buffered(1))


def params(mib):
    return pltpu.CompilerParams(vmem_limit_bytes=mib * MIB)


def shape_of(shape, dtype):
    return jax.ShapeDtypeStruct(shape, dtype)


def by_distance(blocks, axis):
    count = len(blocks)
    return [blocks[0]] + [
        lax.ppermute(blocks[k], axis, [(i, i ^ k) for i in range(count)]) for k in range(1, count)
    ]


def chip_orders(n_seq):
    bits = list(range(1, n_seq.bit_length() - 1))
    middle = len(bits) // 2
    return bits, bits[middle:] + bits[:middle]


def chip_steps():
    n_seq, me = lax.axis_size("seq"), lax.axis_index("seq")
    odd = lax.bitwise_and(me, 1) == 1

    def side(bit):
        return lax.bitwise_and(lax.shift_right_logical(me, jnp.asarray(bit, me.dtype)), 1)

    steps = []
    for even_bit, odd_bit in zip(*chip_orders(n_seq)):
        pairs = [(i, i ^ (1 << (odd_bit if i & 1 else even_bit))) for i in range(n_seq)]
        steps.append((pairs, jnp.where(odd, side(odd_bit), side(even_bit))))
    return steps


def piece(terms, index, count):
    size = terms[0].shape[0] // count
    return functools.reduce(jnp.add, [lax.dynamic_slice_in_dim(t, index * size, size) for t in terms])


def core_pairs():
    return [(i, i ^ 1) for i in range(lax.axis_size("seq"))]


def first_step(quarters, steps):
    pass_on, pass_keep, own_on, own_keep = quarters
    send = own_on + lax.ppermute(pass_on, "seq", core_pairs())
    keep = own_keep + lax.ppermute(pass_keep, "seq", core_pairs())
    return [keep, lax.ppermute(send, "seq", steps[0][0])]


def next_steps(terms, steps):
    half = terms[0].shape[0] // 2
    got = lax.ppermute(terms[0][:half] + terms[1][:half], "seq", steps[1][0])
    terms = [terms[0][half:] + terms[1][half:], got]
    for pairs, side in steps[2:]:
        got = lax.ppermute(piece(terms, 1 - side, 2), "seq", pairs)
        terms = [piece(terms, side, 2), got]
    return terms


def reduce_over_planes(terms):
    n_dp, plane = lax.axis_size("dp"), lax.axis_index("dp")
    pieces = [piece(terms, lax.bitwise_xor(plane, k), n_dp) for k in range(n_dp)]
    return functools.reduce(jnp.add, by_distance(pieces, "dp")).astype(BF16)


def share_over_planes(part):
    n_dp, plane = lax.axis_size("dp"), lax.axis_index("dp")
    shares = jnp.stack(by_distance([part] * n_dp, "dp"))
    return jnp.concatenate(
        [lax.dynamic_index_in_dim(shares, lax.bitwise_xor(plane, p), keepdims=False) for p in range(n_dp)],
        axis=0,
    )


def share_in_plane(part, steps):
    for pairs, side in reversed(steps):
        other = lax.ppermute(part, "seq", pairs)
        part = jnp.where(
            side == 0, jnp.concatenate([part, other], axis=0), jnp.concatenate([other, part], axis=0)
        )
    return part


def per_device(points, cotangent, dest, w_qkv, w_proj, gain):
    feats = points[0]
    grads = cotangent[0]
    rows, width = feats.shape
    n_seq = lax.axis_size("seq")
    capacity = 2 * (rows // n_seq)
    slots = n_seq * capacity
    block = capacity + EXTRA
    pairs = HEADS // 2
    pair = width // pairs
    sum_shape = (width // 4, 4 * width + LANES)
    me = jnp.reshape(lax.axis_index("seq").astype(jnp.int32), (1,))
    gain_row = gain.reshape(1, width)
    in_smem = pl.BlockSpec(memory_space=pltpu.SMEM)
    in_vmem = pl.BlockSpec(memory_space=pltpu.VMEM)
    in_hbm = pl.BlockSpec(memory_space=pl.ANY)
    stay_hbm = pl.BlockSpec(memory_space=pltpu.HBM)

    slot, *feats_sent = pl.pallas_call(
        functools.partial(pack_kernel, n_seq, capacity),
        out_shape=[shape_of((1, rows), jnp.int32)] + [shape_of((block, width), BF16)] * n_seq,
        in_specs=[in_smem] + [stay_hbm] * 2,
        out_specs=[in_vmem] * (1 + n_seq),
        scratch_shapes=[
            pltpu.VMEM((1, rows), jnp.int32),
            pltpu.VMEM((rows, width), BF16),
            pltpu.SemaphoreType.DMA((2,)),
        ],
        compiler_params=params(60),
        cost_estimate=pl.CostEstimate(
            flops=2 * slots * rows * width, bytes_accessed=2 * MIB, transcendentals=0
        ),
        name="pack",
    )(me, dest, feats)
    feats_got = by_distance(feats_sent, "seq")
    feats_got[1], slot = lax.optimization_barrier((feats_got[1], slot))
    grads_sent = pl.pallas_call(
        functools.partial(pack_grads_kernel, n_seq, capacity),
        out_shape=shape_of((slots, width), BF16),
        in_specs=[in_smem] + [in_vmem] * 2,
        out_specs=in_vmem,
        compiler_params=params(20),
        cost_estimate=pl.CostEstimate(
            flops=2 * slots * rows * width, bytes_accessed=2 * MIB, transcendentals=0
        ),
        name="pack_grads",
    )(me, slot, grads)

    def exchange(sent):
        sent = sent.reshape(n_seq, capacity, width)
        got = lax.all_to_all(sent, "seq", split_axis=0, concat_axis=0, tiled=True)
        return got.reshape(slots, width)

    feats_got, grads_sent = lax.optimization_barrier((feats_got, grads_sent))
    grads_got = exchange(grads_sent)

    pos, xhat, inv, normed, qkv, trans, attn_t, stats = pl.pallas_call(
        functools.partial(forward_kernel, n_seq, capacity),
        grid=(pairs,),
        out_shape=(
            shape_of((1, slots), jnp.int32),
            shape_of((rows, width), F32),
            shape_of((rows, LANES), F32),
            shape_of((rows, width), BF16),
            shape_of((rows, 3 * width), BF16),
            shape_of((2 * width, rows), BF16),
            shape_of((width, rows), BF16),
            shape_of((2 * HEADS, rows), F32),
        ),
        in_specs=[in_hbm, whole((1, width))] + [whole((block, width))] * n_seq,
        out_specs=[whole((1, slots))]
        + [in_hbm] * 5
        + [pl.BlockSpec((pair, rows), lambda i: (i, 0)), whole((2 * HEADS, rows))],
        scratch_shapes=[
            pltpu.VMEM((width, 3 * width), BF16),
            pltpu.VMEM((rows, width), F32),
            pltpu.VMEM((rows, LANES), F32),
            pltpu.VMEM((rows, width), BF16),
            pltpu.VMEM((rows, 3 * width), BF16),
            pltpu.VMEM((3 * width, rows), BF16),
            pltpu.SemaphoreType.DMA((6,)),
        ],
        compiler_params=params(60),
        cost_estimate=pl.CostEstimate(
            flops=6 * rows * width * width + 8 * HEADS * rows * rows * pair,
            bytes_accessed=16 * MIB,
            transcendentals=HEADS * rows * rows,
        ),
        name="forward",
    )(w_qkv, gain_row, *feats_got)

    chip_bits = tuple(zip(*chip_orders(n_seq)))[:2]
    *quarters, serial_grad, d_normed = pl.pallas_call(
        functools.partial(backward_kernel, n_seq, chip_bits),
        grid=(pairs,),
        out_shape=[shape_of(sum_shape, F32)] * 4
        + [shape_of((rows, width), BF16), shape_of((rows, width), F32)],
        in_specs=[
            in_smem,
            whole((1, slots)),
            whole((width, width)),
            whole((2 * HEADS, rows)),
        ]
        + [in_hbm] * 7,
        out_specs=[in_hbm] * 6,
        scratch_shapes=[
            pltpu.VMEM((slots, width), BF16),
            pltpu.VMEM((rows, 3 * width), BF16),
            pltpu.VMEM((2 * width, rows), BF16),
            pltpu.VMEM((width, 3 * width), BF16),
            pltpu.VMEM((rows, width), F32),
            pltpu.VMEM((rows, width), BF16),
            pltpu.VMEM((width, rows), BF16),
        ]
        + [pltpu.VMEM(sum_shape, F32)] * 4
        + [
            pltpu.VMEM((rows, width), BF16),
            pltpu.VMEM((rows, width), F32),
            pltpu.VMEM((rows, width), BF16),
            pltpu.VMEM((width, rows), BF16),
            pltpu.VMEM((rows, 3 * width), BF16),
            pltpu.VMEM((width, rows), BF16),
            pltpu.VMEM((width, LANES), F32),
            pltpu.SemaphoreType.DMA((13,)),
        ],
        compiler_params=params(60),
        cost_estimate=pl.CostEstimate(
            flops=12 * rows * width * width + 10 * HEADS * rows * rows * pair,
            bytes_accessed=16 * MIB,
            transcendentals=HEADS * rows * rows,
        ),
        name="backward",
    )(me, pos, w_proj, stats, grads_got, qkv, trans, w_qkv, xhat, normed, attn_t)

    steps = chip_steps()
    terms = first_step(quarters, steps)
    d_normed, terms = lax.optimization_barrier((d_normed, terms))
    back = pl.pallas_call(
        functools.partial(residual_kernel, n_seq),
        out_shape=shape_of((slots, width), BF16),
        in_specs=[in_smem] + [in_vmem] * 6,
        out_specs=in_vmem,
        compiler_params=params(20),
        cost_estimate=pl.CostEstimate(
            flops=2 * slots * rows * width, bytes_accessed=4 * MIB, transcendentals=0
        ),
        name="residual",
    )(me, pos, gain_row, inv, xhat, serial_grad, d_normed)
    returned = exchange(back)
    terms = next_steps(terms, steps)
    part, returned = lax.optimization_barrier((reduce_over_planes(terms), returned))
    own = share_in_plane(share_over_planes(part), steps)
    other = lax.ppermute(own, "seq", core_pairs())
    grad_local = pl.pallas_call(
        functools.partial(unpack_kernel, n_seq),
        out_shape=shape_of((rows, width), BF16),
        in_specs=[in_smem] + [in_vmem] * 2,
        out_specs=in_vmem,
        compiler_params=params(20),
        cost_estimate=pl.CostEstimate(
            flops=2 * slots * rows * width, bytes_accessed=2 * MIB, transcendentals=0
        ),
        name="unpack",
    )(me, slot, returned)
    half = width // 2
    grad_qkv, grad_proj, gain_grad = pl.pallas_call(
        split_kernel,
        grid=(2,),
        out_shape=(
            shape_of((width, 3 * width), F32),
            shape_of((width, width), F32),
            shape_of((1, width), F32),
        ),
        in_specs=[in_smem] + [whole(own.shape)] * 2,
        out_specs=[
            pl.BlockSpec((half, 3 * width), lambda i: (i, 0)),
            pl.BlockSpec((half, width), lambda i: (i, 0)),
            pl.BlockSpec((1, half), lambda i: (0, i)),
        ],
        compiler_params=params(20),
        cost_estimate=pl.CostEstimate(flops=0, bytes_accessed=8 * MIB, transcendentals=0),
        name="split",
    )(lax.bitwise_and(me, 1), own, other)
    return (grad_local[None], grad_qkv, grad_proj, gain_grad[0])


def solution(mesh):
    return jax.shard_map(
        per_device,
        mesh=mesh,
        in_specs=(P("dp", "seq", None), P("dp", "seq", None), P("dp", "seq"), P(), P(), P()),
        out_specs=(P("dp", "seq", None), P(), P(), P()),
        check_vma=False,
    )
```

```python
import functools

import jax
import jax.numpy as jnp
from jax import lax
from jax.experimental import pallas as pl
from jax.experimental.pallas import tpu as pltpu
from jax.sharding import PartitionSpec as P

HEADS = 8
PATCH = 512
EXTRA = 16
LANES = 128
BOUND = 1
EXPONENT = 2
HEADROOM = 10.0
MIB = 1024 * 1024
F32 = jnp.float32
BF16 = jnp.bfloat16
NN = (((1,), (0,)), ((), ()))
NT = (((1,), (1,)), ((), ()))


def mm(lhs, rhs, dims=NN):
    return lax.dot_general(lhs, rhs, dims, preferred_element_type=F32)


def iota(shape, dim):
    return lax.broadcasted_iota(jnp.int32, shape, dim)


def hot(mask):
    return jnp.where(mask, jnp.float32(1), jnp.float32(0)).astype(BF16)


def column_hot(row, count):
    size = row.shape[1]
    column = jnp.transpose(jnp.broadcast_to(row, (LANES, size)))
    lane = iota((size, LANES), 1)
    return jnp.concatenate([hot(column == lane + j * LANES) for j in range(count // LANES)], axis=1)


def by_receiver(me, distance, capacity):
    return pl.ds(pl.multiple_of(lax.bitwise_xor(me, distance) * capacity, capacity), capacity)


def pack_kernel(n_seq, capacity, me_ref, dest_hbm, feats_hbm, slot_out, *refs):
    outs, (dest_ref, feats_ref, sems) = refs[:n_seq], refs[n_seq:]
    rows, width = feats_ref.shape
    slots = n_seq * capacity
    loads = [
        pltpu.make_async_copy(source, target, sems.at[i])
        for i, (source, target) in enumerate(((dest_hbm, dest_ref), (feats_hbm, feats_ref)))
    ]
    for load in loads:
        load.start()
    loads[0].wait()
    shift = rows.bit_length() - 1
    places = dest_ref[...]
    distance = lax.bitwise_xor(lax.shift_right_logical(places, shift), me_ref[0])
    within = lax.bitwise_and(places, rows - 1) + 1
    member = iota((n_seq, rows), 0) == distance
    upper = hot(iota((rows, rows), 0) <= iota((rows, rows), 1))
    counts = mm(hot(member), upper)
    rank = jnp.sum(jnp.where(member, counts, 0.0), axis=0, keepdims=True).astype(jnp.int32) - 1
    slot = distance * capacity + rank
    slot_out[...] = slot
    select = hot(iota((slots, rows), 0) == slot)
    loads[1].wait()
    feats = mm(select, feats_ref[...]).astype(BF16)
    upper_half = slot >= width
    high = lax.shift_right_logical(within, 8).astype(F32)
    low = lax.bitwise_and(within, 255).astype(F32)
    line = iota((n_seq * EXTRA, rows), 0)
    kind = lax.bitwise_and(line, EXTRA - 1)
    digit = jnp.where(kind < 2, high, low)
    wanted = (
        (lax.shift_right_logical(line, EXTRA.bit_length() - 1) == distance)
        & (kind < 4)
        & ((lax.bitwise_and(kind, 1) == 1) == upper_half)
    )
    digits = jnp.where(wanted, digit, 0.0).astype(BF16)
    spread = hot(iota((width, rows), 0) == lax.bitwise_and(slot, width - 1))
    position = mm(digits, spread, NT).astype(BF16)
    for d in range(n_seq):
        outs[d][:capacity, :] = feats[d * capacity : (d + 1) * capacity]
        outs[d][capacity:, :] = position[d * EXTRA : (d + 1) * EXTRA]


def pack_grads_kernel(n_seq, capacity, me_ref, slot_ref, grads_ref, grads_out):
    select = hot(iota((n_seq * capacity, grads_ref.shape[0]), 0) == slot_ref[...])
    grads = mm(select, grads_ref[...]).astype(BF16)
    for d in range(n_seq):
        grads_out[by_receiver(me_ref[0], d, capacity), :] = grads[d * capacity : (d + 1) * capacity]


def forward_kernel(n_seq, capacity, w_hbm, gain_ref, *refs):
    recv, refs = refs[:n_seq], refs[n_seq:]
    pos_out, xhat_hbm, inv_hbm, normed_hbm, qkv_hbm, trans_hbm, attn_out, stats_out = refs[:8]
    w_ref, xhat_ref, inv_ref, normed_ref, qkv_ref, trans, sems = refs[8:]
    width = w_ref.shape[0]
    rows = xhat_ref.shape[0]
    head = width // HEADS
    pair = 2 * head
    step = pl.program_id(0)
    w_copy = pltpu.make_async_copy(w_hbm, w_ref, sems.at[0])
    saves = [
        pltpu.make_async_copy(source, target, sems.at[1 + i])
        for i, (source, target) in enumerate(
            (
                (xhat_ref, xhat_hbm),
                (inv_ref, inv_hbm),
                (normed_ref, normed_hbm),
                (qkv_ref, qkv_hbm),
                (trans.at[pl.ds(0, 2 * width)], trans_hbm),
            )
        )
    ]

    @pl.when(step == 0)
    def _():
        w_copy.start()
        tile = recv[0][capacity:, :].astype(F32)
        for s in range(1, n_seq):
            tile = tile + recv[s][capacity:, :].astype(F32)
        high = jnp.concatenate([tile[0:1], tile[1:2]], axis=1)
        low = jnp.concatenate([tile[2:3], tile[3:4]], axis=1)
        pos = (high * 256.0 + low).astype(jnp.int32) - 1
        pos_out[...] = pos
        place = hot(iota((rows, n_seq * capacity), 0) == pos)
        values = jnp.concatenate([recv[s][:capacity, :] for s in range(n_seq)], axis=0)
        feats = mm(place, values)
        centered = feats - jnp.mean(feats, axis=1, keepdims=True)
        inv = lax.rsqrt(jnp.mean(centered * centered, axis=1, keepdims=True) + 1e-05)
        xhat = centered * inv
        xhat_ref[...] = xhat
        inv_ref[...] = jnp.broadcast_to(inv, inv_ref.shape)
        normed = (xhat * gain_ref[...]).astype(BF16)
        normed_ref[...] = normed
        w_copy.wait()
        qkv = mm(normed, w_ref[...])
        qkv_ref[...] = qkv.astype(BF16)
        trans[...] = jnp.transpose(qkv).astype(BF16)
        for save in saves:
            save.start()

    lo = pl.multiple_of(step * pair, pair)
    keys = qkv_ref[:, pl.ds(pl.multiple_of(width + step * pair, pair), pair)]
    query_t = trans[pl.ds(lo, pair), :] * BF16(0.125)
    zero = jnp.zeros((head, rows), BF16)
    for j in range(2):
        part = query_t[j * head : (j + 1) * head]
        part = jnp.concatenate([part, zero] if j == 0 else [zero, part], axis=0)
        scores = mm(keys, part)
        top = jnp.max(scores, axis=0, keepdims=True)
        expo = jnp.exp(scores - top)
        share = 1.0 / jnp.sum(expo, axis=0, keepdims=True)
        probs = expo * share
        stats_out[pl.ds(2 * step + j, 1), :] = top
        stats_out[pl.ds(HEADS + 2 * step + j, 1), :] = share
        values_t = trans[pl.ds(pl.multiple_of(2 * width + step * pair + j * head, head), head), :]
        attn_out[j * head : (j + 1) * head, :] = mm(values_t, probs.astype(BF16)).astype(BF16)

    @pl.when(step == pl.num_programs(0) - 1)
    def _():
        for save in saves:
            save.wait()


def backward_kernel(n_seq, chip_bits, me_ref, pos_ref, w_proj_ref, stats_ref, *refs):
    (recv_hbm, qkv_hbm, trans_hbm, w_hbm, xhat_hbm, normed_hbm, attn_hbm), refs = refs[:7], refs[7:]
    outs, serial_grad_hbm, d_normed_hbm, refs = refs[:4], refs[4], refs[5], refs[6:]
    recv_ref, qkv_ref, trans_ref, w_ref, xhat_ref, normed_ref, attn_ref, refs = *refs[:7], refs[7:]
    sums, refs = refs[:4], refs[4:]
    serial_grad, d_normed_ref, d_attn, d_attn_t, d_qkv, normed_t, gain_column, sems = refs
    width = w_proj_ref.shape[0]
    rows = xhat_ref.shape[0]
    capacity = recv_ref.shape[0] // n_seq
    head = width // HEADS
    pair = 2 * head
    step = pl.program_id(0)
    me = me_ref[0]
    loads = [
        pltpu.make_async_copy(source, target, sems.at[i])
        for i, (source, target) in enumerate(
            (
                (recv_hbm, recv_ref),
                (qkv_hbm, qkv_ref),
                (trans_hbm, trans_ref),
                (normed_hbm, normed_ref),
                (w_hbm, w_ref),
                (xhat_hbm, xhat_ref),
                (attn_hbm, attn_ref),
            )
        )
    ]
    saves = [
        pltpu.make_async_copy(source, target, sems.at[7 + i])
        for i, (source, target) in enumerate(
            [*zip(sums, outs), (serial_grad, serial_grad_hbm), (d_normed_ref, d_normed_hbm)]
        )
    ]

    @pl.when(step == 0)
    def _():
        for load in loads:
            load.start()
        place = hot(iota((rows, n_seq * capacity), 0) == pos_ref[...])
        loads[0].wait()
        values = jnp.concatenate(
            [recv_ref[by_receiver(me, d, capacity), :] for d in range(n_seq)], axis=0
        )
        grads = mm(place, values).astype(BF16)
        serial_grad[...] = grads
        saves[4].start()
        d_att = mm(grads, w_proj_ref[...], NT).astype(BF16)
        d_attn[...] = d_att
        d_attn_t[...] = jnp.transpose(d_att.astype(F32)).astype(BF16)
        loads[1].wait()
        loads[2].wait()

    lo = pl.multiple_of(step * pair, pair)
    queries = qkv_ref[:, pl.ds(lo, pair)]
    values = qkv_ref[:, pl.ds(pl.multiple_of(2 * width + step * pair, pair), pair)]
    d_att_t = d_attn_t[pl.ds(lo, pair), :] * BF16(0.125)
    d_att = d_attn[:, pl.ds(lo, pair)]
    keys = qkv_ref[:, pl.ds(pl.multiple_of(width + step * pair, pair), pair)]
    query_t = trans_ref[pl.ds(lo, pair), :] * BF16(0.125)
    zero = jnp.zeros((head, rows), BF16)
    d_q, d_k, d_v = [], [], []
    for j in range(2):
        def alone(both):
            part = both[j * head : (j + 1) * head]
            return jnp.concatenate([part, zero] if j == 0 else [zero, part], axis=0)

        top = stats_ref[pl.ds(2 * step + j, 1), :]
        share = stats_ref[pl.ds(HEADS + 2 * step + j, 1), :]
        probs = jnp.exp(mm(keys, alone(query_t)) - top) * share
        d_probs = mm(values, alone(d_att_t))
        total = jnp.sum(d_probs * probs, axis=0, keepdims=True)
        d_scores = (probs * (d_probs - total)).astype(BF16)
        k_t = trans_ref[pl.ds(pl.multiple_of(width + step * pair + j * head, head), head), :]
        d_q.append(mm(k_t, d_scores))
        d_k.append(mm(d_scores, queries))
        d_v.append(mm(probs.astype(BF16), d_att))
    first = iota((rows, pair), 1) < head
    d_qkv[:, pl.ds(lo, pair)] = jnp.transpose(jnp.concatenate(d_q, axis=0)).astype(BF16)
    d_qkv[:, pl.ds(pl.multiple_of(width + step * pair, pair), pair)] = jnp.where(
        first, d_k[0], d_k[1]
    ).astype(BF16)
    d_qkv[:, pl.ds(pl.multiple_of(2 * width + step * pair, pair), pair)] = jnp.where(
        first, d_v[0], d_v[1]
    ).astype(BF16)

    @pl.when(step == pl.num_programs(0) - 1)
    def _():
        for load in loads[3:]:
            load.wait()
        normed_t[...] = jnp.transpose(normed_ref[...].astype(F32)).astype(BF16)
        d_normed = mm(d_qkv[...], w_ref[...], NT)
        d_normed_ref[...] = d_normed
        saves[5].start()
        gain_row = jnp.sum(d_normed * xhat_ref[...], axis=0, keepdims=True)
        gain_column[...] = jnp.transpose(jnp.broadcast_to(gain_row, (LANES, width)))
        eighth = width // 8
        odd = lax.bitwise_and(me, 1)

        def sides(even_bit, odd_bit):
            even_side = lax.bitwise_and(lax.shift_right_logical(me, even_bit), 1)
            odd_side = lax.bitwise_and(lax.shift_right_logical(me, odd_bit), 1)
            mine = jnp.where(odd == 1, odd_side, even_side)
            return mine, even_side + odd_side - mine

        (mine, other), (mine_next, other_next) = (sides(*bits) for bits in chip_bits)
        starts = (
            ((1 - odd) * 2 + 1 - other, other_next),
            ((1 - odd) * 2 + other, other_next),
            (odd * 2 + 1 - mine, mine_next),
            (odd * 2 + mine, mine_next),
        )
        for out, (start, side), save in zip(sums, starts, saves):
            bound = jnp.full((1, 1), 0.0, F32)
            for j, half in enumerate((1 - side, side)):
                part = pl.ds(pl.multiple_of((start * 2 + half) * eighth, eighth), eighth)
                lines = slice(j * eighth, (j + 1) * eighth)
                blocks = (
                    mm(normed_t[part, :], d_qkv[...]),
                    mm(attn_ref[part, :], serial_grad[...]),
                    gain_column[part, :],
                )
                column = 0
                for block in blocks:
                    out[lines, column : column + block.shape[1]] = block
                    column += block.shape[1]
                    largest = jnp.max(jnp.abs(block), axis=0, keepdims=True)
                    bound = jnp.maximum(bound, jnp.max(largest, axis=1, keepdims=True))
            lane = iota((2 * eighth, LANES), 1)
            out[:, 4 * width :] = jnp.where(lane == BOUND, bound, out[:, 4 * width :])
            save.start()
        for save in saves:
            save.wait()


def residual_kernel(
    n_seq, me_ref, pos_ref, gain_ref, inv_ref, xhat_ref, serial_grad_ref, d_normed_ref, back_out
):
    xhat = xhat_ref[...]
    rows = xhat.shape[0]
    capacity = pos_ref.shape[1] // n_seq
    scaled = d_normed_ref[...] * gain_ref[...]
    residual = inv_ref[:, 0:1] * (
        scaled
        - jnp.mean(scaled, axis=1, keepdims=True)
        - xhat * jnp.mean(scaled * xhat, axis=1, keepdims=True)
    )
    serial_dx = (serial_grad_ref[...].astype(F32) + residual).astype(BF16)
    returned = mm(column_hot(pos_ref[...], rows), serial_dx).astype(BF16)
    for d in range(n_seq):
        back_out[by_receiver(me_ref[0], d, capacity), :] = returned[d * capacity : (d + 1) * capacity]


def unpack_kernel(n_seq, me_ref, slot_ref, recv_ref, out_ref):
    capacity = recv_ref.shape[0] // n_seq
    values = jnp.concatenate(
        [recv_ref[by_receiver(me_ref[0], d, capacity), :] for d in range(n_seq)], axis=0
    )
    out_ref[...] = mm(column_hot(slot_ref[...], values.shape[0]), values).astype(BF16)


def split_kernel(side_ref, own_ref, other_ref, qkv_out, proj_out, gain_out):
    width = proj_out.shape[1]

    def write(ref):
        qkv_out[...] = ref[:, : 3 * width].astype(F32)
        proj_out[...] = ref[:, 3 * width : 4 * width].astype(F32)
        gain_out[...] = jnp.transpose(ref[:, 4 * width :].astype(F32))[0:1]

    own = pl.program_id(0) == side_ref[0]
    pl.when(own)(lambda: write(own_ref))
    pl.when(jnp.logical_not(own))(lambda: write(other_ref))


def whole(shape):
    return pl.BlockSpec(shape, lambda *_: (0,) * len(shape), pipeline_mode=pl.Buffered(1))


def params(mib):
    return pltpu.CompilerParams(vmem_limit_bytes=mib * MIB)


def shape_of(shape, dtype):
    return jax.ShapeDtypeStruct(shape, dtype)


def by_distance(blocks, axis):
    count = len(blocks)
    return [blocks[0]] + [
        lax.ppermute(blocks[k], axis, [(i, i ^ k) for i in range(count)]) for k in range(1, count)
    ]


def chip_orders(n_seq):
    bits = list(range(1, n_seq.bit_length() - 1))
    middle = len(bits) // 2
    return bits, bits[middle:] + bits[:middle]


def chip_steps():
    n_seq, me = lax.axis_size("seq"), lax.axis_index("seq")
    odd = lax.bitwise_and(me, 1) == 1

    def side(bit):
        return lax.bitwise_and(lax.shift_right_logical(me, jnp.asarray(bit, me.dtype)), 1)

    steps = []
    for even_bit, odd_bit in zip(*chip_orders(n_seq)):
        pairs = [(i, i ^ (1 << (odd_bit if i & 1 else even_bit))) for i in range(n_seq)]
        steps.append((pairs, jnp.where(odd, side(odd_bit), side(even_bit))))
    return steps


def encode(total, bound):
    exponent = jnp.clip(jnp.ceil(jnp.log2(bound)), -100.0, 100.0)
    lane = lax.broadcasted_iota(jnp.int32, total.shape, 1) - (total.shape[1] - LANES)
    scaled = total * jnp.exp2(HEADROOM - exponent)
    return jnp.where(lane == EXPONENT, exponent, scaled).astype(jnp.float16)


def decode(message):
    exponent = message[0, message.shape[1] - LANES + EXPONENT].astype(F32)
    return message, jnp.exp2(exponent - HEADROOM)


def bound_of(terms):
    return sum(array[0, array.shape[1] - LANES + BOUND].astype(F32) * factor for array, factor in terms)


def piece(terms, index, count):
    size = terms[0][0].shape[0] // count

    def cut(array):
        if isinstance(index, int):
            return array[index * size : (index + 1) * size]
        return lax.dynamic_slice_in_dim(array, index * size, size)

    return functools.reduce(jnp.add, [cut(array).astype(F32) * factor for array, factor in terms])


def core_pairs():
    return [(i, i ^ 1) for i in range(lax.axis_size("seq"))]


def first_step(quarters, steps):
    pass_on, pass_keep, own_on, own_keep = quarters
    got = lax.ppermute(pass_on, "seq", core_pairs())
    send = encode(own_on + got, bound_of([(own_on, 1.0), (got, 1.0)]))
    keep = own_keep + lax.ppermute(pass_keep, "seq", core_pairs())
    return [(keep, 1.0), decode(lax.ppermute(send, "seq", steps[0][0]))]


def next_steps(terms, steps):
    for i, (pairs, side) in enumerate(steps[1:]):
        on, stay = (0, 1) if i == 0 else (1 - side, side)
        send = encode(piece(terms, on, 2), bound_of(terms))
        keep = piece(terms, stay, 2)
        terms = [(keep, 1.0), decode(lax.ppermute(send, "seq", pairs))]
    return terms


def reduce_over_planes(terms):
    n_dp, plane = lax.axis_size("dp"), lax.axis_index("dp")
    bound = bound_of(terms)
    own = piece(terms, plane, n_dp)
    sent = [encode(piece(terms, lax.bitwise_xor(plane, k), n_dp), bound) for k in range(1, n_dp)]
    got = [decode(message) for message in by_distance([None] + sent, "dp")[1:]]
    return piece([(own, 1.0)] + got, 0, 1).astype(BF16)


def share_over_planes(part):
    n_dp, plane = lax.axis_size("dp"), lax.axis_index("dp")
    shares = jnp.stack(by_distance([part] * n_dp, "dp"))
    return jnp.concatenate(
        [lax.dynamic_index_in_dim(shares, lax.bitwise_xor(plane, p), keepdims=False) for p in range(n_dp)],
        axis=0,
    )


def share_in_plane(part, steps):
    for pairs, side in reversed(steps):
        other = lax.ppermute(part, "seq", pairs)
        part = jnp.where(
            side == 0, jnp.concatenate([part, other], axis=0), jnp.concatenate([other, part], axis=0)
        )
    return part


def per_device(points, cotangent, dest, w_qkv, w_proj, gain):
    feats = points[0]
    grads = cotangent[0]
    rows, width = feats.shape
    n_seq = lax.axis_size("seq")
    capacity = 2 * (rows // n_seq)
    slots = n_seq * capacity
    block = capacity + EXTRA
    pairs = HEADS // 2
    pair = width // pairs
    sum_shape = (width // 4, 4 * width + LANES)
    me = jnp.reshape(lax.axis_index("seq").astype(jnp.int32), (1,))
    gain_row = gain.reshape(1, width)
    in_smem = pl.BlockSpec(memory_space=pltpu.SMEM)
    in_vmem = pl.BlockSpec(memory_space=pltpu.VMEM)
    in_hbm = pl.BlockSpec(memory_space=pl.ANY)
    stay_hbm = pl.BlockSpec(memory_space=pltpu.HBM)

    slot, *feats_sent = pl.pallas_call(
        functools.partial(pack_kernel, n_seq, capacity),
        out_shape=[shape_of((1, rows), jnp.int32)] + [shape_of((block, width), BF16)] * n_seq,
        in_specs=[in_smem] + [stay_hbm] * 2,
        out_specs=[in_vmem] * (1 + n_seq),
        scratch_shapes=[
            pltpu.VMEM((1, rows), jnp.int32),
            pltpu.VMEM((rows, width), BF16),
            pltpu.SemaphoreType.DMA((2,)),
        ],
        compiler_params=params(60),
        cost_estimate=pl.CostEstimate(
            flops=2 * slots * rows * width, bytes_accessed=2 * MIB, transcendentals=0
        ),
        name="pack",
    )(me, dest, feats)
    feats_got = by_distance(feats_sent, "seq")
    feats_got[1], slot = lax.optimization_barrier((feats_got[1], slot))
    grads_sent = pl.pallas_call(
        functools.partial(pack_grads_kernel, n_seq, capacity),
        out_shape=shape_of((slots, width), BF16),
        in_specs=[in_smem] + [in_vmem] * 2,
        out_specs=in_vmem,
        compiler_params=params(20),
        cost_estimate=pl.CostEstimate(
            flops=2 * slots * rows * width, bytes_accessed=2 * MIB, transcendentals=0
        ),
        name="pack_grads",
    )(me, slot, grads)

    def exchange(sent):
        sent = sent.reshape(n_seq, capacity, width)
        got = lax.all_to_all(sent, "seq", split_axis=0, concat_axis=0, tiled=True)
        return got.reshape(slots, width)

    grads_got = exchange(grads_sent)

    pos, xhat, inv, normed, qkv, trans, attn_t, stats = pl.pallas_call(
        functools.partial(forward_kernel, n_seq, capacity),
        grid=(pairs,),
        out_shape=(
            shape_of((1, slots), jnp.int32),
            shape_of((rows, width), F32),
            shape_of((rows, LANES), F32),
            shape_of((rows, width), BF16),
            shape_of((rows, 3 * width), BF16),
            shape_of((2 * width, rows), BF16),
            shape_of((width, rows), BF16),
            shape_of((2 * HEADS, rows), F32),
        ),
        in_specs=[in_hbm, whole((1, width))] + [whole((block, width))] * n_seq,
        out_specs=[whole((1, slots))]
        + [in_hbm] * 5
        + [pl.BlockSpec((pair, rows), lambda i: (i, 0)), whole((2 * HEADS, rows))],
        scratch_shapes=[
            pltpu.VMEM((width, 3 * width), BF16),
            pltpu.VMEM((rows, width), F32),
            pltpu.VMEM((rows, LANES), F32),
            pltpu.VMEM((rows, width), BF16),
            pltpu.VMEM((rows, 3 * width), BF16),
            pltpu.VMEM((3 * width, rows), BF16),
            pltpu.SemaphoreType.DMA((6,)),
        ],
        compiler_params=params(60),
        cost_estimate=pl.CostEstimate(
            flops=6 * rows * width * width + 8 * HEADS * rows * rows * pair,
            bytes_accessed=16 * MIB,
            transcendentals=HEADS * rows * rows,
        ),
        name="forward",
    )(w_qkv, gain_row, *feats_got)

    chip_bits = tuple(zip(*chip_orders(n_seq)))[:2]
    *quarters, serial_grad, d_normed = pl.pallas_call(
        functools.partial(backward_kernel, n_seq, chip_bits),
        grid=(pairs,),
        out_shape=[shape_of(sum_shape, F32)] * 4
        + [shape_of((rows, width), BF16), shape_of((rows, width), F32)],
        in_specs=[
            in_smem,
            whole((1, slots)),
            whole((width, width)),
            whole((2 * HEADS, rows)),
        ]
        + [in_hbm] * 7,
        out_specs=[in_hbm] * 6,
        scratch_shapes=[
            pltpu.VMEM((slots, width), BF16),
            pltpu.VMEM((rows, 3 * width), BF16),
            pltpu.VMEM((2 * width, rows), BF16),
            pltpu.VMEM((width, 3 * width), BF16),
            pltpu.VMEM((rows, width), F32),
            pltpu.VMEM((rows, width), BF16),
            pltpu.VMEM((width, rows), BF16),
        ]
        + [pltpu.VMEM(sum_shape, F32)] * 4
        + [
            pltpu.VMEM((rows, width), BF16),
            pltpu.VMEM((rows, width), F32),
            pltpu.VMEM((rows, width), BF16),
            pltpu.VMEM((width, rows), BF16),
            pltpu.VMEM((rows, 3 * width), BF16),
            pltpu.VMEM((width, rows), BF16),
            pltpu.VMEM((width, LANES), F32),
            pltpu.SemaphoreType.DMA((13,)),
        ],
        compiler_params=params(60),
        cost_estimate=pl.CostEstimate(
            flops=12 * rows * width * width + 10 * HEADS * rows * rows * pair,
            bytes_accessed=16 * MIB,
            transcendentals=HEADS * rows * rows,
        ),
        name="backward",
    )(me, pos, w_proj, stats, grads_got, qkv, trans, w_qkv, xhat, normed, attn_t)

    steps = chip_steps()
    terms = first_step(quarters, steps)
    d_normed, terms = lax.optimization_barrier((d_normed, terms))
    back = pl.pallas_call(
        functools.partial(residual_kernel, n_seq),
        out_shape=shape_of((slots, width), BF16),
        in_specs=[in_smem] + [in_vmem] * 6,
        out_specs=in_vmem,
        compiler_params=params(20),
        cost_estimate=pl.CostEstimate(
            flops=2 * slots * rows * width, bytes_accessed=4 * MIB, transcendentals=0
        ),
        name="residual",
    )(me, pos, gain_row, inv, xhat, serial_grad, d_normed)
    returned = exchange(back)
    terms = next_steps(terms, steps)
    part, returned = lax.optimization_barrier((reduce_over_planes(terms), returned))
    own = share_in_plane(share_over_planes(part), steps)
    other = lax.ppermute(own, "seq", core_pairs())
    grad_local = pl.pallas_call(
        functools.partial(unpack_kernel, n_seq),
        out_shape=shape_of((rows, width), BF16),
        in_specs=[in_smem] + [in_vmem] * 2,
        out_specs=in_vmem,
        compiler_params=params(20),
        cost_estimate=pl.CostEstimate(
            flops=2 * slots * rows * width, bytes_accessed=2 * MIB, transcendentals=0
        ),
        name="unpack",
    )(me, slot, returned)
    half = width // 2
    grad_qkv, grad_proj, gain_grad = pl.pallas_call(
        split_kernel,
        grid=(2,),
        out_shape=(
            shape_of((width, 3 * width), F32),
            shape_of((width, width), F32),
            shape_of((1, width), F32),
        ),
        in_specs=[in_smem] + [whole(own.shape)] * 2,
        out_specs=[
            pl.BlockSpec((half, 3 * width), lambda i: (i, 0)),
            pl.BlockSpec((half, width), lambda i: (i, 0)),
            pl.BlockSpec((1, half), lambda i: (0, i)),
        ],
        compiler_params=params(20),
        cost_estimate=pl.CostEstimate(flops=0, bytes_accessed=8 * MIB, transcendentals=0),
        name="split",
    )(lax.bitwise_and(me, 1), own, other)
    return (grad_local[None], grad_qkv, grad_proj, gain_grad[0])


def solution(mesh):
    return jax.shard_map(
        per_device,
        mesh=mesh,
        in_specs=(P("dp", "seq", None), P("dp", "seq", None), P("dp", "seq"), P(), P(), P()),
        out_specs=(P("dp", "seq", None), P(), P(), P()),
        check_vma=False,
    )
```

```python
import functools

import jax
import jax.numpy as jnp
from jax import lax
from jax.experimental import pallas as pl
from jax.experimental.pallas import tpu as pltpu
from jax.sharding import PartitionSpec as P

HEADS = 8
PATCH = 512
EXTRA = 16
LANES = 128
CODE_MAX = 32000.0
DIGIT = 60000.0
MIB = 1024 * 1024
F32 = jnp.float32
BF16 = jnp.bfloat16
NN = (((1,), (0,)), ((), ()))
NT = (((1,), (1,)), ((), ()))


def mm(lhs, rhs, dims=NN):
    return lax.dot_general(lhs, rhs, dims, preferred_element_type=F32)


def iota(shape, dim):
    return lax.broadcasted_iota(jnp.int32, shape, dim)


def hot(mask):
    return jnp.where(mask, jnp.float32(1), jnp.float32(0)).astype(BF16)


def column_hot(row, count):
    size = row.shape[1]
    column = jnp.transpose(jnp.broadcast_to(row, (LANES, size)))
    lane = iota((size, LANES), 1)
    return jnp.concatenate([hot(column == lane + j * LANES) for j in range(count // LANES)], axis=1)


def by_receiver(me, distance, capacity):
    return pl.ds(pl.multiple_of(lax.bitwise_xor(me, distance) * capacity, capacity), capacity)


def pack_kernel(n_seq, capacity, me_ref, dest_hbm, feats_hbm, slot_out, *refs):
    outs, (dest_ref, feats_ref, sems) = refs[:n_seq], refs[n_seq:]
    rows, width = feats_ref.shape
    slots = n_seq * capacity
    loads = [
        pltpu.make_async_copy(source, target, sems.at[i])
        for i, (source, target) in enumerate(((dest_hbm, dest_ref), (feats_hbm, feats_ref)))
    ]
    for load in loads:
        load.start()
    loads[0].wait()
    shift = rows.bit_length() - 1
    places = dest_ref[...]
    distance = lax.bitwise_xor(lax.shift_right_logical(places, shift), me_ref[0])
    within = lax.bitwise_and(places, rows - 1) + 1
    member = iota((n_seq, rows), 0) == distance
    upper = hot(iota((rows, rows), 0) <= iota((rows, rows), 1))
    counts = mm(hot(member), upper)
    rank = jnp.sum(jnp.where(member, counts, 0.0), axis=0, keepdims=True).astype(jnp.int32) - 1
    slot = distance * capacity + rank
    slot_out[...] = slot
    select = hot(iota((slots, rows), 0) == slot)
    loads[1].wait()
    feats = mm(select, feats_ref[...]).astype(BF16)
    upper_half = slot >= width
    high = lax.shift_right_logical(within, 8).astype(F32)
    low = lax.bitwise_and(within, 255).astype(F32)
    line = iota((n_seq * EXTRA, rows), 0)
    kind = lax.bitwise_and(line, EXTRA - 1)
    digit = jnp.where(kind < 2, high, low)
    wanted = (
        (lax.shift_right_logical(line, EXTRA.bit_length() - 1) == distance)
        & (kind < 4)
        & ((lax.bitwise_and(kind, 1) == 1) == upper_half)
    )
    digits = jnp.where(wanted, digit, 0.0).astype(BF16)
    spread = hot(iota((width, rows), 0) == lax.bitwise_and(slot, width - 1))
    position = mm(digits, spread, NT).astype(BF16)
    for d in range(n_seq):
        outs[d][:capacity, :] = feats[d * capacity : (d + 1) * capacity]
        outs[d][capacity:, :] = position[d * EXTRA : (d + 1) * EXTRA]


def pack_grads_kernel(n_seq, capacity, me_ref, slot_ref, grads_ref, grads_out):
    select = hot(iota((n_seq * capacity, grads_ref.shape[0]), 0) == slot_ref[...])
    grads = mm(select, grads_ref[...]).astype(BF16)
    for d in range(n_seq):
        grads_out[by_receiver(me_ref[0], d, capacity), :] = grads[d * capacity : (d + 1) * capacity]


def forward_kernel(n_seq, capacity, w_hbm, gain_ref, *refs):
    recv, refs = refs[:n_seq], refs[n_seq:]
    pos_out, xhat_hbm, inv_hbm, normed_hbm, qkv_hbm, trans_hbm, attn_out, stats_out = refs[:8]
    w_ref, xhat_ref, inv_ref, normed_ref, qkv_ref, trans, sems = refs[8:]
    width = w_ref.shape[0]
    rows = xhat_ref.shape[0]
    head = width // HEADS
    pair = 2 * head
    step = pl.program_id(0)
    w_copy = pltpu.make_async_copy(w_hbm, w_ref, sems.at[0])
    saves = [
        pltpu.make_async_copy(source, target, sems.at[1 + i])
        for i, (source, target) in enumerate(
            (
                (xhat_ref, xhat_hbm),
                (inv_ref, inv_hbm),
                (normed_ref, normed_hbm),
                (qkv_ref, qkv_hbm),
                (trans.at[pl.ds(0, 2 * width)], trans_hbm),
            )
        )
    ]

    @pl.when(step == 0)
    def _():
        w_copy.start()
        tile = recv[0][capacity:, :].astype(F32)
        for s in range(1, n_seq):
            tile = tile + recv[s][capacity:, :].astype(F32)
        high = jnp.concatenate([tile[0:1], tile[1:2]], axis=1)
        low = jnp.concatenate([tile[2:3], tile[3:4]], axis=1)
        pos = (high * 256.0 + low).astype(jnp.int32) - 1
        pos_out[...] = pos
        place = hot(iota((rows, n_seq * capacity), 0) == pos)
        values = jnp.concatenate([recv[s][:capacity, :] for s in range(n_seq)], axis=0)
        feats = mm(place, values)
        centered = feats - jnp.mean(feats, axis=1, keepdims=True)
        inv = lax.rsqrt(jnp.mean(centered * centered, axis=1, keepdims=True) + 1e-05)
        xhat = centered * inv
        xhat_ref[...] = xhat
        inv_ref[...] = jnp.broadcast_to(inv, inv_ref.shape)
        normed = (xhat * gain_ref[...]).astype(BF16)
        normed_ref[...] = normed
        w_copy.wait()
        qkv = mm(normed, w_ref[...])
        qkv_ref[...] = qkv.astype(BF16)
        trans[...] = jnp.transpose(qkv).astype(BF16)
        for save in saves:
            save.start()

    lo = pl.multiple_of(step * pair, pair)
    keys = qkv_ref[:, pl.ds(pl.multiple_of(width + step * pair, pair), pair)]
    query_t = trans[pl.ds(lo, pair), :] * BF16(0.125)
    zero = jnp.zeros((head, rows), BF16)
    for j in range(2):
        part = query_t[j * head : (j + 1) * head]
        part = jnp.concatenate([part, zero] if j == 0 else [zero, part], axis=0)
        scores = mm(keys, part)
        top = jnp.max(scores, axis=0, keepdims=True)
        expo = jnp.exp(scores - top)
        share = 1.0 / jnp.sum(expo, axis=0, keepdims=True)
        probs = expo * share
        stats_out[pl.ds(2 * step + j, 1), :] = top
        stats_out[pl.ds(HEADS + 2 * step + j, 1), :] = share
        values_t = trans[pl.ds(pl.multiple_of(2 * width + step * pair + j * head, head), head), :]
        attn_out[j * head : (j + 1) * head, :] = mm(values_t, probs.astype(BF16)).astype(BF16)

    @pl.when(step == pl.num_programs(0) - 1)
    def _():
        for save in saves:
            save.wait()


def backward_kernel(n_seq, chip_bits, me_ref, pos_ref, w_proj_ref, stats_ref, *refs):
    (recv_hbm, qkv_hbm, trans_hbm, w_hbm, xhat_hbm, normed_hbm, attn_hbm), refs = refs[:7], refs[7:]
    outs, serial_grad_hbm, d_normed_hbm, refs = refs[:4], refs[4], refs[5], refs[6:]
    recv_ref, qkv_ref, trans_ref, w_ref, xhat_ref, normed_ref, attn_ref, refs = *refs[:7], refs[7:]
    sums, refs = refs[:4], refs[4:]
    serial_grad, d_normed_ref, d_attn, d_attn_t, d_qkv, normed_t, gain_column, sems = refs
    width = w_proj_ref.shape[0]
    rows = xhat_ref.shape[0]
    capacity = recv_ref.shape[0] // n_seq
    head = width // HEADS
    pair = 2 * head
    step = pl.program_id(0)
    me = me_ref[0]
    loads = [
        pltpu.make_async_copy(source, target, sems.at[i])
        for i, (source, target) in enumerate(
            (
                (recv_hbm, recv_ref),
                (qkv_hbm, qkv_ref),
                (trans_hbm, trans_ref),
                (normed_hbm, normed_ref),
                (w_hbm, w_ref),
                (xhat_hbm, xhat_ref),
                (attn_hbm, attn_ref),
            )
        )
    ]
    saves = [
        pltpu.make_async_copy(source, target, sems.at[7 + i])
        for i, (source, target) in enumerate(
            [*zip(sums, outs), (serial_grad, serial_grad_hbm), (d_normed_ref, d_normed_hbm)]
        )
    ]

    @pl.when(step == 0)
    def _():
        for load in loads:
            load.start()
        place = hot(iota((rows, n_seq * capacity), 0) == pos_ref[...])
        loads[0].wait()
        values = jnp.concatenate(
            [recv_ref[by_receiver(me, d, capacity), :] for d in range(n_seq)], axis=0
        )
        grads = mm(place, values).astype(BF16)
        serial_grad[...] = grads
        saves[4].start()
        d_att = mm(grads, w_proj_ref[...], NT).astype(BF16)
        d_attn[...] = d_att
        d_attn_t[...] = jnp.transpose(d_att.astype(F32)).astype(BF16)
        loads[1].wait()
        loads[2].wait()

    lo = pl.multiple_of(step * pair, pair)
    queries = qkv_ref[:, pl.ds(lo, pair)]
    values = qkv_ref[:, pl.ds(pl.multiple_of(2 * width + step * pair, pair), pair)]
    d_att_t = d_attn_t[pl.ds(lo, pair), :] * BF16(0.125)
    d_att = d_attn[:, pl.ds(lo, pair)]
    keys = qkv_ref[:, pl.ds(pl.multiple_of(width + step * pair, pair), pair)]
    query_t = trans_ref[pl.ds(lo, pair), :] * BF16(0.125)
    zero = jnp.zeros((head, rows), BF16)
    d_q, d_k, d_v = [], [], []
    for j in range(2):
        def alone(both):
            part = both[j * head : (j + 1) * head]
            return jnp.concatenate([part, zero] if j == 0 else [zero, part], axis=0)

        top = stats_ref[pl.ds(2 * step + j, 1), :]
        share = stats_ref[pl.ds(HEADS + 2 * step + j, 1), :]
        probs = jnp.exp(mm(keys, alone(query_t)) - top) * share
        d_probs = mm(values, alone(d_att_t))
        total = jnp.sum(d_probs * probs, axis=0, keepdims=True)
        d_scores = (probs * (d_probs - total)).astype(BF16)
        k_t = trans_ref[pl.ds(pl.multiple_of(width + step * pair + j * head, head), head), :]
        d_q.append(mm(k_t, d_scores))
        d_k.append(mm(d_scores, queries))
        d_v.append(mm(probs.astype(BF16), d_att))
    first = iota((rows, pair), 1) < head
    d_qkv[:, pl.ds(lo, pair)] = jnp.transpose(jnp.concatenate(d_q, axis=0)).astype(BF16)
    d_qkv[:, pl.ds(pl.multiple_of(width + step * pair, pair), pair)] = jnp.where(
        first, d_k[0], d_k[1]
    ).astype(BF16)
    d_qkv[:, pl.ds(pl.multiple_of(2 * width + step * pair, pair), pair)] = jnp.where(
        first, d_v[0], d_v[1]
    ).astype(BF16)

    @pl.when(step == pl.num_programs(0) - 1)
    def _():
        for load in loads[3:]:
            load.wait()
        normed_t[...] = jnp.transpose(normed_ref[...].astype(F32)).astype(BF16)
        d_normed = mm(d_qkv[...], w_ref[...], NT)
        d_normed_ref[...] = d_normed
        saves[5].start()
        gain_row = jnp.sum(d_normed * xhat_ref[...], axis=0, keepdims=True)
        gain_column[...] = jnp.transpose(jnp.broadcast_to(gain_row, (LANES, width)))
        eighth = width // 8
        odd = lax.bitwise_and(me, 1)

        def sides(even_bit, odd_bit):
            even_side = lax.bitwise_and(lax.shift_right_logical(me, even_bit), 1)
            odd_side = lax.bitwise_and(lax.shift_right_logical(me, odd_bit), 1)
            mine = jnp.where(odd == 1, odd_side, even_side)
            return mine, even_side + odd_side - mine

        (mine, other), (mine_next, other_next) = (sides(*bits) for bits in chip_bits)
        starts = (
            ((1 - odd) * 2 + 1 - other, other_next),
            ((1 - odd) * 2 + other, other_next),
            (odd * 2 + 1 - mine, mine_next),
            (odd * 2 + mine, mine_next),
        )
        for out, (start, side), save in zip(sums, starts, saves):
            for j, half in enumerate((1 - side, side)):
                part = pl.ds(pl.multiple_of((start * 2 + half) * eighth, eighth), eighth)
                lines = slice(j * eighth, (j + 1) * eighth)
                out[lines, : 3 * width] = mm(normed_t[part, :], d_qkv[...])
                out[lines, 3 * width : 4 * width] = mm(attn_ref[part, :], serial_grad[...])
                out[lines, 4 * width :] = gain_column[part, :]
            save.start()
        for save in saves:
            save.wait()


def residual_kernel(
    n_seq, me_ref, pos_ref, gain_ref, inv_ref, xhat_ref, serial_grad_ref, d_normed_ref, back_out
):
    xhat = xhat_ref[...]
    rows = xhat.shape[0]
    capacity = pos_ref.shape[1] // n_seq
    scaled = d_normed_ref[...] * gain_ref[...]
    residual = inv_ref[:, 0:1] * (
        scaled
        - jnp.mean(scaled, axis=1, keepdims=True)
        - xhat * jnp.mean(scaled * xhat, axis=1, keepdims=True)
    )
    serial_dx = (serial_grad_ref[...].astype(F32) + residual).astype(BF16)
    returned = mm(column_hot(pos_ref[...], rows), serial_dx).astype(BF16)
    for d in range(n_seq):
        back_out[by_receiver(me_ref[0], d, capacity), :] = returned[d * capacity : (d + 1) * capacity]


def unpack_kernel(n_seq, me_ref, slot_ref, recv_ref, out_ref):
    capacity = recv_ref.shape[0] // n_seq
    values = jnp.concatenate(
        [recv_ref[by_receiver(me_ref[0], d, capacity), :] for d in range(n_seq)], axis=0
    )
    out_ref[...] = mm(column_hot(slot_ref[...], values.shape[0]), values).astype(BF16)


def split_kernel(side_ref, own_ref, other_ref, qkv_out, proj_out, gain_out):
    width = proj_out.shape[1]

    def write(ref):
        qkv_out[...] = ref[:, : 3 * width].astype(F32)
        proj_out[...] = ref[:, 3 * width : 4 * width].astype(F32)
        gain_out[...] = jnp.transpose(ref[:, 4 * width :].astype(F32))[0:1]

    own = pl.program_id(0) == side_ref[0]
    pl.when(own)(lambda: write(own_ref))
    pl.when(jnp.logical_not(own))(lambda: write(other_ref))


def exponent_of(largest):
    return jnp.clip(jnp.ceil(jnp.log(jnp.maximum(largest, 1e-30)) * 1.4426950408889634), -100.0, 120.0)


def encode(out_ref, total):
    width = total.shape[1] - LANES
    body, gain = total[:, :width], total[:, width : width + 1]
    exponent = exponent_of(jnp.max(jnp.abs(body), axis=1, keepdims=True))
    codes = jnp.round(body * (jnp.exp2(-exponent) * CODE_MAX))
    out_ref[:, :width] = codes.astype(jnp.int32).astype(jnp.int16)
    gain_exponent = exponent_of(jnp.abs(gain))
    scaled = gain * (jnp.exp2(-gain_exponent) * CODE_MAX)
    high = jnp.round(scaled)
    low = jnp.round((scaled - high) * DIGIT)
    lane = iota((total.shape[0], LANES), 1)
    tail = jnp.where(lane == 0, high, jnp.where(lane == 1, low, jnp.where(lane == 2, gain_exponent, exponent)))
    out_ref[:, width:] = tail.astype(jnp.int32).astype(jnp.int16)


def decode(codes):
    values = codes.astype(jnp.int32).astype(F32)
    width = values.shape[1] - LANES
    tail = values[:, width:]
    body = values[:, :width] * (jnp.exp2(tail[:, 3:4]) * (1.0 / CODE_MAX))
    gain = (tail[:, 0:1] + tail[:, 1:2] * (1.0 / DIGIT)) * (jnp.exp2(tail[:, 2:3]) * (1.0 / CODE_MAX))
    return jnp.concatenate([body, jnp.broadcast_to(gain, tail.shape)], axis=1)


def total_of(terms, part):
    half = terms[0].shape[0] // 2
    rows = {"all": slice(None), "first": slice(0, half), "second": slice(half, 2 * half)}[part]
    values = [ref[rows, :] for ref in terms]
    return functools.reduce(jnp.add, [decode(v) if v.dtype == jnp.int16 else v for v in values])


def message_kernel(part, *refs):
    encode(refs[-1], total_of(refs[:-1], part))


def sum_kernel(parts, *refs):
    refs[-1][...] = functools.reduce(jnp.add, [total_of([ref], p) for ref, p in zip(refs, parts)])


def pieces_kernel(parts, n_dp, plane_ref, *refs):
    terms, own, messages, total = refs[: len(parts)], refs[len(parts)], refs[len(parts) + 1 : -1], refs[-1]
    total[...] = functools.reduce(jnp.add, [total_of([ref], p) for ref, p in zip(terms, parts)])
    size = own.shape[0]

    def rows_of(distance):
        start = lax.bitwise_xor(plane_ref[0], distance) * size
        return total[pl.ds(pl.multiple_of(start, size), size), :]

    for k in range(1, n_dp):
        encode(messages[k - 1], rows_of(k))
    own[...] = rows_of(0)


def finish_kernel(*refs):
    refs[-1][...] = total_of(refs[:-1], "all").astype(BF16)


def whole(shape):
    return pl.BlockSpec(shape, lambda *_: (0,) * len(shape), pipeline_mode=pl.Buffered(1))


def params(mib):
    return pltpu.CompilerParams(vmem_limit_bytes=mib * MIB)


def shape_of(shape, dtype):
    return jax.ShapeDtypeStruct(shape, dtype)


def by_distance(blocks, axis):
    count = len(blocks)
    return [blocks[0]] + [
        lax.ppermute(blocks[k], axis, [(i, i ^ k) for i in range(count)]) for k in range(1, count)
    ]


def chip_orders(n_seq):
    bits = list(range(1, n_seq.bit_length() - 1))
    middle = len(bits) // 2
    return bits, bits[middle:] + bits[:middle]


def chip_steps():
    n_seq, me = lax.axis_size("seq"), lax.axis_index("seq")
    odd = lax.bitwise_and(me, 1) == 1

    def side(bit):
        return lax.bitwise_and(lax.shift_right_logical(me, jnp.asarray(bit, me.dtype)), 1)

    steps = []
    for even_bit, odd_bit in zip(*chip_orders(n_seq)):
        pairs = [(i, i ^ (1 << (odd_bit if i & 1 else even_bit))) for i in range(n_seq)]
        steps.append((pairs, jnp.where(odd, side(odd_bit), side(even_bit))))
    return steps


def piece(terms, index, count):
    size = terms[0].shape[0] // count
    return functools.reduce(jnp.add, [lax.dynamic_slice_in_dim(t, index * size, size) for t in terms])


def core_pairs():
    return [(i, i ^ 1) for i in range(lax.axis_size("seq"))]


def small_kernel(kernel, outs, operands, scalars=0, scratch=(), name="sum"):
    in_smem = pl.BlockSpec(memory_space=pltpu.SMEM)
    in_vmem = pl.BlockSpec(memory_space=pltpu.VMEM)
    touched = sum(x.size * x.dtype.itemsize for x in (*operands, *outs))
    return pl.pallas_call(
        kernel,
        out_shape=outs,
        in_specs=[in_smem] * scalars + [in_vmem] * (len(operands) - scalars),
        out_specs=[in_vmem] * len(outs),
        scratch_shapes=list(scratch),
        compiler_params=params(16),
        cost_estimate=pl.CostEstimate(flops=2 * touched, bytes_accessed=touched, transcendentals=0),
        name=name,
    )(*operands)


def message(terms, part, name):
    rows, width = terms[0].shape
    rows = rows if part == "all" else rows // 2
    return small_kernel(
        functools.partial(message_kernel, part), [shape_of((rows, width), jnp.int16)], terms, name=name
    )[0]


def first_step(quarters, steps):
    pass_on, pass_keep, own_on, own_keep = quarters
    got_on = lax.ppermute(pass_on, "seq", core_pairs())
    got_keep = lax.ppermute(pass_keep, "seq", core_pairs())
    sent = message([own_on, got_on], "all", "code_first")
    return [own_keep, got_keep, lax.ppermute(sent, "seq", steps[0][0])]


def second_step(terms, steps):
    sent = message(terms, "first", "code_second")
    return terms, lax.ppermute(sent, "seq", steps[1][0])


def halves_of_plain(part, steps):
    for pairs, side in steps:
        got = lax.ppermute(piece([part], 1 - side, 2), "seq", pairs)
        part = piece([part], side, 2) + got
    return part


def reduce_over_planes(terms, got, steps):
    n_dp, plane = lax.axis_size("dp"), lax.axis_index("dp")
    rows, width = got.shape
    parts = ["second"] * len(terms) + ["all"]
    if len(steps) > 2 or rows // n_dp % 16:
        part = small_kernel(
            functools.partial(sum_kernel, parts), [shape_of((rows, width), F32)], [*terms, got]
        )[0]
        part = halves_of_plain(part, steps[2:])
        pieces = [piece([part], lax.bitwise_xor(plane, k), n_dp) for k in range(n_dp)]
        return functools.reduce(jnp.add, by_distance(pieces, "dp")).astype(BF16)
    size = rows // n_dp
    own, *sent = small_kernel(
        functools.partial(pieces_kernel, parts, n_dp),
        [shape_of((size, width), F32)] + [shape_of((size, width), jnp.int16)] * (n_dp - 1),
        [jnp.reshape(plane.astype(jnp.int32), (1,)), *terms, got],
        scalars=1,
        scratch=[pltpu.VMEM((rows, width), F32)],
        name="code_planes",
    )
    arrived = by_distance([own] + sent, "dp")
    return small_kernel(finish_kernel, [shape_of((size, width), BF16)], arrived, name="finish")[0]


def share_over_planes(part):
    n_dp, plane = lax.axis_size("dp"), lax.axis_index("dp")
    shares = jnp.stack(by_distance([part] * n_dp, "dp"))
    return jnp.concatenate(
        [lax.dynamic_index_in_dim(shares, lax.bitwise_xor(plane, p), keepdims=False) for p in range(n_dp)],
        axis=0,
    )


def share_in_plane(part, steps):
    for pairs, side in reversed(steps):
        other = lax.ppermute(part, "seq", pairs)
        part = jnp.where(
            side == 0, jnp.concatenate([part, other], axis=0), jnp.concatenate([other, part], axis=0)
        )
    return part


def per_device(points, cotangent, dest, w_qkv, w_proj, gain):
    feats = points[0]
    grads = cotangent[0]
    rows, width = feats.shape
    n_seq = lax.axis_size("seq")
    capacity = 2 * (rows // n_seq)
    slots = n_seq * capacity
    block = capacity + EXTRA
    pairs = HEADS // 2
    pair = width // pairs
    sum_shape = (width // 4, 4 * width + LANES)
    me = jnp.reshape(lax.axis_index("seq").astype(jnp.int32), (1,))
    gain_row = gain.reshape(1, width)
    in_smem = pl.BlockSpec(memory_space=pltpu.SMEM)
    in_vmem = pl.BlockSpec(memory_space=pltpu.VMEM)
    in_hbm = pl.BlockSpec(memory_space=pl.ANY)
    stay_hbm = pl.BlockSpec(memory_space=pltpu.HBM)

    slot, *feats_sent = pl.pallas_call(
        functools.partial(pack_kernel, n_seq, capacity),
        out_shape=[shape_of((1, rows), jnp.int32)] + [shape_of((block, width), BF16)] * n_seq,
        in_specs=[in_smem] + [stay_hbm] * 2,
        out_specs=[in_vmem] * (1 + n_seq),
        scratch_shapes=[
            pltpu.VMEM((1, rows), jnp.int32),
            pltpu.VMEM((rows, width), BF16),
            pltpu.SemaphoreType.DMA((2,)),
        ],
        compiler_params=params(60),
        cost_estimate=pl.CostEstimate(
            flops=2 * slots * rows * width, bytes_accessed=2 * MIB, transcendentals=0
        ),
        name="pack",
    )(me, dest, feats)
    feats_got = by_distance(feats_sent, "seq")
    feats_got[1], slot = lax.optimization_barrier((feats_got[1], slot))
    grads_sent = pl.pallas_call(
        functools.partial(pack_grads_kernel, n_seq, capacity),
        out_shape=shape_of((slots, width), BF16),
        in_specs=[in_smem] + [in_vmem] * 2,
        out_specs=in_vmem,
        compiler_params=params(20),
        cost_estimate=pl.CostEstimate(
            flops=2 * slots * rows * width, bytes_accessed=2 * MIB, transcendentals=0
        ),
        name="pack_grads",
    )(me, slot, grads)

    def exchange(sent):
        sent = sent.reshape(n_seq, capacity, width)
        got = lax.all_to_all(sent, "seq", split_axis=0, concat_axis=0, tiled=True)
        return got.reshape(slots, width)

    feats_got, grads_sent = lax.optimization_barrier((feats_got, grads_sent))
    grads_got = exchange(grads_sent)

    pos, xhat, inv, normed, qkv, trans, attn_t, stats = pl.pallas_call(
        functools.partial(forward_kernel, n_seq, capacity),
        grid=(pairs,),
        out_shape=(
            shape_of((1, slots), jnp.int32),
            shape_of((rows, width), F32),
            shape_of((rows, LANES), F32),
            shape_of((rows, width), BF16),
            shape_of((rows, 3 * width), BF16),
            shape_of((2 * width, rows), BF16),
            shape_of((width, rows), BF16),
            shape_of((2 * HEADS, rows), F32),
        ),
        in_specs=[in_hbm, whole((1, width))] + [whole((block, width))] * n_seq,
        out_specs=[whole((1, slots))]
        + [in_hbm] * 5
        + [pl.BlockSpec((pair, rows), lambda i: (i, 0)), whole((2 * HEADS, rows))],
        scratch_shapes=[
            pltpu.VMEM((width, 3 * width), BF16),
            pltpu.VMEM((rows, width), F32),
            pltpu.VMEM((rows, LANES), F32),
            pltpu.VMEM((rows, width), BF16),
            pltpu.VMEM((rows, 3 * width), BF16),
            pltpu.VMEM((3 * width, rows), BF16),
            pltpu.SemaphoreType.DMA((6,)),
        ],
        compiler_params=params(60),
        cost_estimate=pl.CostEstimate(
            flops=6 * rows * width * width + 8 * HEADS * rows * rows * pair,
            bytes_accessed=16 * MIB,
            transcendentals=HEADS * rows * rows,
        ),
        name="forward",
    )(w_qkv, gain_row, *feats_got)

    chip_bits = tuple(zip(*chip_orders(n_seq)))[:2]
    *quarters, serial_grad, d_normed = pl.pallas_call(
        functools.partial(backward_kernel, n_seq, chip_bits),
        grid=(pairs,),
        out_shape=[shape_of(sum_shape, F32)] * 4
        + [shape_of((rows, width), BF16), shape_of((rows, width), F32)],
        in_specs=[
            in_smem,
            whole((1, slots)),
            whole((width, width)),
            whole((2 * HEADS, rows)),
        ]
        + [in_hbm] * 7,
        out_specs=[in_hbm] * 6,
        scratch_shapes=[
            pltpu.VMEM((slots, width), BF16),
            pltpu.VMEM((rows, 3 * width), BF16),
            pltpu.VMEM((2 * width, rows), BF16),
            pltpu.VMEM((width, 3 * width), BF16),
            pltpu.VMEM((rows, width), F32),
            pltpu.VMEM((rows, width), BF16),
            pltpu.VMEM((width, rows), BF16),
        ]
        + [pltpu.VMEM(sum_shape, F32)] * 4
        + [
            pltpu.VMEM((rows, width), BF16),
            pltpu.VMEM((rows, width), F32),
            pltpu.VMEM((rows, width), BF16),
            pltpu.VMEM((width, rows), BF16),
            pltpu.VMEM((rows, 3 * width), BF16),
            pltpu.VMEM((width, rows), BF16),
            pltpu.VMEM((width, LANES), F32),
            pltpu.SemaphoreType.DMA((13,)),
        ],
        compiler_params=params(60),
        cost_estimate=pl.CostEstimate(
            flops=12 * rows * width * width + 10 * HEADS * rows * rows * pair,
            bytes_accessed=16 * MIB,
            transcendentals=HEADS * rows * rows,
        ),
        name="backward",
    )(me, pos, w_proj, stats, grads_got, qkv, trans, w_qkv, xhat, normed, attn_t)

    steps = chip_steps()
    terms = first_step(quarters, steps)
    d_normed, terms = lax.optimization_barrier((d_normed, terms))
    back = pl.pallas_call(
        functools.partial(residual_kernel, n_seq),
        out_shape=shape_of((slots, width), BF16),
        in_specs=[in_smem] + [in_vmem] * 6,
        out_specs=in_vmem,
        compiler_params=params(20),
        cost_estimate=pl.CostEstimate(
            flops=2 * slots * rows * width, bytes_accessed=4 * MIB, transcendentals=0
        ),
        name="residual",
    )(me, pos, gain_row, inv, xhat, serial_grad, d_normed)
    returned = exchange(back)
    terms, got = second_step(terms, steps)
    part, returned = lax.optimization_barrier((reduce_over_planes(terms, got, steps), returned))
    own = share_in_plane(share_over_planes(part), steps)
    other = lax.ppermute(own, "seq", core_pairs())
    grad_local = pl.pallas_call(
        functools.partial(unpack_kernel, n_seq),
        out_shape=shape_of((rows, width), BF16),
        in_specs=[in_smem] + [in_vmem] * 2,
        out_specs=in_vmem,
        compiler_params=params(20),
        cost_estimate=pl.CostEstimate(
            flops=2 * slots * rows * width, bytes_accessed=2 * MIB, transcendentals=0
        ),
        name="unpack",
    )(me, slot, returned)
    half = width // 2
    grad_qkv, grad_proj, gain_grad = pl.pallas_call(
        split_kernel,
        grid=(2,),
        out_shape=(
            shape_of((width, 3 * width), F32),
            shape_of((width, width), F32),
            shape_of((1, width), F32),
        ),
        in_specs=[in_smem] + [whole(own.shape)] * 2,
        out_specs=[
            pl.BlockSpec((half, 3 * width), lambda i: (i, 0)),
            pl.BlockSpec((half, width), lambda i: (i, 0)),
            pl.BlockSpec((1, half), lambda i: (0, i)),
        ],
        compiler_params=params(20),
        cost_estimate=pl.CostEstimate(flops=0, bytes_accessed=8 * MIB, transcendentals=0),
        name="split",
    )(lax.bitwise_and(me, 1), own, other)
    return (grad_local[None], grad_qkv, grad_proj, gain_grad[0])


def solution(mesh):
    return jax.shard_map(
        per_device,
        mesh=mesh,
        in_specs=(P("dp", "seq", None), P("dp", "seq", None), P("dp", "seq"), P(), P(), P()),
        out_specs=(P("dp", "seq", None), P(), P(), P()),
        check_vma=False,
    )
```

```python
import functools

import jax
import jax.numpy as jnp
from jax import lax
from jax.experimental import pallas as pl
from jax.experimental.pallas import tpu as pltpu
from jax.sharding import PartitionSpec as P

HEADS = 8
PATCH = 512
EXTRA = 16
LANES = 128
CODE_MAX = 32000.0
DIGIT = 60000.0
MIB = 1024 * 1024
F32 = jnp.float32
BF16 = jnp.bfloat16
NN = (((1,), (0,)), ((), ()))
NT = (((1,), (1,)), ((), ()))


def mm(lhs, rhs, dims=NN):
    return lax.dot_general(lhs, rhs, dims, preferred_element_type=F32)


def iota(shape, dim):
    return lax.broadcasted_iota(jnp.int32, shape, dim)


def hot(mask):
    return jnp.where(mask, jnp.float32(1), jnp.float32(0)).astype(BF16)


def column_hot(row, count):
    size = row.shape[1]
    column = jnp.transpose(jnp.broadcast_to(row, (LANES, size)))
    lane = iota((size, LANES), 1)
    return jnp.concatenate([hot(column == lane + j * LANES) for j in range(count // LANES)], axis=1)


def by_receiver(me, distance, capacity):
    return pl.ds(pl.multiple_of(lax.bitwise_xor(me, distance) * capacity, capacity), capacity)


def pack_kernel(n_seq, capacity, me_ref, dest_hbm, feats_hbm, slot_out, *refs):
    outs, (dest_ref, feats_ref, sems) = refs[:n_seq], refs[n_seq:]
    rows, width = feats_ref.shape
    slots = n_seq * capacity
    loads = [
        pltpu.make_async_copy(source, target, sems.at[i])
        for i, (source, target) in enumerate(((dest_hbm, dest_ref), (feats_hbm, feats_ref)))
    ]
    for load in loads:
        load.start()
    loads[0].wait()
    shift = rows.bit_length() - 1
    places = dest_ref[...]
    distance = lax.bitwise_xor(lax.shift_right_logical(places, shift), me_ref[0])
    within = lax.bitwise_and(places, rows - 1) + 1
    member = iota((n_seq, rows), 0) == distance
    upper = hot(iota((rows, rows), 0) <= iota((rows, rows), 1))
    counts = mm(hot(member), upper)
    rank = jnp.sum(jnp.where(member, counts, 0.0), axis=0, keepdims=True).astype(jnp.int32) - 1
    slot = distance * capacity + rank
    slot_out[...] = slot
    select = hot(iota((slots, rows), 0) == slot)
    loads[1].wait()
    feats = mm(select, feats_ref[...]).astype(BF16)
    upper_half = slot >= width
    high = lax.shift_right_logical(within, 8).astype(F32)
    low = lax.bitwise_and(within, 255).astype(F32)
    line = iota((n_seq * EXTRA, rows), 0)
    kind = lax.bitwise_and(line, EXTRA - 1)
    digit = jnp.where(kind < 2, high, low)
    wanted = (
        (lax.shift_right_logical(line, EXTRA.bit_length() - 1) == distance)
        & (kind < 4)
        & ((lax.bitwise_and(kind, 1) == 1) == upper_half)
    )
    digits = jnp.where(wanted, digit, 0.0).astype(BF16)
    spread = hot(iota((width, rows), 0) == lax.bitwise_and(slot, width - 1))
    position = mm(digits, spread, NT).astype(BF16)
    for d in range(n_seq):
        outs[d][:capacity, :] = feats[d * capacity : (d + 1) * capacity]
        outs[d][capacity:, :] = position[d * EXTRA : (d + 1) * EXTRA]


def pack_grads_kernel(n_seq, capacity, me_ref, slot_ref, grads_ref, grads_out):
    select = hot(iota((n_seq * capacity, grads_ref.shape[0]), 0) == slot_ref[...])
    grads = mm(select, grads_ref[...]).astype(BF16)
    for d in range(n_seq):
        grads_out[by_receiver(me_ref[0], d, capacity), :] = grads[d * capacity : (d + 1) * capacity]


def forward_kernel(n_seq, capacity, w_hbm, gain_ref, *refs):
    recv, refs = refs[:n_seq], refs[n_seq:]
    pos_out, xhat_hbm, inv_hbm, normed_hbm, qkv_hbm, trans_hbm, attn_out, stats_out = refs[:8]
    w_ref, xhat_ref, inv_ref, normed_ref, qkv_ref, trans, sems = refs[8:]
    width = w_ref.shape[0]
    rows = xhat_ref.shape[0]
    head = width // HEADS
    pair = 2 * head
    step = pl.program_id(0)
    w_copy = pltpu.make_async_copy(w_hbm, w_ref, sems.at[0])
    saves = [
        pltpu.make_async_copy(source, target, sems.at[1 + i])
        for i, (source, target) in enumerate(
            (
                (xhat_ref, xhat_hbm),
                (inv_ref, inv_hbm),
                (normed_ref, normed_hbm),
                (qkv_ref, qkv_hbm),
                (trans.at[pl.ds(0, 2 * width)], trans_hbm),
            )
        )
    ]

    @pl.when(step == 0)
    def _():
        w_copy.start()
        tile = recv[0][capacity:, :].astype(F32)
        for s in range(1, n_seq):
            tile = tile + recv[s][capacity:, :].astype(F32)
        high = jnp.concatenate([tile[0:1], tile[1:2]], axis=1)
        low = jnp.concatenate([tile[2:3], tile[3:4]], axis=1)
        pos = (high * 256.0 + low).astype(jnp.int32) - 1
        pos_out[...] = pos
        place = hot(iota((rows, n_seq * capacity), 0) == pos)
        values = jnp.concatenate([recv[s][:capacity, :] for s in range(n_seq)], axis=0)
        feats = mm(place, values)
        centered = feats - jnp.mean(feats, axis=1, keepdims=True)
        inv = lax.rsqrt(jnp.mean(centered * centered, axis=1, keepdims=True) + 1e-05)
        xhat = centered * inv
        xhat_ref[...] = xhat
        inv_ref[...] = jnp.broadcast_to(inv, inv_ref.shape)
        normed = (xhat * gain_ref[...]).astype(BF16)
        normed_ref[...] = normed
        w_copy.wait()
        qkv = mm(normed, w_ref[...])
        qkv_ref[...] = qkv.astype(BF16)
        trans[...] = jnp.transpose(qkv).astype(BF16)
        for save in saves:
            save.start()

    lo = pl.multiple_of(step * pair, pair)
    keys = qkv_ref[:, pl.ds(pl.multiple_of(width + step * pair, pair), pair)]
    query_t = trans[pl.ds(lo, pair), :] * BF16(0.125)
    zero = jnp.zeros((head, rows), BF16)
    for j in range(2):
        part = query_t[j * head : (j + 1) * head]
        part = jnp.concatenate([part, zero] if j == 0 else [zero, part], axis=0)
        scores = mm(keys, part)
        top = jnp.max(scores, axis=0, keepdims=True)
        expo = jnp.exp(scores - top)
        share = 1.0 / jnp.sum(expo, axis=0, keepdims=True)
        probs = expo * share
        stats_out[pl.ds(2 * step + j, 1), :] = top
        stats_out[pl.ds(HEADS + 2 * step + j, 1), :] = share
        values_t = trans[pl.ds(pl.multiple_of(2 * width + step * pair + j * head, head), head), :]
        attn_out[j * head : (j + 1) * head, :] = mm(values_t, probs.astype(BF16)).astype(BF16)

    @pl.when(step == pl.num_programs(0) - 1)
    def _():
        for save in saves:
            save.wait()


def backward_kernel(n_seq, chip_bits, me_ref, pos_ref, w_proj_ref, stats_ref, *refs):
    (recv_hbm, qkv_hbm, trans_hbm, w_hbm, xhat_hbm, normed_hbm, attn_hbm), refs = refs[:7], refs[7:]
    outs, serial_grad_hbm, d_normed_hbm, refs = refs[:4], refs[4], refs[5], refs[6:]
    recv_ref, qkv_ref, trans_ref, w_ref, xhat_ref, normed_ref, attn_ref, refs = *refs[:7], refs[7:]
    sums, refs = refs[:4], refs[4:]
    serial_grad, d_normed_ref, d_attn, d_attn_t, d_qkv, normed_t, gain_column, sems = refs
    width = w_proj_ref.shape[0]
    rows = xhat_ref.shape[0]
    capacity = recv_ref.shape[0] // n_seq
    head = width // HEADS
    pair = 2 * head
    step = pl.program_id(0)
    me = me_ref[0]
    loads = [
        pltpu.make_async_copy(source, target, sems.at[i])
        for i, (source, target) in enumerate(
            (
                (recv_hbm, recv_ref),
                (qkv_hbm, qkv_ref),
                (trans_hbm, trans_ref),
                (normed_hbm, normed_ref),
                (w_hbm, w_ref),
                (xhat_hbm, xhat_ref),
                (attn_hbm, attn_ref),
            )
        )
    ]
    saves = [
        pltpu.make_async_copy(source, target, sems.at[7 + i])
        for i, (source, target) in enumerate(
            [*zip(sums, outs), (serial_grad, serial_grad_hbm), (d_normed_ref, d_normed_hbm)]
        )
    ]

    @pl.when(step == 0)
    def _():
        for load in loads:
            load.start()
        place = hot(iota((rows, n_seq * capacity), 0) == pos_ref[...])
        loads[0].wait()
        values = jnp.concatenate(
            [recv_ref[by_receiver(me, d, capacity), :] for d in range(n_seq)], axis=0
        )
        grads = mm(place, values).astype(BF16)
        serial_grad[...] = grads
        saves[4].start()
        d_att = mm(grads, w_proj_ref[...], NT).astype(BF16)
        d_attn[...] = d_att
        d_attn_t[...] = jnp.transpose(d_att.astype(F32)).astype(BF16)
        loads[1].wait()
        loads[2].wait()

    lo = pl.multiple_of(step * pair, pair)
    queries = qkv_ref[:, pl.ds(lo, pair)]
    values = qkv_ref[:, pl.ds(pl.multiple_of(2 * width + step * pair, pair), pair)]
    d_att_t = d_attn_t[pl.ds(lo, pair), :] * BF16(0.125)
    d_att = d_attn[:, pl.ds(lo, pair)]
    keys = qkv_ref[:, pl.ds(pl.multiple_of(width + step * pair, pair), pair)]
    query_t = trans_ref[pl.ds(lo, pair), :] * BF16(0.125)
    zero = jnp.zeros((head, rows), BF16)
    d_q, d_k, d_v = [], [], []
    for j in range(2):
        def alone(both):
            part = both[j * head : (j + 1) * head]
            return jnp.concatenate([part, zero] if j == 0 else [zero, part], axis=0)

        top = stats_ref[pl.ds(2 * step + j, 1), :]
        share = stats_ref[pl.ds(HEADS + 2 * step + j, 1), :]
        probs = jnp.exp(mm(keys, alone(query_t)) - top) * share
        d_probs = mm(values, alone(d_att_t))
        total = jnp.sum(d_probs * probs, axis=0, keepdims=True)
        d_scores = (probs * (d_probs - total)).astype(BF16)
        k_t = trans_ref[pl.ds(pl.multiple_of(width + step * pair + j * head, head), head), :]
        d_q.append(mm(k_t, d_scores))
        d_k.append(mm(d_scores, queries))
        d_v.append(mm(probs.astype(BF16), d_att))
    first = iota((rows, pair), 1) < head
    d_qkv[:, pl.ds(lo, pair)] = jnp.transpose(jnp.concatenate(d_q, axis=0)).astype(BF16)
    d_qkv[:, pl.ds(pl.multiple_of(width + step * pair, pair), pair)] = jnp.where(
        first, d_k[0], d_k[1]
    ).astype(BF16)
    d_qkv[:, pl.ds(pl.multiple_of(2 * width + step * pair, pair), pair)] = jnp.where(
        first, d_v[0], d_v[1]
    ).astype(BF16)

    @pl.when(step == pl.num_programs(0) - 1)
    def _():
        for load in loads[3:]:
            load.wait()
        normed_t[...] = jnp.transpose(normed_ref[...].astype(F32)).astype(BF16)
        d_normed = mm(d_qkv[...], w_ref[...], NT)
        d_normed_ref[...] = d_normed
        saves[5].start()
        gain_row = jnp.sum(d_normed * xhat_ref[...], axis=0, keepdims=True)
        gain_column[...] = jnp.transpose(jnp.broadcast_to(gain_row, (LANES, width)))
        eighth = width // 8
        odd = lax.bitwise_and(me, 1)

        def sides(even_bit, odd_bit):
            even_side = lax.bitwise_and(lax.shift_right_logical(me, even_bit), 1)
            odd_side = lax.bitwise_and(lax.shift_right_logical(me, odd_bit), 1)
            mine = jnp.where(odd == 1, odd_side, even_side)
            return mine, even_side + odd_side - mine

        (mine, other), (mine_next, other_next) = (sides(*bits) for bits in chip_bits)
        starts = (
            ((1 - odd) * 2 + 1 - other, other_next),
            ((1 - odd) * 2 + other, other_next),
            (odd * 2 + 1 - mine, mine_next),
            (odd * 2 + mine, mine_next),
        )
        for out, (start, side), save in zip(sums, starts, saves):
            for j, half in enumerate((1 - side, side)):
                part = pl.ds(pl.multiple_of((start * 2 + half) * eighth, eighth), eighth)
                lines = slice(j * eighth, (j + 1) * eighth)
                out[lines, : 3 * width] = mm(normed_t[part, :], d_qkv[...])
                out[lines, 3 * width : 4 * width] = mm(attn_ref[part, :], serial_grad[...])
                out[lines, 4 * width :] = gain_column[part, :]
            save.start()
        for save in saves:
            save.wait()


def residual_kernel(
    n_seq, me_ref, pos_ref, gain_ref, inv_ref, xhat_ref, serial_grad_ref, d_normed_ref, back_out
):
    xhat = xhat_ref[...]
    rows = xhat.shape[0]
    capacity = pos_ref.shape[1] // n_seq
    scaled = d_normed_ref[...] * gain_ref[...]
    residual = inv_ref[:, 0:1] * (
        scaled
        - jnp.mean(scaled, axis=1, keepdims=True)
        - xhat * jnp.mean(scaled * xhat, axis=1, keepdims=True)
    )
    serial_dx = (serial_grad_ref[...].astype(F32) + residual).astype(BF16)
    returned = mm(column_hot(pos_ref[...], rows), serial_dx).astype(BF16)
    for d in range(n_seq):
        back_out[by_receiver(me_ref[0], d, capacity), :] = returned[d * capacity : (d + 1) * capacity]


def unpack_kernel(n_seq, me_ref, slot_ref, recv_ref, out_ref):
    capacity = recv_ref.shape[0] // n_seq
    values = jnp.concatenate(
        [recv_ref[by_receiver(me_ref[0], d, capacity), :] for d in range(n_seq)], axis=0
    )
    out_ref[...] = mm(column_hot(slot_ref[...], values.shape[0]), values).astype(BF16)


def split_kernel(side_ref, own_ref, other_ref, qkv_out, proj_out, gain_out):
    width = proj_out.shape[1]

    def write(ref):
        qkv_out[...] = ref[:, : 3 * width].astype(F32)
        proj_out[...] = ref[:, 3 * width : 4 * width].astype(F32)
        gain_out[...] = jnp.transpose(ref[:, 4 * width :].astype(F32))[0:1]

    own = pl.program_id(0) == side_ref[0]
    pl.when(own)(lambda: write(own_ref))
    pl.when(jnp.logical_not(own))(lambda: write(other_ref))


def exponent_of(largest):
    return jnp.clip(jnp.ceil(jnp.log(jnp.maximum(largest, 1e-30)) * 1.4426950408889634), -100.0, 120.0)


def encode(out_ref, total):
    width = total.shape[1] - LANES
    body, gain = total[:, :width], total[:, width : width + 1]
    exponent = exponent_of(jnp.max(jnp.abs(body), axis=1, keepdims=True))
    codes = jnp.round(body * (jnp.exp2(-exponent) * CODE_MAX))
    out_ref[:, :width] = codes.astype(jnp.int32).astype(jnp.int16)
    gain_exponent = exponent_of(jnp.abs(gain))
    scaled = gain * (jnp.exp2(-gain_exponent) * CODE_MAX)
    high = jnp.round(scaled)
    low = jnp.round((scaled - high) * DIGIT)
    lane = iota((total.shape[0], LANES), 1)
    tail = jnp.where(lane == 0, high, jnp.where(lane == 1, low, jnp.where(lane == 2, gain_exponent, exponent)))
    out_ref[:, width:] = tail.astype(jnp.int32).astype(jnp.int16)


def decode(codes):
    values = codes.astype(jnp.int32).astype(F32)
    width = values.shape[1] - LANES
    tail = values[:, width:]
    body = values[:, :width] * (jnp.exp2(tail[:, 3:4]) * (1.0 / CODE_MAX))
    gain = (tail[:, 0:1] + tail[:, 1:2] * (1.0 / DIGIT)) * (jnp.exp2(tail[:, 2:3]) * (1.0 / CODE_MAX))
    return jnp.concatenate([body, jnp.broadcast_to(gain, tail.shape)], axis=1)


def total_of(terms, part):
    half = terms[0].shape[0] // 2
    rows = {"all": slice(None), "first": slice(0, half), "second": slice(half, 2 * half)}[part]
    values = [ref[rows, :] for ref in terms]
    return functools.reduce(jnp.add, [decode(v) if v.dtype == jnp.int16 else v for v in values])


def message_kernel(part, *refs):
    encode(refs[-1], total_of(refs[:-1], part))


def sum_kernel(parts, *refs):
    refs[-1][...] = functools.reduce(jnp.add, [total_of([ref], p) for ref, p in zip(refs, parts)])


def pieces_kernel(parts, n_dp, plane_ref, *refs):
    terms, own, messages, total = refs[: len(parts)], refs[len(parts)], refs[len(parts) + 1 : -1], refs[-1]
    total[...] = functools.reduce(jnp.add, [total_of([ref], p) for ref, p in zip(terms, parts)])
    size = own.shape[0]

    def rows_of(distance):
        start = lax.bitwise_xor(plane_ref[0], distance) * size
        return total[pl.ds(pl.multiple_of(start, size), size), :]

    for k in range(1, n_dp):
        encode(messages[k - 1], rows_of(k))
    own[...] = rows_of(0)


def finish_kernel(*refs):
    refs[-1][...] = total_of(refs[:-1], "all").astype(BF16)


def whole(shape):
    return pl.BlockSpec(shape, lambda *_: (0,) * len(shape), pipeline_mode=pl.Buffered(1))


def params(mib):
    return pltpu.CompilerParams(vmem_limit_bytes=mib * MIB)


def shape_of(shape, dtype):
    return jax.ShapeDtypeStruct(shape, dtype)


def by_distance(blocks, axis):
    count = len(blocks)
    return [blocks[0]] + [
        lax.ppermute(blocks[k], axis, [(i, i ^ k) for i in range(count)]) for k in range(1, count)
    ]


def chip_orders(n_seq):
    bits = list(range(1, n_seq.bit_length() - 1))
    middle = len(bits) // 2
    return bits, bits[middle:] + bits[:middle]


def chip_steps():
    n_seq, me = lax.axis_size("seq"), lax.axis_index("seq")
    odd = lax.bitwise_and(me, 1) == 1

    def side(bit):
        return lax.bitwise_and(lax.shift_right_logical(me, jnp.asarray(bit, me.dtype)), 1)

    steps = []
    for even_bit, odd_bit in zip(*chip_orders(n_seq)):
        pairs = [(i, i ^ (1 << (odd_bit if i & 1 else even_bit))) for i in range(n_seq)]
        steps.append((pairs, jnp.where(odd, side(odd_bit), side(even_bit))))
    return steps


def piece(terms, index, count):
    size = terms[0].shape[0] // count
    return functools.reduce(jnp.add, [lax.dynamic_slice_in_dim(t, index * size, size) for t in terms])


def core_pairs():
    return [(i, i ^ 1) for i in range(lax.axis_size("seq"))]


def small_kernel(kernel, outs, operands, scalars=0, scratch=(), name="sum"):
    in_smem = pl.BlockSpec(memory_space=pltpu.SMEM)
    in_vmem = pl.BlockSpec(memory_space=pltpu.VMEM)
    touched = sum(x.size * x.dtype.itemsize for x in (*operands, *outs))
    return pl.pallas_call(
        kernel,
        out_shape=outs,
        in_specs=[in_smem] * scalars + [in_vmem] * (len(operands) - scalars),
        out_specs=[in_vmem] * len(outs),
        scratch_shapes=list(scratch),
        compiler_params=params(16),
        cost_estimate=pl.CostEstimate(flops=2 * touched, bytes_accessed=touched, transcendentals=0),
        name=name,
    )(*operands)


def message(terms, part, name):
    rows, width = terms[0].shape
    rows = rows if part == "all" else rows // 2
    return small_kernel(
        functools.partial(message_kernel, part), [shape_of((rows, width), jnp.int16)], terms, name=name
    )[0]


def first_step(quarters, steps):
    pass_on, pass_keep, own_on, own_keep = quarters
    got_on = lax.ppermute(pass_on, "seq", core_pairs())
    got_keep = lax.ppermute(pass_keep, "seq", core_pairs())
    sent = message([own_on, got_on], "all", "code_first")
    return [own_keep, got_keep, lax.ppermute(sent, "seq", steps[0][0])]


def second_step(terms, steps):
    sent = message(terms, "first", "code_second")
    return terms, lax.ppermute(sent, "seq", steps[1][0])


def halves_of_plain(part, steps):
    for pairs, side in steps:
        got = lax.ppermute(piece([part], 1 - side, 2), "seq", pairs)
        part = piece([part], side, 2) + got
    return part


def reduce_over_planes(terms, got, steps, later):
    n_dp, plane = lax.axis_size("dp"), lax.axis_index("dp")
    rows, width = got.shape
    parts = ["second"] * len(terms) + ["all"]
    if len(steps) > 2 or rows // n_dp % 16:
        part = small_kernel(
            functools.partial(sum_kernel, parts), [shape_of((rows, width), F32)], [*terms, got]
        )[0]
        part = halves_of_plain(part, steps[2:])
        pieces = [piece([part], lax.bitwise_xor(plane, k), n_dp) for k in range(n_dp)]
        arrived = by_distance(pieces, "dp")
        arrived[1], later = lax.optimization_barrier((arrived[1], later))
        return functools.reduce(jnp.add, arrived).astype(BF16), later
    size = rows // n_dp
    own, *sent = small_kernel(
        functools.partial(pieces_kernel, parts, n_dp),
        [shape_of((size, width), F32)] + [shape_of((size, width), jnp.int16)] * (n_dp - 1),
        [jnp.reshape(plane.astype(jnp.int32), (1,)), *terms, got],
        scalars=1,
        scratch=[pltpu.VMEM((rows, width), F32)],
        name="code_planes",
    )
    arrived = by_distance([own] + sent, "dp")
    arrived[1], later = lax.optimization_barrier((arrived[1], later))
    return small_kernel(finish_kernel, [shape_of((size, width), BF16)], arrived, name="finish")[0], later


def share_over_planes(part):
    n_dp, plane = lax.axis_size("dp"), lax.axis_index("dp")
    shares = jnp.stack(by_distance([part] * n_dp, "dp"))
    return jnp.concatenate(
        [lax.dynamic_index_in_dim(shares, lax.bitwise_xor(plane, p), keepdims=False) for p in range(n_dp)],
        axis=0,
    )


def share_in_plane(part, steps):
    for pairs, side in reversed(steps):
        other = lax.ppermute(part, "seq", pairs)
        part = jnp.where(
            side == 0, jnp.concatenate([part, other], axis=0), jnp.concatenate([other, part], axis=0)
        )
    return part


def per_device(points, cotangent, dest, w_qkv, w_proj, gain):
    feats = points[0]
    grads = cotangent[0]
    rows, width = feats.shape
    n_seq = lax.axis_size("seq")
    capacity = 2 * (rows // n_seq)
    slots = n_seq * capacity
    block = capacity + EXTRA
    pairs = HEADS // 2
    pair = width // pairs
    sum_shape = (width // 4, 4 * width + LANES)
    me = jnp.reshape(lax.axis_index("seq").astype(jnp.int32), (1,))
    gain_row = gain.reshape(1, width)
    in_smem = pl.BlockSpec(memory_space=pltpu.SMEM)
    in_vmem = pl.BlockSpec(memory_space=pltpu.VMEM)
    in_hbm = pl.BlockSpec(memory_space=pl.ANY)
    stay_hbm = pl.BlockSpec(memory_space=pltpu.HBM)

    slot, *feats_sent = pl.pallas_call(
        functools.partial(pack_kernel, n_seq, capacity),
        out_shape=[shape_of((1, rows), jnp.int32)] + [shape_of((block, width), BF16)] * n_seq,
        in_specs=[in_smem] + [stay_hbm] * 2,
        out_specs=[in_vmem] * (1 + n_seq),
        scratch_shapes=[
            pltpu.VMEM((1, rows), jnp.int32),
            pltpu.VMEM((rows, width), BF16),
            pltpu.SemaphoreType.DMA((2,)),
        ],
        compiler_params=params(60),
        cost_estimate=pl.CostEstimate(
            flops=2 * slots * rows * width, bytes_accessed=2 * MIB, transcendentals=0
        ),
        name="pack",
    )(me, dest, feats)
    feats_got = by_distance(feats_sent, "seq")
    feats_got[1], slot = lax.optimization_barrier((feats_got[1], slot))
    grads_sent = pl.pallas_call(
        functools.partial(pack_grads_kernel, n_seq, capacity),
        out_shape=shape_of((slots, width), BF16),
        in_specs=[in_smem] + [in_vmem] * 2,
        out_specs=in_vmem,
        compiler_params=params(20),
        cost_estimate=pl.CostEstimate(
            flops=2 * slots * rows * width, bytes_accessed=2 * MIB, transcendentals=0
        ),
        name="pack_grads",
    )(me, slot, grads)

    def exchange(sent):
        sent = sent.reshape(n_seq, capacity, width)
        got = lax.all_to_all(sent, "seq", split_axis=0, concat_axis=0, tiled=True)
        return got.reshape(slots, width)

    feats_got, grads_sent = lax.optimization_barrier((feats_got, grads_sent))
    grads_got = exchange(grads_sent)

    pos, xhat, inv, normed, qkv, trans, attn_t, stats = pl.pallas_call(
        functools.partial(forward_kernel, n_seq, capacity),
        grid=(pairs,),
        out_shape=(
            shape_of((1, slots), jnp.int32),
            shape_of((rows, width), F32),
            shape_of((rows, LANES), F32),
            shape_of((rows, width), BF16),
            shape_of((rows, 3 * width), BF16),
            shape_of((2 * width, rows), BF16),
            shape_of((width, rows), BF16),
            shape_of((2 * HEADS, rows), F32),
        ),
        in_specs=[in_hbm, whole((1, width))] + [whole((block, width))] * n_seq,
        out_specs=[whole((1, slots))]
        + [in_hbm] * 5
        + [pl.BlockSpec((pair, rows), lambda i: (i, 0)), whole((2 * HEADS, rows))],
        scratch_shapes=[
            pltpu.VMEM((width, 3 * width), BF16),
            pltpu.VMEM((rows, width), F32),
            pltpu.VMEM((rows, LANES), F32),
            pltpu.VMEM((rows, width), BF16),
            pltpu.VMEM((rows, 3 * width), BF16),
            pltpu.VMEM((3 * width, rows), BF16),
            pltpu.SemaphoreType.DMA((6,)),
        ],
        compiler_params=params(60),
        cost_estimate=pl.CostEstimate(
            flops=6 * rows * width * width + 8 * HEADS * rows * rows * pair,
            bytes_accessed=16 * MIB,
            transcendentals=HEADS * rows * rows,
        ),
        name="forward",
    )(w_qkv, gain_row, *feats_got)

    chip_bits = tuple(zip(*chip_orders(n_seq)))[:2]
    *quarters, serial_grad, d_normed = pl.pallas_call(
        functools.partial(backward_kernel, n_seq, chip_bits),
        grid=(pairs,),
        out_shape=[shape_of(sum_shape, F32)] * 4
        + [shape_of((rows, width), BF16), shape_of((rows, width), F32)],
        in_specs=[
            in_smem,
            whole((1, slots)),
            whole((width, width)),
            whole((2 * HEADS, rows)),
        ]
        + [in_hbm] * 7,
        out_specs=[in_hbm] * 6,
        scratch_shapes=[
            pltpu.VMEM((slots, width), BF16),
            pltpu.VMEM((rows, 3 * width), BF16),
            pltpu.VMEM((2 * width, rows), BF16),
            pltpu.VMEM((width, 3 * width), BF16),
            pltpu.VMEM((rows, width), F32),
            pltpu.VMEM((rows, width), BF16),
            pltpu.VMEM((width, rows), BF16),
        ]
        + [pltpu.VMEM(sum_shape, F32)] * 4
        + [
            pltpu.VMEM((rows, width), BF16),
            pltpu.VMEM((rows, width), F32),
            pltpu.VMEM((rows, width), BF16),
            pltpu.VMEM((width, rows), BF16),
            pltpu.VMEM((rows, 3 * width), BF16),
            pltpu.VMEM((width, rows), BF16),
            pltpu.VMEM((width, LANES), F32),
            pltpu.SemaphoreType.DMA((13,)),
        ],
        compiler_params=params(60),
        cost_estimate=pl.CostEstimate(
            flops=12 * rows * width * width + 10 * HEADS * rows * rows * pair,
            bytes_accessed=16 * MIB,
            transcendentals=HEADS * rows * rows,
        ),
        name="backward",
    )(me, pos, w_proj, stats, grads_got, qkv, trans, w_qkv, xhat, normed, attn_t)

    steps = chip_steps()
    terms = first_step(quarters, steps)
    back = pl.pallas_call(
        functools.partial(residual_kernel, n_seq),
        out_shape=shape_of((slots, width), BF16),
        in_specs=[in_smem] + [in_vmem] * 6,
        out_specs=in_vmem,
        compiler_params=params(20),
        cost_estimate=pl.CostEstimate(
            flops=2 * slots * rows * width, bytes_accessed=4 * MIB, transcendentals=0
        ),
        name="residual",
    )(me, pos, gain_row, inv, xhat, serial_grad, d_normed)
    terms, got = second_step(terms, steps)
    got, back = lax.optimization_barrier((got, back))
    part, back = reduce_over_planes(terms, got, steps, back)
    returned = exchange(back)
    part, returned = lax.optimization_barrier((share_over_planes(part), returned))
    own = share_in_plane(part, steps)
    other = lax.ppermute(own, "seq", core_pairs())
    grad_local = pl.pallas_call(
        functools.partial(unpack_kernel, n_seq),
        out_shape=shape_of((rows, width), BF16),
        in_specs=[in_smem] + [in_vmem] * 2,
        out_specs=in_vmem,
        compiler_params=params(20),
        cost_estimate=pl.CostEstimate(
            flops=2 * slots * rows * width, bytes_accessed=2 * MIB, transcendentals=0
        ),
        name="unpack",
    )(me, slot, returned)
    half = width // 2
    grad_qkv, grad_proj, gain_grad = pl.pallas_call(
        split_kernel,
        grid=(2,),
        out_shape=(
            shape_of((width, 3 * width), F32),
            shape_of((width, width), F32),
            shape_of((1, width), F32),
        ),
        in_specs=[in_smem] + [whole(own.shape)] * 2,
        out_specs=[
            pl.BlockSpec((half, 3 * width), lambda i: (i, 0)),
            pl.BlockSpec((half, width), lambda i: (i, 0)),
            pl.BlockSpec((1, half), lambda i: (0, i)),
        ],
        compiler_params=params(20),
        cost_estimate=pl.CostEstimate(flops=0, bytes_accessed=8 * MIB, transcendentals=0),
        name="split",
    )(lax.bitwise_and(me, 1), own, other)
    return (grad_local[None], grad_qkv, grad_proj, gain_grad[0])


def solution(mesh):
    return jax.shard_map(
        per_device,
        mesh=mesh,
        in_specs=(P("dp", "seq", None), P("dp", "seq", None), P("dp", "seq"), P(), P(), P()),
        out_specs=(P("dp", "seq", None), P(), P(), P()),
        check_vma=False,
    )
```

```python
import functools

import jax
import jax.numpy as jnp
from jax import lax
from jax.experimental import pallas as pl
from jax.experimental.pallas import tpu as pltpu
from jax.sharding import PartitionSpec as P

HEADS = 8
PATCH = 512
EXTRA = 16
LANES = 128
CODE_MAX = 32000.0
DIGIT = 60000.0
MIB = 1024 * 1024
F32 = jnp.float32
BF16 = jnp.bfloat16
NN = (((1,), (0,)), ((), ()))
NT = (((1,), (1,)), ((), ()))


def mm(lhs, rhs, dims=NN):
    return lax.dot_general(lhs, rhs, dims, preferred_element_type=F32)


def iota(shape, dim):
    return lax.broadcasted_iota(jnp.int32, shape, dim)


def hot(mask):
    return jnp.where(mask, jnp.float32(1), jnp.float32(0)).astype(BF16)


def column_hot(row, count):
    size = row.shape[1]
    column = jnp.transpose(jnp.broadcast_to(row, (LANES, size)))
    lane = iota((size, LANES), 1)
    return jnp.concatenate([hot(column == lane + j * LANES) for j in range(count // LANES)], axis=1)


def by_receiver(me, distance, capacity):
    return pl.ds(pl.multiple_of(lax.bitwise_xor(me, distance) * capacity, capacity), capacity)


def pack_kernel(n_seq, capacity, me_ref, dest_hbm, feats_hbm, slot_out, *refs):
    outs, (dest_ref, feats_ref, sems) = refs[:n_seq], refs[n_seq:]
    rows, width = feats_ref.shape
    slots = n_seq * capacity
    loads = [
        pltpu.make_async_copy(source, target, sems.at[i])
        for i, (source, target) in enumerate(((dest_hbm, dest_ref), (feats_hbm, feats_ref)))
    ]
    for load in loads:
        load.start()
    loads[0].wait()
    shift = rows.bit_length() - 1
    places = dest_ref[...]
    distance = lax.bitwise_xor(lax.shift_right_logical(places, shift), me_ref[0])
    within = lax.bitwise_and(places, rows - 1) + 1
    member = iota((n_seq, rows), 0) == distance
    upper = hot(iota((rows, rows), 0) <= iota((rows, rows), 1))
    counts = mm(hot(member), upper)
    rank = jnp.sum(jnp.where(member, counts, 0.0), axis=0, keepdims=True).astype(jnp.int32) - 1
    slot = distance * capacity + rank
    slot_out[...] = slot
    select = hot(iota((slots, rows), 0) == slot)
    loads[1].wait()
    feats = mm(select, feats_ref[...]).astype(BF16)
    upper_half = slot >= width
    high = lax.shift_right_logical(within, 8).astype(F32)
    low = lax.bitwise_and(within, 255).astype(F32)
    line = iota((n_seq * EXTRA, rows), 0)
    kind = lax.bitwise_and(line, EXTRA - 1)
    digit = jnp.where(kind < 2, high, low)
    wanted = (
        (lax.shift_right_logical(line, EXTRA.bit_length() - 1) == distance)
        & (kind < 4)
        & ((lax.bitwise_and(kind, 1) == 1) == upper_half)
    )
    digits = jnp.where(wanted, digit, 0.0).astype(BF16)
    spread = hot(iota((width, rows), 0) == lax.bitwise_and(slot, width - 1))
    position = mm(digits, spread, NT).astype(BF16)
    for d in range(n_seq):
        outs[d][:capacity, :] = feats[d * capacity : (d + 1) * capacity]
        outs[d][capacity:, :] = position[d * EXTRA : (d + 1) * EXTRA]


def pack_grads_kernel(n_seq, capacity, me_ref, slot_ref, grads_ref, grads_out):
    select = hot(iota((n_seq * capacity, grads_ref.shape[0]), 0) == slot_ref[...])
    grads = mm(select, grads_ref[...]).astype(BF16)
    for d in range(n_seq):
        grads_out[by_receiver(me_ref[0], d, capacity), :] = grads[d * capacity : (d + 1) * capacity]


def forward_kernel(n_seq, capacity, w_hbm, gain_ref, *refs):
    recv, refs = refs[:n_seq], refs[n_seq:]
    pos_out, xhat_hbm, inv_hbm, normed_hbm, qkv_hbm, trans_hbm, attn_out, stats_out = refs[:8]
    w_ref, xhat_ref, inv_ref, normed_ref, qkv_ref, trans, sems = refs[8:]
    width = w_ref.shape[0]
    rows = xhat_ref.shape[0]
    head = width // HEADS
    pair = 2 * head
    step = pl.program_id(0)
    w_copy = pltpu.make_async_copy(w_hbm, w_ref, sems.at[0])
    saves = [
        pltpu.make_async_copy(source, target, sems.at[1 + i])
        for i, (source, target) in enumerate(
            (
                (xhat_ref, xhat_hbm),
                (inv_ref, inv_hbm),
                (normed_ref, normed_hbm),
                (qkv_ref, qkv_hbm),
                (trans.at[pl.ds(0, 2 * width)], trans_hbm),
            )
        )
    ]

    @pl.when(step == 0)
    def _():
        w_copy.start()
        tile = recv[0][capacity:, :].astype(F32)
        for s in range(1, n_seq):
            tile = tile + recv[s][capacity:, :].astype(F32)
        high = jnp.concatenate([tile[0:1], tile[1:2]], axis=1)
        low = jnp.concatenate([tile[2:3], tile[3:4]], axis=1)
        pos = (high * 256.0 + low).astype(jnp.int32) - 1
        pos_out[...] = pos
        place = hot(iota((rows, n_seq * capacity), 0) == pos)
        values = jnp.concatenate([recv[s][:capacity, :] for s in range(n_seq)], axis=0)
        feats = mm(place, values)
        centered = feats - jnp.mean(feats, axis=1, keepdims=True)
        inv = lax.rsqrt(jnp.mean(centered * centered, axis=1, keepdims=True) + 1e-05)
        xhat = centered * inv
        xhat_ref[...] = xhat
        inv_ref[...] = jnp.broadcast_to(inv, inv_ref.shape)
        normed = (xhat * gain_ref[...]).astype(BF16)
        normed_ref[...] = normed
        w_copy.wait()
        qkv = mm(normed, w_ref[...])
        qkv_ref[...] = qkv.astype(BF16)
        trans[...] = jnp.transpose(qkv).astype(BF16)
        for save in saves:
            save.start()

    lo = pl.multiple_of(step * pair, pair)
    keys = qkv_ref[:, pl.ds(pl.multiple_of(width + step * pair, pair), pair)]
    query_t = trans[pl.ds(lo, pair), :] * BF16(0.125)
    zero = jnp.zeros((head, rows), BF16)
    for j in range(2):
        part = query_t[j * head : (j + 1) * head]
        part = jnp.concatenate([part, zero] if j == 0 else [zero, part], axis=0)
        scores = mm(keys, part)
        top = jnp.max(scores, axis=0, keepdims=True)
        expo = jnp.exp(scores - top)
        share = 1.0 / jnp.sum(expo, axis=0, keepdims=True)
        probs = expo * share
        stats_out[pl.ds(2 * step + j, 1), :] = top
        stats_out[pl.ds(HEADS + 2 * step + j, 1), :] = share
        values_t = trans[pl.ds(pl.multiple_of(2 * width + step * pair + j * head, head), head), :]
        attn_out[j * head : (j + 1) * head, :] = mm(values_t, probs.astype(BF16)).astype(BF16)

    @pl.when(step == pl.num_programs(0) - 1)
    def _():
        for save in saves:
            save.wait()


def backward_kernel(n_seq, chip_bits, me_ref, pos_ref, w_proj_ref, stats_ref, *refs):
    (recv_hbm, qkv_hbm, trans_hbm, w_hbm, xhat_hbm, normed_hbm, attn_hbm), refs = refs[:7], refs[7:]
    outs, serial_grad_hbm, d_normed_hbm, refs = refs[:4], refs[4], refs[5], refs[6:]
    recv_ref, qkv_ref, trans_ref, w_ref, xhat_ref, normed_ref, attn_ref, refs = *refs[:7], refs[7:]
    sums, refs = refs[:4], refs[4:]
    serial_grad, d_normed_ref, d_attn, d_attn_t, d_qkv, normed_t, gain_column, sems = refs
    width = w_proj_ref.shape[0]
    rows = xhat_ref.shape[0]
    capacity = recv_ref.shape[0] // n_seq
    head = width // HEADS
    pair = 2 * head
    step = pl.program_id(0)
    me = me_ref[0]
    loads = [
        pltpu.make_async_copy(source, target, sems.at[i])
        for i, (source, target) in enumerate(
            (
                (recv_hbm, recv_ref),
                (qkv_hbm, qkv_ref),
                (trans_hbm, trans_ref),
                (normed_hbm, normed_ref),
                (w_hbm, w_ref),
                (xhat_hbm, xhat_ref),
                (attn_hbm, attn_ref),
            )
        )
    ]
    saves = [
        pltpu.make_async_copy(source, target, sems.at[7 + i])
        for i, (source, target) in enumerate(
            [*zip(sums, outs), (serial_grad, serial_grad_hbm), (d_normed_ref, d_normed_hbm)]
        )
    ]

    @pl.when(step == 0)
    def _():
        for load in loads:
            load.start()
        place = hot(iota((rows, n_seq * capacity), 0) == pos_ref[...])
        loads[0].wait()
        values = jnp.concatenate(
            [recv_ref[by_receiver(me, d, capacity), :] for d in range(n_seq)], axis=0
        )
        grads = mm(place, values).astype(BF16)
        serial_grad[...] = grads
        saves[4].start()
        d_att = mm(grads, w_proj_ref[...], NT).astype(BF16)
        d_attn[...] = d_att
        d_attn_t[...] = jnp.transpose(d_att.astype(F32)).astype(BF16)
        loads[1].wait()
        loads[2].wait()

    lo = pl.multiple_of(step * pair, pair)
    queries = qkv_ref[:, pl.ds(lo, pair)]
    values = qkv_ref[:, pl.ds(pl.multiple_of(2 * width + step * pair, pair), pair)]
    d_att_t = d_attn_t[pl.ds(lo, pair), :] * BF16(0.125)
    d_att = d_attn[:, pl.ds(lo, pair)]
    keys = qkv_ref[:, pl.ds(pl.multiple_of(width + step * pair, pair), pair)]
    query_t = trans_ref[pl.ds(lo, pair), :] * BF16(0.125)
    zero = jnp.zeros((head, rows), BF16)
    d_q, d_k, d_v = [], [], []
    for j in range(2):
        def alone(both):
            part = both[j * head : (j + 1) * head]
            return jnp.concatenate([part, zero] if j == 0 else [zero, part], axis=0)

        top = stats_ref[pl.ds(2 * step + j, 1), :]
        share = stats_ref[pl.ds(HEADS + 2 * step + j, 1), :]
        probs = jnp.exp(mm(keys, alone(query_t)) - top) * share
        d_probs = mm(values, alone(d_att_t))
        total = jnp.sum(d_probs * probs, axis=0, keepdims=True)
        d_scores = (probs * (d_probs - total)).astype(BF16)
        k_t = trans_ref[pl.ds(pl.multiple_of(width + step * pair + j * head, head), head), :]
        d_q.append(mm(k_t, d_scores))
        d_k.append(mm(d_scores, queries))
        d_v.append(mm(probs.astype(BF16), d_att))
    first = iota((rows, pair), 1) < head
    d_qkv[:, pl.ds(lo, pair)] = jnp.transpose(jnp.concatenate(d_q, axis=0)).astype(BF16)
    d_qkv[:, pl.ds(pl.multiple_of(width + step * pair, pair), pair)] = jnp.where(
        first, d_k[0], d_k[1]
    ).astype(BF16)
    d_qkv[:, pl.ds(pl.multiple_of(2 * width + step * pair, pair), pair)] = jnp.where(
        first, d_v[0], d_v[1]
    ).astype(BF16)

    @pl.when(step == pl.num_programs(0) - 1)
    def _():
        for load in loads[3:]:
            load.wait()
        normed_t[...] = jnp.transpose(normed_ref[...].astype(F32)).astype(BF16)
        d_normed = mm(d_qkv[...], w_ref[...], NT)
        d_normed_ref[...] = d_normed
        saves[5].start()
        gain_row = jnp.sum(d_normed * xhat_ref[...], axis=0, keepdims=True)
        gain_column[...] = jnp.transpose(jnp.broadcast_to(gain_row, (LANES, width)))
        eighth = width // 8
        odd = lax.bitwise_and(me, 1)

        def sides(even_bit, odd_bit):
            even_side = lax.bitwise_and(lax.shift_right_logical(me, even_bit), 1)
            odd_side = lax.bitwise_and(lax.shift_right_logical(me, odd_bit), 1)
            mine = jnp.where(odd == 1, odd_side, even_side)
            return mine, even_side + odd_side - mine

        (mine, other), (mine_next, other_next) = (sides(*bits) for bits in chip_bits)
        starts = (
            ((1 - odd) * 2 + 1 - other, other_next),
            ((1 - odd) * 2 + other, other_next),
            (odd * 2 + 1 - mine, mine_next),
            (odd * 2 + mine, mine_next),
        )
        for out, (start, side), save in zip(sums, starts, saves):
            for j, half in enumerate((1 - side, side)):
                part = pl.ds(pl.multiple_of((start * 2 + half) * eighth, eighth), eighth)
                lines = slice(j * eighth, (j + 1) * eighth)
                out[lines, : 3 * width] = mm(normed_t[part, :], d_qkv[...])
                out[lines, 3 * width : 4 * width] = mm(attn_ref[part, :], serial_grad[...])
                out[lines, 4 * width :] = gain_column[part, :]
            save.start()
        for save in saves:
            save.wait()


def residual_kernel(
    n_seq, me_ref, pos_ref, gain_ref, inv_ref, xhat_ref, serial_grad_ref, d_normed_ref, back_out
):
    xhat = xhat_ref[...]
    rows = xhat.shape[0]
    capacity = pos_ref.shape[1] // n_seq
    scaled = d_normed_ref[...] * gain_ref[...]
    residual = inv_ref[:, 0:1] * (
        scaled
        - jnp.mean(scaled, axis=1, keepdims=True)
        - xhat * jnp.mean(scaled * xhat, axis=1, keepdims=True)
    )
    serial_dx = (serial_grad_ref[...].astype(F32) + residual).astype(BF16)
    returned = mm(column_hot(pos_ref[...], rows), serial_dx).astype(BF16)
    for d in range(n_seq):
        back_out[by_receiver(me_ref[0], d, capacity), :] = returned[d * capacity : (d + 1) * capacity]


def unpack_kernel(n_seq, me_ref, slot_ref, recv_ref, out_ref):
    capacity = recv_ref.shape[0] // n_seq
    values = jnp.concatenate(
        [recv_ref[by_receiver(me_ref[0], d, capacity), :] for d in range(n_seq)], axis=0
    )
    out_ref[...] = mm(column_hot(slot_ref[...], values.shape[0]), values).astype(BF16)


def split_kernel(side_ref, own_ref, other_ref, qkv_out, proj_out, gain_out):
    width = proj_out.shape[1]

    def write(ref):
        qkv_out[...] = ref[:, : 3 * width].astype(F32)
        proj_out[...] = ref[:, 3 * width : 4 * width].astype(F32)
        gain_out[...] = jnp.transpose(ref[:, 4 * width :].astype(F32))[0:1]

    own = pl.program_id(0) == side_ref[0]
    pl.when(own)(lambda: write(own_ref))
    pl.when(jnp.logical_not(own))(lambda: write(other_ref))


def exponent_of(largest):
    return jnp.clip(jnp.ceil(jnp.log(jnp.maximum(largest, 1e-30)) * 1.4426950408889634), -100.0, 120.0)


def encode(out_ref, total):
    width = total.shape[1] - LANES
    body, gain = total[:, :width], total[:, width : width + 1]
    exponent = exponent_of(jnp.max(jnp.abs(body), axis=1, keepdims=True))
    codes = jnp.round(body * (jnp.exp2(-exponent) * CODE_MAX))
    out_ref[:, :width] = codes.astype(jnp.int32).astype(jnp.int16)
    gain_exponent = exponent_of(jnp.abs(gain))
    scaled = gain * (jnp.exp2(-gain_exponent) * CODE_MAX)
    high = jnp.round(scaled)
    low = jnp.round((scaled - high) * DIGIT)
    lane = iota((total.shape[0], LANES), 1)
    tail = jnp.where(lane == 0, high, jnp.where(lane == 1, low, jnp.where(lane == 2, gain_exponent, exponent)))
    out_ref[:, width:] = tail.astype(jnp.int32).astype(jnp.int16)


def decode(codes):
    values = codes.astype(jnp.int32).astype(F32)
    width = values.shape[1] - LANES
    tail = values[:, width:]
    body = values[:, :width] * (jnp.exp2(tail[:, 3:4]) * (1.0 / CODE_MAX))
    gain = (tail[:, 0:1] + tail[:, 1:2] * (1.0 / DIGIT)) * (jnp.exp2(tail[:, 2:3]) * (1.0 / CODE_MAX))
    return jnp.concatenate([body, jnp.broadcast_to(gain, tail.shape)], axis=1)


def total_of(terms, part):
    half = terms[0].shape[0] // 2
    rows = {"all": slice(None), "first": slice(0, half), "second": slice(half, 2 * half)}[part]
    values = [ref[rows, :] for ref in terms]
    return functools.reduce(jnp.add, [decode(v) if v.dtype == jnp.int16 else v for v in values])


def message_kernel(part, *refs):
    encode(refs[-1], total_of(refs[:-1], part))


def sum_kernel(parts, *refs):
    refs[-1][...] = functools.reduce(jnp.add, [total_of([ref], p) for ref, p in zip(refs, parts)])


def pieces_kernel(parts, n_dp, plane_ref, *refs):
    terms, own, messages, total = refs[: len(parts)], refs[len(parts)], refs[len(parts) + 1 : -1], refs[-1]
    total[...] = functools.reduce(jnp.add, [total_of([ref], p) for ref, p in zip(terms, parts)])
    size = own.shape[0]

    def rows_of(distance):
        start = lax.bitwise_xor(plane_ref[0], distance) * size
        return total[pl.ds(pl.multiple_of(start, size), size), :]

    for k in range(1, n_dp):
        encode(messages[k - 1], rows_of(k))
    own[...] = rows_of(0)


def finish_kernel(*refs):
    refs[-1][...] = total_of(refs[:-1], "all").astype(BF16)


def whole(shape):
    return pl.BlockSpec(shape, lambda *_: (0,) * len(shape), pipeline_mode=pl.Buffered(1))


def params(mib):
    return pltpu.CompilerParams(vmem_limit_bytes=mib * MIB)


def shape_of(shape, dtype):
    return jax.ShapeDtypeStruct(shape, dtype)


def by_distance(blocks, axis):
    count = len(blocks)
    return [blocks[0]] + [
        lax.ppermute(blocks[k], axis, [(i, i ^ k) for i in range(count)]) for k in range(1, count)
    ]


def chip_orders(n_seq):
    bits = list(range(1, n_seq.bit_length() - 1))
    middle = len(bits) // 2
    return bits, bits[middle:] + bits[:middle]


def chip_steps():
    n_seq, me = lax.axis_size("seq"), lax.axis_index("seq")
    odd = lax.bitwise_and(me, 1) == 1

    def side(bit):
        return lax.bitwise_and(lax.shift_right_logical(me, jnp.asarray(bit, me.dtype)), 1)

    steps = []
    for even_bit, odd_bit in zip(*chip_orders(n_seq)):
        pairs = [(i, i ^ (1 << (odd_bit if i & 1 else even_bit))) for i in range(n_seq)]
        steps.append((pairs, jnp.where(odd, side(odd_bit), side(even_bit))))
    return steps


def piece(terms, index, count):
    size = terms[0].shape[0] // count
    return functools.reduce(jnp.add, [lax.dynamic_slice_in_dim(t, index * size, size) for t in terms])


def core_pairs():
    return [(i, i ^ 1) for i in range(lax.axis_size("seq"))]


def small_kernel(kernel, outs, operands, scalars=0, scratch=(), name="sum"):
    in_smem = pl.BlockSpec(memory_space=pltpu.SMEM)
    in_vmem = pl.BlockSpec(memory_space=pltpu.VMEM)
    touched = sum(x.size * x.dtype.itemsize for x in (*operands, *outs))
    return pl.pallas_call(
        kernel,
        out_shape=outs,
        in_specs=[in_smem] * scalars + [in_vmem] * (len(operands) - scalars),
        out_specs=[in_vmem] * len(outs),
        scratch_shapes=list(scratch),
        compiler_params=params(16),
        cost_estimate=pl.CostEstimate(flops=2 * touched, bytes_accessed=touched, transcendentals=0),
        name=name,
    )(*operands)


def message(terms, part, name):
    rows, width = terms[0].shape
    rows = rows if part == "all" else rows // 2
    return small_kernel(
        functools.partial(message_kernel, part), [shape_of((rows, width), jnp.int16)], terms, name=name
    )[0]


def first_step(quarters, steps):
    pass_on, pass_keep, own_on, own_keep = quarters
    got_on = lax.ppermute(pass_on, "seq", core_pairs())
    got_keep = lax.ppermute(pass_keep, "seq", core_pairs())
    sent = message([own_on, got_on], "all", "code_first")
    return [own_keep, got_keep, lax.ppermute(sent, "seq", steps[0][0])]


def second_step(terms, steps):
    sent = message(terms, "first", "code_second")
    return terms, lax.ppermute(sent, "seq", steps[1][0])


def halves_of_plain(part, steps):
    for pairs, side in steps:
        got = lax.ppermute(piece([part], 1 - side, 2), "seq", pairs)
        part = piece([part], side, 2) + got
    return part


def reduce_over_planes(terms, got, steps):
    n_dp, plane = lax.axis_size("dp"), lax.axis_index("dp")
    rows, width = got.shape
    parts = ["second"] * len(terms) + ["all"]
    if len(steps) > 2 or rows // n_dp % 16:
        part = small_kernel(
            functools.partial(sum_kernel, parts), [shape_of((rows, width), F32)], [*terms, got]
        )[0]
        part = halves_of_plain(part, steps[2:])
        pieces = [piece([part], lax.bitwise_xor(plane, k), n_dp) for k in range(n_dp)]
        return functools.reduce(jnp.add, by_distance(pieces, "dp")).astype(BF16)
    size = rows // n_dp
    own, *sent = small_kernel(
        functools.partial(pieces_kernel, parts, n_dp),
        [shape_of((size, width), F32)] + [shape_of((size, width), jnp.int16)] * (n_dp - 1),
        [jnp.reshape(plane.astype(jnp.int32), (1,)), *terms, got],
        scalars=1,
        scratch=[pltpu.VMEM((rows, width), F32)],
        name="code_planes",
    )
    arrived = by_distance([own] + sent, "dp")
    return small_kernel(finish_kernel, [shape_of((size, width), BF16)], arrived, name="finish")[0]


def share_over_planes(part):
    n_dp, plane = lax.axis_size("dp"), lax.axis_index("dp")
    shares = jnp.stack(by_distance([part] * n_dp, "dp"))
    return jnp.concatenate(
        [lax.dynamic_index_in_dim(shares, lax.bitwise_xor(plane, p), keepdims=False) for p in range(n_dp)],
        axis=0,
    )


def share_in_plane(part, steps):
    for pairs, side in reversed(steps):
        other = lax.ppermute(part, "seq", pairs)
        part = jnp.where(
            side == 0, jnp.concatenate([part, other], axis=0), jnp.concatenate([other, part], axis=0)
        )
    return part


def per_device(points, cotangent, dest, w_qkv, w_proj, gain):
    feats = points[0]
    grads = cotangent[0]
    rows, width = feats.shape
    n_seq = lax.axis_size("seq")
    capacity = 2 * (rows // n_seq)
    slots = n_seq * capacity
    block = capacity + EXTRA
    pairs = HEADS // 2
    pair = width // pairs
    sum_shape = (width // 4, 4 * width + LANES)
    me = jnp.reshape(lax.axis_index("seq").astype(jnp.int32), (1,))
    gain_row = gain.reshape(1, width)
    in_smem = pl.BlockSpec(memory_space=pltpu.SMEM)
    in_vmem = pl.BlockSpec(memory_space=pltpu.VMEM)
    in_hbm = pl.BlockSpec(memory_space=pl.ANY)
    stay_hbm = pl.BlockSpec(memory_space=pltpu.HBM)

    slot, *feats_sent = pl.pallas_call(
        functools.partial(pack_kernel, n_seq, capacity),
        out_shape=[shape_of((1, rows), jnp.int32)] + [shape_of((block, width), BF16)] * n_seq,
        in_specs=[in_smem] + [stay_hbm] * 2,
        out_specs=[in_vmem] * (1 + n_seq),
        scratch_shapes=[
            pltpu.VMEM((1, rows), jnp.int32),
            pltpu.VMEM((rows, width), BF16),
            pltpu.SemaphoreType.DMA((2,)),
        ],
        compiler_params=params(60),
        cost_estimate=pl.CostEstimate(
            flops=2 * slots * rows * width, bytes_accessed=2 * MIB, transcendentals=0
        ),
        name="pack",
    )(me, dest, feats)
    feats_got = by_distance(feats_sent, "seq")
    feats_got[1], slot = lax.optimization_barrier((feats_got[1], slot))
    grads_sent = pl.pallas_call(
        functools.partial(pack_grads_kernel, n_seq, capacity),
        out_shape=shape_of((slots, width), BF16),
        in_specs=[in_smem] + [in_vmem] * 2,
        out_specs=in_vmem,
        compiler_params=params(20),
        cost_estimate=pl.CostEstimate(
            flops=2 * slots * rows * width, bytes_accessed=2 * MIB, transcendentals=0
        ),
        name="pack_grads",
    )(me, slot, grads)

    def exchange(sent):
        sent = sent.reshape(n_seq, capacity, width)
        got = lax.all_to_all(sent, "seq", split_axis=0, concat_axis=0, tiled=True)
        return got.reshape(slots, width)

    feats_got, grads_sent = lax.optimization_barrier((feats_got, grads_sent))
    grads_got = exchange(grads_sent)

    pos, xhat, inv, normed, qkv, trans, attn_t, stats = pl.pallas_call(
        functools.partial(forward_kernel, n_seq, capacity),
        grid=(pairs,),
        out_shape=(
            shape_of((1, slots), jnp.int32),
            shape_of((rows, width), F32),
            shape_of((rows, LANES), F32),
            shape_of((rows, width), BF16),
            shape_of((rows, 3 * width), BF16),
            shape_of((2 * width, rows), BF16),
            shape_of((width, rows), BF16),
            shape_of((2 * HEADS, rows), F32),
        ),
        in_specs=[in_hbm, whole((1, width))] + [whole((block, width))] * n_seq,
        out_specs=[whole((1, slots))]
        + [in_hbm] * 5
        + [pl.BlockSpec((pair, rows), lambda i: (i, 0)), whole((2 * HEADS, rows))],
        scratch_shapes=[
            pltpu.VMEM((width, 3 * width), BF16),
            pltpu.VMEM((rows, width), F32),
            pltpu.VMEM((rows, LANES), F32),
            pltpu.VMEM((rows, width), BF16),
            pltpu.VMEM((rows, 3 * width), BF16),
            pltpu.VMEM((3 * width, rows), BF16),
            pltpu.SemaphoreType.DMA((6,)),
        ],
        compiler_params=params(60),
        cost_estimate=pl.CostEstimate(
            flops=6 * rows * width * width + 8 * HEADS * rows * rows * pair,
            bytes_accessed=16 * MIB,
            transcendentals=HEADS * rows * rows,
        ),
        name="forward",
    )(w_qkv, gain_row, *feats_got)

    chip_bits = tuple(zip(*chip_orders(n_seq)))[:2]
    *quarters, serial_grad, d_normed = pl.pallas_call(
        functools.partial(backward_kernel, n_seq, chip_bits),
        grid=(pairs,),
        out_shape=[shape_of(sum_shape, F32)] * 4
        + [shape_of((rows, width), BF16), shape_of((rows, width), F32)],
        in_specs=[
            in_smem,
            whole((1, slots)),
            whole((width, width)),
            whole((2 * HEADS, rows)),
        ]
        + [in_hbm] * 7,
        out_specs=[in_hbm] * 6,
        scratch_shapes=[
            pltpu.VMEM((slots, width), BF16),
            pltpu.VMEM((rows, 3 * width), BF16),
            pltpu.VMEM((2 * width, rows), BF16),
            pltpu.VMEM((width, 3 * width), BF16),
            pltpu.VMEM((rows, width), F32),
            pltpu.VMEM((rows, width), BF16),
            pltpu.VMEM((width, rows), BF16),
        ]
        + [pltpu.VMEM(sum_shape, F32)] * 4
        + [
            pltpu.VMEM((rows, width), BF16),
            pltpu.VMEM((rows, width), F32),
            pltpu.VMEM((rows, width), BF16),
            pltpu.VMEM((width, rows), BF16),
            pltpu.VMEM((rows, 3 * width), BF16),
            pltpu.VMEM((width, rows), BF16),
            pltpu.VMEM((width, LANES), F32),
            pltpu.SemaphoreType.DMA((13,)),
        ],
        compiler_params=params(60),
        cost_estimate=pl.CostEstimate(
            flops=12 * rows * width * width + 10 * HEADS * rows * rows * pair,
            bytes_accessed=16 * MIB,
            transcendentals=HEADS * rows * rows,
        ),
        name="backward",
    )(me, pos, w_proj, stats, grads_got, qkv, trans, w_qkv, xhat, normed, attn_t)

    steps = chip_steps()
    terms = first_step(quarters, steps)
    back = pl.pallas_call(
        functools.partial(residual_kernel, n_seq),
        out_shape=shape_of((slots, width), BF16),
        in_specs=[in_smem] + [in_vmem] * 6,
        out_specs=in_vmem,
        compiler_params=params(20),
        cost_estimate=pl.CostEstimate(
            flops=2 * slots * rows * width, bytes_accessed=4 * MIB, transcendentals=0
        ),
        name="residual",
    )(me, pos, gain_row, inv, xhat, serial_grad, d_normed)
    terms, got = second_step(terms, steps)
    got, back = lax.optimization_barrier((got, back))
    returned = exchange(back)
    part, returned = lax.optimization_barrier((reduce_over_planes(terms, got, steps), returned))
    own = share_in_plane(share_over_planes(part), steps)
    other = lax.ppermute(own, "seq", core_pairs())
    grad_local = pl.pallas_call(
        functools.partial(unpack_kernel, n_seq),
        out_shape=shape_of((rows, width), BF16),
        in_specs=[in_smem] + [in_vmem] * 2,
        out_specs=in_vmem,
        compiler_params=params(20),
        cost_estimate=pl.CostEstimate(
            flops=2 * slots * rows * width, bytes_accessed=2 * MIB, transcendentals=0
        ),
        name="unpack",
    )(me, slot, returned)
    half = width // 2
    grad_qkv, grad_proj, gain_grad = pl.pallas_call(
        split_kernel,
        grid=(2,),
        out_shape=(
            shape_of((width, 3 * width), F32),
            shape_of((width, width), F32),
            shape_of((1, width), F32),
        ),
        in_specs=[in_smem] + [whole(own.shape)] * 2,
        out_specs=[
            pl.BlockSpec((half, 3 * width), lambda i: (i, 0)),
            pl.BlockSpec((half, width), lambda i: (i, 0)),
            pl.BlockSpec((1, half), lambda i: (0, i)),
        ],
        compiler_params=params(20),
        cost_estimate=pl.CostEstimate(flops=0, bytes_accessed=8 * MIB, transcendentals=0),
        name="split",
    )(lax.bitwise_and(me, 1), own, other)
    return (grad_local[None], grad_qkv, grad_proj, gain_grad[0])


def solution(mesh):
    return jax.shard_map(
        per_device,
        mesh=mesh,
        in_specs=(P("dp", "seq", None), P("dp", "seq", None), P("dp", "seq"), P(), P(), P()),
        out_specs=(P("dp", "seq", None), P(), P(), P()),
        check_vma=False,
    )
```

```python
import functools

import jax
import jax.numpy as jnp
from jax import lax
from jax.experimental import pallas as pl
from jax.experimental.pallas import tpu as pltpu
from jax.sharding import PartitionSpec as P

HEADS = 8
PATCH = 512
EXTRA = 16
LANES = 128
CODE_MAX = 32000.0
DIGIT = 60000.0
MIB = 1024 * 1024
F32 = jnp.float32
BF16 = jnp.bfloat16
NN = (((1,), (0,)), ((), ()))
NT = (((1,), (1,)), ((), ()))


def mm(lhs, rhs, dims=NN):
    return lax.dot_general(lhs, rhs, dims, preferred_element_type=F32)


def iota(shape, dim):
    return lax.broadcasted_iota(jnp.int32, shape, dim)


def hot(mask):
    return jnp.where(mask, jnp.float32(1), jnp.float32(0)).astype(BF16)


def column_hot(row, count):
    size = row.shape[1]
    column = jnp.transpose(jnp.broadcast_to(row, (LANES, size)))
    lane = iota((size, LANES), 1)
    return jnp.concatenate([hot(column == lane + j * LANES) for j in range(count // LANES)], axis=1)


def by_receiver(me, distance, capacity):
    return pl.ds(pl.multiple_of(lax.bitwise_xor(me, distance) * capacity, capacity), capacity)


def pack_kernel(n_seq, capacity, me_ref, dest_hbm, feats_hbm, slot_out, *refs):
    outs, (dest_ref, feats_ref, sems) = refs[:n_seq], refs[n_seq:]
    rows, width = feats_ref.shape
    slots = n_seq * capacity
    loads = [
        pltpu.make_async_copy(source, target, sems.at[i])
        for i, (source, target) in enumerate(((dest_hbm, dest_ref), (feats_hbm, feats_ref)))
    ]
    for load in loads:
        load.start()
    loads[0].wait()
    shift = rows.bit_length() - 1
    places = dest_ref[...]
    distance = lax.bitwise_xor(lax.shift_right_logical(places, shift), me_ref[0])
    within = lax.bitwise_and(places, rows - 1) + 1
    member = iota((n_seq, rows), 0) == distance
    upper = hot(iota((rows, rows), 0) <= iota((rows, rows), 1))
    counts = mm(hot(member), upper)
    rank = jnp.sum(jnp.where(member, counts, 0.0), axis=0, keepdims=True).astype(jnp.int32) - 1
    slot = distance * capacity + rank
    slot_out[...] = slot
    select = hot(iota((slots, rows), 0) == slot)
    loads[1].wait()
    feats = mm(select, feats_ref[...]).astype(BF16)
    upper_half = slot >= width
    high = lax.shift_right_logical(within, 8).astype(F32)
    low = lax.bitwise_and(within, 255).astype(F32)
    line = iota((n_seq * EXTRA, rows), 0)
    kind = lax.bitwise_and(line, EXTRA - 1)
    digit = jnp.where(kind < 2, high, low)
    wanted = (
        (lax.shift_right_logical(line, EXTRA.bit_length() - 1) == distance)
        & (kind < 4)
        & ((lax.bitwise_and(kind, 1) == 1) == upper_half)
    )
    digits = jnp.where(wanted, digit, 0.0).astype(BF16)
    spread = hot(iota((width, rows), 0) == lax.bitwise_and(slot, width - 1))
    position = mm(digits, spread, NT).astype(BF16)
    for d in range(n_seq):
        outs[d][:capacity, :] = feats[d * capacity : (d + 1) * capacity]
        outs[d][capacity:, :] = position[d * EXTRA : (d + 1) * EXTRA]


def pack_grads_kernel(n_seq, capacity, me_ref, slot_ref, grads_ref, grads_out):
    select = hot(iota((n_seq * capacity, grads_ref.shape[0]), 0) == slot_ref[...])
    grads = mm(select, grads_ref[...]).astype(BF16)
    for d in range(n_seq):
        grads_out[by_receiver(me_ref[0], d, capacity), :] = grads[d * capacity : (d + 1) * capacity]


def forward_kernel(n_seq, capacity, w_hbm, gain_ref, *refs):
    recv, refs = refs[:n_seq], refs[n_seq:]
    pos_out, xhat_hbm, inv_hbm, normed_hbm, qkv_hbm, trans_hbm, attn_out, stats_out = refs[:8]
    w_ref, xhat_ref, inv_ref, normed_ref, qkv_ref, trans, sems = refs[8:]
    width = w_ref.shape[0]
    rows = xhat_ref.shape[0]
    head = width // HEADS
    pair = 2 * head
    w_copy = pltpu.make_async_copy(w_hbm, w_ref, sems.at[0])
    saves = [
        pltpu.make_async_copy(source, target, sems.at[1 + i])
        for i, (source, target) in enumerate(
            (
                (xhat_ref, xhat_hbm),
                (inv_ref, inv_hbm),
                (normed_ref, normed_hbm),
                (qkv_ref, qkv_hbm),
                (trans.at[pl.ds(0, 2 * width)], trans_hbm),
            )
        )
    ]

    w_copy.start()
    tile = recv[0][capacity:, :].astype(F32)
    for s in range(1, n_seq):
        tile = tile + recv[s][capacity:, :].astype(F32)
    high = jnp.concatenate([tile[0:1], tile[1:2]], axis=1)
    low = jnp.concatenate([tile[2:3], tile[3:4]], axis=1)
    pos = (high * 256.0 + low).astype(jnp.int32) - 1
    pos_out[...] = pos
    place = hot(iota((rows, n_seq * capacity), 0) == pos)
    values = jnp.concatenate([recv[s][:capacity, :] for s in range(n_seq)], axis=0)
    feats = mm(place, values)
    centered = feats - jnp.mean(feats, axis=1, keepdims=True)
    inv = lax.rsqrt(jnp.mean(centered * centered, axis=1, keepdims=True) + 1e-05)
    xhat = centered * inv
    xhat_ref[...] = xhat
    inv_ref[...] = jnp.broadcast_to(inv, inv_ref.shape)
    normed = (xhat * gain_ref[...]).astype(BF16)
    normed_ref[...] = normed
    w_copy.wait()
    qkv = mm(normed, w_ref[...])
    qkv_ref[...] = qkv.astype(BF16)
    trans[...] = jnp.transpose(qkv).astype(BF16)
    for save in saves:
        save.start()

    for step in range(HEADS // 2):
        lo = step * pair
        keys = qkv_ref[:, pl.ds(width + lo, pair)]
        query_t = trans[pl.ds(lo, pair), :] * BF16(0.125)
        zero = jnp.zeros((head, rows), BF16)
        for j in range(2):
            part = query_t[j * head : (j + 1) * head]
            part = jnp.concatenate([part, zero] if j == 0 else [zero, part], axis=0)
            scores = mm(keys, part)
            top = jnp.max(scores, axis=0, keepdims=True)
            expo = jnp.exp(scores - top)
            share = 1.0 / jnp.sum(expo, axis=0, keepdims=True)
            probs = expo * share
            stats_out[pl.ds(2 * step + j, 1), :] = top
            stats_out[pl.ds(HEADS + 2 * step + j, 1), :] = share
            values_t = trans[pl.ds(2 * width + lo + j * head, head), :]
            attn_out[pl.ds(lo + j * head, head), :] = mm(values_t, probs.astype(BF16)).astype(BF16)

    for save in saves:
        save.wait()


def backward_kernel(n_seq, chip_bits, me_ref, pos_ref, w_proj_ref, stats_ref, *refs):
    (recv_hbm, qkv_hbm, trans_hbm, w_hbm, xhat_hbm, normed_hbm, attn_hbm), refs = refs[:7], refs[7:]
    outs, serial_grad_hbm, d_normed_hbm, refs = refs[:4], refs[4], refs[5], refs[6:]
    recv_ref, qkv_ref, trans_ref, w_ref, xhat_ref, normed_ref, attn_ref, refs = *refs[:7], refs[7:]
    sums, refs = refs[:4], refs[4:]
    serial_grad, d_normed_ref, d_attn, d_attn_t, d_qkv, normed_t, gain_column, sems = refs
    width = w_proj_ref.shape[0]
    rows = xhat_ref.shape[0]
    capacity = recv_ref.shape[0] // n_seq
    head = width // HEADS
    pair = 2 * head
    me = me_ref[0]
    loads = [
        pltpu.make_async_copy(source, target, sems.at[i])
        for i, (source, target) in enumerate(
            (
                (recv_hbm, recv_ref),
                (qkv_hbm, qkv_ref),
                (trans_hbm, trans_ref),
                (normed_hbm, normed_ref),
                (w_hbm, w_ref),
                (xhat_hbm, xhat_ref),
                (attn_hbm, attn_ref),
            )
        )
    ]
    saves = [
        pltpu.make_async_copy(source, target, sems.at[7 + i])
        for i, (source, target) in enumerate(
            [*zip(sums, outs), (serial_grad, serial_grad_hbm), (d_normed_ref, d_normed_hbm)]
        )
    ]

    for load in loads:
        load.start()
    place = hot(iota((rows, n_seq * capacity), 0) == pos_ref[...])
    loads[0].wait()
    values = jnp.concatenate(
        [recv_ref[by_receiver(me, d, capacity), :] for d in range(n_seq)], axis=0
    )
    grads = mm(place, values).astype(BF16)
    serial_grad[...] = grads
    saves[4].start()
    d_att = mm(grads, w_proj_ref[...], NT).astype(BF16)
    d_attn[...] = d_att
    d_attn_t[...] = jnp.transpose(d_att.astype(F32)).astype(BF16)
    loads[1].wait()
    loads[2].wait()

    zero = jnp.zeros((head, rows), BF16)
    first = iota((rows, pair), 1) < head

    def alone(both, j):
        part = both[j * head : (j + 1) * head]
        return jnp.concatenate([part, zero] if j == 0 else [zero, part], axis=0)

    for step in range(HEADS // 2):
        lo = step * pair
        queries = qkv_ref[:, pl.ds(lo, pair)]
        values = qkv_ref[:, pl.ds(2 * width + lo, pair)]
        d_att_t = d_attn_t[pl.ds(lo, pair), :] * BF16(0.125)
        d_att = d_attn[:, pl.ds(lo, pair)]
        keys = qkv_ref[:, pl.ds(width + lo, pair)]
        query_t = trans_ref[pl.ds(lo, pair), :] * BF16(0.125)
        d_q, d_k, d_v = [], [], []
        for j in range(2):
            top = stats_ref[pl.ds(2 * step + j, 1), :]
            share = stats_ref[pl.ds(HEADS + 2 * step + j, 1), :]
            probs = jnp.exp(mm(keys, alone(query_t, j)) - top) * share
            d_probs = mm(values, alone(d_att_t, j))
            total = jnp.sum(d_probs * probs, axis=0, keepdims=True)
            d_scores = (probs * (d_probs - total)).astype(BF16)
            k_t = trans_ref[pl.ds(width + lo + j * head, head), :]
            d_q.append(mm(k_t, d_scores))
            d_k.append(mm(d_scores, queries))
            d_v.append(mm(probs.astype(BF16), d_att))
        d_qkv[:, pl.ds(lo, pair)] = jnp.transpose(jnp.concatenate(d_q, axis=0)).astype(BF16)
        d_qkv[:, pl.ds(width + lo, pair)] = jnp.where(
            first, d_k[0], d_k[1]
        ).astype(BF16)
        d_qkv[:, pl.ds(2 * width + lo, pair)] = jnp.where(
            first, d_v[0], d_v[1]
        ).astype(BF16)

    for load in loads[3:]:
        load.wait()
    normed_t[...] = jnp.transpose(normed_ref[...].astype(F32)).astype(BF16)
    d_normed = mm(d_qkv[...], w_ref[...], NT)
    d_normed_ref[...] = d_normed
    saves[5].start()
    gain_row = jnp.sum(d_normed * xhat_ref[...], axis=0, keepdims=True)
    gain_column[...] = jnp.transpose(jnp.broadcast_to(gain_row, (LANES, width)))
    eighth = width // 8
    odd = lax.bitwise_and(me, 1)

    def sides(even_bit, odd_bit):
        even_side = lax.bitwise_and(lax.shift_right_logical(me, even_bit), 1)
        odd_side = lax.bitwise_and(lax.shift_right_logical(me, odd_bit), 1)
        mine = jnp.where(odd == 1, odd_side, even_side)
        return mine, even_side + odd_side - mine

    (mine, other), (mine_next, other_next) = (sides(*bits) for bits in chip_bits)
    starts = (
        ((1 - odd) * 2 + 1 - other, other_next),
        ((1 - odd) * 2 + other, other_next),
        (odd * 2 + 1 - mine, mine_next),
        (odd * 2 + mine, mine_next),
    )
    for out, (start, side), save in zip(sums, starts, saves):
        for j, half in enumerate((1 - side, side)):
            part = pl.ds(pl.multiple_of((start * 2 + half) * eighth, eighth), eighth)
            lines = slice(j * eighth, (j + 1) * eighth)
            out[lines, : 3 * width] = mm(normed_t[part, :], d_qkv[...])
            out[lines, 3 * width : 4 * width] = mm(attn_ref[part, :], serial_grad[...])
            out[lines, 4 * width :] = gain_column[part, :]
        save.start()
    for save in saves:
        save.wait()


def residual_kernel(
    n_seq, me_ref, pos_ref, gain_ref, inv_ref, xhat_ref, serial_grad_ref, d_normed_ref, back_out
):
    xhat = xhat_ref[...]
    rows = xhat.shape[0]
    capacity = pos_ref.shape[1] // n_seq
    scaled = d_normed_ref[...] * gain_ref[...]
    residual = inv_ref[:, 0:1] * (
        scaled
        - jnp.mean(scaled, axis=1, keepdims=True)
        - xhat * jnp.mean(scaled * xhat, axis=1, keepdims=True)
    )
    serial_dx = (serial_grad_ref[...].astype(F32) + residual).astype(BF16)
    returned = mm(column_hot(pos_ref[...], rows), serial_dx).astype(BF16)
    for d in range(n_seq):
        back_out[by_receiver(me_ref[0], d, capacity), :] = returned[d * capacity : (d + 1) * capacity]


def unpack_kernel(n_seq, me_ref, slot_ref, recv_ref, out_ref):
    capacity = recv_ref.shape[0] // n_seq
    values = jnp.concatenate(
        [recv_ref[by_receiver(me_ref[0], d, capacity), :] for d in range(n_seq)], axis=0
    )
    out_ref[...] = mm(column_hot(slot_ref[...], values.shape[0]), values).astype(BF16)


def split_kernel(side_ref, sums_ref, *refs):
    qkv_out, proj_out, gain_out = refs[-3:]
    width = proj_out.shape[1]
    qkv_out[...] = sums_ref[:, : 3 * width].astype(F32)
    proj_out[...] = sums_ref[:, 3 * width : 4 * width].astype(F32)
    gain_out[...] = jnp.transpose(sums_ref[:, 4 * width :].astype(F32))[0:1]


def exponent_of(largest):
    return jnp.clip(jnp.ceil(jnp.log(jnp.maximum(largest, 1e-30)) * 1.4426950408889634), -100.0, 120.0)


def encode(out_ref, total):
    width = total.shape[1] - LANES
    body, gain = total[:, :width], total[:, width : width + 1]
    exponent = exponent_of(jnp.max(jnp.abs(body), axis=1, keepdims=True))
    codes = jnp.round(body * (jnp.exp2(-exponent) * CODE_MAX))
    out_ref[:, :width] = codes.astype(jnp.int32).astype(jnp.int16)
    gain_exponent = exponent_of(jnp.abs(gain))
    scaled = gain * (jnp.exp2(-gain_exponent) * CODE_MAX)
    high = jnp.round(scaled)
    low = jnp.round((scaled - high) * DIGIT)
    lane = iota((total.shape[0], LANES), 1)
    tail = jnp.where(lane == 0, high, jnp.where(lane == 1, low, jnp.where(lane == 2, gain_exponent, exponent)))
    out_ref[:, width:] = tail.astype(jnp.int32).astype(jnp.int16)


def decode(codes):
    values = codes.astype(jnp.int32).astype(F32)
    width = values.shape[1] - LANES
    tail = values[:, width:]
    body = values[:, :width] * (jnp.exp2(tail[:, 3:4]) * (1.0 / CODE_MAX))
    gain = (tail[:, 0:1] + tail[:, 1:2] * (1.0 / DIGIT)) * (jnp.exp2(tail[:, 2:3]) * (1.0 / CODE_MAX))
    return jnp.concatenate([body, jnp.broadcast_to(gain, tail.shape)], axis=1)


def total_of(terms, part):
    half = terms[0].shape[0] // 2
    rows = {"all": slice(None), "first": slice(0, half), "second": slice(half, 2 * half)}[part]
    values = [ref[rows, :] for ref in terms]
    return functools.reduce(jnp.add, [decode(v) if v.dtype == jnp.int16 else v for v in values])


def message_kernel(part, *refs):
    encode(refs[-1], total_of(refs[:-1], part))


def sum_kernel(parts, *refs):
    refs[-1][...] = functools.reduce(jnp.add, [total_of([ref], p) for ref, p in zip(refs, parts)])


def pieces_kernel(parts, n_dp, plane_ref, *refs):
    terms, own, messages, total = refs[: len(parts)], refs[len(parts)], refs[len(parts) + 1 : -1], refs[-1]
    total[...] = functools.reduce(jnp.add, [total_of([ref], p) for ref, p in zip(terms, parts)])
    size = own.shape[0]

    def rows_of(distance):
        start = lax.bitwise_xor(plane_ref[0], distance) * size
        return total[pl.ds(pl.multiple_of(start, size), size), :]

    for k in range(1, n_dp):
        encode(messages[k - 1], rows_of(k))
    own[...] = rows_of(0)


def finish_kernel(*refs):
    refs[-1][...] = total_of(refs[:-1], "all").astype(BF16)


def whole(shape):
    return pl.BlockSpec(shape, lambda *_: (0,) * len(shape), pipeline_mode=pl.Buffered(1))


def params(mib):
    return pltpu.CompilerParams(vmem_limit_bytes=mib * MIB)


def shape_of(shape, dtype):
    return jax.ShapeDtypeStruct(shape, dtype)


def by_distance(blocks, axis):
    count = len(blocks)
    return [blocks[0]] + [
        lax.ppermute(blocks[k], axis, [(i, i ^ k) for i in range(count)]) for k in range(1, count)
    ]


def chip_orders(n_seq):
    bits = list(range(1, n_seq.bit_length() - 1))
    middle = len(bits) // 2
    return bits, bits[middle:] + bits[:middle]


def chip_steps():
    n_seq, me = lax.axis_size("seq"), lax.axis_index("seq")
    odd = lax.bitwise_and(me, 1) == 1

    def side(bit):
        return lax.bitwise_and(lax.shift_right_logical(me, jnp.asarray(bit, me.dtype)), 1)

    steps = []
    for even_bit, odd_bit in zip(*chip_orders(n_seq)):
        pairs = [(i, i ^ (1 << (odd_bit if i & 1 else even_bit))) for i in range(n_seq)]
        steps.append((pairs, jnp.where(odd, side(odd_bit), side(even_bit))))
    return steps


def piece(terms, index, count):
    size = terms[0].shape[0] // count
    return functools.reduce(jnp.add, [lax.dynamic_slice_in_dim(t, index * size, size) for t in terms])


def core_pairs():
    return [(i, i ^ 1) for i in range(lax.axis_size("seq"))]


def small_kernel(kernel, outs, operands, scalars=0, scratch=(), name="sum"):
    in_smem = pl.BlockSpec(memory_space=pltpu.SMEM)
    in_vmem = pl.BlockSpec(memory_space=pltpu.VMEM)
    touched = sum(x.size * x.dtype.itemsize for x in (*operands, *outs))
    return pl.pallas_call(
        kernel,
        out_shape=outs,
        in_specs=[in_smem] * scalars + [in_vmem] * (len(operands) - scalars),
        out_specs=[in_vmem] * len(outs),
        scratch_shapes=list(scratch),
        compiler_params=params(16),
        cost_estimate=pl.CostEstimate(flops=2 * touched, bytes_accessed=touched, transcendentals=0),
        name=name,
    )(*operands)


def message(terms, part, name):
    rows, width = terms[0].shape
    rows = rows if part == "all" else rows // 2
    return small_kernel(
        functools.partial(message_kernel, part), [shape_of((rows, width), jnp.int16)], terms, name=name
    )[0]


def first_step(quarters, steps):
    pass_on, pass_keep, own_on, own_keep = quarters
    got_on = lax.ppermute(pass_on, "seq", core_pairs())
    got_keep = lax.ppermute(pass_keep, "seq", core_pairs())
    sent = message([own_on, got_on], "all", "code_first")
    return [own_keep, got_keep, lax.ppermute(sent, "seq", steps[0][0])]


def second_step(terms, steps):
    sent = message(terms, "first", "code_second")
    return terms, lax.ppermute(sent, "seq", steps[1][0])


def halves_of_plain(part, steps):
    for pairs, side in steps:
        got = lax.ppermute(piece([part], 1 - side, 2), "seq", pairs)
        part = piece([part], side, 2) + got
    return part


def reduce_over_planes(terms, got, steps):
    n_dp, plane = lax.axis_size("dp"), lax.axis_index("dp")
    rows, width = got.shape
    parts = ["second"] * len(terms) + ["all"]
    if len(steps) > 2 or rows // n_dp % 16:
        part = small_kernel(
            functools.partial(sum_kernel, parts), [shape_of((rows, width), F32)], [*terms, got]
        )[0]
        part = halves_of_plain(part, steps[2:])
        pieces = [piece([part], lax.bitwise_xor(plane, k), n_dp) for k in range(n_dp)]
        return functools.reduce(jnp.add, by_distance(pieces, "dp")).astype(BF16)
    size = rows // n_dp
    own, *sent = small_kernel(
        functools.partial(pieces_kernel, parts, n_dp),
        [shape_of((size, width), F32)] + [shape_of((size, width), jnp.int16)] * (n_dp - 1),
        [jnp.reshape(plane.astype(jnp.int32), (1,)), *terms, got],
        scalars=1,
        scratch=[pltpu.VMEM((rows, width), F32)],
        name="code_planes",
    )
    arrived = by_distance([own] + sent, "dp")
    return small_kernel(finish_kernel, [shape_of((size, width), BF16)], arrived, name="finish")[0]


def share_over_planes(part):
    n_dp, plane = lax.axis_size("dp"), lax.axis_index("dp")
    shares = jnp.stack(by_distance([part] * n_dp, "dp"))
    return jnp.concatenate(
        [lax.dynamic_index_in_dim(shares, lax.bitwise_xor(plane, p), keepdims=False) for p in range(n_dp)],
        axis=0,
    )


def share_in_plane(part, steps):
    for pairs, side in reversed(steps):
        other = lax.ppermute(part, "seq", pairs)
        part = jnp.where(
            side == 0, jnp.concatenate([part, other], axis=0), jnp.concatenate([other, part], axis=0)
        )
    return part


def write_half(side, sums, outs=()):
    half, width = sums.shape[0], (sums.shape[1] - LANES) // 4
    return pl.pallas_call(
        split_kernel,
        grid_spec=pltpu.PrefetchScalarGridSpec(
            num_scalar_prefetch=1,
            grid=(2,),
            in_specs=[pl.BlockSpec((half // 2, sums.shape[1]), lambda i, s: (i, 0))]
            + [pl.BlockSpec(memory_space=pl.ANY)] * len(outs),
            out_specs=[
                pl.BlockSpec((half // 2, 3 * width), lambda i, s: (2 * s[0] + i, 0)),
                pl.BlockSpec((half // 2, width), lambda i, s: (2 * s[0] + i, 0)),
                pl.BlockSpec((1, half // 2), lambda i, s: (0, 2 * s[0] + i)),
            ],
        ),
        out_shape=(
            shape_of((2 * half, 3 * width), F32),
            shape_of((2 * half, width), F32),
            shape_of((1, 2 * half), F32),
        ),
        input_output_aliases={2 + i: i for i in range(len(outs))},
        compiler_params=params(20),
        cost_estimate=pl.CostEstimate(flops=0, bytes_accessed=4 * MIB, transcendentals=0),
        name="split",
    )(side, sums, *outs)


def per_device(points, cotangent, dest, w_qkv, w_proj, gain):
    feats = points[0]
    grads = cotangent[0]
    rows, width = feats.shape
    n_seq = lax.axis_size("seq")
    capacity = 2 * (rows // n_seq)
    slots = n_seq * capacity
    block = capacity + EXTRA
    pairs = HEADS // 2
    pair = width // pairs
    sum_shape = (width // 4, 4 * width + LANES)
    me = jnp.reshape(lax.axis_index("seq").astype(jnp.int32), (1,))
    gain_row = gain.reshape(1, width)
    in_smem = pl.BlockSpec(memory_space=pltpu.SMEM)
    in_vmem = pl.BlockSpec(memory_space=pltpu.VMEM)
    in_hbm = pl.BlockSpec(memory_space=pl.ANY)
    stay_hbm = pl.BlockSpec(memory_space=pltpu.HBM)

    slot, *feats_sent = pl.pallas_call(
        functools.partial(pack_kernel, n_seq, capacity),
        out_shape=[shape_of((1, rows), jnp.int32)] + [shape_of((block, width), BF16)] * n_seq,
        in_specs=[in_smem] + [stay_hbm] * 2,
        out_specs=[in_vmem] * (1 + n_seq),
        scratch_shapes=[
            pltpu.VMEM((1, rows), jnp.int32),
            pltpu.VMEM((rows, width), BF16),
            pltpu.SemaphoreType.DMA((2,)),
        ],
        compiler_params=params(60),
        cost_estimate=pl.CostEstimate(
            flops=2 * slots * rows * width, bytes_accessed=2 * MIB, transcendentals=0
        ),
        name="pack",
    )(me, dest, feats)
    feats_got = by_distance(feats_sent, "seq")
    feats_got[1], slot = lax.optimization_barrier((feats_got[1], slot))
    grads_sent = pl.pallas_call(
        functools.partial(pack_grads_kernel, n_seq, capacity),
        out_shape=shape_of((slots, width), BF16),
        in_specs=[in_smem] + [in_vmem] * 2,
        out_specs=in_vmem,
        compiler_params=params(20),
        cost_estimate=pl.CostEstimate(
            flops=2 * slots * rows * width, bytes_accessed=2 * MIB, transcendentals=0
        ),
        name="pack_grads",
    )(me, slot, grads)

    def exchange(sent):
        sent = sent.reshape(n_seq, capacity, width)
        got = lax.all_to_all(sent, "seq", split_axis=0, concat_axis=0, tiled=True)
        return got.reshape(slots, width)

    feats_got, grads_sent = lax.optimization_barrier((feats_got, grads_sent))
    grads_got = exchange(grads_sent)

    pos, xhat, inv, normed, qkv, trans, attn_t, stats = pl.pallas_call(
        functools.partial(forward_kernel, n_seq, capacity),
        grid=(1,),
        out_shape=(
            shape_of((1, slots), jnp.int32),
            shape_of((rows, width), F32),
            shape_of((rows, LANES), F32),
            shape_of((rows, width), BF16),
            shape_of((rows, 3 * width), BF16),
            shape_of((2 * width, rows), BF16),
            shape_of((width, rows), BF16),
            shape_of((2 * HEADS, rows), F32),
        ),
        in_specs=[in_hbm, whole((1, width))] + [whole((block, width))] * n_seq,
        out_specs=[whole((1, slots))]
        + [in_hbm] * 5
        + [whole((width, rows)), whole((2 * HEADS, rows))],
        scratch_shapes=[
            pltpu.VMEM((width, 3 * width), BF16),
            pltpu.VMEM((rows, width), F32),
            pltpu.VMEM((rows, LANES), F32),
            pltpu.VMEM((rows, width), BF16),
            pltpu.VMEM((rows, 3 * width), BF16),
            pltpu.VMEM((3 * width, rows), BF16),
            pltpu.SemaphoreType.DMA((6,)),
        ],
        compiler_params=params(60),
        cost_estimate=pl.CostEstimate(
            flops=6 * rows * width * width + 8 * HEADS * rows * rows * pair,
            bytes_accessed=16 * MIB,
            transcendentals=HEADS * rows * rows,
        ),
        name="forward",
    )(w_qkv, gain_row, *feats_got)

    chip_bits = tuple(zip(*chip_orders(n_seq)))[:2]
    *quarters, serial_grad, d_normed = pl.pallas_call(
        functools.partial(backward_kernel, n_seq, chip_bits),
        grid=(1,),
        out_shape=[shape_of(sum_shape, F32)] * 4
        + [shape_of((rows, width), BF16), shape_of((rows, width), F32)],
        in_specs=[
            in_smem,
            whole((1, slots)),
            whole((width, width)),
            whole((2 * HEADS, rows)),
        ]
        + [in_hbm] * 7,
        out_specs=[in_hbm] * 6,
        scratch_shapes=[
            pltpu.VMEM((slots, width), BF16),
            pltpu.VMEM((rows, 3 * width), BF16),
            pltpu.VMEM((2 * width, rows), BF16),
            pltpu.VMEM((width, 3 * width), BF16),
            pltpu.VMEM((rows, width), F32),
            pltpu.VMEM((rows, width), BF16),
            pltpu.VMEM((width, rows), BF16),
        ]
        + [pltpu.VMEM(sum_shape, F32)] * 4
        + [
            pltpu.VMEM((rows, width), BF16),
            pltpu.VMEM((rows, width), F32),
            pltpu.VMEM((rows, width), BF16),
            pltpu.VMEM((width, rows), BF16),
            pltpu.VMEM((rows, 3 * width), BF16),
            pltpu.VMEM((width, rows), BF16),
            pltpu.VMEM((width, LANES), F32),
            pltpu.SemaphoreType.DMA((13,)),
        ],
        compiler_params=params(60),
        cost_estimate=pl.CostEstimate(
            flops=12 * rows * width * width + 10 * HEADS * rows * rows * pair,
            bytes_accessed=16 * MIB,
            transcendentals=HEADS * rows * rows,
        ),
        name="backward",
    )(me, pos, w_proj, stats, grads_got, qkv, trans, w_qkv, xhat, normed, attn_t)

    steps = chip_steps()
    terms = first_step(quarters, steps)
    back = pl.pallas_call(
        functools.partial(residual_kernel, n_seq),
        out_shape=shape_of((slots, width), BF16),
        in_specs=[in_smem] + [in_vmem] * 6,
        out_specs=in_vmem,
        compiler_params=params(20),
        cost_estimate=pl.CostEstimate(
            flops=2 * slots * rows * width, bytes_accessed=4 * MIB, transcendentals=0
        ),
        name="residual",
    )(me, pos, gain_row, inv, xhat, serial_grad, d_normed)
    terms, got = second_step(terms, steps)
    got, back = lax.optimization_barrier((got, back))
    returned = exchange(back)
    part, returned = lax.optimization_barrier((reduce_over_planes(terms, got, steps), returned))
    own = share_in_plane(share_over_planes(part), steps)
    grad_local = pl.pallas_call(
        functools.partial(unpack_kernel, n_seq),
        out_shape=shape_of((rows, width), BF16),
        in_specs=[in_smem] + [in_vmem] * 2,
        out_specs=in_vmem,
        compiler_params=params(20),
        cost_estimate=pl.CostEstimate(
            flops=2 * slots * rows * width, bytes_accessed=2 * MIB, transcendentals=0
        ),
        name="unpack",
    )(me, slot, returned)
    own, grad_local = lax.optimization_barrier((own, grad_local))
    other = lax.ppermute(own, "seq", core_pairs())
    side = lax.bitwise_and(me, 1)
    outs = write_half(side, own)
    grad_qkv, grad_proj, gain_grad = write_half(1 - side, other, outs)
    return (grad_local[None], grad_qkv, grad_proj, gain_grad[0])


def solution(mesh):
    return jax.shard_map(
        per_device,
        mesh=mesh,
        in_specs=(P("dp", "seq", None), P("dp", "seq", None), P("dp", "seq"), P(), P(), P()),
        out_specs=(P("dp", "seq", None), P(), P(), P()),
        check_vma=False,
    )
```

```python
import functools

import jax
import jax.numpy as jnp
from jax import lax
from jax.experimental import pallas as pl
from jax.experimental.pallas import tpu as pltpu
from jax.sharding import PartitionSpec as P

HEADS = 8
PATCH = 512
EXTRA = 16
LANES = 128
CODE_MAX = 32000.0
DIGIT = 60000.0
MIB = 1024 * 1024
F32 = jnp.float32
BF16 = jnp.bfloat16
NN = (((1,), (0,)), ((), ()))
NT = (((1,), (1,)), ((), ()))


def mm(lhs, rhs, dims=NN):
    return lax.dot_general(lhs, rhs, dims, preferred_element_type=F32)


def iota(shape, dim):
    return lax.broadcasted_iota(jnp.int32, shape, dim)


def hot(mask):
    return jnp.where(mask, jnp.float32(1), jnp.float32(0)).astype(BF16)


def column_hot(row, count):
    size = row.shape[1]
    column = jnp.transpose(jnp.broadcast_to(row, (LANES, size)))
    lane = iota((size, LANES), 1)
    return jnp.concatenate([hot(column == lane + j * LANES) for j in range(count // LANES)], axis=1)


def by_receiver(me, distance, capacity):
    return pl.ds(pl.multiple_of(lax.bitwise_xor(me, distance) * capacity, capacity), capacity)


def pack_kernel(n_seq, capacity, me_ref, dest_hbm, feats_hbm, slot_out, *refs):
    outs, (dest_ref, feats_ref, sems) = refs[:n_seq], refs[n_seq:]
    rows, width = feats_ref.shape
    slots = n_seq * capacity
    loads = [
        pltpu.make_async_copy(source, target, sems.at[i])
        for i, (source, target) in enumerate(((dest_hbm, dest_ref), (feats_hbm, feats_ref)))
    ]
    for load in loads:
        load.start()
    loads[0].wait()
    shift = rows.bit_length() - 1
    places = dest_ref[...]
    distance = lax.bitwise_xor(lax.shift_right_logical(places, shift), me_ref[0])
    within = lax.bitwise_and(places, rows - 1) + 1
    member = iota((n_seq, rows), 0) == distance
    upper = hot(iota((rows, rows), 0) <= iota((rows, rows), 1))
    counts = mm(hot(member), upper)
    rank = jnp.sum(jnp.where(member, counts, 0.0), axis=0, keepdims=True).astype(jnp.int32) - 1
    slot = distance * capacity + rank
    slot_out[...] = slot
    select = hot(iota((slots, rows), 0) == slot)
    loads[1].wait()
    feats = mm(select, feats_ref[...]).astype(BF16)
    upper_half = slot >= width
    high = lax.shift_right_logical(within, 8).astype(F32)
    low = lax.bitwise_and(within, 255).astype(F32)
    line = iota((n_seq * EXTRA, rows), 0)
    kind = lax.bitwise_and(line, EXTRA - 1)
    digit = jnp.where(kind < 2, high, low)
    wanted = (
        (lax.shift_right_logical(line, EXTRA.bit_length() - 1) == distance)
        & (kind < 4)
        & ((lax.bitwise_and(kind, 1) == 1) == upper_half)
    )
    digits = jnp.where(wanted, digit, 0.0).astype(BF16)
    spread = hot(iota((width, rows), 0) == lax.bitwise_and(slot, width - 1))
    position = mm(digits, spread, NT).astype(BF16)
    for d in range(n_seq):
        outs[d][:capacity, :] = feats[d * capacity : (d + 1) * capacity]
        outs[d][capacity:, :] = position[d * EXTRA : (d + 1) * EXTRA]


def pack_grads_kernel(n_seq, capacity, me_ref, slot_ref, grads_ref, grads_out):
    select = hot(iota((n_seq * capacity, grads_ref.shape[0]), 0) == slot_ref[...])
    grads = mm(select, grads_ref[...]).astype(BF16)
    for d in range(n_seq):
        grads_out[by_receiver(me_ref[0], d, capacity), :] = grads[d * capacity : (d + 1) * capacity]


def forward_kernel(n_seq, capacity, w_hbm, gain_ref, *refs):
    recv, refs = refs[:n_seq], refs[n_seq:]
    pos_out, xhat_hbm, inv_hbm, normed_hbm, qkv_hbm, trans_hbm, attn_out, stats_out = refs[:8]
    w_ref, xhat_ref, inv_ref, normed_ref, qkv_ref, trans, sems = refs[8:]
    width = w_ref.shape[0]
    rows = xhat_ref.shape[0]
    head = width // HEADS
    pair = 2 * head
    w_copy = pltpu.make_async_copy(w_hbm, w_ref, sems.at[0])
    saves = [
        pltpu.make_async_copy(source, target, sems.at[1 + i])
        for i, (source, target) in enumerate(
            (
                (xhat_ref, xhat_hbm),
                (inv_ref, inv_hbm),
                (normed_ref, normed_hbm),
                (qkv_ref, qkv_hbm),
                (trans.at[pl.ds(0, 2 * width)], trans_hbm),
            )
        )
    ]

    w_copy.start()
    tile = recv[0][capacity:, :].astype(F32)
    for s in range(1, n_seq):
        tile = tile + recv[s][capacity:, :].astype(F32)
    high = jnp.concatenate([tile[0:1], tile[1:2]], axis=1)
    low = jnp.concatenate([tile[2:3], tile[3:4]], axis=1)
    pos = (high * 256.0 + low).astype(jnp.int32) - 1
    pos_out[...] = pos
    place = hot(iota((rows, n_seq * capacity), 0) == pos)
    values = jnp.concatenate([recv[s][:capacity, :] for s in range(n_seq)], axis=0)
    feats = mm(place, values)
    centered = feats - jnp.mean(feats, axis=1, keepdims=True)
    inv = lax.rsqrt(jnp.mean(centered * centered, axis=1, keepdims=True) + 1e-05)
    xhat = centered * inv
    xhat_ref[...] = xhat
    inv_ref[...] = jnp.broadcast_to(inv, inv_ref.shape)
    scaled = xhat * gain_ref[...]
    normed = scaled.astype(BF16)
    normed_ref[...] = jnp.transpose(scaled).astype(BF16)
    w_copy.wait()
    qkv = mm(normed, w_ref[...])
    qkv_ref[...] = qkv.astype(BF16)
    trans[...] = jnp.transpose(qkv).astype(BF16)
    for save in saves:
        save.start()

    for step in range(HEADS // 2):
        lo = step * pair
        keys = qkv_ref[:, pl.ds(width + lo, pair)]
        query_t = trans[pl.ds(lo, pair), :] * BF16(0.125)
        zero = jnp.zeros((head, rows), BF16)
        for j in range(2):
            part = query_t[j * head : (j + 1) * head]
            part = jnp.concatenate([part, zero] if j == 0 else [zero, part], axis=0)
            scores = mm(keys, part)
            top = jnp.max(scores, axis=0, keepdims=True)
            expo = jnp.exp(scores - top)
            share = 1.0 / jnp.sum(expo, axis=0, keepdims=True)
            probs = expo * share
            stats_out[pl.ds(2 * step + j, 1), :] = top
            stats_out[pl.ds(HEADS + 2 * step + j, 1), :] = share
            values_t = trans[pl.ds(2 * width + lo + j * head, head), :]
            attn_out[pl.ds(lo + j * head, head), :] = mm(values_t, probs.astype(BF16)).astype(BF16)

    for save in saves:
        save.wait()


def backward_kernel(n_seq, chip_bits, me_ref, pos_ref, w_proj_ref, stats_ref, *refs):
    (recv_hbm, qkv_hbm, trans_hbm, w_hbm, xhat_hbm, normed_hbm, attn_hbm), refs = refs[:7], refs[7:]
    outs, serial_grad_hbm, d_normed_hbm, refs = refs[:4], refs[4], refs[5], refs[6:]
    recv_ref, qkv_ref, trans_ref, w_ref, xhat_ref, normed_ref, attn_ref, refs = *refs[:7], refs[7:]
    sums, refs = refs[:4], refs[4:]
    serial_grad, d_normed_ref, d_attn, d_attn_t, d_qkv, gain_column, sems = refs
    width = w_proj_ref.shape[0]
    rows = xhat_ref.shape[0]
    capacity = recv_ref.shape[0] // n_seq
    head = width // HEADS
    pair = 2 * head
    me = me_ref[0]
    loads = [
        pltpu.make_async_copy(source, target, sems.at[i])
        for i, (source, target) in enumerate(
            (
                (recv_hbm, recv_ref),
                (qkv_hbm, qkv_ref),
                (trans_hbm, trans_ref),
                (normed_hbm, normed_ref),
                (w_hbm, w_ref),
                (xhat_hbm, xhat_ref),
                (attn_hbm, attn_ref),
            )
        )
    ]
    saves = [
        pltpu.make_async_copy(source, target, sems.at[7 + i])
        for i, (source, target) in enumerate(
            [*zip(sums, outs), (serial_grad, serial_grad_hbm), (d_normed_ref, d_normed_hbm)]
        )
    ]

    for load in loads:
        load.start()
    place = hot(iota((rows, n_seq * capacity), 0) == pos_ref[...])
    loads[0].wait()
    values = jnp.concatenate(
        [recv_ref[by_receiver(me, d, capacity), :] for d in range(n_seq)], axis=0
    )
    grads = mm(place, values).astype(BF16)
    serial_grad[...] = grads
    saves[4].start()
    d_attn[...] = mm(grads, w_proj_ref[...], NT).astype(BF16)
    d_attn_t[...] = mm(w_proj_ref[...], grads, NT).astype(BF16)
    loads[1].wait()
    loads[2].wait()

    zero = jnp.zeros((head, rows), BF16)
    first = iota((rows, pair), 1) < head

    def alone(both, j):
        part = both[j * head : (j + 1) * head]
        return jnp.concatenate([part, zero] if j == 0 else [zero, part], axis=0)

    for step in range(HEADS // 2):
        lo = step * pair
        queries = qkv_ref[:, pl.ds(lo, pair)]
        values = qkv_ref[:, pl.ds(2 * width + lo, pair)]
        d_att_t = d_attn_t[pl.ds(lo, pair), :] * BF16(0.125)
        d_att = d_attn[:, pl.ds(lo, pair)]
        keys = qkv_ref[:, pl.ds(width + lo, pair)]
        query_t = trans_ref[pl.ds(lo, pair), :] * BF16(0.125)
        d_q, d_k, d_v = [], [], []
        for j in range(2):
            top = stats_ref[pl.ds(2 * step + j, 1), :]
            share = stats_ref[pl.ds(HEADS + 2 * step + j, 1), :]
            probs = jnp.exp(mm(keys, alone(query_t, j)) - top) * share
            d_probs = mm(values, alone(d_att_t, j))
            total = jnp.sum(d_probs * probs, axis=0, keepdims=True)
            d_scores = (probs * (d_probs - total)).astype(BF16)
            k_t = trans_ref[pl.ds(width + lo + j * head, head), :]
            d_q.append(mm(k_t, d_scores))
            d_k.append(mm(d_scores, queries))
            d_v.append(mm(probs.astype(BF16), d_att))
        d_qkv[:, pl.ds(lo, pair)] = jnp.transpose(jnp.concatenate(d_q, axis=0)).astype(BF16)
        d_qkv[:, pl.ds(width + lo, pair)] = jnp.where(
            first, d_k[0], d_k[1]
        ).astype(BF16)
        d_qkv[:, pl.ds(2 * width + lo, pair)] = jnp.where(
            first, d_v[0], d_v[1]
        ).astype(BF16)

    for load in loads[3:]:
        load.wait()
    d_normed = mm(d_qkv[...], w_ref[...], NT)
    d_normed_ref[...] = d_normed
    saves[5].start()
    gain_row = jnp.sum(d_normed * xhat_ref[...], axis=0, keepdims=True)
    gain_column[...] = jnp.transpose(jnp.broadcast_to(gain_row, (LANES, width)))
    eighth = width // 8
    odd = lax.bitwise_and(me, 1)

    def sides(even_bit, odd_bit):
        even_side = lax.bitwise_and(lax.shift_right_logical(me, even_bit), 1)
        odd_side = lax.bitwise_and(lax.shift_right_logical(me, odd_bit), 1)
        mine = jnp.where(odd == 1, odd_side, even_side)
        return mine, even_side + odd_side - mine

    (mine, other), (mine_next, other_next) = (sides(*bits) for bits in chip_bits)
    starts = (
        ((1 - odd) * 2 + 1 - other, other_next),
        ((1 - odd) * 2 + other, other_next),
        (odd * 2 + 1 - mine, mine_next),
        (odd * 2 + mine, mine_next),
    )
    order = [
        pl.ds(pl.multiple_of((start * 2 + half) * eighth, eighth), eighth)
        for start, side in starts
        for half in (1 - side, side)
    ]
    for i in (0, 2):
        parts = order[2 * i : 2 * i + 4]
        of_qkv = mm(jnp.concatenate([normed_ref[part, :] for part in parts], axis=0), d_qkv[...])
        of_proj = mm(jnp.concatenate([attn_ref[part, :] for part in parts], axis=0), serial_grad[...])
        of_gain = jnp.concatenate([gain_column[part, :] for part in parts], axis=0)
        for j in range(2):
            lines = slice(2 * j * eighth, 2 * (j + 1) * eighth)
            sums[i + j][:, : 3 * width] = of_qkv[lines]
            sums[i + j][:, 3 * width : 4 * width] = of_proj[lines]
            sums[i + j][:, 4 * width :] = of_gain[lines]
            saves[i + j].start()
    for save in saves:
        save.wait()


def residual_kernel(
    n_seq, me_ref, pos_ref, gain_ref, inv_ref, xhat_ref, serial_grad_ref, d_normed_ref, back_out
):
    xhat = xhat_ref[...]
    rows = xhat.shape[0]
    capacity = pos_ref.shape[1] // n_seq
    scaled = d_normed_ref[...] * gain_ref[...]
    residual = inv_ref[:, 0:1] * (
        scaled
        - jnp.mean(scaled, axis=1, keepdims=True)
        - xhat * jnp.mean(scaled * xhat, axis=1, keepdims=True)
    )
    serial_dx = (serial_grad_ref[...].astype(F32) + residual).astype(BF16)
    returned = mm(column_hot(pos_ref[...], rows), serial_dx).astype(BF16)
    for d in range(n_seq):
        back_out[by_receiver(me_ref[0], d, capacity), :] = returned[d * capacity : (d + 1) * capacity]


def unpack_kernel(n_seq, me_ref, slot_ref, recv_ref, out_ref):
    capacity = recv_ref.shape[0] // n_seq
    values = jnp.concatenate(
        [recv_ref[by_receiver(me_ref[0], d, capacity), :] for d in range(n_seq)], axis=0
    )
    out_ref[...] = mm(column_hot(slot_ref[...], values.shape[0]), values).astype(BF16)


def split_kernel(side_ref, sums_ref, *refs):
    qkv_out, proj_out, gain_out = refs[-3:]
    width = proj_out.shape[1]
    qkv_out[...] = sums_ref[:, : 3 * width].astype(F32)
    proj_out[...] = sums_ref[:, 3 * width : 4 * width].astype(F32)
    gain_out[...] = jnp.transpose(sums_ref[:, 4 * width :].astype(F32))[0:1]


def exponent_of(largest):
    return jnp.clip(jnp.ceil(jnp.log(jnp.maximum(largest, 1e-30)) * 1.4426950408889634), -100.0, 120.0)


def encode(out_ref, total):
    width = total.shape[1] - LANES
    body, gain = total[:, :width], total[:, width : width + 1]
    exponent = exponent_of(jnp.max(jnp.abs(body), axis=1, keepdims=True))
    codes = jnp.round(body * (jnp.exp2(-exponent) * CODE_MAX))
    out_ref[:, :width] = codes.astype(jnp.int32).astype(jnp.int16)
    gain_exponent = exponent_of(jnp.abs(gain))
    scaled = gain * (jnp.exp2(-gain_exponent) * CODE_MAX)
    high = jnp.round(scaled)
    low = jnp.round((scaled - high) * DIGIT)
    lane = iota((total.shape[0], LANES), 1)
    tail = jnp.where(lane == 0, high, jnp.where(lane == 1, low, jnp.where(lane == 2, gain_exponent, exponent)))
    out_ref[:, width:] = tail.astype(jnp.int32).astype(jnp.int16)


def decode(codes):
    values = codes.astype(jnp.int32).astype(F32)
    width = values.shape[1] - LANES
    tail = values[:, width:]
    body = values[:, :width] * (jnp.exp2(tail[:, 3:4]) * (1.0 / CODE_MAX))
    gain = (tail[:, 0:1] + tail[:, 1:2] * (1.0 / DIGIT)) * (jnp.exp2(tail[:, 2:3]) * (1.0 / CODE_MAX))
    return jnp.concatenate([body, jnp.broadcast_to(gain, tail.shape)], axis=1)


def total_of(terms, part):
    half = terms[0].shape[0] // 2
    rows = {"all": slice(None), "first": slice(0, half), "second": slice(half, 2 * half)}[part]
    values = [ref[rows, :] for ref in terms]
    return functools.reduce(jnp.add, [decode(v) if v.dtype == jnp.int16 else v for v in values])


def message_kernel(part, *refs):
    encode(refs[-1], total_of(refs[:-1], part))


def sum_kernel(parts, *refs):
    refs[-1][...] = functools.reduce(jnp.add, [total_of([ref], p) for ref, p in zip(refs, parts)])


def pieces_kernel(parts, n_dp, plane_ref, *refs):
    terms, own, messages, total = refs[: len(parts)], refs[len(parts)], refs[len(parts) + 1 : -1], refs[-1]
    total[...] = functools.reduce(jnp.add, [total_of([ref], p) for ref, p in zip(terms, parts)])
    size = own.shape[0]

    def rows_of(distance):
        start = lax.bitwise_xor(plane_ref[0], distance) * size
        return total[pl.ds(pl.multiple_of(start, size), size), :]

    for k in range(1, n_dp):
        encode(messages[k - 1], rows_of(k))
    own[...] = rows_of(0)


def finish_kernel(*refs):
    refs[-1][...] = total_of(refs[:-1], "all").astype(BF16)


def whole(shape):
    return pl.BlockSpec(shape, lambda *_: (0,) * len(shape), pipeline_mode=pl.Buffered(1))


def params(mib):
    return pltpu.CompilerParams(vmem_limit_bytes=mib * MIB)


def shape_of(shape, dtype):
    return jax.ShapeDtypeStruct(shape, dtype)


def by_distance(blocks, axis):
    count = len(blocks)
    return [blocks[0]] + [
        lax.ppermute(blocks[k], axis, [(i, i ^ k) for i in range(count)]) for k in range(1, count)
    ]


def chip_orders(n_seq):
    bits = list(range(1, n_seq.bit_length() - 1))
    middle = len(bits) // 2
    return bits, bits[middle:] + bits[:middle]


def chip_steps():
    n_seq, me = lax.axis_size("seq"), lax.axis_index("seq")
    odd = lax.bitwise_and(me, 1) == 1

    def side(bit):
        return lax.bitwise_and(lax.shift_right_logical(me, jnp.asarray(bit, me.dtype)), 1)

    steps = []
    for even_bit, odd_bit in zip(*chip_orders(n_seq)):
        pairs = [(i, i ^ (1 << (odd_bit if i & 1 else even_bit))) for i in range(n_seq)]
        steps.append((pairs, jnp.where(odd, side(odd_bit), side(even_bit))))
    return steps


def piece(terms, index, count):
    size = terms[0].shape[0] // count
    return functools.reduce(jnp.add, [lax.dynamic_slice_in_dim(t, index * size, size) for t in terms])


def core_pairs():
    return [(i, i ^ 1) for i in range(lax.axis_size("seq"))]


def small_kernel(kernel, outs, operands, scalars=0, scratch=(), name="sum"):
    in_smem = pl.BlockSpec(memory_space=pltpu.SMEM)
    in_vmem = pl.BlockSpec(memory_space=pltpu.VMEM)
    touched = sum(x.size * x.dtype.itemsize for x in (*operands, *outs))
    return pl.pallas_call(
        kernel,
        out_shape=outs,
        in_specs=[in_smem] * scalars + [in_vmem] * (len(operands) - scalars),
        out_specs=[in_vmem] * len(outs),
        scratch_shapes=list(scratch),
        compiler_params=params(16),
        cost_estimate=pl.CostEstimate(flops=2 * touched, bytes_accessed=touched, transcendentals=0),
        name=name,
    )(*operands)


def message(terms, part, name):
    rows, width = terms[0].shape
    rows = rows if part == "all" else rows // 2
    return small_kernel(
        functools.partial(message_kernel, part), [shape_of((rows, width), jnp.int16)], terms, name=name
    )[0]


def first_step(quarters, steps):
    pass_on, pass_keep, own_on, own_keep = quarters
    got_on = lax.ppermute(pass_on, "seq", core_pairs())
    got_keep = lax.ppermute(pass_keep, "seq", core_pairs())
    sent = message([own_on, got_on], "all", "code_first")
    return [own_keep, got_keep, lax.ppermute(sent, "seq", steps[0][0])]


def second_step(terms, steps):
    sent = message(terms, "first", "code_second")
    return terms, lax.ppermute(sent, "seq", steps[1][0])


def halves_of_plain(part, steps):
    for pairs, side in steps:
        got = lax.ppermute(piece([part], 1 - side, 2), "seq", pairs)
        part = piece([part], side, 2) + got
    return part


def reduce_over_planes(terms, got, steps):
    n_dp, plane = lax.axis_size("dp"), lax.axis_index("dp")
    rows, width = got.shape
    parts = ["second"] * len(terms) + ["all"]
    if len(steps) > 2 or rows // n_dp % 16:
        part = small_kernel(
            functools.partial(sum_kernel, parts), [shape_of((rows, width), F32)], [*terms, got]
        )[0]
        part = halves_of_plain(part, steps[2:])
        pieces = [piece([part], lax.bitwise_xor(plane, k), n_dp) for k in range(n_dp)]
        return functools.reduce(jnp.add, by_distance(pieces, "dp")).astype(BF16)
    size = rows // n_dp
    own, *sent = small_kernel(
        functools.partial(pieces_kernel, parts, n_dp),
        [shape_of((size, width), F32)] + [shape_of((size, width), jnp.int16)] * (n_dp - 1),
        [jnp.reshape(plane.astype(jnp.int32), (1,)), *terms, got],
        scalars=1,
        scratch=[pltpu.VMEM((rows, width), F32)],
        name="code_planes",
    )
    arrived = by_distance([own] + sent, "dp")
    return small_kernel(finish_kernel, [shape_of((size, width), BF16)], arrived, name="finish")[0]


def share_over_planes(part):
    n_dp, plane = lax.axis_size("dp"), lax.axis_index("dp")
    shares = jnp.stack(by_distance([part] * n_dp, "dp"))
    return jnp.concatenate(
        [lax.dynamic_index_in_dim(shares, lax.bitwise_xor(plane, p), keepdims=False) for p in range(n_dp)],
        axis=0,
    )


def share_in_plane(part, steps):
    for pairs, side in reversed(steps):
        other = lax.ppermute(part, "seq", pairs)
        part = jnp.where(
            side == 0, jnp.concatenate([part, other], axis=0), jnp.concatenate([other, part], axis=0)
        )
    return part


def write_half(side, sums, outs=()):
    half, width = sums.shape[0], (sums.shape[1] - LANES) // 4
    return pl.pallas_call(
        split_kernel,
        grid_spec=pltpu.PrefetchScalarGridSpec(
            num_scalar_prefetch=1,
            grid=(2,),
            in_specs=[pl.BlockSpec((half // 2, sums.shape[1]), lambda i, s: (i, 0))]
            + [pl.BlockSpec(memory_space=pl.ANY)] * len(outs),
            out_specs=[
                pl.BlockSpec((half // 2, 3 * width), lambda i, s: (2 * s[0] + i, 0)),
                pl.BlockSpec((half // 2, width), lambda i, s: (2 * s[0] + i, 0)),
                pl.BlockSpec((1, half // 2), lambda i, s: (0, 2 * s[0] + i)),
            ],
        ),
        out_shape=(
            shape_of((2 * half, 3 * width), F32),
            shape_of((2 * half, width), F32),
            shape_of((1, 2 * half), F32),
        ),
        input_output_aliases={2 + i: i for i in range(len(outs))},
        compiler_params=params(20),
        cost_estimate=pl.CostEstimate(flops=0, bytes_accessed=4 * MIB, transcendentals=0),
        name="split",
    )(side, sums, *outs)


def per_device(points, cotangent, dest, w_qkv, w_proj, gain):
    feats = points[0]
    grads = cotangent[0]
    rows, width = feats.shape
    n_seq = lax.axis_size("seq")
    capacity = 2 * (rows // n_seq)
    slots = n_seq * capacity
    block = capacity + EXTRA
    pairs = HEADS // 2
    pair = width // pairs
    sum_shape = (width // 4, 4 * width + LANES)
    me = jnp.reshape(lax.axis_index("seq").astype(jnp.int32), (1,))
    gain_row = gain.reshape(1, width)
    in_smem = pl.BlockSpec(memory_space=pltpu.SMEM)
    in_vmem = pl.BlockSpec(memory_space=pltpu.VMEM)
    in_hbm = pl.BlockSpec(memory_space=pl.ANY)
    stay_hbm = pl.BlockSpec(memory_space=pltpu.HBM)

    slot, *feats_sent = pl.pallas_call(
        functools.partial(pack_kernel, n_seq, capacity),
        out_shape=[shape_of((1, rows), jnp.int32)] + [shape_of((block, width), BF16)] * n_seq,
        in_specs=[in_smem] + [stay_hbm] * 2,
        out_specs=[in_vmem] * (1 + n_seq),
        scratch_shapes=[
            pltpu.VMEM((1, rows), jnp.int32),
            pltpu.VMEM((rows, width), BF16),
            pltpu.SemaphoreType.DMA((2,)),
        ],
        compiler_params=params(60),
        cost_estimate=pl.CostEstimate(
            flops=2 * slots * rows * width, bytes_accessed=2 * MIB, transcendentals=0
        ),
        name="pack",
    )(me, dest, feats)
    feats_got = by_distance(feats_sent, "seq")
    feats_got[1], slot = lax.optimization_barrier((feats_got[1], slot))
    grads_sent = pl.pallas_call(
        functools.partial(pack_grads_kernel, n_seq, capacity),
        out_shape=shape_of((slots, width), BF16),
        in_specs=[in_smem] + [in_vmem] * 2,
        out_specs=in_vmem,
        compiler_params=params(20),
        cost_estimate=pl.CostEstimate(
            flops=2 * slots * rows * width, bytes_accessed=2 * MIB, transcendentals=0
        ),
        name="pack_grads",
    )(me, slot, grads)

    def exchange(sent):
        sent = sent.reshape(n_seq, capacity, width)
        got = lax.all_to_all(sent, "seq", split_axis=0, concat_axis=0, tiled=True)
        return got.reshape(slots, width)

    feats_got, grads_sent = lax.optimization_barrier((feats_got, grads_sent))
    grads_got = exchange(grads_sent)

    pos, xhat, inv, normed, qkv, trans, attn_t, stats = pl.pallas_call(
        functools.partial(forward_kernel, n_seq, capacity),
        grid=(1,),
        out_shape=(
            shape_of((1, slots), jnp.int32),
            shape_of((rows, width), F32),
            shape_of((rows, LANES), F32),
            shape_of((rows, width), BF16),
            shape_of((rows, 3 * width), BF16),
            shape_of((2 * width, rows), BF16),
            shape_of((width, rows), BF16),
            shape_of((2 * HEADS, rows), F32),
        ),
        in_specs=[in_hbm, whole((1, width))] + [whole((block, width))] * n_seq,
        out_specs=[whole((1, slots))]
        + [in_hbm] * 5
        + [whole((width, rows)), whole((2 * HEADS, rows))],
        scratch_shapes=[
            pltpu.VMEM((width, 3 * width), BF16),
            pltpu.VMEM((rows, width), F32),
            pltpu.VMEM((rows, LANES), F32),
            pltpu.VMEM((rows, width), BF16),
            pltpu.VMEM((rows, 3 * width), BF16),
            pltpu.VMEM((3 * width, rows), BF16),
            pltpu.SemaphoreType.DMA((6,)),
        ],
        compiler_params=params(60),
        cost_estimate=pl.CostEstimate(
            flops=6 * rows * width * width + 8 * HEADS * rows * rows * pair,
            bytes_accessed=16 * MIB,
            transcendentals=HEADS * rows * rows,
        ),
        name="forward",
    )(w_qkv, gain_row, *feats_got)

    chip_bits = tuple(zip(*chip_orders(n_seq)))[:2]
    *quarters, serial_grad, d_normed = pl.pallas_call(
        functools.partial(backward_kernel, n_seq, chip_bits),
        grid=(1,),
        out_shape=[shape_of(sum_shape, F32)] * 4
        + [shape_of((rows, width), BF16), shape_of((rows, width), F32)],
        in_specs=[
            in_smem,
            whole((1, slots)),
            whole((width, width)),
            whole((2 * HEADS, rows)),
        ]
        + [in_hbm] * 7,
        out_specs=[in_hbm] * 6,
        scratch_shapes=[
            pltpu.VMEM((slots, width), BF16),
            pltpu.VMEM((rows, 3 * width), BF16),
            pltpu.VMEM((2 * width, rows), BF16),
            pltpu.VMEM((width, 3 * width), BF16),
            pltpu.VMEM((rows, width), F32),
            pltpu.VMEM((rows, width), BF16),
            pltpu.VMEM((width, rows), BF16),
        ]
        + [pltpu.VMEM(sum_shape, F32)] * 4
        + [
            pltpu.VMEM((rows, width), BF16),
            pltpu.VMEM((rows, width), F32),
            pltpu.VMEM((rows, width), BF16),
            pltpu.VMEM((width, rows), BF16),
            pltpu.VMEM((rows, 3 * width), BF16),
            pltpu.VMEM((width, LANES), F32),
            pltpu.SemaphoreType.DMA((13,)),
        ],
        compiler_params=params(60),
        cost_estimate=pl.CostEstimate(
            flops=12 * rows * width * width + 10 * HEADS * rows * rows * pair,
            bytes_accessed=16 * MIB,
            transcendentals=HEADS * rows * rows,
        ),
        name="backward",
    )(me, pos, w_proj, stats, grads_got, qkv, trans, w_qkv, xhat, normed, attn_t)

    steps = chip_steps()
    terms = first_step(quarters, steps)
    back = pl.pallas_call(
        functools.partial(residual_kernel, n_seq),
        out_shape=shape_of((slots, width), BF16),
        in_specs=[in_smem] + [in_vmem] * 6,
        out_specs=in_vmem,
        compiler_params=params(20),
        cost_estimate=pl.CostEstimate(
            flops=2 * slots * rows * width, bytes_accessed=4 * MIB, transcendentals=0
        ),
        name="residual",
    )(me, pos, gain_row, inv, xhat, serial_grad, d_normed)
    terms, got = second_step(terms, steps)
    got, back = lax.optimization_barrier((got, back))
    returned = exchange(back)
    part, returned = lax.optimization_barrier((reduce_over_planes(terms, got, steps), returned))
    own = share_in_plane(share_over_planes(part), steps)
    grad_local = pl.pallas_call(
        functools.partial(unpack_kernel, n_seq),
        out_shape=shape_of((rows, width), BF16),
        in_specs=[in_smem] + [in_vmem] * 2,
        out_specs=in_vmem,
        compiler_params=params(20),
        cost_estimate=pl.CostEstimate(
            flops=2 * slots * rows * width, bytes_accessed=2 * MIB, transcendentals=0
        ),
        name="unpack",
    )(me, slot, returned)
    own, grad_local = lax.optimization_barrier((own, grad_local))
    other = lax.ppermute(own, "seq", core_pairs())
    side = lax.bitwise_and(me, 1)
    outs = write_half(side, own)
    grad_qkv, grad_proj, gain_grad = write_half(1 - side, other, outs)
    return (grad_local[None], grad_qkv, grad_proj, gain_grad[0])


def solution(mesh):
    return jax.shard_map(
        per_device,
        mesh=mesh,
        in_specs=(P("dp", "seq", None), P("dp", "seq", None), P("dp", "seq"), P(), P(), P()),
        out_specs=(P("dp", "seq", None), P(), P(), P()),
        check_vma=False,
    )
```

```python
import functools

import jax
import jax.numpy as jnp
from jax import lax
from jax.experimental import pallas as pl
from jax.experimental.pallas import tpu as pltpu
from jax.sharding import PartitionSpec as P

HEADS = 8
PATCH = 512
EXTRA = 16
LANES = 128
CODE_MAX = 32000.0
DIGIT = 60000.0
MIB = 1024 * 1024
F32 = jnp.float32
BF16 = jnp.bfloat16
NN = (((1,), (0,)), ((), ()))
NT = (((1,), (1,)), ((), ()))


def mm(lhs, rhs, dims=NN):
    return lax.dot_general(lhs, rhs, dims, preferred_element_type=F32)


def iota(shape, dim):
    return lax.broadcasted_iota(jnp.int32, shape, dim)


def hot(mask):
    return jnp.where(mask, jnp.float32(1), jnp.float32(0)).astype(BF16)


def column_hot(row, count):
    size = row.shape[1]
    column = jnp.transpose(jnp.broadcast_to(row, (LANES, size)))
    lane = iota((size, LANES), 1)
    return jnp.concatenate([hot(column == lane + j * LANES) for j in range(count // LANES)], axis=1)


def by_receiver(me, distance, capacity):
    return pl.ds(pl.multiple_of(lax.bitwise_xor(me, distance) * capacity, capacity), capacity)


def pack_kernel(
    n_seq, capacity, me_ref, dest_hbm, feats_hbm, grads_hbm, slot_out, same_out, cross_out, *refs
):
    outs, (dest_ref, feats_ref, grads_ref, sems) = refs[:n_seq], refs[n_seq:]
    rows, width = feats_ref.shape
    slots = n_seq * capacity
    loads = [
        pltpu.make_async_copy(source, target, sems.at[i])
        for i, (source, target) in enumerate(
            ((dest_hbm, dest_ref), (feats_hbm, feats_ref), (grads_hbm, grads_ref))
        )
    ]
    for load in loads:
        load.start()
    loads[0].wait()
    shift = rows.bit_length() - 1
    places = dest_ref[...]
    distance = lax.bitwise_xor(lax.shift_right_logical(places, shift), me_ref[0])
    within = lax.bitwise_and(places, rows - 1) + 1
    member = iota((n_seq, rows), 0) == distance
    upper = hot(iota((rows, rows), 0) <= iota((rows, rows), 1))
    counts = mm(hot(member), upper)
    rank = jnp.sum(jnp.where(member, counts, 0.0), axis=0, keepdims=True).astype(jnp.int32) - 1
    slot = distance * capacity + rank
    slot_out[...] = slot
    select = hot(iota((slots, rows), 0) == slot)
    loads[1].wait()
    feats = mm(select, feats_ref[...]).astype(BF16)
    upper_half = slot >= width
    high = lax.shift_right_logical(within, 8).astype(F32)
    low = lax.bitwise_and(within, 255).astype(F32)
    line = iota((n_seq * EXTRA, rows), 0)
    kind = lax.bitwise_and(line, EXTRA - 1)
    digit = jnp.where(kind < 2, high, low)
    wanted = (
        (lax.shift_right_logical(line, EXTRA.bit_length() - 1) == distance)
        & (kind < 4)
        & ((lax.bitwise_and(kind, 1) == 1) == upper_half)
    )
    digits = jnp.where(wanted, digit, 0.0).astype(BF16)
    spread = hot(iota((width, rows), 0) == lax.bitwise_and(slot, width - 1))
    position = mm(digits, spread, NT).astype(BF16)
    for d in range(n_seq):
        outs[d][:capacity, :] = feats[d * capacity : (d + 1) * capacity]
        outs[d][capacity:, :] = position[d * EXTRA : (d + 1) * EXTRA]
    loads[2].wait()
    grads = mm(select, grads_ref[...]).astype(BF16)
    for j in range(n_seq // 2):
        lines = slice(j * capacity, (j + 1) * capacity)
        same_out[lines, :] = grads[2 * j * capacity : (2 * j + 1) * capacity]
        cross_out[lines, :] = grads[(2 * j + 1) * capacity : (2 * j + 2) * capacity]


def pair_kernel(capacity, same_ref, cross_ref, *outs):
    for j, out in enumerate(outs):
        lines = slice(j * capacity, (j + 1) * capacity)
        out[:capacity, :] = same_ref[lines, :]
        out[capacity:, :] = cross_ref[lines, :]


def forward_kernel(n_seq, capacity, w_hbm, gain_ref, *refs):
    recv, refs = refs[:n_seq], refs[n_seq:]
    pos_out, xhat_hbm, inv_hbm, normed_hbm, qkv_hbm, trans_hbm, attn_out, stats_out = refs[:8]
    w_ref, xhat_ref, inv_ref, normed_ref, qkv_ref, trans, sems = refs[8:]
    width = w_ref.shape[0]
    rows = xhat_ref.shape[0]
    head = width // HEADS
    pair = 2 * head
    w_copy = pltpu.make_async_copy(w_hbm, w_ref, sems.at[0])
    saves = [
        pltpu.make_async_copy(source, target, sems.at[1 + i])
        for i, (source, target) in enumerate(
            (
                (xhat_ref, xhat_hbm),
                (inv_ref, inv_hbm),
                (normed_ref, normed_hbm),
                (qkv_ref, qkv_hbm),
                (trans.at[pl.ds(0, 2 * width)], trans_hbm),
            )
        )
    ]

    w_copy.start()
    tile = recv[0][capacity:, :].astype(F32)
    for s in range(1, n_seq):
        tile = tile + recv[s][capacity:, :].astype(F32)
    high = jnp.concatenate([tile[0:1], tile[1:2]], axis=1)
    low = jnp.concatenate([tile[2:3], tile[3:4]], axis=1)
    pos = (high * 256.0 + low).astype(jnp.int32) - 1
    pos_out[...] = pos
    place = hot(iota((rows, n_seq * capacity), 0) == pos)
    values = jnp.concatenate([recv[s][:capacity, :] for s in range(n_seq)], axis=0)
    feats = mm(place, values)
    centered = feats - jnp.mean(feats, axis=1, keepdims=True)
    inv = lax.rsqrt(jnp.mean(centered * centered, axis=1, keepdims=True) + 1e-05)
    xhat = centered * inv
    xhat_ref[...] = xhat
    inv_ref[...] = jnp.broadcast_to(inv, inv_ref.shape)
    scaled = xhat * gain_ref[...]
    normed = scaled.astype(BF16)
    normed_ref[...] = jnp.transpose(scaled).astype(BF16)
    w_copy.wait()
    qkv = mm(normed, w_ref[...])
    qkv_ref[...] = qkv.astype(BF16)
    trans[...] = jnp.transpose(qkv).astype(BF16)
    for save in saves:
        save.start()

    for step in range(HEADS // 2):
        lo = step * pair
        keys = qkv_ref[:, pl.ds(width + lo, pair)]
        query_t = trans[pl.ds(lo, pair), :] * BF16(0.125)
        zero = jnp.zeros((head, rows), BF16)
        for j in range(2):
            part = query_t[j * head : (j + 1) * head]
            part = jnp.concatenate([part, zero] if j == 0 else [zero, part], axis=0)
            scores = mm(keys, part)
            top = jnp.max(scores, axis=0, keepdims=True)
            expo = jnp.exp(scores - top)
            share = 1.0 / jnp.sum(expo, axis=0, keepdims=True)
            probs = expo * share
            stats_out[pl.ds(2 * step + j, 1), :] = top
            stats_out[pl.ds(HEADS + 2 * step + j, 1), :] = share
            values_t = trans[pl.ds(2 * width + lo + j * head, head), :]
            attn_out[pl.ds(lo + j * head, head), :] = mm(values_t, probs.astype(BF16)).astype(BF16)

    for save in saves:
        save.wait()


def backward_kernel(n_seq, chip_bits, me_ref, pos_ref, w_proj_ref, stats_ref, *refs):
    (qkv_hbm, trans_hbm, w_hbm, xhat_hbm, normed_hbm, attn_hbm), refs = refs[:6], refs[6:]
    recv_hbm, refs = refs[: n_seq // 2], refs[n_seq // 2 :]
    outs, serial_grad_hbm, d_normed_hbm, refs = refs[:4], refs[4], refs[5], refs[6:]
    recv_ref, qkv_ref, trans_ref, w_ref, xhat_ref, normed_ref, attn_ref, refs = *refs[:7], refs[7:]
    sums, refs = refs[:4], refs[4:]
    serial_grad, d_normed_ref, d_attn, d_attn_t, d_qkv, gain_column, sems = refs
    width = w_proj_ref.shape[0]
    rows = xhat_ref.shape[0]
    capacity = recv_ref.shape[0] // n_seq
    head = width // HEADS
    pair = 2 * head
    me = me_ref[0]
    chips = n_seq // 2
    recv_parts = [recv_ref.at[pl.ds(2 * j * capacity, 2 * capacity)] for j in range(chips)]
    loads = [
        pltpu.make_async_copy(source, target, sems.at[i])
        for i, (source, target) in enumerate(
            (
                *zip(recv_hbm, recv_parts),
                (qkv_hbm, qkv_ref),
                (trans_hbm, trans_ref),
                (normed_hbm, normed_ref),
                (w_hbm, w_ref),
                (xhat_hbm, xhat_ref),
                (attn_hbm, attn_ref),
            )
        )
    ]
    saves = [
        pltpu.make_async_copy(source, target, sems.at[6 + chips + i])
        for i, (source, target) in enumerate(
            [*zip(sums, outs), (serial_grad, serial_grad_hbm), (d_normed_ref, d_normed_hbm)]
        )
    ]

    for load in loads:
        load.start()
    place = hot(iota((rows, n_seq * capacity), 0) == pos_ref[...])
    for load in loads[:chips]:
        load.wait()
    grads = mm(place, recv_ref[...]).astype(BF16)
    serial_grad[...] = grads
    saves[4].start()
    d_attn[...] = mm(grads, w_proj_ref[...], NT).astype(BF16)
    d_attn_t[...] = mm(w_proj_ref[...], grads, NT).astype(BF16)
    for load in loads[chips : chips + 2]:
        load.wait()

    zero = jnp.zeros((head, rows), BF16)
    first = iota((rows, pair), 1) < head

    def alone(both, j):
        part = both[j * head : (j + 1) * head]
        return jnp.concatenate([part, zero] if j == 0 else [zero, part], axis=0)

    for step in range(HEADS // 2):
        lo = step * pair
        queries = qkv_ref[:, pl.ds(lo, pair)]
        values = qkv_ref[:, pl.ds(2 * width + lo, pair)]
        d_att_t = d_attn_t[pl.ds(lo, pair), :] * BF16(0.125)
        d_att = d_attn[:, pl.ds(lo, pair)]
        keys = qkv_ref[:, pl.ds(width + lo, pair)]
        query_t = trans_ref[pl.ds(lo, pair), :] * BF16(0.125)
        d_q, d_k, d_v = [], [], []
        for j in range(2):
            top = stats_ref[pl.ds(2 * step + j, 1), :]
            share = stats_ref[pl.ds(HEADS + 2 * step + j, 1), :]
            probs = jnp.exp(mm(keys, alone(query_t, j)) - top) * share
            d_probs = mm(values, alone(d_att_t, j))
            total = jnp.sum(d_probs * probs, axis=0, keepdims=True)
            d_scores = (probs * (d_probs - total)).astype(BF16)
            k_t = trans_ref[pl.ds(width + lo + j * head, head), :]
            d_q.append(mm(k_t, d_scores))
            d_k.append(mm(d_scores, queries))
            d_v.append(mm(probs.astype(BF16), d_att))
        d_qkv[:, pl.ds(lo, pair)] = jnp.transpose(jnp.concatenate(d_q, axis=0)).astype(BF16)
        d_qkv[:, pl.ds(width + lo, pair)] = jnp.where(
            first, d_k[0], d_k[1]
        ).astype(BF16)
        d_qkv[:, pl.ds(2 * width + lo, pair)] = jnp.where(
            first, d_v[0], d_v[1]
        ).astype(BF16)

    for load in loads[chips + 2 :]:
        load.wait()
    d_normed = mm(d_qkv[...], w_ref[...], NT)
    d_normed_ref[...] = d_normed
    saves[5].start()
    gain_row = jnp.sum(d_normed * xhat_ref[...], axis=0, keepdims=True)
    gain_column[...] = jnp.transpose(jnp.broadcast_to(gain_row, (LANES, width)))
    eighth = width // 8
    odd = lax.bitwise_and(me, 1)

    def sides(even_bit, odd_bit):
        even_side = lax.bitwise_and(lax.shift_right_logical(me, even_bit), 1)
        odd_side = lax.bitwise_and(lax.shift_right_logical(me, odd_bit), 1)
        mine = jnp.where(odd == 1, odd_side, even_side)
        return mine, even_side + odd_side - mine

    (mine, other), (mine_next, other_next) = (sides(*bits) for bits in chip_bits)
    starts = (
        ((1 - odd) * 2 + 1 - other, other_next),
        ((1 - odd) * 2 + other, other_next),
        (odd * 2 + 1 - mine, mine_next),
        (odd * 2 + mine, mine_next),
    )
    order = [
        pl.ds(pl.multiple_of((start * 2 + half) * eighth, eighth), eighth)
        for start, side in starts
        for half in (1 - side, side)
    ]
    for i in (0, 2):
        parts = order[2 * i : 2 * i + 4]
        of_qkv = mm(jnp.concatenate([normed_ref[part, :] for part in parts], axis=0), d_qkv[...])
        of_proj = mm(jnp.concatenate([attn_ref[part, :] for part in parts], axis=0), serial_grad[...])
        of_gain = jnp.concatenate([gain_column[part, :] for part in parts], axis=0)
        for j in range(2):
            lines = slice(2 * j * eighth, 2 * (j + 1) * eighth)
            sums[i + j][:, : 3 * width] = of_qkv[lines]
            sums[i + j][:, 3 * width : 4 * width] = of_proj[lines]
            sums[i + j][:, 4 * width :] = of_gain[lines]
            saves[i + j].start()
    for save in saves:
        save.wait()


def residual_kernel(
    n_seq, me_ref, pos_ref, gain_ref, inv_ref, xhat_ref, serial_grad_ref, d_normed_ref, back_out
):
    xhat = xhat_ref[...]
    rows = xhat.shape[0]
    capacity = pos_ref.shape[1] // n_seq
    scaled = d_normed_ref[...] * gain_ref[...]
    residual = inv_ref[:, 0:1] * (
        scaled
        - jnp.mean(scaled, axis=1, keepdims=True)
        - xhat * jnp.mean(scaled * xhat, axis=1, keepdims=True)
    )
    serial_dx = (serial_grad_ref[...].astype(F32) + residual).astype(BF16)
    returned = mm(column_hot(pos_ref[...], rows), serial_dx).astype(BF16)
    for d in range(n_seq):
        back_out[by_receiver(me_ref[0], d, capacity), :] = returned[d * capacity : (d + 1) * capacity]


def unpack_kernel(n_seq, me_ref, slot_ref, recv_ref, out_ref):
    capacity = recv_ref.shape[0] // n_seq
    values = jnp.concatenate(
        [recv_ref[by_receiver(me_ref[0], d, capacity), :] for d in range(n_seq)], axis=0
    )
    out_ref[...] = mm(column_hot(slot_ref[...], values.shape[0]), values).astype(BF16)


def split_kernel(side_ref, sums_ref, *refs):
    qkv_out, proj_out, gain_out = refs[-3:]
    width = proj_out.shape[1]
    qkv_out[...] = sums_ref[:, : 3 * width].astype(F32)
    proj_out[...] = sums_ref[:, 3 * width : 4 * width].astype(F32)
    gain_out[...] = jnp.transpose(sums_ref[:, 4 * width :].astype(F32))[0:1]


def exponent_of(largest):
    return jnp.clip(jnp.ceil(jnp.log(jnp.maximum(largest, 1e-30)) * 1.4426950408889634), -100.0, 120.0)


def encode(out_ref, total):
    width = total.shape[1] - LANES
    body, gain = total[:, :width], total[:, width : width + 1]
    exponent = exponent_of(jnp.max(jnp.abs(body), axis=1, keepdims=True))
    codes = jnp.round(body * (jnp.exp2(-exponent) * CODE_MAX))
    out_ref[:, :width] = codes.astype(jnp.int32).astype(jnp.int16)
    gain_exponent = exponent_of(jnp.abs(gain))
    scaled = gain * (jnp.exp2(-gain_exponent) * CODE_MAX)
    high = jnp.round(scaled)
    low = jnp.round((scaled - high) * DIGIT)
    lane = iota((total.shape[0], LANES), 1)
    tail = jnp.where(lane == 0, high, jnp.where(lane == 1, low, jnp.where(lane == 2, gain_exponent, exponent)))
    out_ref[:, width:] = tail.astype(jnp.int32).astype(jnp.int16)


def decode(codes):
    values = codes.astype(jnp.int32).astype(F32)
    width = values.shape[1] - LANES
    tail = values[:, width:]
    body = values[:, :width] * (jnp.exp2(tail[:, 3:4]) * (1.0 / CODE_MAX))
    gain = (tail[:, 0:1] + tail[:, 1:2] * (1.0 / DIGIT)) * (jnp.exp2(tail[:, 2:3]) * (1.0 / CODE_MAX))
    return jnp.concatenate([body, jnp.broadcast_to(gain, tail.shape)], axis=1)


def total_of(terms, part):
    half = terms[0].shape[0] // 2
    rows = {"all": slice(None), "first": slice(0, half), "second": slice(half, 2 * half)}[part]
    values = [ref[rows, :] for ref in terms]
    return functools.reduce(jnp.add, [decode(v) if v.dtype == jnp.int16 else v for v in values])


def message_kernel(part, *refs):
    encode(refs[-1], total_of(refs[:-1], part))


def sum_kernel(parts, *refs):
    refs[-1][...] = functools.reduce(jnp.add, [total_of([ref], p) for ref, p in zip(refs, parts)])


def pieces_kernel(parts, n_dp, plane_ref, *refs):
    terms, own, messages, total = refs[: len(parts)], refs[len(parts)], refs[len(parts) + 1 : -1], refs[-1]
    total[...] = functools.reduce(jnp.add, [total_of([ref], p) for ref, p in zip(terms, parts)])
    size = own.shape[0]

    def rows_of(distance):
        start = lax.bitwise_xor(plane_ref[0], distance) * size
        return total[pl.ds(pl.multiple_of(start, size), size), :]

    for k in range(1, n_dp):
        encode(messages[k - 1], rows_of(k))
    own[...] = rows_of(0)


def finish_kernel(*refs):
    refs[-1][...] = total_of(refs[:-1], "all").astype(BF16)


def whole(shape):
    return pl.BlockSpec(shape, lambda *_: (0,) * len(shape), pipeline_mode=pl.Buffered(1))


def params(mib):
    return pltpu.CompilerParams(vmem_limit_bytes=mib * MIB)


def shape_of(shape, dtype):
    return jax.ShapeDtypeStruct(shape, dtype)


def by_distance(blocks, axis):
    count = len(blocks)
    return [blocks[0]] + [
        lax.ppermute(blocks[k], axis, [(i, i ^ k) for i in range(count)]) for k in range(1, count)
    ]


def chip_orders(n_seq):
    bits = list(range(1, n_seq.bit_length() - 1))
    middle = len(bits) // 2
    return bits, bits[middle:] + bits[:middle]


def chip_steps():
    n_seq, me = lax.axis_size("seq"), lax.axis_index("seq")
    odd = lax.bitwise_and(me, 1) == 1

    def side(bit):
        return lax.bitwise_and(lax.shift_right_logical(me, jnp.asarray(bit, me.dtype)), 1)

    steps = []
    for even_bit, odd_bit in zip(*chip_orders(n_seq)):
        pairs = [(i, i ^ (1 << (odd_bit if i & 1 else even_bit))) for i in range(n_seq)]
        steps.append((pairs, jnp.where(odd, side(odd_bit), side(even_bit))))
    return steps


def piece(terms, index, count):
    size = terms[0].shape[0] // count
    return functools.reduce(jnp.add, [lax.dynamic_slice_in_dim(t, index * size, size) for t in terms])


def core_pairs():
    return [(i, i ^ 1) for i in range(lax.axis_size("seq"))]


def small_kernel(kernel, outs, operands, scalars=0, scratch=(), name="sum"):
    in_smem = pl.BlockSpec(memory_space=pltpu.SMEM)
    in_vmem = pl.BlockSpec(memory_space=pltpu.VMEM)
    touched = sum(x.size * x.dtype.itemsize for x in (*operands, *outs))
    return pl.pallas_call(
        kernel,
        out_shape=outs,
        in_specs=[in_smem] * scalars + [in_vmem] * (len(operands) - scalars),
        out_specs=[in_vmem] * len(outs),
        scratch_shapes=list(scratch),
        compiler_params=params(16),
        cost_estimate=pl.CostEstimate(flops=2 * touched, bytes_accessed=touched, transcendentals=0),
        name=name,
    )(*operands)


def message(terms, part, name):
    rows, width = terms[0].shape
    rows = rows if part == "all" else rows // 2
    return small_kernel(
        functools.partial(message_kernel, part), [shape_of((rows, width), jnp.int16)], terms, name=name
    )[0]


def first_step(quarters, steps):
    pass_on, pass_keep, own_on, own_keep = quarters
    got_on = lax.ppermute(pass_on, "seq", core_pairs())
    got_keep = lax.ppermute(pass_keep, "seq", core_pairs())
    sent = message([own_on, got_on], "all", "code_first")
    return [own_keep, got_keep, lax.ppermute(sent, "seq", steps[0][0])]


def second_step(terms, steps):
    sent = message(terms, "first", "code_second")
    return terms, lax.ppermute(sent, "seq", steps[1][0])


def halves_of_plain(part, steps):
    for pairs, side in steps:
        got = lax.ppermute(piece([part], 1 - side, 2), "seq", pairs)
        part = piece([part], side, 2) + got
    return part


def reduce_over_planes(terms, got, steps):
    n_dp, plane = lax.axis_size("dp"), lax.axis_index("dp")
    rows, width = got.shape
    parts = ["second"] * len(terms) + ["all"]
    if len(steps) > 2 or rows // n_dp % 16:
        part = small_kernel(
            functools.partial(sum_kernel, parts), [shape_of((rows, width), F32)], [*terms, got]
        )[0]
        part = halves_of_plain(part, steps[2:])
        pieces = [piece([part], lax.bitwise_xor(plane, k), n_dp) for k in range(n_dp)]
        return functools.reduce(jnp.add, by_distance(pieces, "dp")).astype(BF16)
    size = rows // n_dp
    own, *sent = small_kernel(
        functools.partial(pieces_kernel, parts, n_dp),
        [shape_of((size, width), F32)] + [shape_of((size, width), jnp.int16)] * (n_dp - 1),
        [jnp.reshape(plane.astype(jnp.int32), (1,)), *terms, got],
        scalars=1,
        scratch=[pltpu.VMEM((rows, width), F32)],
        name="code_planes",
    )
    arrived = by_distance([own] + sent, "dp")
    return small_kernel(finish_kernel, [shape_of((size, width), BF16)], arrived, name="finish")[0]


def share_over_planes(part):
    n_dp, plane = lax.axis_size("dp"), lax.axis_index("dp")
    shares = jnp.stack(by_distance([part] * n_dp, "dp"))
    return jnp.concatenate(
        [lax.dynamic_index_in_dim(shares, lax.bitwise_xor(plane, p), keepdims=False) for p in range(n_dp)],
        axis=0,
    )


def share_in_plane(part, steps):
    for pairs, side in reversed(steps):
        other = lax.ppermute(part, "seq", pairs)
        part = jnp.where(
            side == 0, jnp.concatenate([part, other], axis=0), jnp.concatenate([other, part], axis=0)
        )
    return part


def write_half(side, sums, outs=()):
    half, width = sums.shape[0], (sums.shape[1] - LANES) // 4
    return pl.pallas_call(
        split_kernel,
        grid_spec=pltpu.PrefetchScalarGridSpec(
            num_scalar_prefetch=1,
            grid=(2,),
            in_specs=[pl.BlockSpec((half // 2, sums.shape[1]), lambda i, s: (i, 0))]
            + [pl.BlockSpec(memory_space=pl.ANY)] * len(outs),
            out_specs=[
                pl.BlockSpec((half // 2, 3 * width), lambda i, s: (2 * s[0] + i, 0)),
                pl.BlockSpec((half // 2, width), lambda i, s: (2 * s[0] + i, 0)),
                pl.BlockSpec((1, half // 2), lambda i, s: (0, 2 * s[0] + i)),
            ],
        ),
        out_shape=(
            shape_of((2 * half, 3 * width), F32),
            shape_of((2 * half, width), F32),
            shape_of((1, 2 * half), F32),
        ),
        input_output_aliases={2 + i: i for i in range(len(outs))},
        compiler_params=params(20),
        cost_estimate=pl.CostEstimate(flops=0, bytes_accessed=4 * MIB, transcendentals=0),
        name="split",
    )(side, sums, *outs)


def per_device(points, cotangent, dest, w_qkv, w_proj, gain):
    feats = points[0]
    grads = cotangent[0]
    rows, width = feats.shape
    n_seq = lax.axis_size("seq")
    capacity = 2 * (rows // n_seq)
    slots = n_seq * capacity
    block = capacity + EXTRA
    pairs = HEADS // 2
    pair = width // pairs
    sum_shape = (width // 4, 4 * width + LANES)
    me = jnp.reshape(lax.axis_index("seq").astype(jnp.int32), (1,))
    gain_row = gain.reshape(1, width)
    in_smem = pl.BlockSpec(memory_space=pltpu.SMEM)
    in_vmem = pl.BlockSpec(memory_space=pltpu.VMEM)
    in_hbm = pl.BlockSpec(memory_space=pl.ANY)
    stay_hbm = pl.BlockSpec(memory_space=pltpu.HBM)

    slot, same, cross, *feats_sent = pl.pallas_call(
        functools.partial(pack_kernel, n_seq, capacity),
        out_shape=[shape_of((1, rows), jnp.int32)]
        + [shape_of((slots // 2, width), BF16)] * 2
        + [shape_of((block, width), BF16)] * n_seq,
        in_specs=[in_smem] + [stay_hbm] * 3,
        out_specs=[in_vmem] * (3 + n_seq),
        scratch_shapes=[
            pltpu.VMEM((1, rows), jnp.int32),
            pltpu.VMEM((rows, width), BF16),
            pltpu.VMEM((rows, width), BF16),
            pltpu.SemaphoreType.DMA((3,)),
        ],
        compiler_params=params(60),
        cost_estimate=pl.CostEstimate(
            flops=4 * slots * rows * width, bytes_accessed=4 * MIB, transcendentals=0
        ),
        name="pack",
    )(me, dest, feats, grads)
    feats_got = by_distance(feats_sent, "seq")
    messages = small_kernel(
        functools.partial(pair_kernel, capacity),
        [shape_of((2 * capacity, width), BF16)] * (n_seq // 2),
        [same, lax.ppermute(cross, "seq", core_pairs())],
        name="pair_up",
    )
    feats_got, messages = lax.optimization_barrier((feats_got, messages))
    grads_got = [messages[0]] + [
        lax.ppermute(messages[j], "seq", [(i, i ^ (2 * j)) for i in range(n_seq)])
        for j in range(1, n_seq // 2)
    ]

    def exchange(sent):
        sent = sent.reshape(n_seq, capacity, width)
        got = lax.all_to_all(sent, "seq", split_axis=0, concat_axis=0, tiled=True)
        return got.reshape(slots, width)

    pos, xhat, inv, normed, qkv, trans, attn_t, stats = pl.pallas_call(
        functools.partial(forward_kernel, n_seq, capacity),
        grid=(1,),
        out_shape=(
            shape_of((1, slots), jnp.int32),
            shape_of((rows, width), F32),
            shape_of((rows, LANES), F32),
            shape_of((rows, width), BF16),
            shape_of((rows, 3 * width), BF16),
            shape_of((2 * width, rows), BF16),
            shape_of((width, rows), BF16),
            shape_of((2 * HEADS, rows), F32),
        ),
        in_specs=[in_hbm, whole((1, width))] + [whole((block, width))] * n_seq,
        out_specs=[whole((1, slots))]
        + [in_hbm] * 5
        + [whole((width, rows)), whole((2 * HEADS, rows))],
        scratch_shapes=[
            pltpu.VMEM((width, 3 * width), BF16),
            pltpu.VMEM((rows, width), F32),
            pltpu.VMEM((rows, LANES), F32),
            pltpu.VMEM((rows, width), BF16),
            pltpu.VMEM((rows, 3 * width), BF16),
            pltpu.VMEM((3 * width, rows), BF16),
            pltpu.SemaphoreType.DMA((6,)),
        ],
        compiler_params=params(60),
        cost_estimate=pl.CostEstimate(
            flops=6 * rows * width * width + 8 * HEADS * rows * rows * pair,
            bytes_accessed=16 * MIB,
            transcendentals=HEADS * rows * rows,
        ),
        name="forward",
    )(w_qkv, gain_row, *feats_got)

    chip_bits = tuple(zip(*chip_orders(n_seq)))[:2]
    *quarters, serial_grad, d_normed = pl.pallas_call(
        functools.partial(backward_kernel, n_seq, chip_bits),
        grid=(1,),
        out_shape=[shape_of(sum_shape, F32)] * 4
        + [shape_of((rows, width), BF16), shape_of((rows, width), F32)],
        in_specs=[
            in_smem,
            whole((1, slots)),
            whole((width, width)),
            whole((2 * HEADS, rows)),
        ]
        + [in_hbm] * (6 + n_seq // 2),
        out_specs=[in_hbm] * 6,
        scratch_shapes=[
            pltpu.VMEM((slots, width), BF16),
            pltpu.VMEM((rows, 3 * width), BF16),
            pltpu.VMEM((2 * width, rows), BF16),
            pltpu.VMEM((width, 3 * width), BF16),
            pltpu.VMEM((rows, width), F32),
            pltpu.VMEM((rows, width), BF16),
            pltpu.VMEM((width, rows), BF16),
        ]
        + [pltpu.VMEM(sum_shape, F32)] * 4
        + [
            pltpu.VMEM((rows, width), BF16),
            pltpu.VMEM((rows, width), F32),
            pltpu.VMEM((rows, width), BF16),
            pltpu.VMEM((width, rows), BF16),
            pltpu.VMEM((rows, 3 * width), BF16),
            pltpu.VMEM((width, LANES), F32),
            pltpu.SemaphoreType.DMA((12 + n_seq // 2,)),
        ],
        compiler_params=params(60),
        cost_estimate=pl.CostEstimate(
            flops=12 * rows * width * width + 10 * HEADS * rows * rows * pair,
            bytes_accessed=16 * MIB,
            transcendentals=HEADS * rows * rows,
        ),
        name="backward",
    )(me, pos, w_proj, stats, qkv, trans, w_qkv, xhat, normed, attn_t, *grads_got)

    steps = chip_steps()
    terms = first_step(quarters, steps)
    back = pl.pallas_call(
        functools.partial(residual_kernel, n_seq),
        out_shape=shape_of((slots, width), BF16),
        in_specs=[in_smem] + [in_vmem] * 6,
        out_specs=in_vmem,
        compiler_params=params(20),
        cost_estimate=pl.CostEstimate(
            flops=2 * slots * rows * width, bytes_accessed=4 * MIB, transcendentals=0
        ),
        name="residual",
    )(me, pos, gain_row, inv, xhat, serial_grad, d_normed)
    terms, got = second_step(terms, steps)
    got, back = lax.optimization_barrier((got, back))
    returned = exchange(back)
    part, returned = lax.optimization_barrier((reduce_over_planes(terms, got, steps), returned))
    own = share_in_plane(share_over_planes(part), steps)
    grad_local = pl.pallas_call(
        functools.partial(unpack_kernel, n_seq),
        out_shape=shape_of((rows, width), BF16),
        in_specs=[in_smem] + [in_vmem] * 2,
        out_specs=in_vmem,
        compiler_params=params(20),
        cost_estimate=pl.CostEstimate(
            flops=2 * slots * rows * width, bytes_accessed=2 * MIB, transcendentals=0
        ),
        name="unpack",
    )(me, slot, returned)
    own, grad_local = lax.optimization_barrier((own, grad_local))
    other = lax.ppermute(own, "seq", core_pairs())
    side = lax.bitwise_and(me, 1)
    outs = write_half(side, own)
    grad_qkv, grad_proj, gain_grad = write_half(1 - side, other, outs)
    return (grad_local[None], grad_qkv, grad_proj, gain_grad[0])


def solution(mesh):
    return jax.shard_map(
        per_device,
        mesh=mesh,
        in_specs=(P("dp", "seq", None), P("dp", "seq", None), P("dp", "seq"), P(), P(), P()),
        out_specs=(P("dp", "seq", None), P(), P(), P()),
        check_vma=False,
    )
```

```python
import functools

import jax
import jax.numpy as jnp
from jax import lax
from jax.experimental import pallas as pl
from jax.experimental.pallas import tpu as pltpu
from jax.sharding import PartitionSpec as P

HEADS = 8
PATCH = 512
EXTRA = 16
LANES = 128
CODE_MAX = 32000.0
DIGIT = 60000.0
MIB = 1024 * 1024
F32 = jnp.float32
BF16 = jnp.bfloat16
NN = (((1,), (0,)), ((), ()))
NT = (((1,), (1,)), ((), ()))


def mm(lhs, rhs, dims=NN):
    return lax.dot_general(lhs, rhs, dims, preferred_element_type=F32)


def iota(shape, dim):
    return lax.broadcasted_iota(jnp.int32, shape, dim)


def hot(mask):
    return jnp.where(mask, jnp.float32(1), jnp.float32(0)).astype(BF16)


def column_hot(row, count):
    size = row.shape[1]
    column = jnp.transpose(jnp.broadcast_to(row, (LANES, size)))
    lane = iota((size, LANES), 1)
    return jnp.concatenate([hot(column == lane + j * LANES) for j in range(count // LANES)], axis=1)


def pack_kernel(
    n_seq, capacity, me_ref, dest_hbm, feats_hbm, grads_hbm, slot_out, same_out, cross_out, *refs
):
    outs, (dest_ref, feats_ref, grads_ref, sems) = refs[:n_seq], refs[n_seq:]
    rows, width = feats_ref.shape
    slots = n_seq * capacity
    loads = [
        pltpu.make_async_copy(source, target, sems.at[i])
        for i, (source, target) in enumerate(
            ((dest_hbm, dest_ref), (feats_hbm, feats_ref), (grads_hbm, grads_ref))
        )
    ]
    for load in loads:
        load.start()
    loads[0].wait()
    shift = rows.bit_length() - 1
    places = dest_ref[...]
    distance = lax.bitwise_xor(lax.shift_right_logical(places, shift), me_ref[0])
    within = lax.bitwise_and(places, rows - 1) + 1
    member = iota((n_seq, rows), 0) == distance
    upper = hot(iota((rows, rows), 0) <= iota((rows, rows), 1))
    counts = mm(hot(member), upper)
    rank = jnp.sum(jnp.where(member, counts, 0.0), axis=0, keepdims=True).astype(jnp.int32) - 1
    slot = distance * capacity + rank
    slot_out[...] = slot
    select = hot(iota((slots, rows), 0) == slot)
    loads[1].wait()
    feats = mm(select, feats_ref[...]).astype(BF16)
    upper_half = slot >= width
    high = lax.shift_right_logical(within, 8).astype(F32)
    low = lax.bitwise_and(within, 255).astype(F32)
    line = iota((n_seq * EXTRA, rows), 0)
    kind = lax.bitwise_and(line, EXTRA - 1)
    digit = jnp.where(kind < 2, high, low)
    wanted = (
        (lax.shift_right_logical(line, EXTRA.bit_length() - 1) == distance)
        & (kind < 4)
        & ((lax.bitwise_and(kind, 1) == 1) == upper_half)
    )
    digits = jnp.where(wanted, digit, 0.0).astype(BF16)
    spread = hot(iota((width, rows), 0) == lax.bitwise_and(slot, width - 1))
    position = mm(digits, spread, NT).astype(BF16)
    for d in range(n_seq):
        outs[d][:capacity, :] = feats[d * capacity : (d + 1) * capacity]
        outs[d][capacity:, :] = position[d * EXTRA : (d + 1) * EXTRA]
    loads[2].wait()
    grads = mm(select, grads_ref[...]).astype(BF16)
    for j in range(n_seq // 2):
        lines = slice(j * capacity, (j + 1) * capacity)
        same_out[lines, :] = grads[2 * j * capacity : (2 * j + 1) * capacity]
        cross_out[lines, :] = grads[(2 * j + 1) * capacity : (2 * j + 2) * capacity]


def pair_kernel(capacity, same_ref, cross_ref, *outs):
    for j, out in enumerate(outs):
        lines = slice(j * capacity, (j + 1) * capacity)
        out[:capacity, :] = same_ref[lines, :]
        out[capacity:, :] = cross_ref[lines, :]


def forward_kernel(n_seq, capacity, w_hbm, gain_ref, *refs):
    recv, refs = refs[:n_seq], refs[n_seq:]
    pos_out, xhat_hbm, inv_hbm, normed_hbm, qkv_hbm, trans_hbm, attn_out, stats_out = refs[:8]
    w_ref, xhat_ref, inv_ref, normed_ref, qkv_ref, trans, sems = refs[8:]
    width = w_ref.shape[0]
    rows = xhat_ref.shape[0]
    head = width // HEADS
    pair = 2 * head
    w_copy = pltpu.make_async_copy(w_hbm, w_ref, sems.at[0])
    saves = [
        pltpu.make_async_copy(source, target, sems.at[1 + i])
        for i, (source, target) in enumerate(
            (
                (xhat_ref, xhat_hbm),
                (inv_ref, inv_hbm),
                (normed_ref, normed_hbm),
                (qkv_ref, qkv_hbm),
                (trans.at[pl.ds(0, 2 * width)], trans_hbm),
            )
        )
    ]

    w_copy.start()
    tile = recv[0][capacity:, :].astype(F32)
    for s in range(1, n_seq):
        tile = tile + recv[s][capacity:, :].astype(F32)
    high = jnp.concatenate([tile[0:1], tile[1:2]], axis=1)
    low = jnp.concatenate([tile[2:3], tile[3:4]], axis=1)
    pos = (high * 256.0 + low).astype(jnp.int32) - 1
    pos_out[...] = pos
    place = hot(iota((rows, n_seq * capacity), 0) == pos)
    values = jnp.concatenate([recv[s][:capacity, :] for s in range(n_seq)], axis=0)
    feats = mm(place, values)
    centered = feats - jnp.mean(feats, axis=1, keepdims=True)
    inv = lax.rsqrt(jnp.mean(centered * centered, axis=1, keepdims=True) + 1e-05)
    xhat = centered * inv
    xhat_ref[...] = xhat
    inv_ref[...] = jnp.broadcast_to(inv, inv_ref.shape)
    scaled = xhat * gain_ref[...]
    normed = scaled.astype(BF16)
    normed_ref[...] = jnp.transpose(scaled).astype(BF16)
    w_copy.wait()
    qkv = mm(normed, w_ref[...])
    qkv_ref[...] = qkv.astype(BF16)
    trans[...] = jnp.transpose(qkv).astype(BF16)
    for save in saves:
        save.start()

    for step in range(HEADS // 2):
        lo = step * pair
        keys = qkv_ref[:, pl.ds(width + lo, pair)]
        query_t = trans[pl.ds(lo, pair), :] * BF16(0.125)
        zero = jnp.zeros((head, rows), BF16)
        for j in range(2):
            part = query_t[j * head : (j + 1) * head]
            part = jnp.concatenate([part, zero] if j == 0 else [zero, part], axis=0)
            scores = mm(keys, part)
            top = jnp.max(scores, axis=0, keepdims=True)
            expo = jnp.exp(scores - top)
            share = 1.0 / jnp.sum(expo, axis=0, keepdims=True)
            probs = expo * share
            stats_out[pl.ds(2 * step + j, 1), :] = top
            stats_out[pl.ds(HEADS + 2 * step + j, 1), :] = share
            values_t = trans[pl.ds(2 * width + lo + j * head, head), :]
            attn_out[pl.ds(lo + j * head, head), :] = mm(values_t, probs.astype(BF16)).astype(BF16)

    for save in saves:
        save.wait()


def backward_kernel(n_seq, chip_bits, me_ref, pos_ref, w_proj_ref, stats_ref, *refs):
    (qkv_hbm, trans_hbm, w_hbm, xhat_hbm, normed_hbm, attn_hbm), refs = refs[:6], refs[6:]
    recv_hbm, refs = refs[: n_seq // 2], refs[n_seq // 2 :]
    outs, serial_grad_hbm, d_normed_hbm, refs = refs[:4], refs[4], refs[5], refs[6:]
    recv_ref, qkv_ref, trans_ref, w_ref, xhat_ref, normed_ref, attn_ref, refs = *refs[:7], refs[7:]
    sums, refs = refs[:4], refs[4:]
    serial_grad, d_normed_ref, d_attn, d_attn_t, d_qkv, gain_column, sems = refs
    width = w_proj_ref.shape[0]
    rows = xhat_ref.shape[0]
    capacity = recv_ref.shape[0] // n_seq
    head = width // HEADS
    pair = 2 * head
    me = me_ref[0]
    chips = n_seq // 2
    recv_parts = [recv_ref.at[pl.ds(2 * j * capacity, 2 * capacity)] for j in range(chips)]
    loads = [
        pltpu.make_async_copy(source, target, sems.at[i])
        for i, (source, target) in enumerate(
            (
                *zip(recv_hbm, recv_parts),
                (qkv_hbm, qkv_ref),
                (trans_hbm, trans_ref),
                (normed_hbm, normed_ref),
                (w_hbm, w_ref),
                (xhat_hbm, xhat_ref),
                (attn_hbm, attn_ref),
            )
        )
    ]
    saves = [
        pltpu.make_async_copy(source, target, sems.at[6 + chips + i])
        for i, (source, target) in enumerate(
            [*zip(sums, outs), (serial_grad, serial_grad_hbm), (d_normed_ref, d_normed_hbm)]
        )
    ]

    for load in loads:
        load.start()
    place = hot(iota((rows, n_seq * capacity), 0) == pos_ref[...])
    for load in loads[:chips]:
        load.wait()
    grads = mm(place, recv_ref[...]).astype(BF16)
    serial_grad[...] = grads
    saves[4].start()
    d_attn[...] = mm(grads, w_proj_ref[...], NT).astype(BF16)
    d_attn_t[...] = mm(w_proj_ref[...], grads, NT).astype(BF16)
    for load in loads[chips : chips + 2]:
        load.wait()

    zero = jnp.zeros((head, rows), BF16)
    first = iota((rows, pair), 1) < head

    def alone(both, j):
        part = both[j * head : (j + 1) * head]
        return jnp.concatenate([part, zero] if j == 0 else [zero, part], axis=0)

    for step in range(HEADS // 2):
        lo = step * pair
        queries = qkv_ref[:, pl.ds(lo, pair)]
        values = qkv_ref[:, pl.ds(2 * width + lo, pair)]
        d_att_t = d_attn_t[pl.ds(lo, pair), :] * BF16(0.125)
        d_att = d_attn[:, pl.ds(lo, pair)]
        keys = qkv_ref[:, pl.ds(width + lo, pair)]
        query_t = trans_ref[pl.ds(lo, pair), :] * BF16(0.125)
        d_q, d_k, d_v = [], [], []
        for j in range(2):
            top = stats_ref[pl.ds(2 * step + j, 1), :]
            share = stats_ref[pl.ds(HEADS + 2 * step + j, 1), :]
            probs = jnp.exp(mm(keys, alone(query_t, j)) - top) * share
            d_probs = mm(values, alone(d_att_t, j))
            total = jnp.sum(d_probs * probs, axis=0, keepdims=True)
            d_scores = (probs * (d_probs - total)).astype(BF16)
            k_t = trans_ref[pl.ds(width + lo + j * head, head), :]
            d_q.append(mm(k_t, d_scores))
            d_k.append(mm(d_scores, queries))
            d_v.append(mm(probs.astype(BF16), d_att))
        d_qkv[:, pl.ds(lo, pair)] = jnp.transpose(jnp.concatenate(d_q, axis=0)).astype(BF16)
        d_qkv[:, pl.ds(width + lo, pair)] = jnp.where(
            first, d_k[0], d_k[1]
        ).astype(BF16)
        d_qkv[:, pl.ds(2 * width + lo, pair)] = jnp.where(
            first, d_v[0], d_v[1]
        ).astype(BF16)

    for load in loads[chips + 2 :]:
        load.wait()
    d_normed = mm(d_qkv[...], w_ref[...], NT)
    d_normed_ref[...] = d_normed
    saves[5].start()
    gain_row = jnp.sum(d_normed * xhat_ref[...], axis=0, keepdims=True)
    gain_column[...] = jnp.transpose(jnp.broadcast_to(gain_row, (LANES, width)))
    eighth = width // 8
    odd = lax.bitwise_and(me, 1)

    def sides(even_bit, odd_bit):
        even_side = lax.bitwise_and(lax.shift_right_logical(me, even_bit), 1)
        odd_side = lax.bitwise_and(lax.shift_right_logical(me, odd_bit), 1)
        mine = jnp.where(odd == 1, odd_side, even_side)
        return mine, even_side + odd_side - mine

    (mine, other), (mine_next, other_next) = (sides(*bits) for bits in chip_bits)
    starts = (
        ((1 - odd) * 2 + 1 - other, other_next),
        ((1 - odd) * 2 + other, other_next),
        (odd * 2 + 1 - mine, mine_next),
        (odd * 2 + mine, mine_next),
    )
    order = [
        pl.ds(pl.multiple_of((start * 2 + half) * eighth, eighth), eighth)
        for start, side in starts
        for half in (1 - side, side)
    ]
    for i in (0, 2):
        parts = order[2 * i : 2 * i + 4]
        of_qkv = mm(jnp.concatenate([normed_ref[part, :] for part in parts], axis=0), d_qkv[...])
        of_proj = mm(jnp.concatenate([attn_ref[part, :] for part in parts], axis=0), serial_grad[...])
        of_gain = jnp.concatenate([gain_column[part, :] for part in parts], axis=0)
        for j in range(2):
            lines = slice(2 * j * eighth, 2 * (j + 1) * eighth)
            sums[i + j][:, : 3 * width] = of_qkv[lines]
            sums[i + j][:, 3 * width : 4 * width] = of_proj[lines]
            sums[i + j][:, 4 * width :] = of_gain[lines]
            saves[i + j].start()
    for save in saves:
        save.wait()


def residual_kernel(pos_ref, gain_ref, inv_ref, xhat_ref, serial_grad_ref, d_normed_ref, *outs):
    xhat = xhat_ref[...]
    rows = xhat.shape[0]
    scaled = d_normed_ref[...] * gain_ref[...]
    residual = inv_ref[:, 0:1] * (
        scaled
        - jnp.mean(scaled, axis=1, keepdims=True)
        - xhat * jnp.mean(scaled * xhat, axis=1, keepdims=True)
    )
    serial_dx = (serial_grad_ref[...].astype(F32) + residual).astype(BF16)
    returned = mm(column_hot(pos_ref[...], rows), serial_dx).astype(BF16)
    size = outs[0].shape[0]
    for j, out in enumerate(outs):
        out[...] = returned[j * size : (j + 1) * size]


def cross_kernel(*refs):
    size = refs[0].shape[0] // 2
    for j, ref in enumerate(refs[:-1]):
        refs[-1][j * size : (j + 1) * size, :] = ref[size:, :]


def unpack_kernel(slot_ref, cross_ref, *refs):
    size = refs[0].shape[0] // 2
    blocks = []
    for j, ref in enumerate(refs[:-1]):
        blocks += [ref[:size, :], cross_ref[j * size : (j + 1) * size, :]]
    values = jnp.concatenate(blocks, axis=0)
    refs[-1][...] = mm(column_hot(slot_ref[...], values.shape[0]), values).astype(BF16)


def split_kernel(side_ref, sums_ref, *refs):
    qkv_out, proj_out, gain_out = refs[-3:]
    width = proj_out.shape[1]
    qkv_out[...] = sums_ref[:, : 3 * width].astype(F32)
    proj_out[...] = sums_ref[:, 3 * width : 4 * width].astype(F32)
    gain_out[...] = jnp.transpose(sums_ref[:, 4 * width :].astype(F32))[0:1]


def exponent_of(largest):
    return jnp.clip(jnp.ceil(jnp.log(jnp.maximum(largest, 1e-30)) * 1.4426950408889634), -100.0, 120.0)


def encode(out_ref, total):
    width = total.shape[1] - LANES
    body, gain = total[:, :width], total[:, width : width + 1]
    exponent = exponent_of(jnp.max(jnp.abs(body), axis=1, keepdims=True))
    codes = jnp.round(body * (jnp.exp2(-exponent) * CODE_MAX))
    out_ref[:, :width] = codes.astype(jnp.int32).astype(jnp.int16)
    gain_exponent = exponent_of(jnp.abs(gain))
    scaled = gain * (jnp.exp2(-gain_exponent) * CODE_MAX)
    high = jnp.round(scaled)
    low = jnp.round((scaled - high) * DIGIT)
    lane = iota((total.shape[0], LANES), 1)
    tail = jnp.where(lane == 0, high, jnp.where(lane == 1, low, jnp.where(lane == 2, gain_exponent, exponent)))
    out_ref[:, width:] = tail.astype(jnp.int32).astype(jnp.int16)


def decode(codes):
    values = codes.astype(jnp.int32).astype(F32)
    width = values.shape[1] - LANES
    tail = values[:, width:]
    body = values[:, :width] * (jnp.exp2(tail[:, 3:4]) * (1.0 / CODE_MAX))
    gain = (tail[:, 0:1] + tail[:, 1:2] * (1.0 / DIGIT)) * (jnp.exp2(tail[:, 2:3]) * (1.0 / CODE_MAX))
    return jnp.concatenate([body, jnp.broadcast_to(gain, tail.shape)], axis=1)


def total_of(terms, part):
    half = terms[0].shape[0] // 2
    rows = {"all": slice(None), "first": slice(0, half), "second": slice(half, 2 * half)}[part]
    values = [ref[rows, :] for ref in terms]
    return functools.reduce(jnp.add, [decode(v) if v.dtype == jnp.int16 else v for v in values])


def message_kernel(part, *refs):
    encode(refs[-1], total_of(refs[:-1], part))


def sum_kernel(parts, *refs):
    refs[-1][...] = functools.reduce(jnp.add, [total_of([ref], p) for ref, p in zip(refs, parts)])


def pieces_kernel(parts, n_dp, plane_ref, *refs):
    terms, own, messages, total = refs[: len(parts)], refs[len(parts)], refs[len(parts) + 1 : -1], refs[-1]
    total[...] = functools.reduce(jnp.add, [total_of([ref], p) for ref, p in zip(terms, parts)])
    size = own.shape[0]

    def rows_of(distance):
        start = lax.bitwise_xor(plane_ref[0], distance) * size
        return total[pl.ds(pl.multiple_of(start, size), size), :]

    for k in range(1, n_dp):
        encode(messages[k - 1], rows_of(k))
    own[...] = rows_of(0)


def finish_kernel(*refs):
    refs[-1][...] = total_of(refs[:-1], "all").astype(BF16)


def whole(shape):
    return pl.BlockSpec(shape, lambda *_: (0,) * len(shape), pipeline_mode=pl.Buffered(1))


def params(mib):
    return pltpu.CompilerParams(vmem_limit_bytes=mib * MIB)


def shape_of(shape, dtype):
    return jax.ShapeDtypeStruct(shape, dtype)


def by_distance(blocks, axis):
    count = len(blocks)
    return [blocks[0]] + [
        lax.ppermute(blocks[k], axis, [(i, i ^ k) for i in range(count)]) for k in range(1, count)
    ]


def by_chip(messages):
    count = 2 * len(messages)
    return [messages[0]] + [
        lax.ppermute(messages[j], "seq", [(i, i ^ (2 * j)) for i in range(count)])
        for j in range(1, len(messages))
    ]


def chip_orders(n_seq):
    bits = list(range(1, n_seq.bit_length() - 1))
    middle = len(bits) // 2
    return bits, bits[middle:] + bits[:middle]


def chip_steps():
    n_seq, me = lax.axis_size("seq"), lax.axis_index("seq")
    odd = lax.bitwise_and(me, 1) == 1

    def side(bit):
        return lax.bitwise_and(lax.shift_right_logical(me, jnp.asarray(bit, me.dtype)), 1)

    steps = []
    for even_bit, odd_bit in zip(*chip_orders(n_seq)):
        pairs = [(i, i ^ (1 << (odd_bit if i & 1 else even_bit))) for i in range(n_seq)]
        steps.append((pairs, jnp.where(odd, side(odd_bit), side(even_bit))))
    return steps


def piece(terms, index, count):
    size = terms[0].shape[0] // count
    return functools.reduce(jnp.add, [lax.dynamic_slice_in_dim(t, index * size, size) for t in terms])


def core_pairs():
    return [(i, i ^ 1) for i in range(lax.axis_size("seq"))]


def small_kernel(kernel, outs, operands, scalars=0, scratch=(), name="sum"):
    in_smem = pl.BlockSpec(memory_space=pltpu.SMEM)
    in_vmem = pl.BlockSpec(memory_space=pltpu.VMEM)
    touched = sum(x.size * x.dtype.itemsize for x in (*operands, *outs))
    return pl.pallas_call(
        kernel,
        out_shape=outs,
        in_specs=[in_smem] * scalars + [in_vmem] * (len(operands) - scalars),
        out_specs=[in_vmem] * len(outs),
        scratch_shapes=list(scratch),
        compiler_params=params(20),
        cost_estimate=pl.CostEstimate(flops=2 * touched, bytes_accessed=touched, transcendentals=0),
        name=name,
    )(*operands)


def message(terms, part, name):
    rows, width = terms[0].shape
    rows = rows if part == "all" else rows // 2
    return small_kernel(
        functools.partial(message_kernel, part), [shape_of((rows, width), jnp.int16)], terms, name=name
    )[0]


def first_step(quarters, steps):
    pass_on, pass_keep, own_on, own_keep = quarters
    got_on = lax.ppermute(pass_on, "seq", core_pairs())
    got_keep = lax.ppermute(pass_keep, "seq", core_pairs())
    sent = message([own_on, got_on], "all", "code_first")
    return [own_keep, got_keep, lax.ppermute(sent, "seq", steps[0][0])]


def second_step(terms, steps):
    sent = message(terms, "first", "code_second")
    return terms, lax.ppermute(sent, "seq", steps[1][0])


def halves_of_plain(part, steps):
    for pairs, side in steps:
        got = lax.ppermute(piece([part], 1 - side, 2), "seq", pairs)
        part = piece([part], side, 2) + got
    return part


def reduce_over_planes(terms, got, steps):
    n_dp, plane = lax.axis_size("dp"), lax.axis_index("dp")
    rows, width = got.shape
    parts = ["second"] * len(terms) + ["all"]
    if len(steps) > 2 or rows // n_dp % 16:
        part = small_kernel(
            functools.partial(sum_kernel, parts), [shape_of((rows, width), F32)], [*terms, got]
        )[0]
        part = halves_of_plain(part, steps[2:])
        pieces = [piece([part], lax.bitwise_xor(plane, k), n_dp) for k in range(n_dp)]
        return functools.reduce(jnp.add, by_distance(pieces, "dp")).astype(BF16)
    size = rows // n_dp
    own, *sent = small_kernel(
        functools.partial(pieces_kernel, parts, n_dp),
        [shape_of((size, width), F32)] + [shape_of((size, width), jnp.int16)] * (n_dp - 1),
        [jnp.reshape(plane.astype(jnp.int32), (1,)), *terms, got],
        scalars=1,
        scratch=[pltpu.VMEM((rows, width), F32)],
        name="code_planes",
    )
    arrived = by_distance([own] + sent, "dp")
    return small_kernel(finish_kernel, [shape_of((size, width), BF16)], arrived, name="finish")[0]


def share_over_planes(part):
    n_dp, plane = lax.axis_size("dp"), lax.axis_index("dp")
    shares = jnp.stack(by_distance([part] * n_dp, "dp"))
    return jnp.concatenate(
        [lax.dynamic_index_in_dim(shares, lax.bitwise_xor(plane, p), keepdims=False) for p in range(n_dp)],
        axis=0,
    )


def share_in_plane(part, steps):
    for pairs, side in reversed(steps):
        other = lax.ppermute(part, "seq", pairs)
        part = jnp.where(
            side == 0, jnp.concatenate([part, other], axis=0), jnp.concatenate([other, part], axis=0)
        )
    return part


def write_half(side, sums, outs=()):
    half, width = sums.shape[0], (sums.shape[1] - LANES) // 4
    return pl.pallas_call(
        split_kernel,
        grid_spec=pltpu.PrefetchScalarGridSpec(
            num_scalar_prefetch=1,
            grid=(2,),
            in_specs=[pl.BlockSpec((half // 2, sums.shape[1]), lambda i, s: (i, 0))]
            + [pl.BlockSpec(memory_space=pl.ANY)] * len(outs),
            out_specs=[
                pl.BlockSpec((half // 2, 3 * width), lambda i, s: (2 * s[0] + i, 0)),
                pl.BlockSpec((half // 2, width), lambda i, s: (2 * s[0] + i, 0)),
                pl.BlockSpec((1, half // 2), lambda i, s: (0, 2 * s[0] + i)),
            ],
        ),
        out_shape=(
            shape_of((2 * half, 3 * width), F32),
            shape_of((2 * half, width), F32),
            shape_of((1, 2 * half), F32),
        ),
        input_output_aliases={2 + i: i for i in range(len(outs))},
        compiler_params=params(20),
        cost_estimate=pl.CostEstimate(flops=0, bytes_accessed=4 * MIB, transcendentals=0),
        name="split",
    )(side, sums, *outs)


def per_device(points, cotangent, dest, w_qkv, w_proj, gain):
    feats = points[0]
    grads = cotangent[0]
    rows, width = feats.shape
    n_seq = lax.axis_size("seq")
    capacity = 2 * (rows // n_seq)
    slots = n_seq * capacity
    block = capacity + EXTRA
    pairs = HEADS // 2
    pair = width // pairs
    sum_shape = (width // 4, 4 * width + LANES)
    me = jnp.reshape(lax.axis_index("seq").astype(jnp.int32), (1,))
    gain_row = gain.reshape(1, width)
    in_smem = pl.BlockSpec(memory_space=pltpu.SMEM)
    in_vmem = pl.BlockSpec(memory_space=pltpu.VMEM)
    in_hbm = pl.BlockSpec(memory_space=pl.ANY)
    stay_hbm = pl.BlockSpec(memory_space=pltpu.HBM)

    slot, same, cross, *feats_sent = pl.pallas_call(
        functools.partial(pack_kernel, n_seq, capacity),
        out_shape=[shape_of((1, rows), jnp.int32)]
        + [shape_of((slots // 2, width), BF16)] * 2
        + [shape_of((block, width), BF16)] * n_seq,
        in_specs=[in_smem] + [stay_hbm] * 3,
        out_specs=[in_vmem] * (3 + n_seq),
        scratch_shapes=[
            pltpu.VMEM((1, rows), jnp.int32),
            pltpu.VMEM((rows, width), BF16),
            pltpu.VMEM((rows, width), BF16),
            pltpu.SemaphoreType.DMA((3,)),
        ],
        compiler_params=params(60),
        cost_estimate=pl.CostEstimate(
            flops=4 * slots * rows * width, bytes_accessed=4 * MIB, transcendentals=0
        ),
        name="pack",
    )(me, dest, feats, grads)
    feats_got = by_distance(feats_sent, "seq")
    messages = small_kernel(
        functools.partial(pair_kernel, capacity),
        [shape_of((2 * capacity, width), BF16)] * (n_seq // 2),
        [same, lax.ppermute(cross, "seq", core_pairs())],
        name="pair_up",
    )
    feats_got, messages = lax.optimization_barrier((feats_got, messages))
    grads_got = by_chip(messages)

    pos, xhat, inv, normed, qkv, trans, attn_t, stats = pl.pallas_call(
        functools.partial(forward_kernel, n_seq, capacity),
        grid=(1,),
        out_shape=(
            shape_of((1, slots), jnp.int32),
            shape_of((rows, width), F32),
            shape_of((rows, LANES), F32),
            shape_of((rows, width), BF16),
            shape_of((rows, 3 * width), BF16),
            shape_of((2 * width, rows), BF16),
            shape_of((width, rows), BF16),
            shape_of((2 * HEADS, rows), F32),
        ),
        in_specs=[in_hbm, whole((1, width))] + [whole((block, width))] * n_seq,
        out_specs=[whole((1, slots))]
        + [in_hbm] * 5
        + [whole((width, rows)), whole((2 * HEADS, rows))],
        scratch_shapes=[
            pltpu.VMEM((width, 3 * width), BF16),
            pltpu.VMEM((rows, width), F32),
            pltpu.VMEM((rows, LANES), F32),
            pltpu.VMEM((rows, width), BF16),
            pltpu.VMEM((rows, 3 * width), BF16),
            pltpu.VMEM((3 * width, rows), BF16),
            pltpu.SemaphoreType.DMA((6,)),
        ],
        compiler_params=params(60),
        cost_estimate=pl.CostEstimate(
            flops=6 * rows * width * width + 8 * HEADS * rows * rows * pair,
            bytes_accessed=16 * MIB,
            transcendentals=HEADS * rows * rows,
        ),
        name="forward",
    )(w_qkv, gain_row, *feats_got)

    chip_bits = tuple(zip(*chip_orders(n_seq)))[:2]
    *quarters, serial_grad, d_normed = pl.pallas_call(
        functools.partial(backward_kernel, n_seq, chip_bits),
        grid=(1,),
        out_shape=[shape_of(sum_shape, F32)] * 4
        + [shape_of((rows, width), BF16), shape_of((rows, width), F32)],
        in_specs=[
            in_smem,
            whole((1, slots)),
            whole((width, width)),
            whole((2 * HEADS, rows)),
        ]
        + [in_hbm] * (6 + n_seq // 2),
        out_specs=[in_hbm] * 6,
        scratch_shapes=[
            pltpu.VMEM((slots, width), BF16),
            pltpu.VMEM((rows, 3 * width), BF16),
            pltpu.VMEM((2 * width, rows), BF16),
            pltpu.VMEM((width, 3 * width), BF16),
            pltpu.VMEM((rows, width), F32),
            pltpu.VMEM((rows, width), BF16),
            pltpu.VMEM((width, rows), BF16),
        ]
        + [pltpu.VMEM(sum_shape, F32)] * 4
        + [
            pltpu.VMEM((rows, width), BF16),
            pltpu.VMEM((rows, width), F32),
            pltpu.VMEM((rows, width), BF16),
            pltpu.VMEM((width, rows), BF16),
            pltpu.VMEM((rows, 3 * width), BF16),
            pltpu.VMEM((width, LANES), F32),
            pltpu.SemaphoreType.DMA((12 + n_seq // 2,)),
        ],
        compiler_params=params(60),
        cost_estimate=pl.CostEstimate(
            flops=12 * rows * width * width + 10 * HEADS * rows * rows * pair,
            bytes_accessed=16 * MIB,
            transcendentals=HEADS * rows * rows,
        ),
        name="backward",
    )(me, pos, w_proj, stats, qkv, trans, w_qkv, xhat, normed, attn_t, *grads_got)

    steps = chip_steps()
    terms = first_step(quarters, steps)
    back = small_kernel(
        residual_kernel,
        [shape_of((2 * capacity, width), BF16)] * (n_seq // 2),
        [pos, gain_row, inv, xhat, serial_grad, d_normed],
        name="residual",
    )
    terms, got = second_step(terms, steps)
    got, back = lax.optimization_barrier((got, back))
    returned = by_chip(back)
    part, returned = lax.optimization_barrier((reduce_over_planes(terms, got, steps), returned))
    cross = small_kernel(
        cross_kernel, [shape_of((slots // 2, width), BF16)], returned, name="for_core_pair"
    )[0]
    own = share_in_plane(share_over_planes(part), steps)
    grad_local = small_kernel(
        unpack_kernel,
        [shape_of((rows, width), BF16)],
        [slot, lax.ppermute(cross, "seq", core_pairs()), *returned],
        name="unpack",
    )[0]
    own, grad_local = lax.optimization_barrier((own, grad_local))
    other = lax.ppermute(own, "seq", core_pairs())
    side = lax.bitwise_and(me, 1)
    outs = write_half(side, own)
    grad_qkv, grad_proj, gain_grad = write_half(1 - side, other, outs)
    return (grad_local[None], grad_qkv, grad_proj, gain_grad[0])


def solution(mesh):
    return jax.shard_map(
        per_device,
        mesh=mesh,
        in_specs=(P("dp", "seq", None), P("dp", "seq", None), P("dp", "seq"), P(), P(), P()),
        out_specs=(P("dp", "seq", None), P(), P(), P()),
        check_vma=False,
    )
```

```python
import functools

import jax
import jax.numpy as jnp
from jax import lax
from jax.experimental import pallas as pl
from jax.experimental.pallas import tpu as pltpu
from jax.sharding import PartitionSpec as P

HEADS = 8
PATCH = 512
EXTRA = 16
LANES = 128
CODE_MAX = 32000.0
DIGIT = 60000.0
MIB = 1024 * 1024
F32 = jnp.float32
BF16 = jnp.bfloat16
NN = (((1,), (0,)), ((), ()))
NT = (((1,), (1,)), ((), ()))


def mm(lhs, rhs, dims=NN):
    return lax.dot_general(lhs, rhs, dims, preferred_element_type=F32)


def iota(shape, dim):
    return lax.broadcasted_iota(jnp.int32, shape, dim)


def hot(mask):
    return jnp.where(mask, jnp.float32(1), jnp.float32(0)).astype(BF16)


def column_hot(row, count):
    size = row.shape[1]
    column = jnp.transpose(jnp.broadcast_to(row, (LANES, size)))
    lane = iota((size, LANES), 1)
    return jnp.concatenate([hot(column == lane + j * LANES) for j in range(count // LANES)], axis=1)


def pack_kernel(
    n_seq, capacity, me_ref, dest_hbm, feats_hbm, grads_hbm, slot_out, same_out, cross_out, *refs
):
    outs, (dest_ref, feats_ref, grads_ref, sems) = refs[:n_seq], refs[n_seq:]
    rows, width = feats_ref.shape
    slots = n_seq * capacity
    loads = [
        pltpu.make_async_copy(source, target, sems.at[i])
        for i, (source, target) in enumerate(
            ((dest_hbm, dest_ref), (feats_hbm, feats_ref), (grads_hbm, grads_ref))
        )
    ]
    for load in loads:
        load.start()
    loads[0].wait()
    shift = rows.bit_length() - 1
    places = dest_ref[...]
    distance = lax.bitwise_xor(lax.shift_right_logical(places, shift), me_ref[0])
    within = lax.bitwise_and(places, rows - 1) + 1
    member = iota((n_seq, rows), 0) == distance
    upper = hot(iota((rows, rows), 0) <= iota((rows, rows), 1))
    counts = mm(hot(member), upper)
    rank = jnp.sum(jnp.where(member, counts, 0.0), axis=0, keepdims=True).astype(jnp.int32) - 1
    slot = distance * capacity + rank
    slot_out[...] = slot
    select = hot(iota((slots, rows), 0) == slot)
    loads[1].wait()
    feats = mm(select, feats_ref[...]).astype(BF16)
    upper_half = slot >= width
    high = lax.shift_right_logical(within, 8).astype(F32)
    low = lax.bitwise_and(within, 255).astype(F32)
    line = iota((n_seq * EXTRA, rows), 0)
    kind = lax.bitwise_and(line, EXTRA - 1)
    digit = jnp.where(kind < 2, high, low)
    wanted = (
        (lax.shift_right_logical(line, EXTRA.bit_length() - 1) == distance)
        & (kind < 4)
        & ((lax.bitwise_and(kind, 1) == 1) == upper_half)
    )
    digits = jnp.where(wanted, digit, 0.0).astype(BF16)
    spread = hot(iota((width, rows), 0) == lax.bitwise_and(slot, width - 1))
    position = mm(digits, spread, NT).astype(BF16)
    for d in range(n_seq):
        outs[d][:capacity, :] = feats[d * capacity : (d + 1) * capacity]
        outs[d][capacity:, :] = position[d * EXTRA : (d + 1) * EXTRA]
    loads[2].wait()
    grads = mm(select, grads_ref[...]).astype(BF16)
    for j in range(n_seq // 2):
        lines = slice(j * capacity, (j + 1) * capacity)
        same_out[lines, :] = grads[2 * j * capacity : (2 * j + 1) * capacity]
        cross_out[lines, :] = grads[(2 * j + 1) * capacity : (2 * j + 2) * capacity]


def pair_kernel(capacity, same_ref, cross_ref, *outs):
    for j, out in enumerate(outs):
        lines = slice(j * capacity, (j + 1) * capacity)
        out[:capacity, :] = same_ref[lines, :]
        out[capacity:, :] = cross_ref[lines, :]


def forward_kernel(n_seq, capacity, w_hbm, gain_ref, *refs):
    recv, refs = refs[:n_seq], refs[n_seq:]
    pos_out, xhat_hbm, inv_hbm, normed_hbm, qkv_hbm, trans_hbm, attn_out, stats_out = refs[:8]
    w_ref, xhat_ref, inv_ref, normed_ref, qkv_ref, trans, sems = refs[8:]
    width = w_ref.shape[0]
    rows = xhat_ref.shape[0]
    head = width // HEADS
    pair = 2 * head
    w_copy = pltpu.make_async_copy(w_hbm, w_ref, sems.at[0])
    saves = [
        pltpu.make_async_copy(source, target, sems.at[1 + i])
        for i, (source, target) in enumerate(
            (
                (xhat_ref, xhat_hbm),
                (inv_ref, inv_hbm),
                (normed_ref, normed_hbm),
                (qkv_ref, qkv_hbm),
                (trans.at[pl.ds(0, 2 * width)], trans_hbm),
            )
        )
    ]

    w_copy.start()
    tile = recv[0][capacity:, :].astype(F32)
    for s in range(1, n_seq):
        tile = tile + recv[s][capacity:, :].astype(F32)
    high = jnp.concatenate([tile[0:1], tile[1:2]], axis=1)
    low = jnp.concatenate([tile[2:3], tile[3:4]], axis=1)
    pos = (high * 256.0 + low).astype(jnp.int32) - 1
    pos_out[...] = pos
    place = hot(iota((rows, n_seq * capacity), 0) == pos)
    values = jnp.concatenate([recv[s][:capacity, :] for s in range(n_seq)], axis=0)
    feats = mm(place, values)
    centered = feats - jnp.mean(feats, axis=1, keepdims=True)
    inv = lax.rsqrt(jnp.mean(centered * centered, axis=1, keepdims=True) + 1e-05)
    xhat = centered * inv
    xhat_ref[...] = xhat
    inv_ref[...] = jnp.broadcast_to(inv, inv_ref.shape)
    scaled = xhat * gain_ref[...]
    normed = scaled.astype(BF16)
    normed_ref[...] = jnp.transpose(scaled).astype(BF16)
    w_copy.wait()
    qkv = mm(normed, w_ref[...])
    qkv_ref[...] = qkv.astype(BF16)
    trans[...] = jnp.transpose(qkv).astype(BF16)
    for save in saves:
        save.start()

    for step in range(HEADS // 2):
        lo = step * pair
        keys = qkv_ref[:, pl.ds(width + lo, pair)]
        query_t = trans[pl.ds(lo, pair), :] * BF16(0.125)
        zero = jnp.zeros((head, rows), BF16)
        for j in range(2):
            part = query_t[j * head : (j + 1) * head]
            part = jnp.concatenate([part, zero] if j == 0 else [zero, part], axis=0)
            scores = mm(keys, part)
            top = jnp.max(scores, axis=0, keepdims=True)
            expo = jnp.exp(scores - top)
            share = 1.0 / jnp.sum(expo, axis=0, keepdims=True)
            probs = expo * share
            stats_out[pl.ds(2 * step + j, 1), :] = top
            stats_out[pl.ds(HEADS + 2 * step + j, 1), :] = share
            values_t = trans[pl.ds(2 * width + lo + j * head, head), :]
            attn_out[pl.ds(lo + j * head, head), :] = mm(values_t, probs.astype(BF16)).astype(BF16)

    for save in saves:
        save.wait()


def backward_kernel(n_seq, chip_bits, me_ref, pos_ref, w_proj_ref, stats_ref, *refs):
    (qkv_hbm, trans_hbm, w_hbm, xhat_hbm, normed_hbm, attn_hbm), refs = refs[:6], refs[6:]
    recv_hbm, refs = refs[: n_seq // 2], refs[n_seq // 2 :]
    outs, serial_grad_hbm, d_normed_hbm, refs = refs[:4], refs[4], refs[5], refs[6:]
    recv_ref, qkv_ref, trans_ref, w_ref, xhat_ref, normed_ref, attn_ref, refs = *refs[:7], refs[7:]
    sums, refs = refs[:4], refs[4:]
    serial_grad, d_normed_ref, d_attn, d_attn_t, d_qkv, gain_column, sems = refs
    width = w_proj_ref.shape[0]
    rows = xhat_ref.shape[0]
    capacity = recv_ref.shape[0] // n_seq
    head = width // HEADS
    pair = 2 * head
    me = me_ref[0]
    chips = n_seq // 2
    recv_parts = [recv_ref.at[pl.ds(2 * j * capacity, 2 * capacity)] for j in range(chips)]
    loads = [
        pltpu.make_async_copy(source, target, sems.at[i])
        for i, (source, target) in enumerate(
            (
                *zip(recv_hbm, recv_parts),
                (qkv_hbm, qkv_ref),
                (trans_hbm, trans_ref),
                (normed_hbm, normed_ref),
                (w_hbm, w_ref),
                (xhat_hbm, xhat_ref),
                (attn_hbm, attn_ref),
            )
        )
    ]
    body, tail = pl.ds(0, 4 * width), pl.ds(4 * width, LANES)
    saves = [
        pltpu.make_async_copy(source, target, sems.at[6 + chips + i])
        for i, (source, target) in enumerate(
            [
                *[(source.at[:, body], target.at[:, body]) for source, target in zip(sums, outs)],
                (serial_grad, serial_grad_hbm),
                (d_normed_ref, d_normed_hbm),
                *[(source.at[:, tail], target.at[:, tail]) for source, target in zip(sums, outs)],
            ]
        )
    ]

    for load in loads:
        load.start()
    place = hot(iota((rows, n_seq * capacity), 0) == pos_ref[...])
    for load in loads[:chips]:
        load.wait()
    grads = mm(place, recv_ref[...]).astype(BF16)
    serial_grad[...] = grads
    saves[4].start()
    d_attn[...] = mm(grads, w_proj_ref[...], NT).astype(BF16)
    d_attn_t[...] = mm(w_proj_ref[...], grads, NT).astype(BF16)
    for load in loads[chips : chips + 2]:
        load.wait()

    zero = jnp.zeros((head, rows), BF16)
    first = iota((rows, pair), 1) < head

    def alone(both, j):
        part = both[j * head : (j + 1) * head]
        return jnp.concatenate([part, zero] if j == 0 else [zero, part], axis=0)

    for step in range(HEADS // 2):
        lo = step * pair
        queries = qkv_ref[:, pl.ds(lo, pair)]
        values = qkv_ref[:, pl.ds(2 * width + lo, pair)]
        d_att_t = d_attn_t[pl.ds(lo, pair), :] * BF16(0.125)
        d_att = d_attn[:, pl.ds(lo, pair)]
        keys = qkv_ref[:, pl.ds(width + lo, pair)]
        query_t = trans_ref[pl.ds(lo, pair), :] * BF16(0.125)
        d_q, d_k, d_v = [], [], []
        for j in range(2):
            top = stats_ref[pl.ds(2 * step + j, 1), :]
            share = stats_ref[pl.ds(HEADS + 2 * step + j, 1), :]
            probs = jnp.exp(mm(keys, alone(query_t, j)) - top) * share
            d_probs = mm(values, alone(d_att_t, j))
            total = jnp.sum(d_probs * probs, axis=0, keepdims=True)
            d_scores = (probs * (d_probs - total)).astype(BF16)
            k_t = trans_ref[pl.ds(width + lo + j * head, head), :]
            d_q.append(mm(k_t, d_scores))
            d_k.append(mm(d_scores, queries))
            d_v.append(mm(probs.astype(BF16), d_att))
        d_qkv[:, pl.ds(lo, pair)] = jnp.transpose(jnp.concatenate(d_q, axis=0)).astype(BF16)
        d_qkv[:, pl.ds(width + lo, pair)] = jnp.where(
            first, d_k[0], d_k[1]
        ).astype(BF16)
        d_qkv[:, pl.ds(2 * width + lo, pair)] = jnp.where(
            first, d_v[0], d_v[1]
        ).astype(BF16)

    for load in loads[chips + 2 :]:
        load.wait()
    eighth = width // 8
    odd = lax.bitwise_and(me, 1)

    def sides(even_bit, odd_bit):
        even_side = lax.bitwise_and(lax.shift_right_logical(me, even_bit), 1)
        odd_side = lax.bitwise_and(lax.shift_right_logical(me, odd_bit), 1)
        mine = jnp.where(odd == 1, odd_side, even_side)
        return mine, even_side + odd_side - mine

    (mine, other), (mine_next, other_next) = (sides(*bits) for bits in chip_bits)
    starts = (
        ((1 - odd) * 2 + 1 - other, other_next),
        ((1 - odd) * 2 + other, other_next),
        (odd * 2 + 1 - mine, mine_next),
        (odd * 2 + mine, mine_next),
    )
    order = [
        pl.ds(pl.multiple_of((start * 2 + half) * eighth, eighth), eighth)
        for start, side in starts
        for half in (1 - side, side)
    ]
    for i in (0, 2):
        parts = order[2 * i : 2 * i + 4]
        of_qkv = mm(jnp.concatenate([normed_ref[part, :] for part in parts], axis=0), d_qkv[...])
        of_proj = mm(jnp.concatenate([attn_ref[part, :] for part in parts], axis=0), serial_grad[...])
        for j in range(2):
            lines = slice(2 * j * eighth, 2 * (j + 1) * eighth)
            sums[i + j][:, : 3 * width] = of_qkv[lines]
            sums[i + j][:, 3 * width : 4 * width] = of_proj[lines]
            saves[i + j].start()
    d_normed = mm(d_qkv[...], w_ref[...], NT)
    d_normed_ref[...] = d_normed
    saves[5].start()
    gain_row = jnp.sum(d_normed * xhat_ref[...], axis=0, keepdims=True)
    gain_column[...] = jnp.transpose(jnp.broadcast_to(gain_row, (LANES, width)))
    for i in range(4):
        parts = order[2 * i : 2 * i + 2]
        sums[i][:, 4 * width :] = jnp.concatenate([gain_column[part, :] for part in parts], axis=0)
        saves[6 + i].start()
    for save in saves:
        save.wait()


def residual_kernel(
    capacity, pos_ref, gain_ref, inv_ref, xhat_ref, serial_grad_ref, d_normed_ref, same_out, cross_out
):
    xhat = xhat_ref[...]
    rows = xhat.shape[0]
    scaled = d_normed_ref[...] * gain_ref[...]
    residual = inv_ref[:, 0:1] * (
        scaled
        - jnp.mean(scaled, axis=1, keepdims=True)
        - xhat * jnp.mean(scaled * xhat, axis=1, keepdims=True)
    )
    serial_dx = (serial_grad_ref[...].astype(F32) + residual).astype(BF16)
    returned = mm(column_hot(pos_ref[...], rows), serial_dx).astype(BF16)
    for j in range(same_out.shape[0] // capacity):
        lines = slice(j * capacity, (j + 1) * capacity)
        same_out[lines, :] = returned[2 * j * capacity : (2 * j + 1) * capacity]
        cross_out[lines, :] = returned[(2 * j + 1) * capacity : (2 * j + 2) * capacity]


def unpack_kernel(slot_ref, *refs):
    values = jnp.concatenate([ref[...] for ref in refs[:-1]], axis=0)
    refs[-1][...] = mm(column_hot(slot_ref[...], values.shape[0]), values).astype(BF16)


def split_kernel(side_ref, sums_ref, *refs):
    qkv_out, proj_out, gain_out = refs[-3:]
    width = proj_out.shape[1]
    qkv_out[...] = sums_ref[:, : 3 * width].astype(F32)
    proj_out[...] = sums_ref[:, 3 * width : 4 * width].astype(F32)
    gain_out[...] = jnp.transpose(sums_ref[:, 4 * width :].astype(F32))[0:1]


def exponent_of(largest):
    return jnp.clip(jnp.ceil(jnp.log(jnp.maximum(largest, 1e-30)) * 1.4426950408889634), -100.0, 120.0)


def encode(out_ref, total):
    width = total.shape[1] - LANES
    body, gain = total[:, :width], total[:, width : width + 1]
    exponent = exponent_of(jnp.max(jnp.abs(body), axis=1, keepdims=True))
    codes = jnp.round(body * (jnp.exp2(-exponent) * CODE_MAX))
    out_ref[:, :width] = codes.astype(jnp.int32).astype(jnp.int16)
    gain_exponent = exponent_of(jnp.abs(gain))
    scaled = gain * (jnp.exp2(-gain_exponent) * CODE_MAX)
    high = jnp.round(scaled)
    low = jnp.round((scaled - high) * DIGIT)
    lane = iota((total.shape[0], LANES), 1)
    tail = jnp.where(lane == 0, high, jnp.where(lane == 1, low, jnp.where(lane == 2, gain_exponent, exponent)))
    out_ref[:, width:] = tail.astype(jnp.int32).astype(jnp.int16)


def decode(codes):
    values = codes.astype(jnp.int32).astype(F32)
    width = values.shape[1] - LANES
    tail = values[:, width:]
    body = values[:, :width] * (jnp.exp2(tail[:, 3:4]) * (1.0 / CODE_MAX))
    gain = (tail[:, 0:1] + tail[:, 1:2] * (1.0 / DIGIT)) * (jnp.exp2(tail[:, 2:3]) * (1.0 / CODE_MAX))
    return jnp.concatenate([body, jnp.broadcast_to(gain, tail.shape)], axis=1)


def total_of(terms, part):
    half = terms[0].shape[0] // 2
    rows = {"all": slice(None), "first": slice(0, half), "second": slice(half, 2 * half)}[part]
    values = [ref[rows, :] for ref in terms]
    return functools.reduce(jnp.add, [decode(v) if v.dtype == jnp.int16 else v for v in values])


def message_kernel(part, *refs):
    encode(refs[-1], total_of(refs[:-1], part))


def sum_kernel(parts, *refs):
    refs[-1][...] = functools.reduce(jnp.add, [total_of([ref], p) for ref, p in zip(refs, parts)])


def pieces_kernel(parts, n_dp, plane_ref, *refs):
    terms, own, messages, total = refs[: len(parts)], refs[len(parts)], refs[len(parts) + 1 : -1], refs[-1]
    total[...] = functools.reduce(jnp.add, [total_of([ref], p) for ref, p in zip(terms, parts)])
    size = own.shape[0]

    def rows_of(distance):
        start = lax.bitwise_xor(plane_ref[0], distance) * size
        return total[pl.ds(pl.multiple_of(start, size), size), :]

    for k in range(1, n_dp):
        encode(messages[k - 1], rows_of(k))
    own[...] = rows_of(0)


def finish_kernel(*refs):
    refs[-1][...] = total_of(refs[:-1], "all").astype(BF16)


def whole(shape):
    return pl.BlockSpec(shape, lambda *_: (0,) * len(shape), pipeline_mode=pl.Buffered(1))


def params(mib):
    return pltpu.CompilerParams(vmem_limit_bytes=mib * MIB)


def shape_of(shape, dtype):
    return jax.ShapeDtypeStruct(shape, dtype)


def by_distance(blocks, axis):
    count = len(blocks)
    return [blocks[0]] + [
        lax.ppermute(blocks[k], axis, [(i, i ^ k) for i in range(count)]) for k in range(1, count)
    ]


def by_chip(messages):
    count = 2 * len(messages)
    return [messages[0]] + [
        lax.ppermute(messages[j], "seq", [(i, i ^ (2 * j)) for i in range(count)])
        for j in range(1, len(messages))
    ]


def chip_orders(n_seq):
    bits = list(range(1, n_seq.bit_length() - 1))
    middle = len(bits) // 2
    return bits, bits[middle:] + bits[:middle]


def chip_steps():
    n_seq, me = lax.axis_size("seq"), lax.axis_index("seq")
    odd = lax.bitwise_and(me, 1) == 1

    def side(bit):
        return lax.bitwise_and(lax.shift_right_logical(me, jnp.asarray(bit, me.dtype)), 1)

    steps = []
    for even_bit, odd_bit in zip(*chip_orders(n_seq)):
        pairs = [(i, i ^ (1 << (odd_bit if i & 1 else even_bit))) for i in range(n_seq)]
        steps.append((pairs, jnp.where(odd, side(odd_bit), side(even_bit))))
    return steps


def piece(terms, index, count):
    size = terms[0].shape[0] // count
    return functools.reduce(jnp.add, [lax.dynamic_slice_in_dim(t, index * size, size) for t in terms])


def core_pairs():
    return [(i, i ^ 1) for i in range(lax.axis_size("seq"))]


def small_kernel(kernel, outs, operands, scalars=0, scratch=(), name="sum"):
    in_smem = pl.BlockSpec(memory_space=pltpu.SMEM)
    in_vmem = pl.BlockSpec(memory_space=pltpu.VMEM)
    touched = sum(x.size * x.dtype.itemsize for x in (*operands, *outs))
    return pl.pallas_call(
        kernel,
        out_shape=outs,
        in_specs=[in_smem] * scalars + [in_vmem] * (len(operands) - scalars),
        out_specs=[in_vmem] * len(outs),
        scratch_shapes=list(scratch),
        compiler_params=params(20),
        cost_estimate=pl.CostEstimate(flops=2 * touched, bytes_accessed=touched, transcendentals=0),
        name=name,
    )(*operands)


def message(terms, part, name):
    rows, width = terms[0].shape
    rows = rows if part == "all" else rows // 2
    return small_kernel(
        functools.partial(message_kernel, part), [shape_of((rows, width), jnp.int16)], terms, name=name
    )[0]


def first_step(quarters, steps):
    pass_on, pass_keep, own_on, own_keep = quarters
    got_on = lax.ppermute(pass_on, "seq", core_pairs())
    got_keep = lax.ppermute(pass_keep, "seq", core_pairs())
    sent = message([own_on, got_on], "all", "code_first")
    return [own_keep, got_keep, lax.ppermute(sent, "seq", steps[0][0])]


def second_step(terms, steps):
    sent = message(terms, "first", "code_second")
    return terms, lax.ppermute(sent, "seq", steps[1][0])


def halves_of_plain(part, steps):
    for pairs, side in steps:
        got = lax.ppermute(piece([part], 1 - side, 2), "seq", pairs)
        part = piece([part], side, 2) + got
    return part


def reduce_over_planes(terms, got, steps):
    n_dp, plane = lax.axis_size("dp"), lax.axis_index("dp")
    rows, width = got.shape
    parts = ["second"] * len(terms) + ["all"]
    if len(steps) > 2 or rows // n_dp % 16:
        part = small_kernel(
            functools.partial(sum_kernel, parts), [shape_of((rows, width), F32)], [*terms, got]
        )[0]
        part = halves_of_plain(part, steps[2:])
        pieces = [piece([part], lax.bitwise_xor(plane, k), n_dp) for k in range(n_dp)]
        return functools.reduce(jnp.add, by_distance(pieces, "dp")).astype(BF16)
    size = rows // n_dp
    own, *sent = small_kernel(
        functools.partial(pieces_kernel, parts, n_dp),
        [shape_of((size, width), F32)] + [shape_of((size, width), jnp.int16)] * (n_dp - 1),
        [jnp.reshape(plane.astype(jnp.int32), (1,)), *terms, got],
        scalars=1,
        scratch=[pltpu.VMEM((rows, width), F32)],
        name="code_planes",
    )
    arrived = by_distance([own] + sent, "dp")
    return small_kernel(finish_kernel, [shape_of((size, width), BF16)], arrived, name="finish")[0]


def share_over_planes(part):
    n_dp, plane = lax.axis_size("dp"), lax.axis_index("dp")
    shares = jnp.stack(by_distance([part] * n_dp, "dp"))
    return jnp.concatenate(
        [lax.dynamic_index_in_dim(shares, lax.bitwise_xor(plane, p), keepdims=False) for p in range(n_dp)],
        axis=0,
    )


def share_in_plane(part, steps):
    for pairs, side in reversed(steps):
        other = lax.ppermute(part, "seq", pairs)
        part = jnp.where(
            side == 0, jnp.concatenate([part, other], axis=0), jnp.concatenate([other, part], axis=0)
        )
    return part


def write_half(side, sums, outs=()):
    half, width = sums.shape[0], (sums.shape[1] - LANES) // 4
    return pl.pallas_call(
        split_kernel,
        grid_spec=pltpu.PrefetchScalarGridSpec(
            num_scalar_prefetch=1,
            grid=(2,),
            in_specs=[pl.BlockSpec((half // 2, sums.shape[1]), lambda i, s: (i, 0))]
            + [pl.BlockSpec(memory_space=pl.ANY)] * len(outs),
            out_specs=[
                pl.BlockSpec((half // 2, 3 * width), lambda i, s: (2 * s[0] + i, 0)),
                pl.BlockSpec((half // 2, width), lambda i, s: (2 * s[0] + i, 0)),
                pl.BlockSpec((1, half // 2), lambda i, s: (0, 2 * s[0] + i)),
            ],
        ),
        out_shape=(
            shape_of((2 * half, 3 * width), F32),
            shape_of((2 * half, width), F32),
            shape_of((1, 2 * half), F32),
        ),
        input_output_aliases={2 + i: i for i in range(len(outs))},
        compiler_params=params(20),
        cost_estimate=pl.CostEstimate(flops=0, bytes_accessed=4 * MIB, transcendentals=0),
        name="split",
    )(side, sums, *outs)


def per_device(points, cotangent, dest, w_qkv, w_proj, gain):
    feats = points[0]
    grads = cotangent[0]
    rows, width = feats.shape
    n_seq = lax.axis_size("seq")
    capacity = 2 * (rows // n_seq)
    slots = n_seq * capacity
    block = capacity + EXTRA
    pairs = HEADS // 2
    pair = width // pairs
    sum_shape = (width // 4, 4 * width + LANES)
    me = jnp.reshape(lax.axis_index("seq").astype(jnp.int32), (1,))
    gain_row = gain.reshape(1, width)
    in_smem = pl.BlockSpec(memory_space=pltpu.SMEM)
    in_vmem = pl.BlockSpec(memory_space=pltpu.VMEM)
    in_hbm = pl.BlockSpec(memory_space=pl.ANY)
    stay_hbm = pl.BlockSpec(memory_space=pltpu.HBM)

    slot, same, cross, *feats_sent = pl.pallas_call(
        functools.partial(pack_kernel, n_seq, capacity),
        out_shape=[shape_of((1, rows), jnp.int32)]
        + [shape_of((slots // 2, width), BF16)] * 2
        + [shape_of((block, width), BF16)] * n_seq,
        in_specs=[in_smem] + [stay_hbm] * 3,
        out_specs=[in_vmem] * (3 + n_seq),
        scratch_shapes=[
            pltpu.VMEM((1, rows), jnp.int32),
            pltpu.VMEM((rows, width), BF16),
            pltpu.VMEM((rows, width), BF16),
            pltpu.SemaphoreType.DMA((3,)),
        ],
        compiler_params=params(60),
        cost_estimate=pl.CostEstimate(
            flops=4 * slots * rows * width, bytes_accessed=4 * MIB, transcendentals=0
        ),
        name="pack",
    )(me, dest, feats, grads)
    feats_got = by_distance(feats_sent, "seq")
    def by_core(same, cross):
        return small_kernel(
            functools.partial(pair_kernel, capacity),
            [shape_of((2 * capacity, width), BF16)] * (n_seq // 2),
            [same, lax.ppermute(cross, "seq", core_pairs())],
            name="pair_up",
        )

    messages = by_core(same, cross)
    feats_got, messages = lax.optimization_barrier((feats_got, messages))
    grads_got = by_chip(messages)

    pos, xhat, inv, normed, qkv, trans, attn_t, stats = pl.pallas_call(
        functools.partial(forward_kernel, n_seq, capacity),
        grid=(1,),
        out_shape=(
            shape_of((1, slots), jnp.int32),
            shape_of((rows, width), F32),
            shape_of((rows, LANES), F32),
            shape_of((rows, width), BF16),
            shape_of((rows, 3 * width), BF16),
            shape_of((2 * width, rows), BF16),
            shape_of((width, rows), BF16),
            shape_of((2 * HEADS, rows), F32),
        ),
        in_specs=[in_hbm, whole((1, width))] + [whole((block, width))] * n_seq,
        out_specs=[whole((1, slots))]
        + [in_hbm] * 5
        + [whole((width, rows)), whole((2 * HEADS, rows))],
        scratch_shapes=[
            pltpu.VMEM((width, 3 * width), BF16),
            pltpu.VMEM((rows, width), F32),
            pltpu.VMEM((rows, LANES), F32),
            pltpu.VMEM((rows, width), BF16),
            pltpu.VMEM((rows, 3 * width), BF16),
            pltpu.VMEM((3 * width, rows), BF16),
            pltpu.SemaphoreType.DMA((6,)),
        ],
        compiler_params=params(60),
        cost_estimate=pl.CostEstimate(
            flops=6 * rows * width * width + 8 * HEADS * rows * rows * pair,
            bytes_accessed=16 * MIB,
            transcendentals=HEADS * rows * rows,
        ),
        name="forward",
    )(w_qkv, gain_row, *feats_got)

    chip_bits = tuple(zip(*chip_orders(n_seq)))[:2]
    *quarters, serial_grad, d_normed = pl.pallas_call(
        functools.partial(backward_kernel, n_seq, chip_bits),
        grid=(1,),
        out_shape=[shape_of(sum_shape, F32)] * 4
        + [shape_of((rows, width), BF16), shape_of((rows, width), F32)],
        in_specs=[
            in_smem,
            whole((1, slots)),
            whole((width, width)),
            whole((2 * HEADS, rows)),
        ]
        + [in_hbm] * (6 + n_seq // 2),
        out_specs=[in_hbm] * 6,
        scratch_shapes=[
            pltpu.VMEM((slots, width), BF16),
            pltpu.VMEM((rows, 3 * width), BF16),
            pltpu.VMEM((2 * width, rows), BF16),
            pltpu.VMEM((width, 3 * width), BF16),
            pltpu.VMEM((rows, width), F32),
            pltpu.VMEM((rows, width), BF16),
            pltpu.VMEM((width, rows), BF16),
        ]
        + [pltpu.VMEM(sum_shape, F32)] * 4
        + [
            pltpu.VMEM((rows, width), BF16),
            pltpu.VMEM((rows, width), F32),
            pltpu.VMEM((rows, width), BF16),
            pltpu.VMEM((width, rows), BF16),
            pltpu.VMEM((rows, 3 * width), BF16),
            pltpu.VMEM((width, LANES), F32),
            pltpu.SemaphoreType.DMA((16 + n_seq // 2,)),
        ],
        compiler_params=params(60),
        cost_estimate=pl.CostEstimate(
            flops=12 * rows * width * width + 10 * HEADS * rows * rows * pair,
            bytes_accessed=16 * MIB,
            transcendentals=HEADS * rows * rows,
        ),
        name="backward",
    )(me, pos, w_proj, stats, qkv, trans, w_qkv, xhat, normed, attn_t, *grads_got)

    steps = chip_steps()
    terms = first_step(quarters, steps)
    same, cross = small_kernel(
        functools.partial(residual_kernel, capacity),
        [shape_of((slots // 2, width), BF16)] * 2,
        [pos, gain_row, inv, xhat, serial_grad, d_normed],
        name="residual",
    )
    back = by_core(same, cross)
    terms, got = second_step(terms, steps)
    got, back = lax.optimization_barrier((got, back))
    returned = by_chip(back)
    part, returned = lax.optimization_barrier((reduce_over_planes(terms, got, steps), returned))
    own = share_in_plane(share_over_planes(part), steps)
    grad_local = small_kernel(
        unpack_kernel, [shape_of((rows, width), BF16)], [slot, *returned], name="unpack"
    )[0]
    own, grad_local = lax.optimization_barrier((own, grad_local))
    other = lax.ppermute(own, "seq", core_pairs())
    side = lax.bitwise_and(me, 1)
    outs = write_half(side, own)
    grad_qkv, grad_proj, gain_grad = write_half(1 - side, other, outs)
    return (grad_local[None], grad_qkv, grad_proj, gain_grad[0])


def solution(mesh):
    return jax.shard_map(
        per_device,
        mesh=mesh,
        in_specs=(P("dp", "seq", None), P("dp", "seq", None), P("dp", "seq"), P(), P(), P()),
        out_specs=(P("dp", "seq", None), P(), P(), P()),
        check_vma=False,
    )
```

```python
import functools

import jax
import jax.numpy as jnp
from jax import lax
from jax.experimental import pallas as pl
from jax.experimental.pallas import tpu as pltpu
from jax.sharding import PartitionSpec as P

HEADS = 8
PATCH = 512
EXTRA = 16
LANES = 128
CODE_MAX = 32000.0
DIGIT = 60000.0
MIB = 1024 * 1024
F32 = jnp.float32
BF16 = jnp.bfloat16
NN = (((1,), (0,)), ((), ()))
NT = (((1,), (1,)), ((), ()))


def mm(lhs, rhs, dims=NN):
    return lax.dot_general(lhs, rhs, dims, preferred_element_type=F32)


def iota(shape, dim):
    return lax.broadcasted_iota(jnp.int32, shape, dim)


def hot(mask):
    return jnp.where(mask, jnp.float32(1), jnp.float32(0)).astype(BF16)


def column_hot(row, count):
    size = row.shape[1]
    column = jnp.transpose(jnp.broadcast_to(row, (LANES, size)))
    lane = iota((size, LANES), 1)
    return jnp.concatenate([hot(column == lane + j * LANES) for j in range(count // LANES)], axis=1)


def pack_kernel(
    n_seq, capacity, me_ref, dest_hbm, feats_hbm, grads_hbm, slot_out, same_out, cross_out, *refs
):
    outs, (dest_ref, feats_ref, grads_ref, sems) = refs[:n_seq], refs[n_seq:]
    rows, width = feats_ref.shape
    slots = n_seq * capacity
    loads = [
        pltpu.make_async_copy(source, target, sems.at[i])
        for i, (source, target) in enumerate(
            ((dest_hbm, dest_ref), (feats_hbm, feats_ref), (grads_hbm, grads_ref))
        )
    ]
    for load in loads:
        load.start()
    loads[0].wait()
    shift = rows.bit_length() - 1
    places = dest_ref[...]
    distance = lax.bitwise_xor(lax.shift_right_logical(places, shift), me_ref[0])
    within = lax.bitwise_and(places, rows - 1) + 1
    member = iota((n_seq, rows), 0) == distance
    upper = hot(iota((rows, rows), 0) <= iota((rows, rows), 1))
    counts = mm(hot(member), upper)
    rank = jnp.sum(jnp.where(member, counts, 0.0), axis=0, keepdims=True).astype(jnp.int32) - 1
    slot = distance * capacity + rank
    slot_out[...] = slot
    select = hot(iota((slots, rows), 0) == slot)
    loads[1].wait()
    feats = mm(select, feats_ref[...]).astype(BF16)
    upper_half = slot >= width
    high = lax.shift_right_logical(within, 8).astype(F32)
    low = lax.bitwise_and(within, 255).astype(F32)
    line = iota((n_seq * EXTRA, rows), 0)
    kind = lax.bitwise_and(line, EXTRA - 1)
    digit = jnp.where(kind < 2, high, low)
    wanted = (
        (lax.shift_right_logical(line, EXTRA.bit_length() - 1) == distance)
        & (kind < 4)
        & ((lax.bitwise_and(kind, 1) == 1) == upper_half)
    )
    digits = jnp.where(wanted, digit, 0.0).astype(BF16)
    spread = hot(iota((width, rows), 0) == lax.bitwise_and(slot, width - 1))
    position = mm(digits, spread, NT).astype(BF16)
    for d in range(n_seq):
        outs[d][:capacity, :] = feats[d * capacity : (d + 1) * capacity]
        outs[d][capacity:, :] = position[d * EXTRA : (d + 1) * EXTRA]
    loads[2].wait()
    grads = mm(select, grads_ref[...]).astype(BF16)
    for j in range(n_seq // 2):
        lines = slice(j * capacity, (j + 1) * capacity)
        same_out[lines, :] = grads[2 * j * capacity : (2 * j + 1) * capacity]
        cross_out[lines, :] = grads[(2 * j + 1) * capacity : (2 * j + 2) * capacity]


def pair_kernel(capacity, same_ref, cross_ref, *outs):
    for j, out in enumerate(outs):
        lines = slice(j * capacity, (j + 1) * capacity)
        out[:capacity, :] = same_ref[lines, :]
        out[capacity:, :] = cross_ref[lines, :]


def forward_kernel(n_seq, capacity, w_hbm, gain_ref, *refs):
    recv, refs = refs[:n_seq], refs[n_seq:]
    pos_out, xhat_hbm, inv_hbm, normed_hbm, qkv_hbm, trans_hbm, attn_out, stats_out = refs[:8]
    w_ref, xhat_ref, inv_ref, normed_ref, qkv_ref, trans, sems = refs[8:]
    width = w_ref.shape[0]
    rows = xhat_ref.shape[0]
    head = width // HEADS
    pair = 2 * head
    w_copy = pltpu.make_async_copy(w_hbm, w_ref, sems.at[0])
    saves = [
        pltpu.make_async_copy(source, target, sems.at[1 + i])
        for i, (source, target) in enumerate(
            (
                (xhat_ref, xhat_hbm),
                (inv_ref, inv_hbm),
                (normed_ref, normed_hbm),
                (qkv_ref, qkv_hbm),
                (trans.at[pl.ds(0, 2 * width)], trans_hbm),
            )
        )
    ]

    w_copy.start()
    tile = recv[0][capacity:, :].astype(F32)
    for s in range(1, n_seq):
        tile = tile + recv[s][capacity:, :].astype(F32)
    high = jnp.concatenate([tile[0:1], tile[1:2]], axis=1)
    low = jnp.concatenate([tile[2:3], tile[3:4]], axis=1)
    pos = (high * 256.0 + low).astype(jnp.int32) - 1
    pos_out[...] = pos
    place = hot(iota((rows, n_seq * capacity), 0) == pos)
    values = jnp.concatenate([recv[s][:capacity, :] for s in range(n_seq)], axis=0)
    feats = mm(place, values)
    centered = feats - jnp.mean(feats, axis=1, keepdims=True)
    inv = lax.rsqrt(jnp.mean(centered * centered, axis=1, keepdims=True) + 1e-05)
    xhat = centered * inv
    xhat_ref[...] = xhat
    inv_ref[...] = jnp.broadcast_to(inv, inv_ref.shape)
    scaled = xhat * gain_ref[...]
    normed = scaled.astype(BF16)
    normed_ref[...] = jnp.transpose(scaled).astype(BF16)
    w_copy.wait()
    qkv = mm(normed, w_ref[...])
    qkv_ref[...] = qkv.astype(BF16)
    trans[...] = jnp.transpose(qkv).astype(BF16)
    for save in saves:
        save.start()

    for step in range(HEADS // 2):
        lo = step * pair
        keys = qkv_ref[:, pl.ds(width + lo, pair)]
        query_t = trans[pl.ds(lo, pair), :] * BF16(0.125)
        zero = jnp.zeros((head, rows), BF16)
        for j in range(2):
            part = query_t[j * head : (j + 1) * head]
            part = jnp.concatenate([part, zero] if j == 0 else [zero, part], axis=0)
            scores = mm(keys, part)
            top = jnp.max(scores, axis=0, keepdims=True)
            expo = jnp.exp(scores - top)
            share = 1.0 / jnp.sum(expo, axis=0, keepdims=True)
            probs = expo * share
            stats_out[pl.ds(2 * step + j, 1), :] = top
            stats_out[pl.ds(HEADS + 2 * step + j, 1), :] = share
            values_t = trans[pl.ds(2 * width + lo + j * head, head), :]
            attn_out[pl.ds(lo + j * head, head), :] = mm(values_t, probs.astype(BF16)).astype(BF16)

    for save in saves:
        save.wait()


def backward_kernel(n_seq, chip_bits, me_ref, pos_ref, w_proj_ref, stats_ref, *refs):
    (qkv_hbm, trans_hbm, w_hbm, xhat_hbm, normed_hbm, attn_hbm), refs = refs[:6], refs[6:]
    recv_hbm, refs = refs[: n_seq // 2], refs[n_seq // 2 :]
    outs, serial_grad_hbm, d_normed_hbm, refs = refs[:4], refs[4], refs[5], refs[6:]
    recv_ref, qkv_ref, trans_ref, w_ref, xhat_ref, normed_ref, attn_ref, refs = *refs[:7], refs[7:]
    sums, refs = refs[:4], refs[4:]
    serial_grad, d_normed_ref, d_attn, d_attn_t, d_qkv, gain_column, sems = refs
    width = w_proj_ref.shape[0]
    rows = xhat_ref.shape[0]
    capacity = recv_ref.shape[0] // n_seq
    head = width // HEADS
    pair = 2 * head
    me = me_ref[0]
    chips = n_seq // 2
    recv_parts = [recv_ref.at[pl.ds(2 * j * capacity, 2 * capacity)] for j in range(chips)]
    loads = [
        pltpu.make_async_copy(source, target, sems.at[i])
        for i, (source, target) in enumerate(
            (
                *zip(recv_hbm, recv_parts),
                (qkv_hbm, qkv_ref),
                (trans_hbm, trans_ref),
                (normed_hbm, normed_ref),
                (w_hbm, w_ref),
                (xhat_hbm, xhat_ref),
                (attn_hbm, attn_ref),
            )
        )
    ]
    body, tail = pl.ds(0, 4 * width), pl.ds(4 * width, LANES)
    saves = [
        pltpu.make_async_copy(source, target, sems.at[6 + chips + i])
        for i, (source, target) in enumerate(
            [
                *[(source.at[:, body], target.at[:, body]) for source, target in zip(sums, outs)],
                (serial_grad, serial_grad_hbm),
                (d_normed_ref, d_normed_hbm),
                *[(source.at[:, tail], target.at[:, tail]) for source, target in zip(sums, outs)],
            ]
        )
    ]

    for load in loads:
        load.start()
    place = hot(iota((rows, n_seq * capacity), 0) == pos_ref[...])
    for load in loads[:chips]:
        load.wait()
    grads = mm(place, recv_ref[...]).astype(BF16)
    serial_grad[...] = grads
    saves[4].start()
    d_attn[...] = mm(grads, w_proj_ref[...], NT).astype(BF16)
    d_attn_t[...] = mm(w_proj_ref[...], grads, NT).astype(BF16)
    for load in loads[chips : chips + 2]:
        load.wait()

    zero = jnp.zeros((head, rows), BF16)
    first = iota((rows, pair), 1) < head

    def alone(both, j):
        part = both[j * head : (j + 1) * head]
        return jnp.concatenate([part, zero] if j == 0 else [zero, part], axis=0)

    for step in range(HEADS // 2):
        lo = step * pair
        queries = qkv_ref[:, pl.ds(lo, pair)]
        values = qkv_ref[:, pl.ds(2 * width + lo, pair)]
        d_att_t = d_attn_t[pl.ds(lo, pair), :] * BF16(0.125)
        d_att = d_attn[:, pl.ds(lo, pair)]
        keys = qkv_ref[:, pl.ds(width + lo, pair)]
        query_t = trans_ref[pl.ds(lo, pair), :] * BF16(0.125)
        d_q, d_k, d_v = [], [], []
        for j in range(2):
            top = stats_ref[pl.ds(2 * step + j, 1), :]
            share = stats_ref[pl.ds(HEADS + 2 * step + j, 1), :]
            probs = jnp.exp(mm(keys, alone(query_t, j)) - top) * share
            d_probs = mm(values, alone(d_att_t, j))
            total = jnp.sum(d_probs * probs, axis=0, keepdims=True)
            d_scores = (probs * (d_probs - total)).astype(BF16)
            k_t = trans_ref[pl.ds(width + lo + j * head, head), :]
            d_q.append(mm(k_t, d_scores))
            d_k.append(mm(d_scores, queries))
            d_v.append(mm(probs.astype(BF16), d_att))
        d_qkv[:, pl.ds(lo, pair)] = jnp.transpose(jnp.concatenate(d_q, axis=0)).astype(BF16)
        d_qkv[:, pl.ds(width + lo, pair)] = jnp.where(
            first, d_k[0], d_k[1]
        ).astype(BF16)
        d_qkv[:, pl.ds(2 * width + lo, pair)] = jnp.where(
            first, d_v[0], d_v[1]
        ).astype(BF16)

    for load in loads[chips + 2 :]:
        load.wait()
    eighth = width // 8
    odd = lax.bitwise_and(me, 1)

    def sides(even_bit, odd_bit):
        even_side = lax.bitwise_and(lax.shift_right_logical(me, even_bit), 1)
        odd_side = lax.bitwise_and(lax.shift_right_logical(me, odd_bit), 1)
        mine = jnp.where(odd == 1, odd_side, even_side)
        return mine, even_side + odd_side - mine

    (mine, other), (mine_next, other_next) = (sides(*bits) for bits in chip_bits)
    starts = (
        ((1 - odd) * 2 + 1 - other, other_next),
        ((1 - odd) * 2 + other, other_next),
        (odd * 2 + 1 - mine, mine_next),
        (odd * 2 + mine, mine_next),
    )
    order = [
        pl.ds(pl.multiple_of((start * 2 + half) * eighth, eighth), eighth)
        for start, side in starts
        for half in (1 - side, side)
    ]
    for i in (0, 2):
        parts = order[2 * i : 2 * i + 4]
        of_qkv = mm(jnp.concatenate([normed_ref[part, :] for part in parts], axis=0), d_qkv[...])
        of_proj = mm(jnp.concatenate([attn_ref[part, :] for part in parts], axis=0), serial_grad[...])
        for j in range(2):
            lines = slice(2 * j * eighth, 2 * (j + 1) * eighth)
            sums[i + j][:, : 3 * width] = of_qkv[lines]
            sums[i + j][:, 3 * width : 4 * width] = of_proj[lines]
            saves[i + j].start()
    d_normed = mm(d_qkv[...], w_ref[...], NT)
    d_normed_ref[...] = d_normed
    saves[5].start()
    gain_row = jnp.sum(d_normed * xhat_ref[...], axis=0, keepdims=True)
    gain_column[...] = jnp.transpose(jnp.broadcast_to(gain_row, (LANES, width)))
    for i in range(4):
        parts = order[2 * i : 2 * i + 2]
        sums[i][:, 4 * width :] = jnp.concatenate([gain_column[part, :] for part in parts], axis=0)
        saves[6 + i].start()
    for save in saves:
        save.wait()


def residual_kernel(
    capacity, pos_ref, gain_ref, inv_ref, xhat_ref, serial_grad_ref, d_normed_ref, same_out, cross_out
):
    xhat = xhat_ref[...]
    rows = xhat.shape[0]
    scaled = d_normed_ref[...] * gain_ref[...]
    residual = inv_ref[:, 0:1] * (
        scaled
        - jnp.mean(scaled, axis=1, keepdims=True)
        - xhat * jnp.mean(scaled * xhat, axis=1, keepdims=True)
    )
    serial_dx = (serial_grad_ref[...].astype(F32) + residual).astype(BF16)
    returned = mm(column_hot(pos_ref[...], rows), serial_dx).astype(BF16)
    for j in range(same_out.shape[0] // capacity):
        lines = slice(j * capacity, (j + 1) * capacity)
        same_out[lines, :] = returned[2 * j * capacity : (2 * j + 1) * capacity]
        cross_out[lines, :] = returned[(2 * j + 1) * capacity : (2 * j + 2) * capacity]


def unpack_kernel(slot_ref, *refs):
    values = jnp.concatenate([ref[...] for ref in refs[:-1]], axis=0)
    refs[-1][...] = mm(column_hot(slot_ref[...], values.shape[0]), values).astype(BF16)


def split_kernel(side_ref, sums_ref, *refs):
    qkv_out, proj_out, gain_out = refs[-3:]
    width = proj_out.shape[1]
    qkv_out[...] = sums_ref[:, : 3 * width].astype(F32)
    proj_out[...] = sums_ref[:, 3 * width : 4 * width].astype(F32)
    gain_out[...] = jnp.transpose(sums_ref[:, 4 * width :].astype(F32))[0:1]


def exponent_of(largest):
    return jnp.clip(jnp.ceil(jnp.log(jnp.maximum(largest, 1e-30)) * 1.4426950408889634), -100.0, 120.0)


def encode(out_ref, total):
    width = total.shape[1] - LANES
    body, gain = total[:, :width], total[:, width : width + 1]
    exponent = exponent_of(jnp.max(jnp.abs(body), axis=1, keepdims=True))
    codes = jnp.round(body * (jnp.exp2(-exponent) * CODE_MAX))
    out_ref[:, :width] = codes.astype(jnp.int32).astype(jnp.int16)
    gain_exponent = exponent_of(jnp.abs(gain))
    scaled = gain * (jnp.exp2(-gain_exponent) * CODE_MAX)
    high = jnp.round(scaled)
    low = jnp.round((scaled - high) * DIGIT)
    lane = iota((total.shape[0], LANES), 1)
    tail = jnp.where(lane == 0, high, jnp.where(lane == 1, low, jnp.where(lane == 2, gain_exponent, exponent)))
    out_ref[:, width:] = tail.astype(jnp.int32).astype(jnp.int16)


def decode(codes):
    values = codes.astype(jnp.int32).astype(F32)
    width = values.shape[1] - LANES
    tail = values[:, width:]
    body = values[:, :width] * (jnp.exp2(tail[:, 3:4]) * (1.0 / CODE_MAX))
    gain = (tail[:, 0:1] + tail[:, 1:2] * (1.0 / DIGIT)) * (jnp.exp2(tail[:, 2:3]) * (1.0 / CODE_MAX))
    return jnp.concatenate([body, jnp.broadcast_to(gain, tail.shape)], axis=1)


def total_of(terms, part):
    half = terms[0].shape[0] // 2
    rows = {"all": slice(None), "first": slice(0, half), "second": slice(half, 2 * half)}[part]
    values = [ref[rows, :] for ref in terms]
    return functools.reduce(jnp.add, [decode(v) if v.dtype == jnp.int16 else v for v in values])


def message_kernel(part, *refs):
    encode(refs[-1], total_of(refs[:-1], part))


def sum_kernel(parts, *refs):
    refs[-1][...] = functools.reduce(jnp.add, [total_of([ref], p) for ref, p in zip(refs, parts)])


def pieces_kernel(parts, n_dp, plane_ref, *refs):
    terms, own, messages, total = refs[: len(parts)], refs[len(parts)], refs[len(parts) + 1 : -1], refs[-1]
    total[...] = functools.reduce(jnp.add, [total_of([ref], p) for ref, p in zip(terms, parts)])
    size = own.shape[0]

    def rows_of(distance):
        start = lax.bitwise_xor(plane_ref[0], distance) * size
        return total[pl.ds(pl.multiple_of(start, size), size), :]

    for k in range(1, n_dp):
        encode(messages[k - 1], rows_of(k))
    own[...] = rows_of(0)


def finish_kernel(*refs):
    refs[-1][...] = total_of(refs[:-1], "all").astype(BF16)


def whole(shape):
    return pl.BlockSpec(shape, lambda *_: (0,) * len(shape), pipeline_mode=pl.Buffered(1))


def params(mib):
    return pltpu.CompilerParams(vmem_limit_bytes=mib * MIB)


def shape_of(shape, dtype):
    return jax.ShapeDtypeStruct(shape, dtype)


def by_distance(blocks, axis):
    count = len(blocks)
    return [blocks[0]] + [
        lax.ppermute(blocks[k], axis, [(i, i ^ k) for i in range(count)]) for k in range(1, count)
    ]


def by_chip(messages):
    count = 2 * len(messages)
    return [messages[0]] + [
        lax.ppermute(messages[j], "seq", [(i, i ^ (2 * j)) for i in range(count)])
        for j in range(1, len(messages))
    ]


def chip_orders(n_seq):
    bits = list(range(1, n_seq.bit_length() - 1))
    middle = len(bits) // 2
    return bits, bits[middle:] + bits[:middle]


def chip_steps():
    n_seq, me = lax.axis_size("seq"), lax.axis_index("seq")
    odd = lax.bitwise_and(me, 1) == 1

    def side(bit):
        return lax.bitwise_and(lax.shift_right_logical(me, jnp.asarray(bit, me.dtype)), 1)

    steps = []
    for even_bit, odd_bit in zip(*chip_orders(n_seq)):
        pairs = [(i, i ^ (1 << (odd_bit if i & 1 else even_bit))) for i in range(n_seq)]
        steps.append((pairs, jnp.where(odd, side(odd_bit), side(even_bit))))
    return steps


def piece(terms, index, count):
    size = terms[0].shape[0] // count
    return functools.reduce(jnp.add, [lax.dynamic_slice_in_dim(t, index * size, size) for t in terms])


def core_pairs():
    return [(i, i ^ 1) for i in range(lax.axis_size("seq"))]


def small_kernel(kernel, outs, operands, scalars=0, scratch=(), name="sum"):
    in_smem = pl.BlockSpec(memory_space=pltpu.SMEM)
    in_vmem = pl.BlockSpec(memory_space=pltpu.VMEM)
    touched = sum(x.size * x.dtype.itemsize for x in (*operands, *outs))
    return pl.pallas_call(
        kernel,
        out_shape=outs,
        in_specs=[in_smem] * scalars + [in_vmem] * (len(operands) - scalars),
        out_specs=[in_vmem] * len(outs),
        scratch_shapes=list(scratch),
        compiler_params=params(20),
        cost_estimate=pl.CostEstimate(flops=2 * touched, bytes_accessed=touched, transcendentals=0),
        name=name,
    )(*operands)


def message(terms, part, name):
    rows, width = terms[0].shape
    rows = rows if part == "all" else rows // 2
    return small_kernel(
        functools.partial(message_kernel, part), [shape_of((rows, width), jnp.int16)], terms, name=name
    )[0]


def first_step(quarters, steps):
    pass_on, pass_keep, own_on, own_keep = quarters
    got_on = lax.ppermute(pass_on, "seq", core_pairs())
    got_keep = lax.ppermute(pass_keep, "seq", core_pairs())
    sent = message([own_on, got_on], "all", "code_first")
    return [own_keep, got_keep, lax.ppermute(sent, "seq", steps[0][0])]


def second_step(terms, steps, later):
    sent = message(terms, "first", "code_second")
    sent, later = lax.optimization_barrier((sent, later))
    return terms, lax.ppermute(sent, "seq", steps[1][0]), later


def halves_of_plain(part, steps):
    for pairs, side in steps:
        got = lax.ppermute(piece([part], 1 - side, 2), "seq", pairs)
        part = piece([part], side, 2) + got
    return part


def reduce_over_planes(terms, got, steps):
    n_dp, plane = lax.axis_size("dp"), lax.axis_index("dp")
    rows, width = got.shape
    parts = ["second"] * len(terms) + ["all"]
    if len(steps) > 2 or rows // n_dp % 16:
        part = small_kernel(
            functools.partial(sum_kernel, parts), [shape_of((rows, width), F32)], [*terms, got]
        )[0]
        part = halves_of_plain(part, steps[2:])
        pieces = [piece([part], lax.bitwise_xor(plane, k), n_dp) for k in range(n_dp)]
        return functools.reduce(jnp.add, by_distance(pieces, "dp")).astype(BF16)
    size = rows // n_dp
    own, *sent = small_kernel(
        functools.partial(pieces_kernel, parts, n_dp),
        [shape_of((size, width), F32)] + [shape_of((size, width), jnp.int16)] * (n_dp - 1),
        [jnp.reshape(plane.astype(jnp.int32), (1,)), *terms, got],
        scalars=1,
        scratch=[pltpu.VMEM((rows, width), F32)],
        name="code_planes",
    )
    arrived = by_distance([own] + sent, "dp")
    return small_kernel(finish_kernel, [shape_of((size, width), BF16)], arrived, name="finish")[0]


def share_over_planes(part):
    n_dp, plane = lax.axis_size("dp"), lax.axis_index("dp")
    shares = jnp.stack(by_distance([part] * n_dp, "dp"))
    return jnp.concatenate(
        [lax.dynamic_index_in_dim(shares, lax.bitwise_xor(plane, p), keepdims=False) for p in range(n_dp)],
        axis=0,
    )


def share_in_plane(part, steps):
    for pairs, side in reversed(steps):
        other = lax.ppermute(part, "seq", pairs)
        part = jnp.where(
            side == 0, jnp.concatenate([part, other], axis=0), jnp.concatenate([other, part], axis=0)
        )
    return part


def write_half(side, sums, outs=()):
    half, width = sums.shape[0], (sums.shape[1] - LANES) // 4
    return pl.pallas_call(
        split_kernel,
        grid_spec=pltpu.PrefetchScalarGridSpec(
            num_scalar_prefetch=1,
            grid=(2,),
            in_specs=[pl.BlockSpec((half // 2, sums.shape[1]), lambda i, s: (i, 0))]
            + [pl.BlockSpec(memory_space=pl.ANY)] * len(outs),
            out_specs=[
                pl.BlockSpec((half // 2, 3 * width), lambda i, s: (2 * s[0] + i, 0)),
                pl.BlockSpec((half // 2, width), lambda i, s: (2 * s[0] + i, 0)),
                pl.BlockSpec((1, half // 2), lambda i, s: (0, 2 * s[0] + i)),
            ],
        ),
        out_shape=(
            shape_of((2 * half, 3 * width), F32),
            shape_of((2 * half, width), F32),
            shape_of((1, 2 * half), F32),
        ),
        input_output_aliases={2 + i: i for i in range(len(outs))},
        compiler_params=params(20),
        cost_estimate=pl.CostEstimate(flops=0, bytes_accessed=4 * MIB, transcendentals=0),
        name="split",
    )(side, sums, *outs)


def per_device(points, cotangent, dest, w_qkv, w_proj, gain):
    feats = points[0]
    grads = cotangent[0]
    rows, width = feats.shape
    n_seq = lax.axis_size("seq")
    capacity = 2 * (rows // n_seq)
    slots = n_seq * capacity
    block = capacity + EXTRA
    pairs = HEADS // 2
    pair = width // pairs
    sum_shape = (width // 4, 4 * width + LANES)
    me = jnp.reshape(lax.axis_index("seq").astype(jnp.int32), (1,))
    gain_row = gain.reshape(1, width)
    in_smem = pl.BlockSpec(memory_space=pltpu.SMEM)
    in_vmem = pl.BlockSpec(memory_space=pltpu.VMEM)
    in_hbm = pl.BlockSpec(memory_space=pl.ANY)
    stay_hbm = pl.BlockSpec(memory_space=pltpu.HBM)

    slot, same, cross, *feats_sent = pl.pallas_call(
        functools.partial(pack_kernel, n_seq, capacity),
        out_shape=[shape_of((1, rows), jnp.int32)]
        + [shape_of((slots // 2, width), BF16)] * 2
        + [shape_of((block, width), BF16)] * n_seq,
        in_specs=[in_smem] + [stay_hbm] * 3,
        out_specs=[in_vmem] * (3 + n_seq),
        scratch_shapes=[
            pltpu.VMEM((1, rows), jnp.int32),
            pltpu.VMEM((rows, width), BF16),
            pltpu.VMEM((rows, width), BF16),
            pltpu.SemaphoreType.DMA((3,)),
        ],
        compiler_params=params(60),
        cost_estimate=pl.CostEstimate(
            flops=4 * slots * rows * width, bytes_accessed=4 * MIB, transcendentals=0
        ),
        name="pack",
    )(me, dest, feats, grads)
    feats_got = by_distance(feats_sent, "seq")
    def by_core(same, cross):
        return small_kernel(
            functools.partial(pair_kernel, capacity),
            [shape_of((2 * capacity, width), BF16)] * (n_seq // 2),
            [same, lax.ppermute(cross, "seq", core_pairs())],
            name="pair_up",
        )

    messages = by_core(same, cross)
    feats_got, messages = lax.optimization_barrier((feats_got, messages))
    grads_got = by_chip(messages)

    pos, xhat, inv, normed, qkv, trans, attn_t, stats = pl.pallas_call(
        functools.partial(forward_kernel, n_seq, capacity),
        grid=(1,),
        out_shape=(
            shape_of((1, slots), jnp.int32),
            shape_of((rows, width), F32),
            shape_of((rows, LANES), F32),
            shape_of((rows, width), BF16),
            shape_of((rows, 3 * width), BF16),
            shape_of((2 * width, rows), BF16),
            shape_of((width, rows), BF16),
            shape_of((2 * HEADS, rows), F32),
        ),
        in_specs=[in_hbm, whole((1, width))] + [whole((block, width))] * n_seq,
        out_specs=[whole((1, slots))]
        + [in_hbm] * 5
        + [whole((width, rows)), whole((2 * HEADS, rows))],
        scratch_shapes=[
            pltpu.VMEM((width, 3 * width), BF16),
            pltpu.VMEM((rows, width), F32),
            pltpu.VMEM((rows, LANES), F32),
            pltpu.VMEM((rows, width), BF16),
            pltpu.VMEM((rows, 3 * width), BF16),
            pltpu.VMEM((3 * width, rows), BF16),
            pltpu.SemaphoreType.DMA((6,)),
        ],
        compiler_params=params(60),
        cost_estimate=pl.CostEstimate(
            flops=6 * rows * width * width + 8 * HEADS * rows * rows * pair,
            bytes_accessed=16 * MIB,
            transcendentals=HEADS * rows * rows,
        ),
        name="forward",
    )(w_qkv, gain_row, *feats_got)

    chip_bits = tuple(zip(*chip_orders(n_seq)))[:2]
    *quarters, serial_grad, d_normed = pl.pallas_call(
        functools.partial(backward_kernel, n_seq, chip_bits),
        grid=(1,),
        out_shape=[shape_of(sum_shape, F32)] * 4
        + [shape_of((rows, width), BF16), shape_of((rows, width), F32)],
        in_specs=[
            in_smem,
            whole((1, slots)),
            whole((width, width)),
            whole((2 * HEADS, rows)),
        ]
        + [in_hbm] * (6 + n_seq // 2),
        out_specs=[in_hbm] * 6,
        scratch_shapes=[
            pltpu.VMEM((slots, width), BF16),
            pltpu.VMEM((rows, 3 * width), BF16),
            pltpu.VMEM((2 * width, rows), BF16),
            pltpu.VMEM((width, 3 * width), BF16),
            pltpu.VMEM((rows, width), F32),
            pltpu.VMEM((rows, width), BF16),
            pltpu.VMEM((width, rows), BF16),
        ]
        + [pltpu.VMEM(sum_shape, F32)] * 4
        + [
            pltpu.VMEM((rows, width), BF16),
            pltpu.VMEM((rows, width), F32),
            pltpu.VMEM((rows, width), BF16),
            pltpu.VMEM((width, rows), BF16),
            pltpu.VMEM((rows, 3 * width), BF16),
            pltpu.VMEM((width, LANES), F32),
            pltpu.SemaphoreType.DMA((16 + n_seq // 2,)),
        ],
        compiler_params=params(60),
        cost_estimate=pl.CostEstimate(
            flops=12 * rows * width * width + 10 * HEADS * rows * rows * pair,
            bytes_accessed=16 * MIB,
            transcendentals=HEADS * rows * rows,
        ),
        name="backward",
    )(me, pos, w_proj, stats, qkv, trans, w_qkv, xhat, normed, attn_t, *grads_got)

    steps = chip_steps()
    terms = first_step(quarters, steps)
    same, cross = small_kernel(
        functools.partial(residual_kernel, capacity),
        [shape_of((slots // 2, width), BF16)] * 2,
        [pos, gain_row, inv, xhat, serial_grad, d_normed],
        name="residual",
    )
    terms, got, same = second_step(terms, steps, same)
    returned = by_chip(by_core(same, cross))
    part, returned = lax.optimization_barrier((reduce_over_planes(terms, got, steps), returned))
    own = share_in_plane(share_over_planes(part), steps)
    grad_local = small_kernel(
        unpack_kernel, [shape_of((rows, width), BF16)], [slot, *returned], name="unpack"
    )[0]
    own, grad_local = lax.optimization_barrier((own, grad_local))
    other = lax.ppermute(own, "seq", core_pairs())
    side = lax.bitwise_and(me, 1)
    outs = write_half(side, own)
    grad_qkv, grad_proj, gain_grad = write_half(1 - side, other, outs)
    return (grad_local[None], grad_qkv, grad_proj, gain_grad[0])


def solution(mesh):
    return jax.shard_map(
        per_device,
        mesh=mesh,
        in_specs=(P("dp", "seq", None), P("dp", "seq", None), P("dp", "seq"), P(), P(), P()),
        out_specs=(P("dp", "seq", None), P(), P(), P()),
        check_vma=False,
    )
```

```python
import functools

import jax
import jax.numpy as jnp
from jax import lax
from jax.experimental import pallas as pl
from jax.experimental.pallas import tpu as pltpu
from jax.sharding import PartitionSpec as P

HEADS = 8
PATCH = 512
EXTRA = 16
LANES = 128
CODE_MAX = 32000.0
DIGIT = 60000.0
MIB = 1024 * 1024
F32 = jnp.float32
BF16 = jnp.bfloat16
NN = (((1,), (0,)), ((), ()))
NT = (((1,), (1,)), ((), ()))


def mm(lhs, rhs, dims=NN):
    return lax.dot_general(lhs, rhs, dims, preferred_element_type=F32)


def iota(shape, dim):
    return lax.broadcasted_iota(jnp.int32, shape, dim)


def hot(mask):
    return jnp.where(mask, jnp.float32(1), jnp.float32(0)).astype(BF16)


def column_hot(row, count):
    size = row.shape[1]
    column = jnp.transpose(jnp.broadcast_to(row, (LANES, size)))
    lane = iota((size, LANES), 1)
    return jnp.concatenate([hot(column == lane + j * LANES) for j in range(count // LANES)], axis=1)


def pack_kernel(
    n_seq, capacity, me_ref, dest_hbm, feats_hbm, grads_hbm, slot_out, same_out, cross_out, *refs
):
    outs, (dest_ref, feats_ref, grads_ref, sems) = refs[:n_seq], refs[n_seq:]
    rows, width = feats_ref.shape
    slots = n_seq * capacity
    loads = [
        pltpu.make_async_copy(source, target, sems.at[i])
        for i, (source, target) in enumerate(
            ((dest_hbm, dest_ref), (feats_hbm, feats_ref), (grads_hbm, grads_ref))
        )
    ]
    for load in loads:
        load.start()
    loads[0].wait()
    shift = rows.bit_length() - 1
    places = dest_ref[...]
    distance = lax.bitwise_xor(lax.shift_right_logical(places, shift), me_ref[0])
    within = lax.bitwise_and(places, rows - 1) + 1
    member = iota((n_seq, rows), 0) == distance
    upper = hot(iota((rows, rows), 0) <= iota((rows, rows), 1))
    counts = mm(hot(member), upper)
    rank = jnp.sum(jnp.where(member, counts, 0.0), axis=0, keepdims=True).astype(jnp.int32) - 1
    slot = distance * capacity + rank
    slot_out[...] = slot
    select = hot(iota((slots, rows), 0) == slot)
    loads[1].wait()
    feats = mm(select, feats_ref[...]).astype(BF16)
    upper_half = slot >= width
    high = lax.shift_right_logical(within, 8).astype(F32)
    low = lax.bitwise_and(within, 255).astype(F32)
    line = iota((n_seq * EXTRA, rows), 0)
    kind = lax.bitwise_and(line, EXTRA - 1)
    digit = jnp.where(kind < 2, high, low)
    wanted = (
        (lax.shift_right_logical(line, EXTRA.bit_length() - 1) == distance)
        & (kind < 4)
        & ((lax.bitwise_and(kind, 1) == 1) == upper_half)
    )
    digits = jnp.where(wanted, digit, 0.0).astype(BF16)
    spread = hot(iota((width, rows), 0) == lax.bitwise_and(slot, width - 1))
    position = mm(digits, spread, NT).astype(BF16)
    for d in range(n_seq):
        outs[d][:capacity, :] = feats[d * capacity : (d + 1) * capacity]
        outs[d][capacity:, :] = position[d * EXTRA : (d + 1) * EXTRA]
    loads[2].wait()
    grads = mm(select, grads_ref[...]).astype(BF16)
    for j in range(n_seq // 2):
        lines = slice(j * capacity, (j + 1) * capacity)
        same_out[lines, :] = grads[2 * j * capacity : (2 * j + 1) * capacity]
        cross_out[lines, :] = grads[(2 * j + 1) * capacity : (2 * j + 2) * capacity]


def pair_kernel(capacity, same_ref, cross_ref, *outs):
    for j, out in enumerate(outs):
        lines = slice(j * capacity, (j + 1) * capacity)
        out[:capacity, :] = same_ref[lines, :]
        out[capacity:, :] = cross_ref[lines, :]


def forward_kernel(n_seq, capacity, w_hbm, gain_ref, *refs):
    recv, refs = refs[:n_seq], refs[n_seq:]
    pos_out, xhat_hbm, inv_hbm, normed_hbm, qkv_hbm, trans_hbm, attn_out, stats_out = refs[:8]
    w_ref, xhat_ref, inv_ref, normed_ref, qkv_ref, trans, sems = refs[8:]
    width = w_ref.shape[0]
    rows = xhat_ref.shape[0]
    head = width // HEADS
    pair = 2 * head
    w_copy = pltpu.make_async_copy(w_hbm, w_ref, sems.at[0])
    saves = [
        pltpu.make_async_copy(source, target, sems.at[1 + i])
        for i, (source, target) in enumerate(
            (
                (xhat_ref, xhat_hbm),
                (inv_ref, inv_hbm),
                (normed_ref, normed_hbm),
                (qkv_ref, qkv_hbm),
                (trans.at[pl.ds(0, 2 * width)], trans_hbm),
            )
        )
    ]

    w_copy.start()
    tile = recv[0][capacity:, :].astype(F32)
    for s in range(1, n_seq):
        tile = tile + recv[s][capacity:, :].astype(F32)
    high = jnp.concatenate([tile[0:1], tile[1:2]], axis=1)
    low = jnp.concatenate([tile[2:3], tile[3:4]], axis=1)
    pos = (high * 256.0 + low).astype(jnp.int32) - 1
    pos_out[...] = pos
    place = hot(iota((rows, n_seq * capacity), 0) == pos)
    values = jnp.concatenate([recv[s][:capacity, :] for s in range(n_seq)], axis=0)
    feats = mm(place, values)
    centered = feats - jnp.mean(feats, axis=1, keepdims=True)
    inv = lax.rsqrt(jnp.mean(centered * centered, axis=1, keepdims=True) + 1e-05)
    xhat = centered * inv
    xhat_ref[...] = xhat
    inv_ref[...] = jnp.broadcast_to(inv, inv_ref.shape)
    scaled = xhat * gain_ref[...]
    normed = scaled.astype(BF16)
    normed_ref[...] = jnp.transpose(scaled).astype(BF16)
    w_copy.wait()
    qkv = mm(normed, w_ref[...])
    qkv_ref[...] = qkv.astype(BF16)
    trans[...] = jnp.transpose(qkv).astype(BF16)
    for save in saves:
        save.start()

    for step in range(HEADS // 2):
        lo = step * pair
        keys = qkv_ref[:, pl.ds(width + lo, pair)]
        query_t = trans[pl.ds(lo, pair), :] * BF16(0.125)
        zero = jnp.zeros((head, rows), BF16)
        for j in range(2):
            part = query_t[j * head : (j + 1) * head]
            part = jnp.concatenate([part, zero] if j == 0 else [zero, part], axis=0)
            scores = mm(keys, part)
            top = jnp.max(scores, axis=0, keepdims=True)
            expo = jnp.exp(scores - top)
            share = 1.0 / jnp.sum(expo, axis=0, keepdims=True)
            probs = expo * share
            stats_out[pl.ds(2 * step + j, 1), :] = top
            stats_out[pl.ds(HEADS + 2 * step + j, 1), :] = share
            values_t = trans[pl.ds(2 * width + lo + j * head, head), :]
            attn_out[pl.ds(lo + j * head, head), :] = mm(values_t, probs.astype(BF16)).astype(BF16)

    for save in saves:
        save.wait()


def backward_kernel(n_seq, chip_bits, me_ref, pos_ref, w_proj_ref, stats_ref, *refs):
    (qkv_hbm, trans_hbm, w_hbm, xhat_hbm, normed_hbm, attn_hbm), refs = refs[:6], refs[6:]
    recv_hbm, refs = refs[: n_seq // 2], refs[n_seq // 2 :]
    outs, serial_grad_hbm, d_normed_hbm, refs = refs[:4], refs[4], refs[5], refs[6:]
    recv_ref, qkv_ref, trans_ref, w_ref, xhat_ref, normed_ref, attn_ref, refs = *refs[:7], refs[7:]
    sums, refs = refs[:4], refs[4:]
    serial_grad, d_normed_ref, d_attn, d_attn_t, d_qkv, gain_column, sems = refs
    width = w_proj_ref.shape[0]
    rows = xhat_ref.shape[0]
    capacity = recv_ref.shape[0] // n_seq
    head = width // HEADS
    pair = 2 * head
    me = me_ref[0]
    chips = n_seq // 2
    recv_parts = [recv_ref.at[pl.ds(2 * j * capacity, 2 * capacity)] for j in range(chips)]
    loads = [
        pltpu.make_async_copy(source, target, sems.at[i])
        for i, (source, target) in enumerate(
            (
                *zip(recv_hbm, recv_parts),
                (qkv_hbm, qkv_ref),
                (trans_hbm, trans_ref),
                (normed_hbm, normed_ref),
                (w_hbm, w_ref),
                (xhat_hbm, xhat_ref),
                (attn_hbm, attn_ref),
            )
        )
    ]
    body, tail = pl.ds(0, 4 * width), pl.ds(4 * width, LANES)
    saves = [
        pltpu.make_async_copy(source, target, sems.at[6 + chips + i])
        for i, (source, target) in enumerate(
            [
                *[(source.at[:, body], target.at[:, body]) for source, target in zip(sums, outs)],
                (serial_grad, serial_grad_hbm),
                (d_normed_ref, d_normed_hbm),
                *[(source.at[:, tail], target.at[:, tail]) for source, target in zip(sums, outs)],
            ]
        )
    ]

    for load in loads:
        load.start()
    place = hot(iota((rows, n_seq * capacity), 0) == pos_ref[...])
    for load in loads[:chips]:
        load.wait()
    grads = mm(place, recv_ref[...]).astype(BF16)
    serial_grad[...] = grads
    saves[4].start()
    d_attn[...] = mm(grads, w_proj_ref[...], NT).astype(BF16)
    d_attn_t[...] = mm(w_proj_ref[...], grads, NT).astype(BF16)
    for load in loads[chips : chips + 2]:
        load.wait()

    zero = jnp.zeros((head, rows), BF16)
    first = iota((rows, pair), 1) < head

    def alone(both, j):
        part = both[j * head : (j + 1) * head]
        return jnp.concatenate([part, zero] if j == 0 else [zero, part], axis=0)

    for step in range(HEADS // 2):
        lo = step * pair
        queries = qkv_ref[:, pl.ds(lo, pair)]
        values = qkv_ref[:, pl.ds(2 * width + lo, pair)]
        d_att_t = d_attn_t[pl.ds(lo, pair), :] * BF16(0.125)
        d_att = d_attn[:, pl.ds(lo, pair)]
        keys = qkv_ref[:, pl.ds(width + lo, pair)]
        query_t = trans_ref[pl.ds(lo, pair), :] * BF16(0.125)
        d_q, d_k, d_v = [], [], []
        for j in range(2):
            top = stats_ref[pl.ds(2 * step + j, 1), :]
            share = stats_ref[pl.ds(HEADS + 2 * step + j, 1), :]
            probs = jnp.exp(mm(keys, alone(query_t, j)) - top) * share
            d_probs = mm(values, alone(d_att_t, j))
            total = jnp.sum(d_probs * probs, axis=0, keepdims=True)
            d_scores = (probs * (d_probs - total)).astype(BF16)
            k_t = trans_ref[pl.ds(width + lo + j * head, head), :]
            d_q.append(mm(k_t, d_scores))
            d_k.append(mm(d_scores, queries))
            d_v.append(mm(probs.astype(BF16), d_att))
        d_qkv[:, pl.ds(lo, pair)] = jnp.transpose(jnp.concatenate(d_q, axis=0)).astype(BF16)
        d_qkv[:, pl.ds(width + lo, pair)] = jnp.where(
            first, d_k[0], d_k[1]
        ).astype(BF16)
        d_qkv[:, pl.ds(2 * width + lo, pair)] = jnp.where(
            first, d_v[0], d_v[1]
        ).astype(BF16)

    for load in loads[chips + 2 :]:
        load.wait()
    eighth = width // 8
    odd = lax.bitwise_and(me, 1)

    def sides(even_bit, odd_bit):
        even_side = lax.bitwise_and(lax.shift_right_logical(me, even_bit), 1)
        odd_side = lax.bitwise_and(lax.shift_right_logical(me, odd_bit), 1)
        mine = jnp.where(odd == 1, odd_side, even_side)
        return mine, even_side + odd_side - mine

    (mine, other), (mine_next, other_next) = (sides(*bits) for bits in chip_bits)
    starts = (
        ((1 - odd) * 2 + 1 - other, other_next),
        ((1 - odd) * 2 + other, other_next),
        (odd * 2 + 1 - mine, mine_next),
        (odd * 2 + mine, mine_next),
    )
    order = [
        pl.ds(pl.multiple_of((start * 2 + half) * eighth, eighth), eighth)
        for start, side in starts
        for half in (1 - side, side)
    ]
    for i in (0, 2):
        parts = order[2 * i : 2 * i + 4]
        of_qkv = mm(jnp.concatenate([normed_ref[part, :] for part in parts], axis=0), d_qkv[...])
        of_proj = mm(jnp.concatenate([attn_ref[part, :] for part in parts], axis=0), serial_grad[...])
        for j in range(2):
            lines = slice(2 * j * eighth, 2 * (j + 1) * eighth)
            sums[i + j][:, : 3 * width] = of_qkv[lines]
            sums[i + j][:, 3 * width : 4 * width] = of_proj[lines]
            saves[i + j].start()
    d_normed = mm(d_qkv[...], w_ref[...], NT)
    d_normed_ref[...] = d_normed
    saves[5].start()
    gain_row = jnp.sum(d_normed * xhat_ref[...], axis=0, keepdims=True)
    gain_column[...] = jnp.transpose(jnp.broadcast_to(gain_row, (LANES, width)))
    for i in range(4):
        parts = order[2 * i : 2 * i + 2]
        sums[i][:, 4 * width :] = jnp.concatenate([gain_column[part, :] for part in parts], axis=0)
        saves[6 + i].start()
    for save in saves:
        save.wait()


def residual_kernel(
    capacity, pos_ref, gain_ref, inv_ref, xhat_ref, serial_grad_ref, d_normed_ref, same_out, cross_out
):
    xhat = xhat_ref[...]
    rows = xhat.shape[0]
    scaled = d_normed_ref[...] * gain_ref[...]
    residual = inv_ref[:, 0:1] * (
        scaled
        - jnp.mean(scaled, axis=1, keepdims=True)
        - xhat * jnp.mean(scaled * xhat, axis=1, keepdims=True)
    )
    serial_dx = (serial_grad_ref[...].astype(F32) + residual).astype(BF16)
    returned = mm(column_hot(pos_ref[...], rows), serial_dx).astype(BF16)
    for j in range(same_out.shape[0] // capacity):
        lines = slice(j * capacity, (j + 1) * capacity)
        same_out[lines, :] = returned[2 * j * capacity : (2 * j + 1) * capacity]
        cross_out[lines, :] = returned[(2 * j + 1) * capacity : (2 * j + 2) * capacity]


def unpack_kernel(slot_ref, *refs):
    values = jnp.concatenate([ref[...] for ref in refs[:-1]], axis=0)
    refs[-1][...] = mm(column_hot(slot_ref[...], values.shape[0]), values).astype(BF16)


def split_kernel(side_ref, sums_ref, *refs):
    qkv_out, proj_out, gain_out = refs[-3:]
    width = proj_out.shape[1]
    qkv_out[...] = sums_ref[:, : 3 * width].astype(F32)
    proj_out[...] = sums_ref[:, 3 * width : 4 * width].astype(F32)
    gain_out[...] = jnp.transpose(sums_ref[:, 4 * width :].astype(F32))[0:1]


def exponent_of(largest):
    return jnp.clip(jnp.ceil(jnp.log(jnp.maximum(largest, 1e-30)) * 1.4426950408889634), -100.0, 120.0)


def encode(out_ref, total):
    width = total.shape[1] - LANES
    body, gain = total[:, :width], total[:, width : width + 1]
    exponent = exponent_of(jnp.max(jnp.abs(body), axis=1, keepdims=True))
    codes = jnp.round(body * (jnp.exp2(-exponent) * CODE_MAX))
    out_ref[:, :width] = codes.astype(jnp.int32).astype(jnp.int16)
    gain_exponent = exponent_of(jnp.abs(gain))
    scaled = gain * (jnp.exp2(-gain_exponent) * CODE_MAX)
    high = jnp.round(scaled)
    low = jnp.round((scaled - high) * DIGIT)
    lane = iota((total.shape[0], LANES), 1)
    tail = jnp.where(lane == 0, high, jnp.where(lane == 1, low, jnp.where(lane == 2, gain_exponent, exponent)))
    out_ref[:, width:] = tail.astype(jnp.int32).astype(jnp.int16)


def decode(codes):
    values = codes.astype(jnp.int32).astype(F32)
    width = values.shape[1] - LANES
    tail = values[:, width:]
    body = values[:, :width] * (jnp.exp2(tail[:, 3:4]) * (1.0 / CODE_MAX))
    gain = (tail[:, 0:1] + tail[:, 1:2] * (1.0 / DIGIT)) * (jnp.exp2(tail[:, 2:3]) * (1.0 / CODE_MAX))
    return jnp.concatenate([body, jnp.broadcast_to(gain, tail.shape)], axis=1)


def total_of(terms, part):
    half = terms[0].shape[0] // 2
    rows = {"all": slice(None), "first": slice(0, half), "second": slice(half, 2 * half)}[part]
    values = [ref[rows, :] for ref in terms]
    return functools.reduce(jnp.add, [decode(v) if v.dtype == jnp.int16 else v for v in values])


def message_kernel(part, *refs):
    encode(refs[-1], total_of(refs[:-1], part))


def sum_kernel(parts, *refs):
    refs[-1][...] = functools.reduce(jnp.add, [total_of([ref], p) for ref, p in zip(refs, parts)])


def pieces_kernel(parts, n_dp, plane_ref, *refs):
    terms, own, messages, total = refs[: len(parts)], refs[len(parts)], refs[len(parts) + 1 : -1], refs[-1]
    total[...] = functools.reduce(jnp.add, [total_of([ref], p) for ref, p in zip(terms, parts)])
    size = own.shape[0]

    def rows_of(distance):
        start = lax.bitwise_xor(plane_ref[0], distance) * size
        return total[pl.ds(pl.multiple_of(start, size), size), :]

    for k in range(1, n_dp):
        encode(messages[k - 1], rows_of(k))
    own[...] = rows_of(0)


def finish_kernel(*refs):
    refs[-1][...] = total_of(refs[:-1], "all").astype(BF16)


def whole(shape):
    return pl.BlockSpec(shape, lambda *_: (0,) * len(shape), pipeline_mode=pl.Buffered(1))


def params(mib):
    return pltpu.CompilerParams(vmem_limit_bytes=mib * MIB)


def shape_of(shape, dtype):
    return jax.ShapeDtypeStruct(shape, dtype)


def by_distance(blocks, axis):
    count = len(blocks)
    return [blocks[0]] + [
        lax.ppermute(blocks[k], axis, [(i, i ^ k) for i in range(count)]) for k in range(1, count)
    ]


def by_chip(messages):
    count = 2 * len(messages)
    return [messages[0]] + [
        lax.ppermute(messages[j], "seq", [(i, i ^ (2 * j)) for i in range(count)])
        for j in range(1, len(messages))
    ]


def chip_orders(n_seq):
    bits = list(range(1, n_seq.bit_length() - 1))
    middle = len(bits) // 2
    return bits, bits[middle:] + bits[:middle]


def chip_steps():
    n_seq, me = lax.axis_size("seq"), lax.axis_index("seq")
    odd = lax.bitwise_and(me, 1) == 1

    def side(bit):
        return lax.bitwise_and(lax.shift_right_logical(me, jnp.asarray(bit, me.dtype)), 1)

    steps = []
    for even_bit, odd_bit in zip(*chip_orders(n_seq)):
        pairs = [(i, i ^ (1 << (odd_bit if i & 1 else even_bit))) for i in range(n_seq)]
        steps.append((pairs, jnp.where(odd, side(odd_bit), side(even_bit))))
    return steps


def piece(terms, index, count):
    size = terms[0].shape[0] // count
    return functools.reduce(jnp.add, [lax.dynamic_slice_in_dim(t, index * size, size) for t in terms])


def core_pairs():
    return [(i, i ^ 1) for i in range(lax.axis_size("seq"))]


def small_kernel(kernel, outs, operands, scalars=0, scratch=(), name="sum"):
    in_smem = pl.BlockSpec(memory_space=pltpu.SMEM)
    in_vmem = pl.BlockSpec(memory_space=pltpu.VMEM)
    touched = sum(x.size * x.dtype.itemsize for x in (*operands, *outs))
    return pl.pallas_call(
        kernel,
        out_shape=outs,
        in_specs=[in_smem] * scalars + [in_vmem] * (len(operands) - scalars),
        out_specs=[in_vmem] * len(outs),
        scratch_shapes=list(scratch),
        compiler_params=params(20),
        cost_estimate=pl.CostEstimate(flops=2 * touched, bytes_accessed=touched, transcendentals=0),
        name=name,
    )(*operands)


def message(terms, part, name):
    rows, width = terms[0].shape
    if part == "all":
        spec = pl.BlockSpec((rows // 4, width), lambda i: (i, 0))
        return pl.pallas_call(
            functools.partial(message_kernel, part),
            grid=(4,),
            out_shape=shape_of((rows, width), jnp.int16),
            in_specs=[spec] * len(terms),
            out_specs=spec,
            compiler_params=params(60),
            cost_estimate=pl.CostEstimate(flops=2 * MIB, bytes_accessed=3 * MIB, transcendentals=0),
            name=name,
        )(*terms)
    rows = rows // 2
    return small_kernel(
        functools.partial(message_kernel, part), [shape_of((rows, width), jnp.int16)], terms, name=name
    )[0]


def first_step(quarters, steps):
    pass_on, pass_keep, own_on, own_keep = quarters
    got_on = lax.ppermute(pass_on, "seq", core_pairs())
    got_keep = lax.ppermute(pass_keep, "seq", core_pairs())
    sent = message([own_on, got_on], "all", "code_first")
    return [own_keep, got_keep, lax.ppermute(sent, "seq", steps[0][0])]


def second_step(terms, steps, later):
    sent = message(terms, "first", "code_second")
    sent, later = lax.optimization_barrier((sent, later))
    return terms, lax.ppermute(sent, "seq", steps[1][0]), later


def halves_of_plain(part, steps):
    for pairs, side in steps:
        got = lax.ppermute(piece([part], 1 - side, 2), "seq", pairs)
        part = piece([part], side, 2) + got
    return part


def reduce_over_planes(terms, got, steps):
    n_dp, plane = lax.axis_size("dp"), lax.axis_index("dp")
    rows, width = got.shape
    parts = ["second"] * len(terms) + ["all"]
    if len(steps) > 2 or rows // n_dp % 16:
        part = small_kernel(
            functools.partial(sum_kernel, parts), [shape_of((rows, width), F32)], [*terms, got]
        )[0]
        part = halves_of_plain(part, steps[2:])
        pieces = [piece([part], lax.bitwise_xor(plane, k), n_dp) for k in range(n_dp)]
        return functools.reduce(jnp.add, by_distance(pieces, "dp")).astype(BF16)
    size = rows // n_dp
    own, *sent = small_kernel(
        functools.partial(pieces_kernel, parts, n_dp),
        [shape_of((size, width), F32)] + [shape_of((size, width), jnp.int16)] * (n_dp - 1),
        [jnp.reshape(plane.astype(jnp.int32), (1,)), *terms, got],
        scalars=1,
        scratch=[pltpu.VMEM((rows, width), F32)],
        name="code_planes",
    )
    arrived = by_distance([own] + sent, "dp")
    return small_kernel(finish_kernel, [shape_of((size, width), BF16)], arrived, name="finish")[0]


def share_over_planes(part):
    n_dp, plane = lax.axis_size("dp"), lax.axis_index("dp")
    shares = jnp.stack(by_distance([part] * n_dp, "dp"))
    return jnp.concatenate(
        [lax.dynamic_index_in_dim(shares, lax.bitwise_xor(plane, p), keepdims=False) for p in range(n_dp)],
        axis=0,
    )


def share_in_plane(part, steps):
    for pairs, side in reversed(steps):
        other = lax.ppermute(part, "seq", pairs)
        part = jnp.where(
            side == 0, jnp.concatenate([part, other], axis=0), jnp.concatenate([other, part], axis=0)
        )
    return part


def write_half(side, sums, outs=()):
    half, width = sums.shape[0], (sums.shape[1] - LANES) // 4
    return pl.pallas_call(
        split_kernel,
        grid_spec=pltpu.PrefetchScalarGridSpec(
            num_scalar_prefetch=1,
            grid=(2,),
            in_specs=[pl.BlockSpec((half // 2, sums.shape[1]), lambda i, s: (i, 0))]
            + [pl.BlockSpec(memory_space=pl.ANY)] * len(outs),
            out_specs=[
                pl.BlockSpec((half // 2, 3 * width), lambda i, s: (2 * s[0] + i, 0)),
                pl.BlockSpec((half // 2, width), lambda i, s: (2 * s[0] + i, 0)),
                pl.BlockSpec((1, half // 2), lambda i, s: (0, 2 * s[0] + i)),
            ],
        ),
        out_shape=(
            shape_of((2 * half, 3 * width), F32),
            shape_of((2 * half, width), F32),
            shape_of((1, 2 * half), F32),
        ),
        input_output_aliases={2 + i: i for i in range(len(outs))},
        compiler_params=params(20),
        cost_estimate=pl.CostEstimate(flops=0, bytes_accessed=4 * MIB, transcendentals=0),
        name="split",
    )(side, sums, *outs)


def per_device(points, cotangent, dest, w_qkv, w_proj, gain):
    feats = points[0]
    grads = cotangent[0]
    rows, width = feats.shape
    n_seq = lax.axis_size("seq")
    capacity = 2 * (rows // n_seq)
    slots = n_seq * capacity
    block = capacity + EXTRA
    pairs = HEADS // 2
    pair = width // pairs
    sum_shape = (width // 4, 4 * width + LANES)
    me = jnp.reshape(lax.axis_index("seq").astype(jnp.int32), (1,))
    gain_row = gain.reshape(1, width)
    in_smem = pl.BlockSpec(memory_space=pltpu.SMEM)
    in_vmem = pl.BlockSpec(memory_space=pltpu.VMEM)
    in_hbm = pl.BlockSpec(memory_space=pl.ANY)
    stay_hbm = pl.BlockSpec(memory_space=pltpu.HBM)

    slot, same, cross, *feats_sent = pl.pallas_call(
        functools.partial(pack_kernel, n_seq, capacity),
        out_shape=[shape_of((1, rows), jnp.int32)]
        + [shape_of((slots // 2, width), BF16)] * 2
        + [shape_of((block, width), BF16)] * n_seq,
        in_specs=[in_smem] + [stay_hbm] * 3,
        out_specs=[in_vmem] * (3 + n_seq),
        scratch_shapes=[
            pltpu.VMEM((1, rows), jnp.int32),
            pltpu.VMEM((rows, width), BF16),
            pltpu.VMEM((rows, width), BF16),
            pltpu.SemaphoreType.DMA((3,)),
        ],
        compiler_params=params(60),
        cost_estimate=pl.CostEstimate(
            flops=4 * slots * rows * width, bytes_accessed=4 * MIB, transcendentals=0
        ),
        name="pack",
    )(me, dest, feats, grads)
    feats_got = by_distance(feats_sent, "seq")
    def by_core(same, cross):
        return small_kernel(
            functools.partial(pair_kernel, capacity),
            [shape_of((2 * capacity, width), BF16)] * (n_seq // 2),
            [same, lax.ppermute(cross, "seq", core_pairs())],
            name="pair_up",
        )

    messages = by_core(same, cross)
    feats_got, messages = lax.optimization_barrier((feats_got, messages))
    grads_got = by_chip(messages)

    pos, xhat, inv, normed, qkv, trans, attn_t, stats = pl.pallas_call(
        functools.partial(forward_kernel, n_seq, capacity),
        grid=(1,),
        out_shape=(
            shape_of((1, slots), jnp.int32),
            shape_of((rows, width), F32),
            shape_of((rows, LANES), F32),
            shape_of((rows, width), BF16),
            shape_of((rows, 3 * width), BF16),
            shape_of((2 * width, rows), BF16),
            shape_of((width, rows), BF16),
            shape_of((2 * HEADS, rows), F32),
        ),
        in_specs=[in_hbm, whole((1, width))] + [whole((block, width))] * n_seq,
        out_specs=[whole((1, slots))]
        + [in_hbm] * 5
        + [whole((width, rows)), whole((2 * HEADS, rows))],
        scratch_shapes=[
            pltpu.VMEM((width, 3 * width), BF16),
            pltpu.VMEM((rows, width), F32),
            pltpu.VMEM((rows, LANES), F32),
            pltpu.VMEM((rows, width), BF16),
            pltpu.VMEM((rows, 3 * width), BF16),
            pltpu.VMEM((3 * width, rows), BF16),
            pltpu.SemaphoreType.DMA((6,)),
        ],
        compiler_params=params(60),
        cost_estimate=pl.CostEstimate(
            flops=6 * rows * width * width + 8 * HEADS * rows * rows * pair,
            bytes_accessed=16 * MIB,
            transcendentals=HEADS * rows * rows,
        ),
        name="forward",
    )(w_qkv, gain_row, *feats_got)

    chip_bits = tuple(zip(*chip_orders(n_seq)))[:2]
    *quarters, serial_grad, d_normed = pl.pallas_call(
        functools.partial(backward_kernel, n_seq, chip_bits),
        grid=(1,),
        out_shape=[shape_of(sum_shape, F32)] * 4
        + [shape_of((rows, width), BF16), shape_of((rows, width), F32)],
        in_specs=[
            in_smem,
            whole((1, slots)),
            whole((width, width)),
            whole((2 * HEADS, rows)),
        ]
        + [in_hbm] * (6 + n_seq // 2),
        out_specs=[in_hbm] * 6,
        scratch_shapes=[
            pltpu.VMEM((slots, width), BF16),
            pltpu.VMEM((rows, 3 * width), BF16),
            pltpu.VMEM((2 * width, rows), BF16),
            pltpu.VMEM((width, 3 * width), BF16),
            pltpu.VMEM((rows, width), F32),
            pltpu.VMEM((rows, width), BF16),
            pltpu.VMEM((width, rows), BF16),
        ]
        + [pltpu.VMEM(sum_shape, F32)] * 4
        + [
            pltpu.VMEM((rows, width), BF16),
            pltpu.VMEM((rows, width), F32),
            pltpu.VMEM((rows, width), BF16),
            pltpu.VMEM((width, rows), BF16),
            pltpu.VMEM((rows, 3 * width), BF16),
            pltpu.VMEM((width, LANES), F32),
            pltpu.SemaphoreType.DMA((16 + n_seq // 2,)),
        ],
        compiler_params=params(60),
        cost_estimate=pl.CostEstimate(
            flops=12 * rows * width * width + 10 * HEADS * rows * rows * pair,
            bytes_accessed=16 * MIB,
            transcendentals=HEADS * rows * rows,
        ),
        name="backward",
    )(me, pos, w_proj, stats, qkv, trans, w_qkv, xhat, normed, attn_t, *grads_got)

    steps = chip_steps()
    terms = first_step(quarters, steps)
    same, cross = small_kernel(
        functools.partial(residual_kernel, capacity),
        [shape_of((slots // 2, width), BF16)] * 2,
        [pos, gain_row, inv, xhat, serial_grad, d_normed],
        name="residual",
    )
    terms, got, same = second_step(terms, steps, same)
    returned = by_chip(by_core(same, cross))
    part, returned = lax.optimization_barrier((reduce_over_planes(terms, got, steps), returned))
    own = share_in_plane(share_over_planes(part), steps)
    grad_local = small_kernel(
        unpack_kernel, [shape_of((rows, width), BF16)], [slot, *returned], name="unpack"
    )[0]
    own, grad_local = lax.optimization_barrier((own, grad_local))
    other = lax.ppermute(own, "seq", core_pairs())
    side = lax.bitwise_and(me, 1)
    outs = write_half(side, own)
    grad_qkv, grad_proj, gain_grad = write_half(1 - side, other, outs)
    return (grad_local[None], grad_qkv, grad_proj, gain_grad[0])


def solution(mesh):
    return jax.shard_map(
        per_device,
        mesh=mesh,
        in_specs=(P("dp", "seq", None), P("dp", "seq", None), P("dp", "seq"), P(), P(), P()),
        out_specs=(P("dp", "seq", None), P(), P(), P()),
        check_vma=False,
    )
```
